32 devices in a mesh: dp: 8 (over z, y), block: 4 (over x, core).
Axes of the slice: x: 2, y: 2, z: 4, core: 2. Of those that a mesh axis runs over, the one named last changes fastest.
Arguments:
- block_in: bfloat16 [8, 1024, 1024], P('dp', 'block'), may hold values from -6 to 6
- doc_starts: int32 [8, 4], P('dp'), may hold values from 0 to 1023, as said below
- norm1_gain: float32 [1024], replicated, may hold values from 0.5 to 1.5
- norm1_bias: float32 [1024], replicated, may hold values from -1.25 to 1.25
- w_in: bfloat16 [1024, 3072], P(None, 'dp'), may hold values from -0.1875 to 0.1875
- b_in: float32 [3072], replicated, may hold values from -1.25 to 1.25
- short_taps: float32 [3, 3072], replicated, may hold values from -3 to 3
- short_bias: float32 [3072], replicated, may hold values from -1.25 to 1.25
- filter_w1: float32 [33, 64], replicated, may hold values from -1 to 1
- filter_b1: float32 [64], replicated, may hold values from -6 to 6
- filter_w2: float32 [64, 64], replicated, may hold values from -0.75 to 0.75
- filter_b2: float32 [64], replicated, may hold values from -6 to 6
- filter_w3: float32 [64, 1024], replicated, may hold values from -0.0234375 to 0.0234375
- filter_decay: float32 [1024], replicated, may hold values from 0.5 to 25
- conv_bias: float32 [1024], replicated, may hold values from -6 to 6
- w_out: bfloat16 [1024, 1024], P(None, 'dp'), may hold values from -0.1875 to 0.1875
- b_out: float32 [1024], replicated, may hold values from -1.25 to 1.25
- norm2_gain: float32 [1024], replicated, may hold values from 0.5 to 1.5
- norm2_bias: float32 [1024], replicated, may hold values from -1.25 to 1.25
- w_up: bfloat16 [1024, 4096], P(None, 'dp'), may hold values from -0.1875 to 0.1875
- b_up: float32 [4096], replicated, may hold values from -1.25 to 1.25
- w_down: bfloat16 [4096, 1024], P(None, 'dp'), may hold values from -0.09375 to 0.09375
- b_down: float32 [1024], replicated, may hold values from -1.25 to 1.25
- cotangent: bfloat16 [8, 1024, 1024], P('dp', 'block'), may hold values from -6 to 6
Outputs:
- block_out: bfloat16 [8, 1024, 1024], P('dp', 'block')
- grad_in: float32 [8, 1024, 1024], P('dp', 'block')
- grad_norm1_gain: float32 [1024], replicated
- grad_norm1_bias: float32 [1024], replicated
- grad_w_in: float32 [1024, 3072], P(None, 'dp')
- grad_b_in: float32 [3072], replicated
- grad_short_taps: float32 [3, 3072], replicated
- grad_short_bias: float32 [3072], replicated
- grad_filter_w1: float32 [33, 64], replicated
- grad_filter_b1: float32 [64], replicated
- grad_filter_w2: float32 [64, 64], replicated
- grad_filter_b2: float32 [64], replicated
- grad_filter_w3: float32 [64, 1024], replicated
- grad_filter_decay: float32 [1024], replicated
- grad_conv_bias: float32 [1024], replicated
- grad_w_out: float32 [1024, 1024], P(None, 'dp')
- grad_b_out: float32 [1024], replicated
- grad_norm2_gain: float32 [1024], replicated
- grad_norm2_bias: float32 [1024], replicated
- grad_w_up: float32 [1024, 4096], P(None, 'dp')
- grad_b_up: float32 [4096], replicated
- grad_w_down: float32 [4096, 1024], P(None, 'dp')
- grad_b_down: float32 [1024], replicated
The draws below stay inside these ranges and needn't reach their ends.
Inputs may be any that keep to these rules, and one draw needn't show every extreme that they name: `doc_starts`: in each row the starts rise strictly from 0; one document begins within the first 256 positions and ends within the last 256.
All inputs are finite; a program needn't handle non-finite values.
Results may differ from the reference program's by a relative error of at most 0.0096.
Values may be sent and summed in bfloat16 or wider, within the bound.
No kernel may reach another device: no remote copies, remote signals or barrier semaphores. Data moves between devices by JAX's collectives and lax.ppermute only.
A program may use at most 448 MiB of HBM per device.

```python
import math
import jax
import jax.numpy as jnp
from jax import lax

D = 1024
FF = 4096
EMB = 33
FW = 64
DOCS = 4
BL = 256
ROWS = 8
SEQ = 1024


def draw_doc_starts(key, part):
    key = jax.random.fold_in(key, 11)
    gap_key, long_key = jax.random.split(key)
    most_gap = max((BL - 1) // (DOCS - 1), 1)
    gaps = jax.random.randint(gap_key, (ROWS, DOCS), 1, most_gap + 1)
    long_place = jax.random.randint(long_key, (ROWS, 1), 0, DOCS)
    doc_ids = jnp.arange(DOCS, dtype=jnp.int32)[None, :]
    before = doc_ids < long_place
    after = doc_ids > long_place
    gaps_before = jnp.where(before, gaps, 0)
    start_before = jnp.cumsum(gaps_before, axis=1) - gaps_before
    gaps_after = jnp.where(after, gaps, 0)
    total_after = jnp.sum(gaps_after, axis=1, keepdims=True)
    start_after = SEQ - total_after + jnp.cumsum(gaps_after, axis=1) - gaps_after
    return jnp.where(after, start_after, start_before).astype(jnp.int32)


def block_levels(rng, extent, cuts, least, high):
    level = 1.0
    for position, blocks in cuts:
        draws = jax.random.uniform(jax.random.fold_in(jax.random.fold_in(rng, 6), position), (blocks,), jnp.float32, least / len(cuts), high / len(cuts))
        level = level * jnp.repeat(jnp.exp(draws), extent[position] // blocks).reshape((-1,) + (1,) * (len(extent) - 1 - position))
    return level


def centred(stream_key, dims, scale, most, cuts=(), kind=jnp.bfloat16):
    result = scale * jax.random.normal(stream_key, dims, jnp.float32)
    if cuts:
        result = result * block_levels(stream_key, dims, cuts, -0.22, 0.18)
    return jnp.clip(result, -most, most).astype(kind)


def setup_inputs(seed: int = 0) -> dict:
    streams_of = jax.random.split(jax.random.key(seed), 25)
    return {
        "block_in": centred(streams_of[0], (ROWS, SEQ, D), 1.0, 6.0, ((0, 8), (1, 4))),
        "doc_starts": draw_doc_starts(jax.random.fold_in(streams_of[24], 71), 0),
        "norm1_gain": jnp.clip(1.0 + 0.1 * jax.random.normal(streams_of[2], (D,), jnp.float32), 0.5, 1.5),
        "norm1_bias": centred(streams_of[3], (D,), 0.2, 1.25, (), jnp.float32),
        "w_in": centred(streams_of[4], (D, 3 * D), D ** -0.5, 0.1875, ((1, 8),)),
        "b_in": centred(streams_of[5], (3 * D,), 0.2, 1.25, (), jnp.float32),
        "short_taps": centred(streams_of[6], (3, 3 * D), 0.5, 3.0, (), jnp.float32),
        "short_bias": centred(streams_of[7], (3 * D,), 0.2, 1.25, (), jnp.float32),
        "filter_w1": centred(streams_of[8], (EMB, FW), EMB ** -0.5, 1.0, (), jnp.float32),
        "filter_b1": centred(streams_of[9], (FW,), 1.0, 6.0, (), jnp.float32),
        "filter_w2": centred(streams_of[10], (FW, FW), FW ** -0.5, 0.75, (), jnp.float32),
        "filter_b2": centred(streams_of[11], (FW,), 1.0, 6.0, (), jnp.float32),
        "filter_w3": centred(streams_of[12], (FW, D), (FW * SEQ) ** -0.5, 0.0234375, (), jnp.float32),
        "filter_decay": jnp.clip(jnp.exp(jax.random.uniform(streams_of[13], (D,), jnp.float32, math.log(0.5), math.log(25.0))), 0.5, 25.0),
        "conv_bias": centred(streams_of[14], (D,), 1.0, 6.0, (), jnp.float32),
        "w_out": centred(streams_of[15], (D, D), D ** -0.5, 0.1875, ((1, 8),)),
        "b_out": centred(streams_of[16], (D,), 0.2, 1.25, (), jnp.float32),
        "norm2_gain": jnp.clip(1.0 + 0.1 * jax.random.normal(streams_of[17], (D,), jnp.float32), 0.5, 1.5),
        "norm2_bias": centred(streams_of[18], (D,), 0.2, 1.25, (), jnp.float32),
        "w_up": centred(streams_of[19], (D, FF), D ** -0.5, 0.1875, ((1, 8),)),
        "b_up": centred(streams_of[20], (FF,), 0.2, 1.25, (), jnp.float32),
        "w_down": centred(streams_of[21], (FF, D), FF ** -0.5, 0.09375, ((1, 8),)),
        "b_down": centred(streams_of[22], (D,), 0.2, 1.25, (), jnp.float32),
        "cotangent": centred(streams_of[23], (ROWS, SEQ, D), 1.0, 6.0, ((0, 8), (1, 4))),
    }


EPSILON = 1e-05
MOD_SHIFT = 0.05

@jax.custom_vjp
def low(v):
    return lax.optimization_barrier(v.astype(jnp.bfloat16)).astype(jnp.float32)

@jax.custom_vjp
def low_back(v):
    return v

def low_keep(v):
    return (low(v), None)

def low_pass(kept, grad):
    return (grad,)

def back_keep(v):
    return (v, None)

def back_low(kept, grad):
    return (low(grad),)
low.defvjp(low_keep, low_pass)
low_back.defvjp(back_keep, back_low)

def dot_high(left, right):
    return jnp.dot(left, right, precision=lax.Precision.HIGHEST, preferred_element_type=jnp.float32)

def layer_norm(values, gain, bias):
    mean = lax.optimization_barrier(jnp.mean(values, axis=-1, keepdims=True))
    centered = values - mean
    variance = lax.optimization_barrier(jnp.mean(centered * centered, axis=-1, keepdims=True))
    return centered * lax.rsqrt(variance + EPSILON) * gain + bias

def position_table(length, emb_dim):
    bands = (emb_dim - 1) // 2
    sample = jnp.arange(length).astype(jnp.float32)
    times = sample / (length - 1)
    frequency = jnp.linspace(0.0001, bands - 1, bands).astype(jnp.float32)
    angle = 2.0 * math.pi * sample[:, None] * frequency[None, :] / length
    return (jnp.concatenate([times[:, None], jnp.cos(angle), -jnp.sin(angle)], axis=1), times)

def long_filter(length, first_w, first_b, second_w, second_b, third_w, rates):
    table, times = position_table(length, first_w.shape[0])
    first = jnp.sin(dot_high(table, first_w) + first_b)
    second = jnp.sin(dot_high(first, second_w) + second_b)
    return dot_high(second, third_w) * (jnp.exp(-times[:, None] * rates[None, :]) + MOD_SHIFT)

def segment_ids(doc_starts, length):
    positions = jnp.arange(length, dtype=jnp.int32)
    return lax.optimization_barrier(jnp.sum((doc_starts[..., None, :] <= positions[:, None]).astype(jnp.int32), axis=-1)) - 1

def masked_conv(inner, kernel, segment):
    length = inner.shape[0]
    size = 2 * length
    kernel_spec = jnp.fft.rfft(kernel, n=size, axis=0)
    total = jnp.zeros_like(inner)
    for doc in range(DOCS):
        mask = (segment == doc).astype(inner.dtype)[:, None]
        spec = jnp.fft.rfft(inner * mask, n=size, axis=0)
        total = total + mask * jnp.fft.irfft(spec * kernel_spec, n=size, axis=0)[:length]
    return total

def short_conv(proj, segment, short_taps, short_bias):
    prev_one = jnp.concatenate([jnp.zeros_like(proj[:1]), proj[:-1]], axis=0)
    prev_two = jnp.concatenate([jnp.zeros_like(proj[:2]), proj[:-2]], axis=0)
    keep_one = jnp.concatenate([jnp.zeros((1,), jnp.bool_), segment[1:] == segment[:-1]]).astype(proj.dtype)[:, None]
    keep_two = jnp.concatenate([jnp.zeros((2,), jnp.bool_), segment[2:] == segment[:-2]]).astype(proj.dtype)[:, None]
    return short_bias + short_taps[0] * proj + short_taps[1] * prev_one * keep_one + short_taps[2] * prev_two * keep_two

def row_forward(row_values, segment, kernel, weights):
    normed = low(layer_norm(row_values, weights[0], weights[1]))
    proj = low_back(dot_high(normed, weights[2]) + weights[3])
    short = short_conv(proj, segment, weights[4], weights[5])
    gate_part = short[:, :D]
    mult = short[:, D:2 * D]
    value = short[:, 2 * D:]
    inner = value * mult
    mixed = masked_conv(inner, kernel, segment) + weights[12] * inner
    gated = low(gate_part * mixed)
    branch = low_back(dot_high(gated, weights[13]) + weights[14])
    resid = row_values + branch
    normed2 = low(layer_norm(resid, weights[15], weights[16]))
    hidden = low_back(dot_high(normed2, weights[17]) + weights[18])
    act = low(jax.nn.gelu(hidden, approximate=False))
    return resid + dot_high(act, weights[19]) + weights[20]

def reference(block_in, doc_starts, norm1_gain, norm1_bias, w_in, b_in, short_taps, short_bias, filter_w1, filter_b1, filter_w2, filter_b2, filter_w3, filter_decay, conv_bias, w_out, b_out, norm2_gain, norm2_bias, w_up, b_up, w_down, b_down, cotangent):
    length = block_in.shape[1]
    segment = segment_ids(doc_starts, length)
    params = (norm1_gain, norm1_bias, w_in.astype(jnp.float32), b_in, short_taps, short_bias, filter_w1, filter_b1, filter_w2, filter_b2, filter_w3, filter_decay, conv_bias, w_out.astype(jnp.float32), b_out, norm2_gain, norm2_bias, w_up.astype(jnp.float32), b_up, w_down.astype(jnp.float32), b_down)

    def whole(inputs, weights):
        kernel = long_filter(length, weights[6], weights[7], weights[8], weights[9], weights[10], weights[11])

        def one_row(pair):
            return row_forward(pair[0], pair[1], kernel, weights)
        return lax.map(jax.checkpoint(one_row), (inputs, segment))
    output, pullback = jax.vjp(whole, block_in.astype(jnp.float32), params)
    grad_in, grads = pullback(cotangent.astype(jnp.float32))
    return (output.astype(jnp.bfloat16), grad_in, grads[0], grads[1], grads[2], grads[3], grads[4], grads[5], grads[6], grads[7], grads[8], grads[9], grads[10], grads[11], grads[12], grads[13], grads[14], grads[15], grads[16], grads[17], grads[18], grads[19], grads[20])
```

```python
import math

import jax
import jax.numpy as jnp
import numpy as np
from jax import lax
from jax.sharding import PartitionSpec as P

EPSILON = 1e-05
MOD_SHIFT = 0.05
HIGHEST = lax.Precision.HIGHEST
HIGH = lax.Precision.HIGH
LOW = jnp.bfloat16
WIDE = jnp.float32


def dot_high(left, right):
    return jnp.dot(left, right, precision=HIGHEST, preferred_element_type=WIDE)


def dot_near(left, right):
    return jnp.dot(left, right, precision=HIGH, preferred_element_type=WIDE)


def dot_plain(left, right):
    return jnp.dot(left, right, preferred_element_type=WIDE)


def dot_first(left, right):
    return lax.dot_general(left, right, (((0,), (0,)), ((), ())), preferred_element_type=WIDE)


def dot_last(left, right):
    return lax.dot_general(left, right, (((1,), (1,)), ((), ())), preferred_element_type=WIDE)


def layer_norm(values, gain, bias):
    mean = jnp.mean(values, axis=-1, keepdims=True)
    centered = values - mean
    variance = jnp.mean(centered * centered, axis=-1, keepdims=True)
    return centered * lax.rsqrt(variance + EPSILON) * gain + bias


def exact_gelu(values):
    return jax.nn.gelu(values, approximate=False)


def position_table(length, emb_dim):
    bands = (emb_dim - 1) // 2
    sample = np.arange(length, dtype=np.float32)
    times = sample / np.float32(length - 1)
    frequency = np.linspace(0.0001, bands - 1, bands).astype(np.float32)
    angle = np.float32(2.0 * math.pi) * sample[:, None] * frequency[None, :] / np.float32(length)
    table = np.concatenate([times[:, None], np.cos(angle), -np.sin(angle)], axis=1)
    return (table.astype(np.float32), times)


def transform_tables(block_len):
    span = 2 * block_len
    frequency = np.arange(block_len)
    sample = np.arange(block_len)
    is_zero = (frequency == 0)[:, None]
    angle = 2.0 * math.pi * (frequency[:, None] * sample[None, :] % span) / span
    alternate = np.where(sample % 2 == 0, 1.0, -1.0)
    real_rows = np.cos(angle)
    imag_rows = np.where(is_zero, alternate[None, :], -np.sin(angle))
    forward_table = np.concatenate([real_rows, imag_rows], axis=0)
    outputs = sample + block_len
    out_angle = 2.0 * math.pi * (outputs[:, None] * frequency[None, :] % span) / span
    out_alternate = np.where(outputs % 2 == 0, 1.0, -1.0)
    zero_col = (frequency == 0)[None, :]
    real_cols = np.where(zero_col, 1.0, 2.0) * np.cos(out_angle) / span
    imag_cols = np.where(zero_col, out_alternate[:, None] / span, -2.0 * np.sin(out_angle) / span)
    inverse_table = np.concatenate([real_cols, imag_cols], axis=1)
    parity = np.where(frequency % 2 == 0, 1.0, -1.0)
    sign = np.concatenate([parity, np.where(frequency == 0, 1.0, parity)])
    edge = (frequency == 0).astype(np.float32)[:, None]
    return tuple(item.astype(np.float32) for item in (forward_table, inverse_table, sign, edge))


def spectral_product(left, right, edge):
    half = left.shape[-2] // 2
    left_re, left_im = (left[..., :half, :], left[..., half:, :])
    right_re, right_im = (right[..., :half, :], right[..., half:, :])
    inside = 1.0 - edge
    out_re = left_re * right_re - inside * left_im * right_im
    out_im = inside * (left_re * right_im + left_im * right_re) + edge * left_im * right_im
    return jnp.concatenate([out_re, out_im], axis=-2)


def spectral_back(grad, other, edge):
    half = grad.shape[-2] // 2
    grad_re, grad_im = (grad[..., :half, :], grad[..., half:, :])
    other_re, other_im = (other[..., :half, :], other[..., half:, :])
    inside = 1.0 - edge
    back_re = grad_re * other_re + inside * grad_im * other_im
    back_im = inside * (grad_im * other_re - grad_re * other_im) + edge * grad_im * other_im
    return jnp.concatenate([back_re, back_im], axis=-2)


class Grid:
    def __init__(self, count_dp, count_block):
        self.count_dp = count_dp
        self.count_block = count_block
        self.row = lax.axis_index("dp")
        self.place = lax.axis_index("block")
        self.dp_steps = []
        bit = 1
        while bit < count_dp:
            self.dp_steps.append((bit | (bit >> 1) if bit == 4 else bit, 0))
            bit *= 2
        self.chip_steps = []
        bit = 2
        while bit < count_block:
            self.chip_steps.append((0, bit | (bit >> 1) if bit == 4 else bit))
            bit *= 2
        self.core_step = (0, 1)

    def swap(self, value, step):
        pairs = []
        for row in range(self.count_dp):
            for place in range(self.count_block):
                to = (row ^ step[0]) * self.count_block + (place ^ step[1])
                pairs.append((row * self.count_block + place, to))
        return lax.ppermute(value, ("dp", "block"), pairs)

    def gather(self, value, steps):
        held = value[None]
        for step in steps:
            held = jnp.concatenate([held, self.swap(held, step)], axis=0)
        return held

    def scatter(self, held, steps):
        for step in reversed(steps):
            half = held.shape[0] // 2
            arrived = self.swap(held[half:], step)
            held = (held[:half].astype(WIDE) + arrived.astype(WIDE)).astype(held.dtype)
        return held[0]


def offsets_of(steps):
    offsets = [(0, 0)]
    for step in steps:
        offsets = offsets + [(a ^ step[0], b ^ step[1]) for a, b in offsets]
    return offsets


def pick(held, places):
    return jnp.concatenate(
        [lax.dynamic_slice_in_dim(held, places[i], 1, 0) for i in range(len(places))], axis=0
    )


def places_of(steps, wanted):
    return wanted


def lookup(table, index):
    return lax.dynamic_index_in_dim(jnp.asarray(np.asarray(table, np.int32)), index, 0, keepdims=False)


def local(
    block_in,
    doc_starts,
    norm1_gain,
    norm1_bias,
    w_in,
    b_in,
    short_taps,
    short_bias,
    filter_w1,
    filter_b1,
    filter_w2,
    filter_b2,
    filter_w3,
    filter_decay,
    conv_bias,
    w_out,
    b_out,
    norm2_gain,
    norm2_bias,
    w_up,
    b_up,
    w_down,
    b_down,
    cotangent,
):
    count_dp, blocks = lax.axis_size("dp"), lax.axis_size("block")
    grid = Grid(count_dp, blocks)
    row, place = grid.row, grid.place
    chips, core, chip = blocks // 2, place % 2, place // 2
    _, block_len, width = block_in.shape
    length = block_len * blocks
    hidden_width = w_up.shape[1] * count_dp
    dp_steps, chip_steps, core_step = grid.dp_steps, grid.chip_steps, grid.core_step
    block_steps = chip_steps + [core_step]

    def dp_places(steps):
        code = {a: i for i, (a, _) in enumerate(offsets_of(steps))}
        return [lookup([code[k ^ r] for r in range(count_dp)], row) for k in range(count_dp)]

    def block_places(steps):
        code = {b: i for i, (_, b) in enumerate(offsets_of(steps))}
        return [lookup([code[k ^ r] for r in range(blocks)], place) for k in range(blocks)]

    def pair_places(steps):
        code = {pair: i for i, pair in enumerate(offsets_of(steps))}
        flat = row * chips + chip
        return [
            lookup(
                [code[(k ^ r, (x ^ c) * 2)] for r in range(count_dp) for c in range(chips)], flat
            )
            for k in range(count_dp)
            for x in range(chips)
        ]

    def inverse_places(steps, count, mine, part):
        return [mine ^ offset[part] for offset in offsets_of(steps)]

    def rotated(steps, turn):
        turn = turn % len(steps)
        return steps[turn:] + steps[:turn]

    shard_in = w_in.shape[1]
    group = math.gcd(width, shard_in)
    groups_here, share = shard_in // group, group // blocks
    channels = width // blocks

    def own(values, lead=()):
        total = values.shape[-1]
        split = values.reshape(*values.shape[:-1], total // group, blocks, share)
        kept = lax.dynamic_index_in_dim(split, place, split.ndim - 2, keepdims=False)
        return kept.reshape(*values.shape[:-1], total // blocks)

    in_turned = w_in.T.reshape(groups_here, blocks, share, width)
    in_own = lax.dynamic_index_in_dim(in_turned, place, 1, keepdims=False)
    in_orders = [rotated(dp_steps, i) for i in range(groups_here)]
    in_parts = [
        pick(grid.gather(in_own[i], in_orders[i]), dp_places(in_orders[i]))
        for i in range(groups_here)
    ]
    in_rows = jnp.stack(in_parts, axis=1).reshape(3 * channels, width)

    inputs = block_in.astype(WIDE).reshape(block_len, width)
    normed, norm1_back = jax.vjp(layer_norm, inputs, norm1_gain, norm1_bias)
    normed_low = normed.astype(LOW)
    normed_all = pick(grid.gather(normed_low, block_steps), block_places(block_steps)).reshape(
        length, width
    )

    out_order = dp_steps[::-1] + block_steps
    out_split = w_out.reshape(width // group, blocks, share, w_out.shape[1])
    out_own = lax.dynamic_index_in_dim(out_split, place, 1, keepdims=False).reshape(
        channels, w_out.shape[1]
    )
    out_held = grid.gather(out_own, out_order).reshape(blocks, count_dp, channels, w_out.shape[1])
    out_places = dp_places(dp_steps[::-1])
    full_out = jnp.concatenate(
        [lax.dynamic_slice_in_dim(out_held, p, 1, 1) for p in out_places], axis=1
    )
    full_out = full_out.transpose(0, 2, 1, 3).reshape(width, width)

    pair_steps = dp_steps + chip_steps
    piece = w_up.shape[1] // blocks
    up_own = lax.dynamic_slice_in_dim(w_up, place_column(core, chip, chips) * piece, piece, 1)
    up_own = up_own.reshape(2, width // 2, piece)
    down_own = w_down.reshape(count_dp, 2 * chips, piece, w_down.shape[1])
    down_own = lax.dynamic_index_in_dim(down_own, core * chips + chip, 1, keepdims=False)
    down_own = down_own.reshape(2, count_dp // 2 * piece, w_down.shape[1])
    ff_orders = [rotated(pair_steps, i) for i in range(4)]
    up_parts = [
        pick(grid.gather(up_own[i], ff_orders[i]), pair_places(ff_orders[i])) for i in range(2)
    ]
    down_parts = [
        pick(grid.gather(down_own[i], ff_orders[2 + i]), pair_places(ff_orders[2 + i]))
        for i in range(2)
    ]
    half_hidden = hidden_width // 2
    up_here = jnp.concatenate(
        [part.transpose(1, 0, 2).reshape(width // 2, half_hidden) for part in up_parts], axis=0
    )
    down_here = jnp.stack(
        [
            part.reshape(count_dp, chips, count_dp // 2, piece, w_down.shape[1]).transpose(
                2, 1, 3, 0, 4
            )
            for part in down_parts
        ],
        axis=0,
    ).reshape(half_hidden, width)
    b_up_here = lax.dynamic_index_in_dim(
        b_up.reshape(count_dp, 2, chips * piece), core, 1, keepdims=False
    ).reshape(half_hidden)
    cot_flat = cotangent.reshape(block_len, width)
    cot_pair = jnp.concatenate([cot_flat, grid.swap(cot_flat, core_step)], axis=0)

    forward_table, inverse_table, sign, edge = transform_tables(block_len)
    starts = doc_starts[0]
    positions = jnp.arange(length, dtype=jnp.int32)
    segment = jnp.sum((starts[None, :] <= positions[:, None]).astype(jnp.int32), axis=-1) - 1
    keep_one = jnp.concatenate([jnp.zeros((1,), WIDE), (segment[1:] == segment[:-1]).astype(WIDE)])
    keep_two = jnp.concatenate([jnp.zeros((2,), WIDE), (segment[2:] == segment[:-2]).astype(WIDE)])
    keep_one, keep_two = keep_one[:, None], keep_two[:, None]
    num_docs = doc_starts.shape[1]
    long_doc = jnp.sum((starts <= block_len).astype(jnp.int32)) - 1
    long_mask = (segment == long_doc).astype(WIDE)[:, None]
    first_segment, last_segment = segment[:block_len], segment[length - block_len :]
    short_early, short_masks = [], []
    for number in range(num_docs - 1):
        early = number < long_doc
        doc = jnp.where(early, number, number + 1)
        where = jnp.where(early, first_segment, last_segment)
        short_early.append(early.astype(WIDE))
        short_masks.append((where == doc).astype(WIDE)[:, None])

    def spread(values):
        masked = values * long_mask
        parts = [masked[i * block_len : (i + 1) * block_len] for i in range(blocks)]
        first, last = values[:block_len], values[length - block_len :]
        for early, mask in zip(short_early, short_masks):
            parts.append(mask * (early * first + (1.0 - early) * last))
        return jnp.concatenate(parts, axis=1)

    def collect(values):
        parts = [
            values[:, i * channels : (i + 1) * channels] for i in range(blocks + num_docs - 1)
        ]
        first, last = jnp.zeros_like(parts[0]), jnp.zeros_like(parts[0])
        for early, mask, part in zip(short_early, short_masks, parts[blocks:]):
            first = first + early * mask * part
            last = last + (1.0 - early) * mask * part
        joined = jnp.concatenate(parts[:blocks], axis=0) * long_mask
        middle = jnp.zeros((length - 2 * block_len, channels), WIDE)
        return joined + jnp.concatenate([first, middle, last], axis=0)

    def cut(values, count):
        return [values[:, i * channels : (i + 1) * channels] for i in range(count)]

    table, times = position_table(length, filter_w1.shape[0])

    def filter_spectra(params):
        first = jnp.sin(dot_high(table, params[0]) + params[1])
        second = jnp.sin(dot_high(first, params[2]) + params[3])
        kernel = dot_high(second, params[4]) * (
            jnp.exp(-times[:, None] * params[5][None, :]) + MOD_SHIFT
        )
        pieces = jnp.concatenate(
            [kernel[i * block_len : (i + 1) * block_len] for i in range(blocks)], axis=1
        )
        halves = dot_near(forward_table, pieces)
        earlier = jnp.concatenate(
            [jnp.zeros((2 * block_len, channels), WIDE), halves[:, : (blocks - 1) * channels]],
            axis=1,
        )
        return earlier + sign[:, None] * halves

    spectra_flat, filter_back = jax.vjp(
        filter_spectra,
        (filter_w1, filter_b1, filter_w2, filter_b2, own(filter_w3), own(filter_decay)),
    )
    spectra = cut(spectra_flat, blocks)

    proj = dot_last(normed_all, in_rows) + own(b_in)
    taps, short_shift = own(short_taps), own(short_bias)
    three = 3 * channels
    prev_one = jnp.concatenate([jnp.zeros((1, three), WIDE), proj[:-1]], axis=0) * keep_one
    prev_two = jnp.concatenate([jnp.zeros((2, three), WIDE), proj[:-2]], axis=0) * keep_two
    short = short_shift + taps[0] * proj + taps[1] * prev_one + taps[2] * prev_two
    gate_part, mult, value = cut(short, 3)
    inner = value * mult
    direct = own(conv_bias)

    entries = cut(dot_near(forward_table, spread(inner)), blocks + num_docs - 1)
    totals = []
    for i in range(blocks):
        total = spectral_product(entries[i], spectra[0], edge)
        for j in range(i):
            total = total + spectral_product(entries[j], spectra[i - j], edge)
        totals.append(total)
    for entry in entries[blocks:]:
        totals.append(spectral_product(entry, spectra[0], edge))
    mixed = collect(dot_near(inverse_table, jnp.concatenate(totals, axis=1))) + direct * inner
    gated_low = (gate_part * mixed).astype(LOW)

    block_offsets = [b for _, b in offsets_of(block_steps)]
    gated_parts = []
    for offset in block_offsets:
        part = lax.dynamic_slice_in_dim(gated_low, (place ^ offset) * block_len, block_len, 0)
        gated_parts.append(grid.swap(part, (0, offset)) if offset else part)
    gated_rows = jnp.concatenate(gated_parts, axis=1)
    resid = inputs + dot_plain(gated_rows, full_out) + b_out
    normed2, norm2_back = jax.vjp(layer_norm, resid, norm2_gain, norm2_bias)
    normed2_low = normed2.astype(LOW)

    pair = jnp.concatenate([normed2_low, grid.swap(normed2_low, core_step)], axis=0)
    hidden = dot_plain(pair, up_here) + b_up_here
    act, gelu_back = jax.vjp(exact_gelu, hidden)
    act_low = act.astype(LOW)
    grad_act = dot_last(cot_pair, down_here)
    grad_hidden = gelu_back(grad_act)[0].astype(LOW)
    grad_pair = dot_last(grad_hidden, up_here)
    grad_normed2 = grad_pair[:block_len] + grid.swap(
        grad_pair[block_len:].astype(LOW), core_step
    ).astype(WIDE)
    out_pair = dot_plain(act_low, down_here)
    output = (
        resid
        + out_pair[:block_len]
        + grid.swap(out_pair[block_len:].astype(LOW), core_step).astype(WIDE)
        + b_down
    )
    block_out = output.astype(LOW)[None]
    grad_down_here = dot_first(act_low, cot_pair).astype(LOW)
    grad_up_here = dot_first(pair, grad_hidden).astype(LOW)
    grad_b_up_here = jnp.sum(grad_hidden.astype(WIDE), axis=0)
    grad_b_down = jnp.sum(cot_flat.astype(WIDE), axis=0)

    def send_home(natural, order):
        wanted = [
            ((row ^ a) * chips + (chip ^ (b >> 1))) for a, b in offsets_of(order)
        ]
        return grid.scatter(pick(natural, wanted), order)

    up_grads = [
        send_home(
            grad_up_here[i * (width // 2) : (i + 1) * (width // 2)]
            .reshape(width // 2, count_dp * chips, piece)
            .transpose(1, 0, 2),
            ff_orders[i],
        )
        for i in range(2)
    ]
    down_split = grad_down_here.reshape(
        2, count_dp // 2, chips, piece, count_dp, w_down.shape[1]
    )
    down_grads = [
        send_home(
            down_split[i]
            .transpose(3, 1, 0, 2, 4)
            .reshape(count_dp * chips, count_dp // 2 * piece, w_down.shape[1]),
            ff_orders[2 + i],
        )
        for i in range(2)
    ]

    resid_part, grad_gain_two, grad_bias_two = norm2_back(grad_normed2)
    grad_resid = cot_flat.astype(WIDE) + resid_part
    grad_branch = grad_resid.astype(LOW)
    grad_b_out = jnp.sum(grad_branch.astype(WIDE), axis=0)
    grad_gated_rows = dot_last(grad_branch, full_out).astype(LOW)
    grad_out_here = dot_first(gated_rows, grad_branch).astype(LOW)
    grad_out_split = grad_out_here.reshape(blocks, channels, count_dp, w_out.shape[1]).transpose(
        0, 2, 1, 3
    )
    out_wanted = [row ^ a for a, _ in offsets_of(dp_steps[::-1])]
    grad_out_split = jnp.concatenate(
        [lax.dynamic_slice_in_dim(grad_out_split, p, 1, 1) for p in out_wanted], axis=1
    ).reshape(blocks * count_dp, channels, w_out.shape[1])
    out_grad = grid.scatter(grad_out_split, out_order)

    grad_parts = []
    for index, offset in enumerate(block_offsets):
        part = grad_gated_rows[:, index * channels : (index + 1) * channels]
        grad_parts.append((grid.swap(part, (0, offset)) if offset else part)[None])
    grad_gated = pick(jnp.concatenate(grad_parts, axis=0), block_places(block_steps))
    grad_gated = grad_gated.reshape(length, channels).astype(WIDE)

    grad_gate_part = grad_gated * mixed
    grad_mixed = grad_gated * gate_part
    grad_conv_bias = jnp.sum(grad_mixed * inner, axis=0)
    grad_totals = cut(
        lax.dot_general(
            inverse_table,
            spread(grad_mixed),
            (((0,), (0,)), ((), ())),
            precision=HIGH,
            preferred_element_type=WIDE,
        ),
        blocks + num_docs - 1,
    )
    grad_entries = []
    grad_lags = [None] * blocks
    for i in range(blocks + num_docs - 1):
        lag = spectral_back(grad_totals[i], entries[i], edge)
        grad_lags[0] = lag if grad_lags[0] is None else grad_lags[0] + lag
        grad_entries.append(spectral_back(grad_totals[i], spectra[0], edge))
    for j in range(blocks):
        for i in range(j + 1, blocks):
            grad_entries[j] = grad_entries[j] + spectral_back(
                grad_totals[i], spectra[i - j], edge
            )
            lag = spectral_back(grad_totals[i], entries[j], edge)
            grad_lags[i - j] = lag if grad_lags[i - j] is None else grad_lags[i - j] + lag
    filter_grads = filter_back(jnp.concatenate(grad_lags, axis=1))[0]
    grad_inner = (
        collect(
            lax.dot_general(
                forward_table,
                jnp.concatenate(grad_entries, axis=1),
                (((0,), (0,)), ((), ())),
                precision=HIGH,
                preferred_element_type=WIDE,
            )
        )
        + direct * grad_mixed
    )
    grad_short = jnp.concatenate([grad_gate_part, grad_inner * value, grad_inner * mult], axis=1)
    grad_taps = jnp.stack(
        [
            jnp.sum(grad_short * proj, axis=0),
            jnp.sum(grad_short * prev_one, axis=0),
            jnp.sum(grad_short * prev_two, axis=0),
        ],
        axis=0,
    )
    grad_short_bias = jnp.sum(grad_short, axis=0)
    pass_one = grad_short * keep_one
    pass_two = grad_short * keep_two
    grad_proj = (
        taps[0] * grad_short
        + taps[1] * jnp.concatenate([pass_one[1:], jnp.zeros((1, three), WIDE)], axis=0)
        + taps[2] * jnp.concatenate([pass_two[2:], jnp.zeros((2, three), WIDE)], axis=0)
    )
    grad_proj_low = grad_proj.astype(LOW)
    grad_b_in = jnp.sum(grad_proj_low.astype(WIDE), axis=0)
    grad_in_rows = dot_first(grad_proj_low, normed_all).astype(LOW)
    grad_in_split = grad_in_rows.reshape(count_dp, groups_here, share, width)
    in_grads = []
    for i in range(groups_here):
        wanted = [row ^ a for a, _ in offsets_of(in_orders[i])]
        in_grads.append(grid.scatter(pick(grad_in_split[:, i], wanted), in_orders[i]))
    grad_normed_part = dot_plain(grad_proj_low, in_rows).astype(LOW).reshape(
        blocks, block_len, width
    )
    grad_normed = grid.scatter(
        pick(grad_normed_part, [place ^ offset for offset in block_offsets]), block_steps
    ).astype(WIDE)
    input_part, grad_gain_one, grad_bias_one = norm1_back(grad_normed)
    grad_input = (grad_resid + input_part)[None]

    def all_places(value):
        return pick(grid.gather(value, block_steps), block_places(block_steps))

    in_whole = all_places(jnp.stack(in_grads, axis=0))
    in_whole = in_whole.transpose(1, 0, 2, 3).reshape(shard_in, width).T.astype(WIDE)
    out_whole = all_places(out_grad).reshape(blocks, width // group, share, w_out.shape[1])
    out_whole = out_whole.transpose(1, 0, 2, 3).reshape(width, w_out.shape[1]).astype(WIDE)
    core_major = [b for c in range(2) for b in range(c, blocks, 2)]
    up_whole = all_places(jnp.concatenate(up_grads, axis=0))
    up_whole = jnp.concatenate([up_whole[b] for b in core_major], axis=1).astype(WIDE)
    down_whole = all_places(jnp.concatenate(down_grads, axis=0))
    down_whole = jnp.stack([down_whole[b] for b in core_major], axis=0).reshape(
        2 * chips, count_dp, piece, w_down.shape[1]
    )
    down_whole = down_whole.transpose(1, 0, 2, 3).reshape(hidden_width, w_down.shape[1])
    down_whole = down_whole.astype(WIDE)

    shared = [
        grad_gain_one,
        grad_bias_one,
        grad_b_out,
        grad_gain_two,
        grad_bias_two,
        grad_b_down,
        filter_grads[0],
        filter_grads[1],
        filter_grads[2],
        filter_grads[3],
    ]
    up_home = jnp.zeros((2, half_hidden), WIDE)
    up_home = lax.dynamic_update_slice_in_dim(up_home, grad_b_up_here[None], core, 0)
    shared.append(up_home)
    flat = jnp.concatenate([item.reshape(-1) for item in shared])
    chunk = -(-flat.shape[0] // (blocks * 128)) * 128
    flat = jnp.pad(flat, (0, chunk * blocks - flat.shape[0])).reshape(blocks, chunk)
    shared_part = grid.scatter(
        pick(flat, [place ^ offset for offset in block_offsets]), block_steps
    )
    parted = [
        grad_b_in[None],
        grad_taps,
        grad_short_bias[None],
        filter_grads[4],
        filter_grads[5][None],
        grad_conv_bias[None],
    ]
    joined = jnp.concatenate([shared_part] + [item.reshape(-1) for item in parted])
    for step in dp_steps:
        joined = joined + grid.swap(joined, step)
    every = all_places(joined)
    whole_flat = every[:, :chunk].reshape(-1)
    shared_out, at = [], 0
    for item in shared:
        shared_out.append(whole_flat[at : at + item.size].reshape(item.shape))
        at += item.size
    parted_out, at = [], chunk
    for item in parted:
        lead, size = item.shape[0], item.size
        values = every[:, at : at + size].reshape(blocks, lead, item.shape[1] // share, share)
        parted_out.append(values.transpose(1, 2, 0, 3).reshape(lead, item.shape[1] * blocks))
        at += size
    grad_b_up = shared_out[10].reshape(2, count_dp, chips * piece)
    grad_b_up = grad_b_up.transpose(1, 0, 2).reshape(hidden_width)
    return (
        block_out,
        grad_input,
        shared_out[0],
        shared_out[1],
        in_whole,
        parted_out[0][0],
        parted_out[1],
        parted_out[2][0],
        shared_out[6],
        shared_out[7],
        shared_out[8],
        shared_out[9],
        parted_out[3],
        parted_out[4][0],
        parted_out[5][0],
        out_whole,
        shared_out[2],
        shared_out[3],
        shared_out[4],
        up_whole,
        grad_b_up,
        down_whole,
        shared_out[5],
    )


def place_column(core, chip, chips):
    return core * chips + chip


def solution(mesh):
    placed = (
        P("dp", "block", None),
        P("dp", None),
        P(),
        P(),
        P(None, "dp"),
        P(),
        P(),
        P(),
        P(),
        P(),
        P(),
        P(),
        P(),
        P(),
        P(),
        P(None, "dp"),
        P(),
        P(),
        P(),
        P(None, "dp"),
        P(),
        P(None, "dp"),
        P(),
        P("dp", "block", None),
    )
    return jax.shard_map(
        local,
        mesh=mesh,
        in_specs=placed,
        out_specs=(
            P("dp", "block", None),
            P("dp", "block", None),
            P(),
            P(),
            P(None, "dp"),
            P(),
            P(),
            P(),
            P(),
            P(),
            P(),
            P(),
            P(),
            P(),
            P(),
            P(None, "dp"),
            P(),
            P(),
            P(),
            P(None, "dp"),
            P(),
            P(None, "dp"),
            P(),
        ),
        check_vma=False,
    )
```

```python
import math

import jax
import jax.numpy as jnp
import numpy as np
from jax import lax
from jax.sharding import PartitionSpec as P

EPSILON = 1e-05
MOD_SHIFT = 0.05
HIGHEST = lax.Precision.HIGHEST
HIGH = lax.Precision.HIGH
LOW = jnp.bfloat16
WIDE = jnp.float32


def dot_high(left, right):
    return jnp.dot(left, right, precision=HIGHEST, preferred_element_type=WIDE)


def dot_near(left, right):
    return jnp.dot(left, right, precision=HIGH, preferred_element_type=WIDE)


def dot_plain(left, right):
    return jnp.dot(left, right, preferred_element_type=WIDE)


def dot_first(left, right):
    return lax.dot_general(left, right, (((0,), (0,)), ((), ())), preferred_element_type=WIDE)


def dot_last(left, right):
    return lax.dot_general(left, right, (((1,), (1,)), ((), ())), preferred_element_type=WIDE)


def layer_norm(values, gain, bias):
    mean = jnp.mean(values, axis=-1, keepdims=True)
    centered = values - mean
    variance = jnp.mean(centered * centered, axis=-1, keepdims=True)
    return centered * lax.rsqrt(variance + EPSILON) * gain + bias


def exact_gelu(values):
    return jax.nn.gelu(values, approximate=False)


def position_table(length, emb_dim):
    bands = (emb_dim - 1) // 2
    sample = np.arange(length, dtype=np.float32)
    times = sample / np.float32(length - 1)
    frequency = np.linspace(0.0001, bands - 1, bands).astype(np.float32)
    angle = np.float32(2.0 * math.pi) * sample[:, None] * frequency[None, :] / np.float32(length)
    table = np.concatenate([times[:, None], np.cos(angle), -np.sin(angle)], axis=1)
    return (table.astype(np.float32), times)


def transform_tables(block_len):
    span = 2 * block_len
    frequency = np.arange(block_len)
    sample = np.arange(block_len)
    is_zero = (frequency == 0)[:, None]
    angle = 2.0 * math.pi * (frequency[:, None] * sample[None, :] % span) / span
    alternate = np.where(sample % 2 == 0, 1.0, -1.0)
    real_rows = np.cos(angle)
    imag_rows = np.where(is_zero, alternate[None, :], -np.sin(angle))
    forward_table = np.concatenate([real_rows, imag_rows], axis=0)
    outputs = sample + block_len
    out_angle = 2.0 * math.pi * (outputs[:, None] * frequency[None, :] % span) / span
    out_alternate = np.where(outputs % 2 == 0, 1.0, -1.0)
    zero_col = (frequency == 0)[None, :]
    real_cols = np.where(zero_col, 1.0, 2.0) * np.cos(out_angle) / span
    imag_cols = np.where(zero_col, out_alternate[:, None] / span, -2.0 * np.sin(out_angle) / span)
    inverse_table = np.concatenate([real_cols, imag_cols], axis=1)
    parity = np.where(frequency % 2 == 0, 1.0, -1.0)
    sign = np.concatenate([parity, np.where(frequency == 0, 1.0, parity)])
    edge = (frequency == 0).astype(np.float32)[:, None]
    return tuple(item.astype(np.float32) for item in (forward_table, inverse_table, sign, edge))


def spectral_product(left, right, edge):
    half = left.shape[-2] // 2
    left_re, left_im = (left[..., :half, :], left[..., half:, :])
    right_re, right_im = (right[..., :half, :], right[..., half:, :])
    inside = 1.0 - edge
    out_re = left_re * right_re - inside * left_im * right_im
    out_im = inside * (left_re * right_im + left_im * right_re) + edge * left_im * right_im
    return jnp.concatenate([out_re, out_im], axis=-2)


def spectral_back(grad, other, edge):
    half = grad.shape[-2] // 2
    grad_re, grad_im = (grad[..., :half, :], grad[..., half:, :])
    other_re, other_im = (other[..., :half, :], other[..., half:, :])
    inside = 1.0 - edge
    back_re = grad_re * other_re + inside * grad_im * other_im
    back_im = inside * (grad_im * other_re - grad_re * other_im) + edge * grad_im * other_im
    return jnp.concatenate([back_re, back_im], axis=-2)


class Grid:
    def __init__(self, count_dp, count_block):
        self.count_dp = count_dp
        self.count_block = count_block
        self.row = lax.axis_index("dp")
        self.place = lax.axis_index("block")
        self.dp_steps = []
        bit = 1
        while bit < count_dp:
            self.dp_steps.append((bit | (bit >> 1) if bit == 4 else bit, 0))
            bit *= 2
        self.chip_steps = []
        bit = 2
        while bit < count_block:
            self.chip_steps.append((0, bit | (bit >> 1) if bit == 4 else bit))
            bit *= 2
        self.core_step = (0, 1)

    def swap(self, value, step):
        pairs = []
        for row in range(self.count_dp):
            for place in range(self.count_block):
                to = (row ^ step[0]) * self.count_block + (place ^ step[1])
                pairs.append((row * self.count_block + place, to))
        return lax.ppermute(value, ("dp", "block"), pairs)

    def gather(self, value, steps):
        held = value[None]
        for step in steps:
            held = jnp.concatenate([held, self.swap(held, step)], axis=0)
        return held

    def scatter(self, held, steps):
        for step in reversed(steps):
            half = held.shape[0] // 2
            arrived = self.swap(held[half:], step)
            held = (held[:half].astype(WIDE) + arrived.astype(WIDE)).astype(held.dtype)
        return held[0]


def offsets_of(steps):
    offsets = [(0, 0)]
    for step in steps:
        offsets = offsets + [(a ^ step[0], b ^ step[1]) for a, b in offsets]
    return offsets


def pick(held, places):
    return jnp.concatenate(
        [lax.dynamic_slice_in_dim(held, places[i], 1, 0) for i in range(len(places))], axis=0
    )


def place_in(codes, offset):
    place = 0
    for j, code in enumerate(codes):
        place = place ^ (((offset >> j) & 1) * code)
    return place


def codes_of(offsets, count):
    codes, bit = [], 1
    while bit < count:
        codes.append(offsets.index(bit))
        bit *= 2
    return codes


def local(
    block_in,
    doc_starts,
    norm1_gain,
    norm1_bias,
    w_in,
    b_in,
    short_taps,
    short_bias,
    filter_w1,
    filter_b1,
    filter_w2,
    filter_b2,
    filter_w3,
    filter_decay,
    conv_bias,
    w_out,
    b_out,
    norm2_gain,
    norm2_bias,
    w_up,
    b_up,
    w_down,
    b_down,
    cotangent,
):
    count_dp, blocks = lax.axis_size("dp"), lax.axis_size("block")
    grid = Grid(count_dp, blocks)
    row, place = grid.row, grid.place
    chips, core, chip = blocks // 2, place % 2, place // 2
    _, block_len, width = block_in.shape
    length = block_len * blocks
    hidden_width = w_up.shape[1] * count_dp
    dp_steps, chip_steps, core_step = grid.dp_steps, grid.chip_steps, grid.core_step
    block_steps = chip_steps + [core_step]

    def dp_places(steps):
        codes = codes_of([a for a, _ in offsets_of(steps)], count_dp)
        return [place_in(codes, k ^ row) for k in range(count_dp)]

    def block_places(steps):
        codes = codes_of([b for _, b in offsets_of(steps)], blocks)
        return [place_in(codes, k ^ place) for k in range(blocks)]

    def pair_places(steps):
        codes = codes_of([a * chips + b // 2 for a, b in offsets_of(steps)], count_dp * chips)
        flat = row * chips + chip
        return [place_in(codes, k ^ flat) for k in range(count_dp * chips)]

    def rotated(steps, turn):
        turn = turn % len(steps)
        return steps[turn:] + steps[:turn]

    shard_in = w_in.shape[1]
    group = math.gcd(width, shard_in)
    groups_here, share = shard_in // group, group // blocks
    channels = width // blocks

    def own(values, lead=()):
        total = values.shape[-1]
        split = values.reshape(*values.shape[:-1], total // group, blocks, share)
        kept = lax.dynamic_index_in_dim(split, place, split.ndim - 2, keepdims=False)
        return kept.reshape(*values.shape[:-1], total // blocks)

    in_turned = w_in.T.reshape(groups_here, blocks, share, width)
    in_own = lax.dynamic_index_in_dim(in_turned, place, 1, keepdims=False)
    in_orders = [rotated(dp_steps, i) for i in range(groups_here)]
    in_parts = [
        pick(grid.gather(in_own[i], in_orders[i]), dp_places(in_orders[i]))
        for i in range(groups_here)
    ]
    in_rows = jnp.stack(in_parts, axis=1).reshape(3 * channels, width)

    inputs = block_in.astype(WIDE).reshape(block_len, width)
    normed, norm1_back = jax.vjp(layer_norm, inputs, norm1_gain, norm1_bias)
    normed_low = normed.astype(LOW)
    normed_all = pick(grid.gather(normed_low, block_steps), block_places(block_steps)).reshape(
        length, width
    )

    out_order = dp_steps[::-1] + block_steps
    out_split = w_out.reshape(width // group, blocks, share, w_out.shape[1])
    out_own = lax.dynamic_index_in_dim(out_split, place, 1, keepdims=False).reshape(
        channels, w_out.shape[1]
    )
    out_held = grid.gather(out_own, out_order).reshape(blocks, count_dp, channels, w_out.shape[1])
    out_places = dp_places(dp_steps[::-1])
    full_out = jnp.concatenate(
        [lax.dynamic_slice_in_dim(out_held, p, 1, 1) for p in out_places], axis=1
    )
    full_out = full_out.transpose(0, 2, 1, 3).reshape(width, width)

    pair_steps = dp_steps + chip_steps
    piece = w_up.shape[1] // blocks
    up_own = lax.dynamic_slice_in_dim(w_up, place_column(core, chip, chips) * piece, piece, 1)
    up_own = up_own.reshape(2, width // 2, piece)
    down_own = w_down.reshape(count_dp, 2 * chips, piece, w_down.shape[1])
    down_own = lax.dynamic_index_in_dim(down_own, core * chips + chip, 1, keepdims=False)
    down_own = down_own.reshape(2, count_dp // 2 * piece, w_down.shape[1])
    ff_orders = [rotated(pair_steps, i) for i in range(4)]
    up_parts = [
        pick(grid.gather(up_own[i], ff_orders[i]), pair_places(ff_orders[i])) for i in range(2)
    ]
    down_parts = [
        pick(grid.gather(down_own[i], ff_orders[2 + i]), pair_places(ff_orders[2 + i]))
        for i in range(2)
    ]
    half_hidden = hidden_width // 2
    up_here = jnp.concatenate(
        [part.transpose(1, 0, 2).reshape(width // 2, half_hidden) for part in up_parts], axis=0
    )
    down_here = jnp.stack(
        [
            part.reshape(count_dp, chips, count_dp // 2, piece, w_down.shape[1]).transpose(
                2, 1, 3, 0, 4
            )
            for part in down_parts
        ],
        axis=0,
    ).reshape(half_hidden, width)
    b_up_here = lax.dynamic_index_in_dim(
        b_up.reshape(count_dp, 2, chips * piece), core, 1, keepdims=False
    ).reshape(half_hidden)
    cot_flat = cotangent.reshape(block_len, width)
    cot_pair = jnp.concatenate([cot_flat, grid.swap(cot_flat, core_step)], axis=0)

    forward_table, inverse_table, sign, edge = transform_tables(block_len)
    starts = doc_starts[0]
    positions = jnp.arange(length, dtype=jnp.int32)
    segment = jnp.sum((starts[None, :] <= positions[:, None]).astype(jnp.int32), axis=-1) - 1
    keep_one = jnp.concatenate([jnp.zeros((1,), WIDE), (segment[1:] == segment[:-1]).astype(WIDE)])
    keep_two = jnp.concatenate([jnp.zeros((2,), WIDE), (segment[2:] == segment[:-2]).astype(WIDE)])
    keep_one, keep_two = keep_one[:, None], keep_two[:, None]
    num_docs = doc_starts.shape[1]
    long_doc = jnp.sum((starts <= block_len).astype(jnp.int32)) - 1
    long_mask = (segment == long_doc).astype(WIDE)[:, None]
    first_segment, last_segment = segment[:block_len], segment[length - block_len :]
    short_early, short_masks = [], []
    for number in range(num_docs - 1):
        early = number < long_doc
        doc = jnp.where(early, number, number + 1)
        where = jnp.where(early, first_segment, last_segment)
        short_early.append(early.astype(WIDE))
        short_masks.append((where == doc).astype(WIDE)[:, None])

    def spread(values):
        masked = values * long_mask
        parts = [masked[i * block_len : (i + 1) * block_len] for i in range(blocks)]
        first, last = values[:block_len], values[length - block_len :]
        for early, mask in zip(short_early, short_masks):
            parts.append(mask * (early * first + (1.0 - early) * last))
        return jnp.concatenate(parts, axis=1)

    def collect(values):
        parts = [
            values[:, i * channels : (i + 1) * channels] for i in range(blocks + num_docs - 1)
        ]
        first, last = jnp.zeros_like(parts[0]), jnp.zeros_like(parts[0])
        for early, mask, part in zip(short_early, short_masks, parts[blocks:]):
            first = first + early * mask * part
            last = last + (1.0 - early) * mask * part
        joined = jnp.concatenate(parts[:blocks], axis=0) * long_mask
        middle = jnp.zeros((length - 2 * block_len, channels), WIDE)
        return joined + jnp.concatenate([first, middle, last], axis=0)

    def cut(values, count):
        return [values[:, i * channels : (i + 1) * channels] for i in range(count)]

    table, times = position_table(length, filter_w1.shape[0])

    def filter_spectra(params):
        first = jnp.sin(dot_high(table, params[0]) + params[1])
        second = jnp.sin(dot_high(first, params[2]) + params[3])
        kernel = dot_high(second, params[4]) * (
            jnp.exp(-times[:, None] * params[5][None, :]) + MOD_SHIFT
        )
        pieces = jnp.concatenate(
            [kernel[i * block_len : (i + 1) * block_len] for i in range(blocks)], axis=1
        )
        halves = dot_near(forward_table, pieces)
        earlier = jnp.concatenate(
            [jnp.zeros((2 * block_len, channels), WIDE), halves[:, : (blocks - 1) * channels]],
            axis=1,
        )
        return earlier + sign[:, None] * halves

    spectra_flat, filter_back = jax.vjp(
        filter_spectra,
        (filter_w1, filter_b1, filter_w2, filter_b2, own(filter_w3), own(filter_decay)),
    )
    spectra = cut(spectra_flat, blocks)

    proj = dot_last(normed_all, in_rows) + own(b_in)
    taps, short_shift = own(short_taps), own(short_bias)
    three = 3 * channels
    prev_one = jnp.concatenate([jnp.zeros((1, three), WIDE), proj[:-1]], axis=0) * keep_one
    prev_two = jnp.concatenate([jnp.zeros((2, three), WIDE), proj[:-2]], axis=0) * keep_two
    short = short_shift + taps[0] * proj + taps[1] * prev_one + taps[2] * prev_two
    gate_part, mult, value = cut(short, 3)
    inner = value * mult
    direct = own(conv_bias)

    entries = cut(dot_near(forward_table, spread(inner)), blocks + num_docs - 1)
    totals = []
    for i in range(blocks):
        total = spectral_product(entries[i], spectra[0], edge)
        for j in range(i):
            total = total + spectral_product(entries[j], spectra[i - j], edge)
        totals.append(total)
    for entry in entries[blocks:]:
        totals.append(spectral_product(entry, spectra[0], edge))
    mixed = collect(dot_near(inverse_table, jnp.concatenate(totals, axis=1))) + direct * inner
    gated_low = (gate_part * mixed).astype(LOW)

    block_offsets = [b for _, b in offsets_of(block_steps)]
    gated_parts = []
    for offset in block_offsets:
        part = lax.dynamic_slice_in_dim(gated_low, (place ^ offset) * block_len, block_len, 0)
        gated_parts.append(grid.swap(part, (0, offset)) if offset else part)
    gated_rows = jnp.concatenate(gated_parts, axis=1)
    resid = inputs + dot_plain(gated_rows, full_out) + b_out
    normed2, norm2_back = jax.vjp(layer_norm, resid, norm2_gain, norm2_bias)
    normed2_low = normed2.astype(LOW)

    pair = jnp.concatenate([normed2_low, grid.swap(normed2_low, core_step)], axis=0)
    hidden = dot_plain(pair, up_here) + b_up_here
    act, gelu_back = jax.vjp(exact_gelu, hidden)
    act_low = act.astype(LOW)
    grad_act = dot_last(cot_pair, down_here)
    grad_hidden = gelu_back(grad_act)[0].astype(LOW)
    grad_pair = dot_last(grad_hidden, up_here)
    grad_normed2 = grad_pair[:block_len] + grid.swap(
        grad_pair[block_len:].astype(LOW), core_step
    ).astype(WIDE)
    out_pair = dot_plain(act_low, down_here)
    output = (
        resid
        + out_pair[:block_len]
        + grid.swap(out_pair[block_len:].astype(LOW), core_step).astype(WIDE)
        + b_down
    )
    block_out = output.astype(LOW)[None]
    grad_down_here = dot_first(act_low, cot_pair).astype(LOW)
    grad_up_here = dot_first(pair, grad_hidden).astype(LOW)
    grad_b_up_here = jnp.sum(grad_hidden.astype(WIDE), axis=0)
    grad_b_down = jnp.sum(cot_flat.astype(WIDE), axis=0)

    def send_home(natural, order):
        wanted = [
            ((row ^ a) * chips + (chip ^ (b >> 1))) for a, b in offsets_of(order)
        ]
        return grid.scatter(pick(natural, wanted), order)

    up_grads = [
        send_home(
            grad_up_here[i * (width // 2) : (i + 1) * (width // 2)]
            .reshape(width // 2, count_dp * chips, piece)
            .transpose(1, 0, 2),
            ff_orders[i],
        )
        for i in range(2)
    ]
    down_split = grad_down_here.reshape(
        2, count_dp // 2, chips, piece, count_dp, w_down.shape[1]
    )
    down_grads = [
        send_home(
            down_split[i]
            .transpose(3, 1, 0, 2, 4)
            .reshape(count_dp * chips, count_dp // 2 * piece, w_down.shape[1]),
            ff_orders[2 + i],
        )
        for i in range(2)
    ]

    resid_part, grad_gain_two, grad_bias_two = norm2_back(grad_normed2)
    grad_resid = cot_flat.astype(WIDE) + resid_part
    grad_branch = grad_resid.astype(LOW)
    grad_b_out = jnp.sum(grad_branch.astype(WIDE), axis=0)
    grad_gated_rows = dot_last(grad_branch, full_out).astype(LOW)
    grad_out_here = dot_first(gated_rows, grad_branch).astype(LOW)
    grad_out_split = grad_out_here.reshape(blocks, channels, count_dp, w_out.shape[1]).transpose(
        0, 2, 1, 3
    )
    out_wanted = [row ^ a for a, _ in offsets_of(dp_steps[::-1])]
    grad_out_split = jnp.concatenate(
        [lax.dynamic_slice_in_dim(grad_out_split, p, 1, 1) for p in out_wanted], axis=1
    ).reshape(blocks * count_dp, channels, w_out.shape[1])
    out_grad = grid.scatter(grad_out_split, out_order)

    grad_parts = []
    for index, offset in enumerate(block_offsets):
        part = grad_gated_rows[:, index * channels : (index + 1) * channels]
        grad_parts.append((grid.swap(part, (0, offset)) if offset else part)[None])
    grad_gated = pick(jnp.concatenate(grad_parts, axis=0), block_places(block_steps))
    grad_gated = grad_gated.reshape(length, channels).astype(WIDE)

    grad_gate_part = grad_gated * mixed
    grad_mixed = grad_gated * gate_part
    grad_conv_bias = jnp.sum(grad_mixed * inner, axis=0)
    grad_totals = cut(
        lax.dot_general(
            inverse_table,
            spread(grad_mixed),
            (((0,), (0,)), ((), ())),
            precision=HIGH,
            preferred_element_type=WIDE,
        ),
        blocks + num_docs - 1,
    )
    grad_entries = []
    grad_lags = [None] * blocks
    for i in range(blocks + num_docs - 1):
        lag = spectral_back(grad_totals[i], entries[i], edge)
        grad_lags[0] = lag if grad_lags[0] is None else grad_lags[0] + lag
        grad_entries.append(spectral_back(grad_totals[i], spectra[0], edge))
    for j in range(blocks):
        for i in range(j + 1, blocks):
            grad_entries[j] = grad_entries[j] + spectral_back(
                grad_totals[i], spectra[i - j], edge
            )
            lag = spectral_back(grad_totals[i], entries[j], edge)
            grad_lags[i - j] = lag if grad_lags[i - j] is None else grad_lags[i - j] + lag
    filter_grads = filter_back(jnp.concatenate(grad_lags, axis=1))[0]
    grad_inner = (
        collect(
            lax.dot_general(
                forward_table,
                jnp.concatenate(grad_entries, axis=1),
                (((0,), (0,)), ((), ())),
                precision=HIGH,
                preferred_element_type=WIDE,
            )
        )
        + direct * grad_mixed
    )
    grad_short = jnp.concatenate([grad_gate_part, grad_inner * value, grad_inner * mult], axis=1)
    grad_taps = jnp.stack(
        [
            jnp.sum(grad_short * proj, axis=0),
            jnp.sum(grad_short * prev_one, axis=0),
            jnp.sum(grad_short * prev_two, axis=0),
        ],
        axis=0,
    )
    grad_short_bias = jnp.sum(grad_short, axis=0)
    pass_one = grad_short * keep_one
    pass_two = grad_short * keep_two
    grad_proj = (
        taps[0] * grad_short
        + taps[1] * jnp.concatenate([pass_one[1:], jnp.zeros((1, three), WIDE)], axis=0)
        + taps[2] * jnp.concatenate([pass_two[2:], jnp.zeros((2, three), WIDE)], axis=0)
    )
    grad_proj_low = grad_proj.astype(LOW)
    grad_b_in = jnp.sum(grad_proj_low.astype(WIDE), axis=0)
    grad_in_rows = dot_first(grad_proj_low, normed_all).astype(LOW)
    grad_in_split = grad_in_rows.reshape(count_dp, groups_here, share, width)
    in_grads = []
    for i in range(groups_here):
        wanted = [row ^ a for a, _ in offsets_of(in_orders[i])]
        in_grads.append(grid.scatter(pick(grad_in_split[:, i], wanted), in_orders[i]))
    grad_normed_part = dot_plain(grad_proj_low, in_rows).astype(LOW).reshape(
        blocks, block_len, width
    )
    grad_normed = grid.scatter(
        pick(grad_normed_part, [place ^ offset for offset in block_offsets]), block_steps
    ).astype(WIDE)
    input_part, grad_gain_one, grad_bias_one = norm1_back(grad_normed)
    grad_input = (grad_resid + input_part)[None]

    def all_places(value):
        return pick(grid.gather(value, block_steps), block_places(block_steps))

    in_whole = all_places(jnp.stack(in_grads, axis=0))
    in_whole = in_whole.transpose(1, 0, 2, 3).reshape(shard_in, width).T.astype(WIDE)
    out_whole = all_places(out_grad).reshape(blocks, width // group, share, w_out.shape[1])
    out_whole = out_whole.transpose(1, 0, 2, 3).reshape(width, w_out.shape[1]).astype(WIDE)
    core_major = [b for c in range(2) for b in range(c, blocks, 2)]
    up_whole = all_places(jnp.concatenate(up_grads, axis=0))
    up_whole = jnp.concatenate([up_whole[b] for b in core_major], axis=1).astype(WIDE)
    down_whole = all_places(jnp.concatenate(down_grads, axis=0))
    down_whole = jnp.stack([down_whole[b] for b in core_major], axis=0).reshape(
        2 * chips, count_dp, piece, w_down.shape[1]
    )
    down_whole = down_whole.transpose(1, 0, 2, 3).reshape(hidden_width, w_down.shape[1])
    down_whole = down_whole.astype(WIDE)

    shared = [
        grad_gain_one,
        grad_bias_one,
        grad_b_out,
        grad_gain_two,
        grad_bias_two,
        grad_b_down,
        filter_grads[0],
        filter_grads[1],
        filter_grads[2],
        filter_grads[3],
    ]
    up_home = jnp.zeros((2, half_hidden), WIDE)
    up_home = lax.dynamic_update_slice_in_dim(up_home, grad_b_up_here[None], core, 0)
    shared.append(up_home)
    flat = jnp.concatenate([item.reshape(-1) for item in shared])
    chunk = -(-flat.shape[0] // (blocks * 128)) * 128
    flat = jnp.pad(flat, (0, chunk * blocks - flat.shape[0])).reshape(blocks, chunk)
    shared_part = grid.scatter(
        pick(flat, [place ^ offset for offset in block_offsets]), block_steps
    )
    parted = [
        grad_b_in[None],
        grad_taps,
        grad_short_bias[None],
        filter_grads[4],
        filter_grads[5][None],
        grad_conv_bias[None],
    ]
    joined = jnp.concatenate([shared_part] + [item.reshape(-1) for item in parted])
    for step in dp_steps:
        joined = joined + grid.swap(joined, step)
    every = all_places(joined)
    whole_flat = every[:, :chunk].reshape(-1)
    shared_out, at = [], 0
    for item in shared:
        shared_out.append(whole_flat[at : at + item.size].reshape(item.shape))
        at += item.size
    parted_out, at = [], chunk
    for item in parted:
        lead, size = item.shape[0], item.size
        values = every[:, at : at + size].reshape(blocks, lead, item.shape[1] // share, share)
        parted_out.append(values.transpose(1, 2, 0, 3).reshape(lead, item.shape[1] * blocks))
        at += size
    grad_b_up = shared_out[10].reshape(2, count_dp, chips * piece)
    grad_b_up = grad_b_up.transpose(1, 0, 2).reshape(hidden_width)
    return (
        block_out,
        grad_input,
        shared_out[0],
        shared_out[1],
        in_whole,
        parted_out[0][0],
        parted_out[1],
        parted_out[2][0],
        shared_out[6],
        shared_out[7],
        shared_out[8],
        shared_out[9],
        parted_out[3],
        parted_out[4][0],
        parted_out[5][0],
        out_whole,
        shared_out[2],
        shared_out[3],
        shared_out[4],
        up_whole,
        grad_b_up,
        down_whole,
        shared_out[5],
    )


def place_column(core, chip, chips):
    return core * chips + chip


def solution(mesh):
    placed = (
        P("dp", "block", None),
        P("dp", None),
        P(),
        P(),
        P(None, "dp"),
        P(),
        P(),
        P(),
        P(),
        P(),
        P(),
        P(),
        P(),
        P(),
        P(),
        P(None, "dp"),
        P(),
        P(),
        P(),
        P(None, "dp"),
        P(),
        P(None, "dp"),
        P(),
        P("dp", "block", None),
    )
    return jax.shard_map(
        local,
        mesh=mesh,
        in_specs=placed,
        out_specs=(
            P("dp", "block", None),
            P("dp", "block", None),
            P(),
            P(),
            P(None, "dp"),
            P(),
            P(),
            P(),
            P(),
            P(),
            P(),
            P(),
            P(),
            P(),
            P(),
            P(None, "dp"),
            P(),
            P(),
            P(),
            P(None, "dp"),
            P(),
            P(None, "dp"),
            P(),
        ),
        check_vma=False,
    )
```

```python
import math

import jax
import jax.numpy as jnp
import ml_dtypes
import numpy as np
from jax import lax
from jax.experimental import pallas as pl
from jax.experimental.pallas import tpu as pltpu
from jax.sharding import PartitionSpec as P

EPSILON = 1e-05
MOD_SHIFT = 0.05
HIGHEST = lax.Precision.HIGHEST
HIGH = lax.Precision.HIGH
LOW = jnp.bfloat16
WIDE = jnp.float32


def dot_high(left, right):
    return jnp.dot(left, right, precision=HIGHEST, preferred_element_type=WIDE)


def dot_near(left, right):
    return jnp.dot(left, right, precision=HIGH, preferred_element_type=WIDE)


def dot_plain(left, right):
    return jnp.dot(left, right, preferred_element_type=WIDE)


def dot_first(left, right):
    return lax.dot_general(left, right, (((0,), (0,)), ((), ())), preferred_element_type=WIDE)


def dot_last(left, right):
    return lax.dot_general(left, right, (((1,), (1,)), ((), ())), preferred_element_type=WIDE)


def layer_norm(values, gain, bias):
    mean = jnp.mean(values, axis=-1, keepdims=True)
    centered = values - mean
    variance = jnp.mean(centered * centered, axis=-1, keepdims=True)
    return centered * lax.rsqrt(variance + EPSILON) * gain + bias


def exact_gelu(values):
    return jax.nn.gelu(values, approximate=False)


def position_table(length, emb_dim):
    bands = (emb_dim - 1) // 2
    sample = np.arange(length, dtype=np.float32)
    times = sample / np.float32(length - 1)
    frequency = np.linspace(0.0001, bands - 1, bands).astype(np.float32)
    angle = np.float32(2.0 * math.pi) * sample[:, None] * frequency[None, :] / np.float32(length)
    table = np.concatenate([times[:, None], np.cos(angle), -np.sin(angle)], axis=1)
    return (table.astype(np.float32), times)


def transform_tables(block_len):
    span = 2 * block_len
    frequency = np.arange(block_len)
    sample = np.arange(block_len)
    is_zero = (frequency == 0)[:, None]
    angle = 2.0 * math.pi * (frequency[:, None] * sample[None, :] % span) / span
    alternate = np.where(sample % 2 == 0, 1.0, -1.0)
    real_rows = np.cos(angle)
    imag_rows = np.where(is_zero, alternate[None, :], -np.sin(angle))
    forward_table = np.concatenate([real_rows, imag_rows], axis=0)
    outputs = sample + block_len
    out_angle = 2.0 * math.pi * (outputs[:, None] * frequency[None, :] % span) / span
    out_alternate = np.where(outputs % 2 == 0, 1.0, -1.0)
    zero_col = (frequency == 0)[None, :]
    real_cols = np.where(zero_col, 1.0, 2.0) * np.cos(out_angle) / span
    imag_cols = np.where(zero_col, out_alternate[:, None] / span, -2.0 * np.sin(out_angle) / span)
    inverse_table = np.concatenate([real_cols, imag_cols], axis=1)
    parity = np.where(frequency % 2 == 0, 1.0, -1.0)
    sign = np.concatenate([parity, np.where(frequency == 0, 1.0, parity)])
    edge = (frequency == 0).astype(np.float32)[:, None]
    return tuple(item.astype(np.float32) for item in (forward_table, inverse_table, sign, edge))


def spectral_product(left, right, edge):
    half = left.shape[-2] // 2
    left_re, left_im = (left[..., :half, :], left[..., half:, :])
    right_re, right_im = (right[..., :half, :], right[..., half:, :])
    inside = 1.0 - edge
    out_re = left_re * right_re - inside * left_im * right_im
    out_im = inside * (left_re * right_im + left_im * right_re) + edge * left_im * right_im
    return jnp.concatenate([out_re, out_im], axis=-2)


def spectral_back(grad, other, edge):
    half = grad.shape[-2] // 2
    grad_re, grad_im = (grad[..., :half, :], grad[..., half:, :])
    other_re, other_im = (other[..., :half, :], other[..., half:, :])
    inside = 1.0 - edge
    back_re = grad_re * other_re + inside * grad_im * other_im
    back_im = inside * (grad_im * other_re - grad_re * other_im) + edge * grad_im * other_im
    return jnp.concatenate([back_re, back_im], axis=-2)


class Grid:
    def __init__(self, count_dp, count_block):
        self.count_dp = count_dp
        self.count_block = count_block
        self.row = lax.axis_index("dp")
        self.place = lax.axis_index("block")
        self.dp_steps = []
        bit = 1
        while bit < count_dp:
            self.dp_steps.append((bit | (bit >> 1) if bit == 4 else bit, 0))
            bit *= 2
        self.chip_steps = []
        bit = 2
        while bit < count_block:
            self.chip_steps.append((0, bit | (bit >> 1) if bit == 4 else bit))
            bit *= 2
        self.core_step = (0, 1)

    def swap(self, value, step):
        pairs = []
        for row in range(self.count_dp):
            for place in range(self.count_block):
                to = (row ^ step[0]) * self.count_block + (place ^ step[1])
                pairs.append((row * self.count_block + place, to))
        return lax.ppermute(value, ("dp", "block"), pairs)

    def gather(self, value, steps):
        held = value[None]
        pieces = [held]
        for number, step in enumerate(steps):
            pieces.append(self.swap(held, step))
            if number + 1 < len(steps):
                held = jnp.concatenate(pieces, axis=0)
        return pieces

    def scatter(self, kept, sent, steps):
        for step in reversed(steps):
            arrived = self.swap(sent, step)
            half = kept.shape[0] // 2
            if half:
                sent = add_low(kept[half:], arrived[half:])
                kept = add_low(kept[:half], arrived[:half])
            else:
                kept = add_low(kept, arrived)
        return kept[0]


def add_low(left, right):
    return (left.astype(WIDE) + right.astype(WIDE)).astype(left.dtype)


def offsets_of(steps):
    offsets = [(0, 0)]
    for step in steps:
        offsets = offsets + [(a ^ step[0], b ^ step[1]) for a, b in offsets]
    return offsets


def arrange(pieces, mine, offsets):
    shape = pieces[0].shape[1:]
    if shape[-2] % 32 or shape[-1] % 128:
        held = jnp.concatenate(pieces, axis=0)
        codes = codes_of(offsets, len(offsets))
        return jnp.concatenate(
            [
                lax.dynamic_slice_in_dim(held, place_in(codes, k ^ mine), 1, 0)
                for k in range(len(offsets))
            ],
            axis=0,
        )
    count = len(pieces)

    def kernel(mine_ref, *refs):
        source, target = refs[:count], refs[count]
        at = 0
        for ref in source:
            for i in range(ref.shape[0]):
                target[mine_ref[0] ^ offsets[at]] = ref[i]
                at += 1

    return pl.pallas_call(
        kernel,
        out_shape=jax.ShapeDtypeStruct((len(offsets), *shape), pieces[0].dtype),
        in_specs=[pl.BlockSpec(memory_space=pltpu.SMEM)]
        + [pl.BlockSpec(memory_space=pltpu.VMEM)] * count,
        out_specs=pl.BlockSpec(memory_space=pltpu.VMEM),
    )(jnp.reshape(mine, (1,)).astype(jnp.int32), *pieces)


def deal(natural, mine, offsets):
    half = len(offsets) // 2
    shape = natural.shape[1:]
    if shape[-2] % 32 or shape[-1] % 128:
        dealt = [lax.dynamic_slice_in_dim(natural, mine ^ offset, 1, 0) for offset in offsets]
        return jnp.concatenate(dealt[:half], axis=0), jnp.concatenate(dealt[half:], axis=0)

    def kernel(mine_ref, source, kept, sent):
        for at, offset in enumerate(offsets):
            if at < half:
                kept[at] = source[mine_ref[0] ^ offset]
            else:
                sent[at - half] = source[mine_ref[0] ^ offset]

    out = jax.ShapeDtypeStruct((half, *shape), natural.dtype)
    vmem = pl.BlockSpec(memory_space=pltpu.VMEM)
    return pl.pallas_call(
        kernel,
        out_shape=(out, out),
        in_specs=[pl.BlockSpec(memory_space=pltpu.SMEM), vmem],
        out_specs=(vmem, vmem),
    )(jnp.reshape(mine, (1,)).astype(jnp.int32), natural)


def place_in(codes, offset):
    place = 0
    for j, code in enumerate(codes):
        place = place ^ (((offset >> j) & 1) * code)
    return place


def codes_of(offsets, count):
    codes, bit = [], 1
    while bit < count:
        codes.append(offsets.index(bit))
        bit *= 2
    return codes


def split_low(values):
    high = values.astype(LOW)
    return high, (values - high.astype(WIDE)).astype(LOW)


def triple(table):
    high = table.astype(ml_dtypes.bfloat16)
    low = (table - high.astype(np.float32)).astype(ml_dtypes.bfloat16)
    return np.concatenate([high, high, low], axis=1)


def store_triple(target, columns, values):
    high, low = split_low(values)
    size = values.shape[0]
    target[0:size, columns] = high
    target[size : 2 * size, columns] = low
    target[2 * size : 3 * size, columns] = high


def long_range(starts, count, block_len, length):
    begin, end, before = starts[0], jnp.int32(length), jnp.int32(-1)
    for d in range(count):
        begin = jnp.where(starts[d] <= block_len, starts[d], begin)
        before = before + jnp.where(starts[d] <= block_len, 1, 0)
    for d in reversed(range(count)):
        end = jnp.where(starts[d] > block_len, starts[d], end)
    return begin, end, before


def short_range(starts, count, number, before, block_len, length):
    early = number < before
    bounds = [starts[d] for d in range(count)] + [jnp.int32(length)]
    begin = jnp.where(early, bounds[number], bounds[number + 1])
    end = jnp.where(early, bounds[number + 1], bounds[number + 2])
    return begin, end, jnp.where(early, 0, length - block_len)


def rows_from(base, size, lanes):
    return lax.broadcasted_iota(jnp.int32, (size, lanes), 0) + base


def inside_mask(base, size, lanes, begin, end):
    rows = rows_from(base, size, lanes)
    return (rows >= begin) & (rows < end)


def keep_masks(starts, count, base, size, lanes):
    rows = rows_from(base, size, lanes)
    one = rows != starts[0]
    for d in range(1, count):
        one = one & (rows != starts[d])
    two = one
    for d in range(count):
        two = two & (rows != starts[d] + 1)
    return one, two


VMEM_SPACE = pl.BlockSpec(memory_space=pltpu.VMEM)
ANY_SPACE = pl.BlockSpec(memory_space=pl.ANY)
SMEM_SPACE = pl.BlockSpec(memory_space=pltpu.SMEM)
LIMIT = 56 * 1024 * 1024


class Copies:
    def __init__(self, sems):
        self.sems, self.used = sems, 0

    def start(self, source, target):
        copy = pltpu.make_async_copy(source, target, self.sems.at[self.used])
        self.used += 1
        copy.start()
        return copy


def filter_kernel(block_len, blocks, table_ref, w1, w2, vec, third_at, f3_ref, spectra):
    length = block_len * blocks
    channels = vec.shape[1]
    one_row = jnp.where(lax.broadcasted_iota(jnp.int32, (8, length), 0) == 0, 1.0, 0.0)

    def turned(left, right):
        return lax.dot_general(
            left, right, (((0,), (0,)), ((), ())), precision=HIGHEST, preferred_element_type=WIDE
        )

    first = jnp.sin(turned(w1[...], table_ref[...]))
    second = jnp.sin(turned(w2[...], jnp.concatenate([first, one_row], axis=0)))
    decay = vec[third_at - 2 : third_at - 1, :]
    third_w = vec[third_at : third_at + second.shape[0], :]
    before = None
    half_rows = lax.broadcasted_iota(jnp.int32, (2 * block_len, channels), 0)
    parity = jnp.where(half_rows % 2 == 0, 1.0, -1.0)
    sign = jnp.where(half_rows == block_len, 1.0, parity)
    for i in range(blocks):
        part = turned(second[:, i * block_len : (i + 1) * block_len], third_w)
        times = rows_from(i * block_len, block_len, channels).astype(WIDE) / (length - 1)
        part = part * (jnp.exp(-times * decay) + MOD_SHIFT)
        high, low = split_low(part)
        stacked = jnp.concatenate([high, low, high], axis=0)
        half = jnp.dot(f3_ref[...], stacked, preferred_element_type=WIDE)
        spectra[i] = sign * half if before is None else before + sign * half
        before = half


def with_bias(weights, bias):
    rows = weights.shape[0]
    return jnp.pad(jnp.concatenate([weights, bias[None]], axis=0), ((0, -(rows + 1) % 8), (0, 0)))


def turned_table(table):
    length, count = table.shape
    rows = [table.T, np.ones((1, length), np.float32)]
    rows.append(np.zeros((-(count + 1) % 8, length), np.float32))
    return np.concatenate(rows, axis=0)


def filter_call(block_len, blocks, table, f3, w1, w2, vec, third_at):
    channels = vec.shape[1]

    def body(table_ref, w1_ref, w2_ref, vec_ref, f3_ref, spectra):
        filter_kernel(
            block_len, blocks, table_ref, w1_ref, w2_ref, vec_ref, third_at, f3_ref, spectra
        )

    return pl.pallas_call(
        body,
        out_shape=jax.ShapeDtypeStruct((blocks, 2 * block_len, channels), WIDE),
        in_specs=[VMEM_SPACE] * 5,
        out_specs=VMEM_SPACE,
        compiler_params=pltpu.CompilerParams(vmem_limit_bytes=LIMIT),
    )(table, w1, w2, vec, f3)


def gather_in(copies, pieces, mine, offsets, target):
    started, at = [], 0
    for ref in pieces:
        for i in range(ref.shape[0]):
            started.append(copies.start(ref.at[i], target.at[mine ^ offsets[at]]))
            at += 1
    return started


def conv_call(
    block_len, blocks, places, starts, normed_pieces, in_pieces, in_offsets, block_offsets, vec, spectra, f3, i3
):
    length = block_len * blocks
    channels = vec.shape[1]
    docs = starts.shape[0]
    entries = blocks + docs - 1
    width = normed_pieces[0].shape[-1]
    groups = len(in_pieces)
    share = in_pieces[0][0].shape[1]
    count_dp = len(in_offsets[0])
    flat_in = [piece for pieces in in_pieces for piece in pieces]
    n_norm, n_in, n_out = len(normed_pieces), len(flat_in), blocks
    step = 16

    def body(place_ref, starts_ref, vec_ref, f3_ref, i3_ref, spectra_ref, *refs):
        norm_refs, in_refs = refs[:n_norm], refs[n_norm : n_norm + n_in]
        refs = refs[n_norm + n_in :]
        gated_refs, (proj_out, entry_out, mixed_out, rows_out, norm_out) = refs[:n_out], refs[n_out : n_out + 5]
        norm, rows, proj, inner, gate, xs, ent, ys, mixed, spec, sems = refs[n_out + 5 :]
        row, place = place_ref[0], place_ref[1]
        copies = Copies(sems)
        waiting = gather_in(copies, norm_refs, place, block_offsets, norm)
        at = 0
        for g in range(groups):
            count = len(in_pieces[g])
            index = 0
            for ref in in_refs[at : at + count]:
                for i in range(ref.shape[0]):
                    to = row ^ in_offsets[g][index]
                    waiting.append(copies.start(ref.at[i], rows.at[to, g]))
                    index += 1
            at += count
        spec_copy = copies.start(spectra_ref, spec)
        for copy in waiting:
            copy.wait()
        leaving = [copies.start(norm, norm_out), copies.start(rows, rows_out)]

        flat_rows = rows[...].reshape(3 * channels, width)
        for role in range(3):
            weights = flat_rows[role * channels : (role + 1) * channels]
            bias = vec_ref[role : role + 1, :]
            for b in range(blocks):
                proj[b * block_len : (b + 1) * block_len, role * channels : (role + 1) * channels] = (
                    lax.dot_general(
                        norm[b],
                        weights,
                        (((1,), (1,)), ((), ())),
                        preferred_element_type=WIDE,
                    )
                    + bias
                )
        leaving.append(copies.start(proj, proj_out))
        for b in range(blocks):
            base = b * block_len
            one, two = keep_masks(starts_ref, docs, base, block_len, channels)
            parts = []
            for role in range(3):
                lanes = slice(role * channels, (role + 1) * channels)
                here = proj[base : base + block_len, lanes]
                if b:
                    back = proj[base - 8 : base + block_len, lanes]
                    prev_one = pltpu.roll(back, 1, 0)[8:]
                    prev_two = pltpu.roll(back, 2, 0)[8:]
                else:
                    prev_one, prev_two = pltpu.roll(here, 1, 0), pltpu.roll(here, 2, 0)
                tap = [vec_ref[3 + 3 * j + role : 4 + 3 * j + role, :] for j in range(3)]
                short = (
                    vec_ref[12 + role : 13 + role, :]
                    + tap[0] * here
                    + tap[1] * jnp.where(one, prev_one, 0.0)
                    + tap[2] * jnp.where(two, prev_two, 0.0)
                )
                parts.append(short)
            gate[base : base + block_len] = parts[0]
            inner[base : base + block_len] = parts[1] * parts[2]
        begin, end, before = long_range(starts_ref, docs, block_len, length)
        for b in range(blocks):
            mask = inside_mask(b * block_len, block_len, channels, begin, end)
            part = jnp.where(mask, inner[b * block_len : (b + 1) * block_len], 0.0)
            store_triple(xs, slice(b * channels, (b + 1) * channels), part)
        for m in range(docs - 1):
            first, last, base = short_range(starts_ref, docs, m, before, block_len, length)
            base = pl.multiple_of(base, block_len)
            mask = inside_mask(base, block_len, channels, first, last)
            part = jnp.where(mask, inner[pl.ds(base, block_len)], 0.0)
            store_triple(xs, slice((blocks + m) * channels, (blocks + m + 1) * channels), part)
        for e in range(entries):
            ent[e] = jnp.dot(
                f3_ref[...], xs[:, e * channels : (e + 1) * channels], preferred_element_type=WIDE
            )
        leaving.append(copies.start(ent, entry_out))
        spec_copy.wait()

        @pl.loop(0, block_len // step)
        def _(number):
            at_re = pl.multiple_of(number * step, step)
            at_im = pl.multiple_of(number * step + block_len, step)
            edge = jnp.where(rows_from(at_re, step, channels) == 0, 1.0, 0.0)
            inside = 1.0 - edge
            keys = [(spec[k, pl.ds(at_re, step)], spec[k, pl.ds(at_im, step)]) for k in range(blocks)]
            held = [(ent[k, pl.ds(at_re, step)], ent[k, pl.ds(at_im, step)]) for k in range(blocks)]
            for e in range(entries):
                pairs = (
                    [(held[j], keys[e - j]) for j in range(e + 1)]
                    if e < blocks
                    else [((ent[e, pl.ds(at_re, step)], ent[e, pl.ds(at_im, step)]), keys[0])]
                )
                rr = ii = ri = None
                for (a, b), (c, d) in pairs:
                    rr = a * c if rr is None else rr + a * c
                    ii = b * d if ii is None else ii + b * d
                    ri = a * d + b * c if ri is None else ri + (a * d + b * c)
                lanes = slice(e * channels, (e + 1) * channels)
                out_re = rr - inside * ii
                out_im = inside * ri + edge * ii
                for part, at in ((out_re, at_re), (out_im, at_im)):
                    high, low = split_low(part)
                    ys[pl.ds(at, step), lanes] = high
                    ys[pl.ds(at + 2 * block_len, step), lanes] = low
                    ys[pl.ds(at + 4 * block_len, step), lanes] = high

        direct = vec_ref[16:17, :]
        for b in range(blocks):
            back = jnp.dot(
                i3_ref[...], ys[:, b * channels : (b + 1) * channels], preferred_element_type=WIDE
            )
            rows_here = slice(b * block_len, (b + 1) * block_len)
            mask = inside_mask(b * block_len, block_len, channels, begin, end)
            mixed[rows_here] = jnp.where(mask, back, 0.0) + direct * inner[rows_here]
        for m in range(docs - 1):
            lanes = slice((blocks + m) * channels, (blocks + m + 1) * channels)
            back = jnp.dot(i3_ref[...], ys[:, lanes], preferred_element_type=WIDE)
            first, last, base = short_range(starts_ref, docs, m, before, block_len, length)
            base = pl.multiple_of(base, block_len)
            mask = inside_mask(base, block_len, channels, first, last)
            where = pl.ds(base, block_len)
            mixed[where] = mixed[where] + jnp.where(mask, back, 0.0)
        leaving.append(copies.start(mixed, mixed_out))
        for index, offset in enumerate(block_offsets):
            where = pl.ds(pl.multiple_of((place ^ offset) * block_len, block_len), block_len)
            gated_refs[index][...] = (gate[where] * mixed[where]).astype(LOW)
        for copy in leaving:
            copy.wait()

    shape = jax.ShapeDtypeStruct
    sem_count = blocks + groups * count_dp + 6
    return pl.pallas_call(
        body,
        out_shape=[shape((block_len, channels), LOW)] * blocks
        + [
            shape((length, 3 * channels), WIDE),
            shape((entries, 2 * block_len, channels), WIDE),
            shape((length, channels), WIDE),
            shape((count_dp, groups, share, width), LOW),
            shape((blocks, block_len, width), LOW),
        ],
        in_specs=[SMEM_SPACE, SMEM_SPACE, VMEM_SPACE, VMEM_SPACE, VMEM_SPACE, ANY_SPACE]
        + [ANY_SPACE] * (n_norm + n_in),
        out_specs=[VMEM_SPACE] * blocks + [ANY_SPACE] * 5,
        scratch_shapes=[
            pltpu.VMEM((blocks, block_len, width), LOW),
            pltpu.VMEM((count_dp, groups, share, width), LOW),
            pltpu.VMEM((length, 3 * channels), WIDE),
            pltpu.VMEM((length, channels), WIDE),
            pltpu.VMEM((length, channels), WIDE),
            pltpu.VMEM((3 * block_len, entries * channels), LOW),
            pltpu.VMEM((entries, 2 * block_len, channels), WIDE),
            pltpu.VMEM((6 * block_len, entries * channels), LOW),
            pltpu.VMEM((length, channels), WIDE),
            pltpu.VMEM((blocks, 2 * block_len, channels), WIDE),
            pltpu.SemaphoreType.DMA((sem_count,)),
        ],
        compiler_params=pltpu.CompilerParams(vmem_limit_bytes=LIMIT),
    )(places, starts, vec, f3, i3, spectra, *normed_pieces, *flat_in)


def back_call(
    block_len,
    blocks,
    places,
    starts,
    grad_pieces,
    in_offsets,
    block_offsets,
    vec,
    norm1,
    spectra,
    proj,
    entries,
    mixed,
    in_rows,
    normed,
    it3,
    ft3,
):
    length = block_len * blocks
    channels = vec.shape[1]
    docs = starts.shape[0]
    count = entries.shape[0]
    count_dp, groups, share, width = in_rows.shape
    three = 3 * channels
    step = 16
    half_dp, half_block = count_dp // 2, blocks // 2

    def body(place_ref, starts_ref, vec_ref, norm1_ref, it3_ref, ft3_ref, *refs):
        grad_refs, refs = refs[:blocks], refs[blocks:]
        spectra_ref, proj_ref, entry_ref, mixed_ref, rows_ref, norm_ref = refs[:6]
        refs = refs[6:]
        dealt_refs = [(refs[2 * g], refs[2 * g + 1]) for g in range(groups)]
        refs = refs[2 * groups :]
        gn_kept, gn_sent, lags, sums, norm_sums = refs[:5]
        spec, proj, ent, mixed, rows, norm, gg, short, gs, gm, xs, gt, ys, gi, gp, gr, sems = refs[5:]
        row, place = place_ref[0], place_ref[1]
        copies = Copies(sems)
        proj_copy = copies.start(proj_ref, proj)
        mixed_copy = copies.start(mixed_ref, mixed)
        spec_copy = copies.start(spectra_ref, spec)
        entry_copy = copies.start(entry_ref, ent)
        rows_copy = copies.start(rows_ref, rows)
        norm_copy = copies.start(norm_ref, norm)
        for index, offset in enumerate(block_offsets):
            where = pl.ds(pl.multiple_of((place ^ offset) * block_len, block_len), block_len)
            gg[where] = grad_refs[index][...]
        proj_copy.wait()
        mixed_copy.wait()
        direct = vec_ref[16:17, :]
        direct_sum = jnp.zeros((1, channels), WIDE)
        for b in range(blocks):
            base = b * block_len
            here = slice(base, base + block_len)
            one, two = keep_masks(starts_ref, docs, base, block_len, channels)
            parts = []
            for role in range(3):
                lanes = slice(role * channels, (role + 1) * channels)
                now = proj[here, lanes]
                if b:
                    back = proj[base - 8 : base + block_len, lanes]
                    prev_one, prev_two = pltpu.roll(back, 1, 0)[8:], pltpu.roll(back, 2, 0)[8:]
                else:
                    prev_one, prev_two = pltpu.roll(now, 1, 0), pltpu.roll(now, 2, 0)
                tap = [vec_ref[3 + 3 * j + role : 4 + 3 * j + role, :] for j in range(3)]
                parts.append(
                    vec_ref[12 + role : 13 + role, :]
                    + tap[0] * now
                    + tap[1] * jnp.where(one, prev_one, 0.0)
                    + tap[2] * jnp.where(two, prev_two, 0.0)
                )
            grad = gg[here].astype(WIDE)
            gs[here, :channels] = grad * mixed[here]
            grad = grad * parts[0]
            gm[here] = grad
            short[here, :channels] = parts[1]
            short[here, channels:] = parts[2]
            direct_sum = direct_sum + jnp.sum(
                grad * (parts[1] * parts[2]), axis=0, keepdims=True
            )
        gs[length:, :] = jnp.zeros((8, three), WIDE)
        sums[15:16, :] = direct_sum
        begin, end, before = long_range(starts_ref, docs, block_len, length)
        ranges = []
        for m in range(docs - 1):
            first, last, base = short_range(starts_ref, docs, m, before, block_len, length)
            base = pl.multiple_of(base, block_len)
            ranges.append((base, inside_mask(base, block_len, channels, first, last)))
        for b in range(blocks):
            mask = inside_mask(b * block_len, block_len, channels, begin, end)
            part = jnp.where(mask, gm[b * block_len : (b + 1) * block_len], 0.0)
            store_triple(xs, slice(b * channels, (b + 1) * channels), part)
        for m, (base, mask) in enumerate(ranges):
            part = jnp.where(mask, gm[pl.ds(base, block_len)], 0.0)
            store_triple(xs, slice((blocks + m) * channels, (blocks + m + 1) * channels), part)
        for e in range(count):
            gt[e] = jnp.dot(
                it3_ref[...], xs[:, e * channels : (e + 1) * channels], preferred_element_type=WIDE
            )
        spec_copy.wait()
        entry_copy.wait()

        @pl.loop(0, block_len // step)
        def _(number):
            at_re = pl.multiple_of(number * step, step)
            at_im = pl.multiple_of(number * step + block_len, step)
            edge = jnp.where(rows_from(at_re, step, channels) == 0, 1.0, 0.0)
            inside = 1.0 - edge

            def load(ref, k):
                return ref[k, pl.ds(at_re, step)], ref[k, pl.ds(at_im, step)]

            def combine(pairs):
                rr = ii = ri = None
                for (a, b), (c, d) in pairs:
                    rr = a * c if rr is None else rr + a * c
                    ii = b * d if ii is None else ii + b * d
                    ri = b * c - a * d if ri is None else ri + (b * c - a * d)
                return rr + inside * ii, inside * ri + edge * ii

            for e in range(count):
                if e < blocks:
                    pairs = [(load(gt, i), load(spec, i - e)) for i in range(e, blocks)]
                else:
                    pairs = [(load(gt, e), load(spec, 0))]
                lanes = slice(e * channels, (e + 1) * channels)
                for part, at in zip(combine(pairs), (at_re, at_im)):
                    high, low = split_low(part)
                    ys[pl.ds(at, step), lanes] = high
                    ys[pl.ds(at + 2 * block_len, step), lanes] = low
                    ys[pl.ds(at + 4 * block_len, step), lanes] = high
            for k in range(blocks):
                pairs = [(load(gt, j + k), load(ent, j)) for j in range(blocks - k)]
                if k == 0:
                    pairs += [(load(gt, e), load(ent, e)) for e in range(blocks, count)]
                out_re, out_im = combine(pairs)
                lags[k, pl.ds(at_re, step)] = out_re
                lags[k, pl.ds(at_im, step)] = out_im

        for b in range(blocks):
            here = slice(b * block_len, (b + 1) * block_len)
            back = jnp.dot(
                ft3_ref[...], ys[:, b * channels : (b + 1) * channels], preferred_element_type=WIDE
            )
            mask = inside_mask(b * block_len, block_len, channels, begin, end)
            gi[here] = jnp.where(mask, back, 0.0) + direct * gm[here]
        for m, (base, mask) in enumerate(ranges):
            lanes = slice((blocks + m) * channels, (blocks + m + 1) * channels)
            back = jnp.dot(ft3_ref[...], ys[:, lanes], preferred_element_type=WIDE)
            where = pl.ds(base, block_len)
            gi[where] = gi[where] + jnp.where(mask, back, 0.0)
        for b in range(blocks):
            here = slice(b * block_len, (b + 1) * block_len)
            gs[here, channels : 2 * channels] = gi[here] * short[here, channels:]
            gs[here, 2 * channels :] = gi[here] * short[here, :channels]
        for role in range(3):
            lanes = slice(role * channels, (role + 1) * channels)
            tap = [vec_ref[3 + 3 * j + role : 4 + 3 * j + role, :] for j in range(3)]
            totals = [jnp.zeros((1, channels), WIDE) for _ in range(5)]
            for b in range(blocks):
                base = b * block_len
                here = slice(base, base + block_len)
                one, two = keep_masks(starts_ref, docs, base, block_len + 8, channels)
                grad = gs[base : base + block_len + 8, lanes]
                pass_one, pass_two = jnp.where(one, grad, 0.0), jnp.where(two, grad, 0.0)
                size = block_len + 8
                result = (
                    tap[0] * grad[:block_len]
                    + tap[1] * pltpu.roll(pass_one, size - 1, 0)[:block_len]
                    + tap[2] * pltpu.roll(pass_two, size - 2, 0)[:block_len]
                ).astype(LOW)
                gp[here, lanes] = result
                now = proj[here, lanes]
                if b:
                    back = proj[base - 8 : base + block_len, lanes]
                    prev_one, prev_two = pltpu.roll(back, 1, 0)[8:], pltpu.roll(back, 2, 0)[8:]
                else:
                    prev_one, prev_two = pltpu.roll(now, 1, 0), pltpu.roll(now, 2, 0)
                terms = [
                    result.astype(WIDE),
                    grad[:block_len] * now,
                    pass_one[:block_len] * prev_one,
                    pass_two[:block_len] * prev_two,
                    grad[:block_len],
                ]
                totals = [
                    total + jnp.sum(term, axis=0, keepdims=True)
                    for total, term in zip(totals, terms)
                ]
            sums[role : role + 1, :] = totals[0]
            for j in range(3):
                sums[3 + 3 * j + role : 4 + 3 * j + role, :] = totals[1 + j]
            sums[12 + role : 13 + role, :] = totals[4]
        rows_copy.wait()
        norm_copy.wait()
        weights = rows[...].reshape(three, width)
        shift_sum = jnp.zeros((1, width), WIDE)
        scale_sum = jnp.zeros((1, width), WIDE)
        for index, offset in enumerate(block_offsets):
            other = place ^ offset
            where = pl.ds(pl.multiple_of(other * block_len, block_len), block_len)
            part = jnp.dot(gp[where], weights, preferred_element_type=WIDE)
            shift_sum = shift_sum + jnp.sum(part, axis=0, keepdims=True)
            scale_sum = scale_sum + jnp.sum(
                part * norm[other].astype(WIDE), axis=0, keepdims=True
            )
            if index < half_block:
                gn_kept[index] = part.astype(LOW)
            else:
                gn_sent[index - half_block] = part.astype(LOW)
        norm_sums[0:1, :] = (scale_sum - norm1_ref[1:2, :] * shift_sum) / norm1_ref[0:1, :]
        norm_sums[1:2, :] = shift_sum
        for c in range(3):
            lanes = slice(c * channels, (c + 1) * channels)
            total = lax.dot_general(
                gp[:, lanes],
                norm[...].reshape(length, width),
                (((0,), (0,)), ((), ())),
                preferred_element_type=WIDE,
            )
            gr[lanes] = total.astype(LOW)
        dealt = gr.reshape(count_dp, groups, share, width)
        leaving = []
        for g in range(groups):
            for index, offset in enumerate(in_offsets[g]):
                target = dealt_refs[g][index // half_dp].at[index % half_dp]
                leaving.append(copies.start(dealt.at[row ^ offset, g], target))
        for copy in leaving:
            copy.wait()

    shape = jax.ShapeDtypeStruct
    half_in = shape((half_dp, share, width), LOW)
    return pl.pallas_call(
        body,
        out_shape=[half_in] * (2 * groups)
        + [
            shape((half_block, block_len, width), LOW),
            shape((half_block, block_len, width), LOW),
            shape((blocks, 2 * block_len, channels), WIDE),
            shape((16, channels), WIDE),
            shape((2, width), WIDE),
        ],
        in_specs=[SMEM_SPACE] * 2 + [VMEM_SPACE] * (4 + blocks) + [ANY_SPACE] * 6,
        out_specs=[ANY_SPACE] * (2 * groups) + [VMEM_SPACE] * 5,
        scratch_shapes=[
            pltpu.VMEM((blocks, 2 * block_len, channels), WIDE),
            pltpu.VMEM((length, three), WIDE),
            pltpu.VMEM((count, 2 * block_len, channels), WIDE),
            pltpu.VMEM((length, channels), WIDE),
            pltpu.VMEM((count_dp, groups, share, width), LOW),
            pltpu.VMEM((blocks, block_len, width), LOW),
            pltpu.VMEM((length, channels), LOW),
            pltpu.VMEM((length, 2 * channels), WIDE),
            pltpu.VMEM((length + 8, three), WIDE),
            pltpu.VMEM((length, channels), WIDE),
            pltpu.VMEM((3 * block_len, count * channels), LOW),
            pltpu.VMEM((count, 2 * block_len, channels), WIDE),
            pltpu.VMEM((6 * block_len, count * channels), LOW),
            pltpu.VMEM((length, channels), WIDE),
            pltpu.VMEM((length, three), LOW),
            pltpu.VMEM((three, width), LOW),
            pltpu.SemaphoreType.DMA((6 + groups * count_dp,)),
        ],
        compiler_params=pltpu.CompilerParams(vmem_limit_bytes=LIMIT),
    )(
        places,
        starts,
        vec,
        norm1,
        it3,
        ft3,
        *grad_pieces,
        spectra,
        proj,
        entries,
        mixed,
        in_rows,
        normed,
    )


def filter_back_call(block_len, blocks, table, ft3, w1, w2, vec, third_at, lags):
    length = block_len * blocks
    channels = vec.shape[1]
    units = w2.shape[1]

    def body(table_ref, w1_ref, w2_ref, vec_ref, ft3_ref, lags_ref, g1, g2, g3, gd):
        one_row = jnp.where(lax.broadcasted_iota(jnp.int32, (8, length), 0) == 0, 1.0, 0.0)

        def product(left, right, dims):
            return lax.dot_general(
                left, right, (dims, ((), ())), precision=HIGHEST, preferred_element_type=WIDE
            )

        z1 = product(w1_ref[...], table_ref[...], ((0,), (0,)))
        first = jnp.concatenate([jnp.sin(z1), one_row], axis=0)
        z2 = product(w2_ref[...], first, ((0,), (0,)))
        second = jnp.sin(z2)
        decay = vec_ref[third_at - 2 : third_at - 1, :]
        third_w = vec_ref[third_at : third_at + units, :]
        half_rows = lax.broadcasted_iota(jnp.int32, (2 * block_len, channels), 0)
        parity = jnp.where(half_rows % 2 == 0, 1.0, -1.0)
        sign = jnp.where(half_rows == block_len, 1.0, parity)
        third_sum = jnp.zeros((units, channels), WIDE)
        decay_sum = jnp.zeros((1, channels), WIDE)
        back = []
        for i in range(blocks):
            grad = sign * lags_ref[i]
            if i + 1 < blocks:
                grad = grad + lags_ref[i + 1]
            high, low = split_low(grad)
            stacked = jnp.concatenate([high, low, high], axis=0)
            grad = jnp.dot(ft3_ref[...], stacked, preferred_element_type=WIDE)
            here = second[:, i * block_len : (i + 1) * block_len]
            third = product(here, third_w, ((0,), (0,)))
            times = rows_from(i * block_len, block_len, channels).astype(WIDE) / (length - 1)
            fall = jnp.exp(-times * decay)
            decay_sum = decay_sum - jnp.sum(grad * third * fall * times, axis=0, keepdims=True)
            grad = grad * (fall + MOD_SHIFT)
            third_sum = third_sum + product(here, grad, ((1,), (0,)))
            back.append(product(third_w, grad, ((1,), (1,))))
        gz2 = jnp.concatenate(back, axis=1) * jnp.cos(z2)
        g2[...] = product(first, gz2, ((1,), (1,)))
        gz1 = product(w2_ref[:units, :], gz2, ((1,), (0,))) * jnp.cos(z1)
        g1[...] = product(table_ref[...], gz1, ((1,), (1,)))
        g3[...] = third_sum
        gd[...] = decay_sum

    shape = jax.ShapeDtypeStruct
    return pl.pallas_call(
        body,
        out_shape=[
            shape(w1.shape, WIDE),
            shape(w2.shape, WIDE),
            shape((units, channels), WIDE),
            shape((1, channels), WIDE),
        ],
        in_specs=[VMEM_SPACE] * 6,
        out_specs=[VMEM_SPACE] * 4,
        compiler_params=pltpu.CompilerParams(vmem_limit_bytes=LIMIT),
    )(table, w1, w2, vec, ft3, lags)


def local(
    block_in,
    doc_starts,
    norm1_gain,
    norm1_bias,
    w_in,
    b_in,
    short_taps,
    short_bias,
    filter_w1,
    filter_b1,
    filter_w2,
    filter_b2,
    filter_w3,
    filter_decay,
    conv_bias,
    w_out,
    b_out,
    norm2_gain,
    norm2_bias,
    w_up,
    b_up,
    w_down,
    b_down,
    cotangent,
):
    count_dp, blocks = lax.axis_size("dp"), lax.axis_size("block")
    grid = Grid(count_dp, blocks)
    row, place = grid.row, grid.place
    _, block_len, width = block_in.shape
    length = block_len * blocks
    hidden_width = w_up.shape[1] * count_dp
    hidden_here = hidden_width // blocks
    dp_steps = grid.dp_steps
    block_steps = grid.chip_steps + [grid.core_step]
    block_offsets = [b for _, b in offsets_of(block_steps)]

    def rotated(turn):
        turn = turn % len(dp_steps)
        return dp_steps[turn:] + dp_steps[:turn]

    def dp_offsets(steps):
        return [a for a, _ in offsets_of(steps)]

    shard_in, shard_out = w_in.shape[1], w_out.shape[1]
    group = math.gcd(width, shard_in)
    groups_here, share = shard_in // group, group // blocks
    channels = width // blocks
    bands = width // group
    vectors = jnp.concatenate(
        [
            b_in.reshape(3, width),
            short_taps.reshape(9, width),
            short_bias.reshape(3, width),
            filter_decay[None],
            conv_bias[None],
            filter_w3,
        ],
        axis=0,
    )
    vectors = lax.dynamic_index_in_dim(
        vectors.reshape(vectors.shape[0], bands, blocks, share), place, 2, keepdims=False
    ).reshape(vectors.shape[0], channels)
    b_in_here = vectors[:3].reshape(-1)
    taps = vectors[3:12].reshape(3, 3 * channels)
    short_shift = vectors[12:15].reshape(-1)
    decay_here, direct, third_here = vectors[15], vectors[16], vectors[17:]

    in_turned = w_in.T.reshape(groups_here, blocks, share, width)
    in_own = lax.dynamic_index_in_dim(in_turned, place, 1, keepdims=False)
    in_orders = [rotated(i) for i in range(groups_here)]
    in_offsets = [dp_offsets(order) for order in in_orders]
    in_pieces = [grid.gather(in_own[i], in_orders[i]) for i in range(groups_here)]
    kernels = channels % 128 == 0 and share % 32 == 0 and groups_here == 3

    inputs = block_in.astype(WIDE).reshape(block_len, width)
    normed, norm1_back = jax.vjp(layer_norm, inputs, norm1_gain, norm1_bias)
    normed_low = normed.astype(LOW)
    normed_pieces = grid.gather(normed_low, block_steps)

    up_order, down_order, out_dp_order = rotated(1), rotated(2), rotated(0)
    piece = w_up.shape[1] // blocks
    up_own = lax.dynamic_slice_in_dim(w_up, place * piece, piece, 1).T
    up_rows = arrange(grid.gather(up_own, up_order), row, dp_offsets(up_order)).reshape(
        hidden_here, width
    )
    b_up_here = lax.dynamic_index_in_dim(
        b_up.reshape(count_dp, blocks, piece), place, 1, keepdims=False
    ).reshape(hidden_here)
    down_own = w_down.reshape(count_dp, blocks, piece, w_down.shape[1])
    down_own = lax.dynamic_index_in_dim(down_own, place, 1, keepdims=False)
    down_own = down_own.reshape(hidden_here, w_down.shape[1]).T
    down_rows = arrange(grid.gather(down_own, down_order), row, dp_offsets(down_order)).reshape(
        width, hidden_here
    )

    out_own = w_out.reshape(bands, blocks, share, shard_out)
    out_own = lax.dynamic_index_in_dim(out_own, place, 1, keepdims=False)
    out_own = out_own.reshape(channels, shard_out).T
    out_dealt = arrange(grid.gather(out_own, out_dp_order), row, dp_offsets(out_dp_order))
    out_rows = jnp.concatenate(grid.gather(out_dealt.reshape(width, channels), block_steps), axis=0)
    cot_flat = cotangent.reshape(block_len, width)
    cot_all = jnp.concatenate(grid.gather(cot_flat, block_steps), axis=0).reshape(length, width)

    forward_table, inverse_table, sign, edge = transform_tables(block_len)
    starts = doc_starts[0]
    positions = jnp.arange(length, dtype=jnp.int32)
    segment = jnp.sum((starts[None, :] <= positions[:, None]).astype(jnp.int32), axis=-1) - 1
    keep_one = jnp.concatenate([jnp.zeros((1,), WIDE), (segment[1:] == segment[:-1]).astype(WIDE)])
    keep_two = jnp.concatenate([jnp.zeros((2,), WIDE), (segment[2:] == segment[:-2]).astype(WIDE)])
    keep_one, keep_two = keep_one[:, None], keep_two[:, None]
    num_docs = doc_starts.shape[1]
    long_doc = jnp.sum((starts <= block_len).astype(jnp.int32)) - 1
    long_mask = (segment == long_doc).astype(WIDE)[:, None]
    first_segment, last_segment = segment[:block_len], segment[length - block_len :]
    short_early, short_masks = [], []
    for number in range(num_docs - 1):
        early = number < long_doc
        doc = jnp.where(early, number, number + 1)
        where = jnp.where(early, first_segment, last_segment)
        short_early.append(early.astype(WIDE))
        short_masks.append((where == doc).astype(WIDE)[:, None])

    def spread(values):
        masked = values * long_mask
        parts = [masked[i * block_len : (i + 1) * block_len] for i in range(blocks)]
        first, last = values[:block_len], values[length - block_len :]
        for early, mask in zip(short_early, short_masks):
            parts.append(mask * (early * first + (1.0 - early) * last))
        return jnp.concatenate(parts, axis=1)

    def collect(values):
        parts = [
            values[:, i * channels : (i + 1) * channels] for i in range(blocks + num_docs - 1)
        ]
        first, last = jnp.zeros_like(parts[0]), jnp.zeros_like(parts[0])
        for early, mask, part in zip(short_early, short_masks, parts[blocks:]):
            first = first + early * mask * part
            last = last + (1.0 - early) * mask * part
        joined = jnp.concatenate(parts[:blocks], axis=0) * long_mask
        middle = jnp.zeros((length - 2 * block_len, channels), WIDE)
        return joined + jnp.concatenate([first, middle, last], axis=0)

    def cut(values, count):
        return [values[:, i * channels : (i + 1) * channels] for i in range(count)]

    forward_three, inverse_three = triple(forward_table), triple(inverse_table)
    table, times = position_table(length, filter_w1.shape[0])

    if kernels:
        spectra_held = filter_call(
            block_len,
            blocks,
            turned_table(table),
            forward_three,
            with_bias(filter_w1, filter_b1),
            with_bias(filter_w2, filter_b2),
            vectors,
            17,
        )
        made = conv_call(
            block_len,
            blocks,
            jnp.stack([row, place]).astype(jnp.int32),
            starts,
            normed_pieces,
            in_pieces,
            in_offsets,
            block_offsets,
            vectors,
            spectra_held,
            forward_three,
            inverse_three,
        )
        gated_own, (proj, entries_held, mixed, in_rows, normed_all) = made[:blocks], made[blocks:]
    else:
        def filter_spectra(params):
            first = jnp.sin(dot_high(table, params[0]) + params[1])
            second = jnp.sin(dot_high(first, params[2]) + params[3])
            kernel = dot_high(second, params[4]) * (
                jnp.exp(-times[:, None] * params[5][None, :]) + MOD_SHIFT
            )
            pieces = jnp.concatenate(
                [kernel[i * block_len : (i + 1) * block_len] for i in range(blocks)], axis=1
            )
            halves = dot_near(forward_table, pieces)
            earlier = jnp.concatenate(
                [jnp.zeros((2 * block_len, channels), WIDE), halves[:, : (blocks - 1) * channels]],
                axis=1,
            )
            return earlier + sign[:, None] * halves

        spectra_flat, filter_back = jax.vjp(
            filter_spectra,
            (filter_w1, filter_b1, filter_w2, filter_b2, third_here, decay_here),
        )
        normed_all = arrange(normed_pieces, place, block_offsets).reshape(length, width)
        in_rows = jnp.stack(
            [arrange(in_pieces[i], row, in_offsets[i]) for i in range(groups_here)], axis=1
        ).reshape(3 * channels, width)
        spectra = cut(spectra_flat, blocks)
        proj = dot_last(normed_all, in_rows) + b_in_here
    three = 3 * channels
    prev_one = jnp.concatenate([jnp.zeros((1, three), WIDE), proj[:-1]], axis=0) * keep_one
    prev_two = jnp.concatenate([jnp.zeros((2, three), WIDE), proj[:-2]], axis=0) * keep_two
    short = short_shift + taps[0] * proj + taps[1] * prev_one + taps[2] * prev_two
    gate_part, mult, value = cut(short, 3)
    inner = value * mult

    if not kernels:
        entries = cut(dot_near(forward_table, spread(inner)), blocks + num_docs - 1)
        totals = []
        for i in range(blocks):
            total = spectral_product(entries[i], spectra[0], edge)
            for j in range(i):
                total = total + spectral_product(entries[j], spectra[i - j], edge)
            totals.append(total)
        for entry in entries[blocks:]:
            totals.append(spectral_product(entry, spectra[0], edge))
        mixed = collect(dot_near(inverse_table, jnp.concatenate(totals, axis=1))) + direct * inner
        gated_low = (gate_part * mixed).astype(LOW)

        gated_own = [
            lax.dynamic_slice_in_dim(gated_low, (place ^ offset) * block_len, block_len, 0)
            for offset in block_offsets
        ]

    gated_parts = [
        grid.swap(part, (0, offset)) if offset else part
        for part, offset in zip(gated_own, block_offsets)
    ]
    branch = b_out
    for part, rows in zip(gated_parts, out_rows):
        branch = branch + dot_last(part, rows)
    resid = inputs + branch
    normed2, norm2_back = jax.vjp(layer_norm, resid, norm2_gain, norm2_bias)
    normed2_low = normed2.astype(LOW)

    normed2_all = jnp.concatenate(grid.gather(normed2_low, block_steps), axis=0)
    normed2_all = normed2_all.reshape(length, width)
    hidden = dot_last(normed2_all, up_rows) + b_up_here
    act, gelu_back = jax.vjp(exact_gelu, hidden)
    act_low = act.astype(LOW)
    grad_act = dot_plain(cot_all, down_rows)
    grad_hidden = gelu_back(grad_act)[0].astype(LOW)

    def to_tokens(partial):
        split = partial.astype(LOW).reshape(blocks, block_len, width)
        return grid.scatter(split[: blocks // 2], split[blocks // 2 :], block_steps).astype(WIDE)

    grad_normed2 = to_tokens(dot_plain(grad_hidden, up_rows))
    output = resid + to_tokens(dot_last(act_low, down_rows)) + b_down
    block_out = output.astype(LOW)[None]
    grad_b_up_here = jnp.sum(grad_hidden.astype(WIDE), axis=0)
    grad_b_down = jnp.sum(cot_flat.astype(WIDE), axis=0)

    def send_home(natural, order):
        natural = natural.astype(LOW).reshape(count_dp, -1, natural.shape[-1])
        return grid.scatter(*deal(natural, row, dp_offsets(order)), order)

    up_grad = send_home(dot_first(grad_hidden, normed2_all), up_order)
    down_grad = send_home(dot_first(cot_all, act_low), down_order)

    resid_part, grad_gain_two, grad_bias_two = norm2_back(grad_normed2)
    grad_resid = cot_flat.astype(WIDE) + resid_part
    grad_branch = grad_resid.astype(LOW)
    grad_b_out = jnp.sum(grad_branch.astype(WIDE), axis=0)
    grad_parts = []
    for index, offset in enumerate(block_offsets):
        part = dot_plain(grad_branch, out_rows[index]).astype(LOW)
        grad_parts.append((grid.swap(part, (0, offset)) if offset else part)[None])
    out_sums = jnp.stack([dot_first(grad_branch, part).astype(LOW) for part in gated_parts], axis=0)
    out_sums = grid.scatter(out_sums[: blocks // 2], out_sums[blocks // 2 :], block_steps)
    out_grad = send_home(out_sums, out_dp_order)

    if kernels:
        made = back_call(
            block_len,
            blocks,
            jnp.stack([row, place]).astype(jnp.int32),
            starts,
            [part[0] for part in grad_parts],
            in_offsets,
            block_offsets,
            vectors,
            jnp.stack([norm1_gain, norm1_bias]),
            spectra_held,
            proj,
            entries_held,
            mixed,
            in_rows,
            normed_all,
            triple(inverse_table.T),
            triple(forward_table.T),
        )
        in_dealt = [(made[2 * i], made[2 * i + 1]) for i in range(groups_here)]
        made = made[2 * groups_here :]
        normed_dealt, (grad_lags, sums, norm_sums) = made[:2], made[2:]
        grad_b_in, grad_taps, grad_short_bias = sums[:3], sums[3:12], sums[12:15]
        grad_conv_bias = sums[15]
        filter_grads = filter_back_call(
            block_len,
            blocks,
            turned_table(table),
            triple(forward_table.T),
            with_bias(filter_w1, filter_b1),
            with_bias(filter_w2, filter_b2),
            vectors,
            17,
            grad_lags,
        )
        rows_one, rows_two = filter_w1.shape[0], filter_w2.shape[0]
        filter_grads = (
            filter_grads[0][:rows_one],
            filter_grads[0][rows_one],
            filter_grads[1][:rows_two],
            filter_grads[1][rows_two],
            filter_grads[2],
            filter_grads[3][0],
        )
    else:
        grad_gated = arrange(grad_parts, place, block_offsets)
        grad_gated = grad_gated.reshape(length, channels).astype(WIDE)
        grad_gate_part = grad_gated * mixed
        grad_mixed = grad_gated * gate_part
        grad_conv_bias = jnp.sum(grad_mixed * inner, axis=0)
        grad_totals = cut(
            lax.dot_general(
                inverse_table,
                spread(grad_mixed),
                (((0,), (0,)), ((), ())),
                precision=HIGH,
                preferred_element_type=WIDE,
            ),
            blocks + num_docs - 1,
        )
        grad_entries = []
        grad_lags = [None] * blocks
        for i in range(blocks + num_docs - 1):
            lag = spectral_back(grad_totals[i], entries[i], edge)
            grad_lags[0] = lag if grad_lags[0] is None else grad_lags[0] + lag
            grad_entries.append(spectral_back(grad_totals[i], spectra[0], edge))
        for j in range(blocks):
            for i in range(j + 1, blocks):
                grad_entries[j] = grad_entries[j] + spectral_back(
                    grad_totals[i], spectra[i - j], edge
                )
                lag = spectral_back(grad_totals[i], entries[j], edge)
                grad_lags[i - j] = lag if grad_lags[i - j] is None else grad_lags[i - j] + lag
        filter_grads = filter_back(jnp.concatenate(grad_lags, axis=1))[0]
        grad_inner = (
            collect(
                lax.dot_general(
                    forward_table,
                    jnp.concatenate(grad_entries, axis=1),
                    (((0,), (0,)), ((), ())),
                    precision=HIGH,
                    preferred_element_type=WIDE,
                )
            )
            + direct * grad_mixed
        )
        grad_short = jnp.concatenate([grad_gate_part, grad_inner * value, grad_inner * mult], axis=1)
        grad_taps = jnp.stack(
            [
                jnp.sum(grad_short * proj, axis=0),
                jnp.sum(grad_short * prev_one, axis=0),
                jnp.sum(grad_short * prev_two, axis=0),
            ],
            axis=0,
        )
        grad_short_bias = jnp.sum(grad_short, axis=0)
        pass_one = grad_short * keep_one
        pass_two = grad_short * keep_two
        grad_proj = (
            taps[0] * grad_short
            + taps[1] * jnp.concatenate([pass_one[1:], jnp.zeros((1, three), WIDE)], axis=0)
            + taps[2] * jnp.concatenate([pass_two[2:], jnp.zeros((2, three), WIDE)], axis=0)
        )
        grad_proj_low = grad_proj.astype(LOW)
        grad_b_in = jnp.sum(grad_proj_low.astype(WIDE), axis=0)
        grad_in_rows = dot_first(grad_proj_low, normed_all)
        grad_in_split = grad_in_rows.reshape(count_dp, groups_here, share, width)
        in_dealt = [
            deal(grad_in_split[:, i].astype(LOW), row, in_offsets[i]) for i in range(groups_here)
        ]
        grad_normed_part = dot_plain(grad_proj_low, in_rows).astype(LOW)
        normed_dealt = deal(
            grad_normed_part.reshape(blocks, block_len, width), place, block_offsets
        )
    in_grads = [grid.scatter(*in_dealt[i], in_orders[i]) for i in range(groups_here)]
    grad_normed = grid.scatter(*normed_dealt, block_steps).astype(WIDE)
    input_part, grad_gain_one, grad_bias_one = norm1_back(grad_normed)
    if kernels:
        grad_gain_one, grad_bias_one = norm_sums[0], norm_sums[1]
    grad_input = (grad_resid + input_part)[None]

    def all_places(value):
        return arrange(grid.gather(value, block_steps), place, block_offsets)

    in_whole = all_places(jnp.concatenate(in_grads, axis=0))
    in_whole = in_whole.reshape(blocks, groups_here, share, width)
    in_whole = in_whole.transpose(3, 1, 0, 2).reshape(width, shard_in).astype(WIDE)
    if up_grad.shape[1] == down_grad.shape[1]:
        ff_whole = all_places(jnp.concatenate([up_grad, down_grad], axis=0))
        up_whole, down_whole = ff_whole[:, :piece], ff_whole[:, piece:]
    else:
        up_whole, down_whole = all_places(up_grad), all_places(down_grad)
    up_whole = up_whole.reshape(blocks * piece, width).T.astype(WIDE)
    down_whole = down_whole.reshape(blocks, w_down.shape[1], count_dp, piece)
    down_whole = down_whole.transpose(2, 0, 3, 1).reshape(hidden_width, w_down.shape[1])
    down_whole = down_whole.astype(WIDE)
    out_whole = all_places(out_grad).reshape(blocks, shard_out, bands, share)
    out_whole = out_whole.transpose(2, 0, 3, 1).reshape(width, shard_out).astype(WIDE)

    shared = [
        grad_gain_one,
        grad_bias_one,
        grad_b_out,
        grad_gain_two,
        grad_bias_two,
        grad_b_down,
        filter_grads[0],
        filter_grads[1],
        filter_grads[2],
        filter_grads[3],
    ]
    flat = jnp.concatenate([item.reshape(-1) for item in shared])
    unit = blocks * channels
    chunk = -(-flat.shape[0] // unit)
    flat = jnp.pad(flat, (0, chunk * unit - flat.shape[0])).reshape(blocks, chunk, channels)
    dealt = [lax.dynamic_slice_in_dim(flat, place ^ offset, 1, 0) for offset in block_offsets]
    half = blocks // 2
    shared_part = grid.scatter(
        jnp.concatenate(dealt[:half], axis=0), jnp.concatenate(dealt[half:], axis=0), block_steps
    )
    joined = jnp.concatenate(
        [
            shared_part,
            jnp.pad(grad_b_up_here, (0, -hidden_here % channels)).reshape(-1, channels),
            grad_b_in.reshape(3, channels),
            grad_taps.reshape(9, channels),
            grad_short_bias.reshape(3, channels),
            filter_grads[5][None],
            grad_conv_bias[None],
            filter_grads[4],
        ],
        axis=0,
    )
    for step in dp_steps:
        joined = joined + grid.swap(joined, step)
    every = all_places(joined)
    whole_flat = every[:, :chunk].reshape(-1)
    shared_out, at = [], 0
    for item in shared:
        shared_out.append(whole_flat[at : at + item.size].reshape(item.shape))
        at += item.size
    at = chunk + -(-hidden_here // channels)
    grad_b_up = every[:, chunk:at].reshape(blocks, -1)[:, :hidden_here]
    grad_b_up = grad_b_up.reshape(blocks, count_dp, piece)
    grad_b_up = grad_b_up.transpose(1, 0, 2).reshape(hidden_width)
    rest = every[:, at:].reshape(blocks, -1, bands, share).transpose(1, 2, 0, 3)
    rest = rest.reshape(-1, width)
    return (
        block_out,
        grad_input,
        shared_out[0],
        shared_out[1],
        in_whole,
        rest[:3].reshape(3 * width),
        rest[3:12].reshape(3, 3 * width),
        rest[12:15].reshape(3 * width),
        shared_out[6],
        shared_out[7],
        shared_out[8],
        shared_out[9],
        rest[17:],
        rest[15],
        rest[16],
        out_whole,
        shared_out[2],
        shared_out[3],
        shared_out[4],
        up_whole,
        grad_b_up,
        down_whole,
        shared_out[5],
    )


def solution(mesh):
    placed = (
        P("dp", "block", None),
        P("dp", None),
        P(),
        P(),
        P(None, "dp"),
        P(),
        P(),
        P(),
        P(),
        P(),
        P(),
        P(),
        P(),
        P(),
        P(),
        P(None, "dp"),
        P(),
        P(),
        P(),
        P(None, "dp"),
        P(),
        P(None, "dp"),
        P(),
        P("dp", "block", None),
    )
    return jax.shard_map(
        local,
        mesh=mesh,
        in_specs=placed,
        out_specs=(
            P("dp", "block", None),
            P("dp", "block", None),
            P(),
            P(),
            P(None, "dp"),
            P(),
            P(),
            P(),
            P(),
            P(),
            P(),
            P(),
            P(),
            P(),
            P(),
            P(None, "dp"),
            P(),
            P(),
            P(),
            P(None, "dp"),
            P(),
            P(None, "dp"),
            P(),
        ),
        check_vma=False,
    )
```

```python
import math

import jax
import jax.numpy as jnp
import ml_dtypes
import numpy as np
from jax import lax
from jax.experimental import pallas as pl
from jax.experimental.pallas import tpu as pltpu
from jax.sharding import PartitionSpec as P

EPSILON = 1e-05
MOD_SHIFT = 0.05
HIGHEST = lax.Precision.HIGHEST
HIGH = lax.Precision.HIGH
LOW = jnp.bfloat16
WIDE = jnp.float32


def dot_high(left, right):
    return jnp.dot(left, right, precision=HIGHEST, preferred_element_type=WIDE)


def dot_near(left, right):
    return jnp.dot(left, right, precision=HIGH, preferred_element_type=WIDE)


def dot_plain(left, right):
    return jnp.dot(left, right, preferred_element_type=WIDE)


def dot_first(left, right):
    return lax.dot_general(left, right, (((0,), (0,)), ((), ())), preferred_element_type=WIDE)


def dot_last(left, right):
    return lax.dot_general(left, right, (((1,), (1,)), ((), ())), preferred_element_type=WIDE)


def layer_norm(values, gain, bias):
    mean = jnp.mean(values, axis=-1, keepdims=True)
    centered = values - mean
    variance = jnp.mean(centered * centered, axis=-1, keepdims=True)
    return centered * lax.rsqrt(variance + EPSILON) * gain + bias


def exact_gelu(values):
    return jax.nn.gelu(values, approximate=False)


def position_table(length, emb_dim):
    bands = (emb_dim - 1) // 2
    sample = np.arange(length, dtype=np.float32)
    times = sample / np.float32(length - 1)
    frequency = np.linspace(0.0001, bands - 1, bands).astype(np.float32)
    angle = np.float32(2.0 * math.pi) * sample[:, None] * frequency[None, :] / np.float32(length)
    table = np.concatenate([times[:, None], np.cos(angle), -np.sin(angle)], axis=1)
    return (table.astype(np.float32), times)


def transform_tables(block_len):
    span = 2 * block_len
    frequency = np.arange(block_len)
    sample = np.arange(block_len)
    is_zero = (frequency == 0)[:, None]
    angle = 2.0 * math.pi * (frequency[:, None] * sample[None, :] % span) / span
    alternate = np.where(sample % 2 == 0, 1.0, -1.0)
    real_rows = np.cos(angle)
    imag_rows = np.where(is_zero, alternate[None, :], -np.sin(angle))
    forward_table = np.concatenate([real_rows, imag_rows], axis=0)
    outputs = sample + block_len
    out_angle = 2.0 * math.pi * (outputs[:, None] * frequency[None, :] % span) / span
    out_alternate = np.where(outputs % 2 == 0, 1.0, -1.0)
    zero_col = (frequency == 0)[None, :]
    real_cols = np.where(zero_col, 1.0, 2.0) * np.cos(out_angle) / span
    imag_cols = np.where(zero_col, out_alternate[:, None] / span, -2.0 * np.sin(out_angle) / span)
    inverse_table = np.concatenate([real_cols, imag_cols], axis=1)
    parity = np.where(frequency % 2 == 0, 1.0, -1.0)
    sign = np.concatenate([parity, np.where(frequency == 0, 1.0, parity)])
    edge = (frequency == 0).astype(np.float32)[:, None]
    return tuple(item.astype(np.float32) for item in (forward_table, inverse_table, sign, edge))


def spectral_product(left, right, edge):
    half = left.shape[-2] // 2
    left_re, left_im = (left[..., :half, :], left[..., half:, :])
    right_re, right_im = (right[..., :half, :], right[..., half:, :])
    inside = 1.0 - edge
    out_re = left_re * right_re - inside * left_im * right_im
    out_im = inside * (left_re * right_im + left_im * right_re) + edge * left_im * right_im
    return jnp.concatenate([out_re, out_im], axis=-2)


def spectral_back(grad, other, edge):
    half = grad.shape[-2] // 2
    grad_re, grad_im = (grad[..., :half, :], grad[..., half:, :])
    other_re, other_im = (other[..., :half, :], other[..., half:, :])
    inside = 1.0 - edge
    back_re = grad_re * other_re + inside * grad_im * other_im
    back_im = inside * (grad_im * other_re - grad_re * other_im) + edge * grad_im * other_im
    return jnp.concatenate([back_re, back_im], axis=-2)


class Grid:
    def __init__(self, count_dp, count_block):
        self.count_dp = count_dp
        self.count_block = count_block
        self.row = lax.axis_index("dp")
        self.place = lax.axis_index("block")
        self.dp_steps = []
        bit = 1
        while bit < count_dp:
            self.dp_steps.append((bit | (bit >> 1) if bit == 4 else bit, 0))
            bit *= 2
        self.chip_steps = []
        bit = 2
        while bit < count_block:
            self.chip_steps.append((0, bit | (bit >> 1) if bit == 4 else bit))
            bit *= 2
        self.core_step = (0, 1)

    def swap(self, value, step):
        pairs = []
        for row in range(self.count_dp):
            for place in range(self.count_block):
                to = (row ^ step[0]) * self.count_block + (place ^ step[1])
                pairs.append((row * self.count_block + place, to))
        return lax.ppermute(value, ("dp", "block"), pairs)

    def gather(self, value, steps, gates=()):
        held = value[None]
        pieces = [held]
        for number, step in enumerate(steps):
            if number < len(gates):
                held = after(held, *gates[number])
            pieces.append(self.swap(held, step))
            if number + 1 < len(steps):
                held = jnp.concatenate(pieces, axis=0)
        return pieces

    def scatter(self, kept, sent, steps, whole=True, sends=None, adds=None):
        for number, step in enumerate(reversed(steps)):
            if sends and number in sends:
                sent = after(sent, *sends[number])
            arrived = self.swap(sent, step)
            if adds and number in adds:
                arrived = after(arrived, *adds[number])
            half = kept.shape[0] // 2
            if not half and not whole:
                return kept[0], arrived[0]
            if half:
                sent = add_low(kept[half:], arrived[half:])
                kept = add_low(kept[:half], arrived[:half])
            else:
                kept = add_low(kept, arrived)
        return kept[0]

    def halve(self, kept, sent, step):
        return halves(kept, self.swap(sent, step))


def halves(left, right):
    half = left.shape[0] // 2
    return add_low(left[:half], right[:half]), add_low(left[half:], right[half:])


def add_low(left, right):
    return (left.astype(WIDE) + right.astype(WIDE)).astype(left.dtype)


def offsets_of(steps):
    offsets = [(0, 0)]
    for step in steps:
        offsets = offsets + [(a ^ step[0], b ^ step[1]) for a, b in offsets]
    return offsets


def arrange(pieces, mine, offsets):
    shape = pieces[0].shape[1:]
    if shape[-2] % 32 or shape[-1] % 128:
        held = jnp.concatenate(pieces, axis=0)
        codes = codes_of(offsets, len(offsets))
        return jnp.concatenate(
            [
                lax.dynamic_slice_in_dim(held, place_in(codes, k ^ mine), 1, 0)
                for k in range(len(offsets))
            ],
            axis=0,
        )
    count = len(pieces)

    def kernel(mine_ref, *refs):
        source, target = refs[:count], refs[count]
        at = 0
        for ref in source:
            for i in range(ref.shape[0]):
                target[mine_ref[0] ^ offsets[at]] = ref[i]
                at += 1

    return pl.pallas_call(
        kernel,
        out_shape=jax.ShapeDtypeStruct((len(offsets), *shape), pieces[0].dtype),
        in_specs=[pl.BlockSpec(memory_space=pltpu.SMEM)]
        + [pl.BlockSpec(memory_space=pltpu.VMEM)] * count,
        out_specs=pl.BlockSpec(memory_space=pltpu.VMEM),
    )(jnp.reshape(mine, (1,)).astype(jnp.int32), *pieces)


def deal(natural, mine, offsets):
    half = len(offsets) // 2
    shape = natural.shape[1:]
    if shape[-2] % 32 or shape[-1] % 128:
        dealt = [lax.dynamic_slice_in_dim(natural, mine ^ offset, 1, 0) for offset in offsets]
        return jnp.concatenate(dealt[:half], axis=0), jnp.concatenate(dealt[half:], axis=0)

    def kernel(mine_ref, source, kept, sent):
        for at, offset in enumerate(offsets):
            if at < half:
                kept[at] = source[mine_ref[0] ^ offset]
            else:
                sent[at - half] = source[mine_ref[0] ^ offset]

    out = jax.ShapeDtypeStruct((half, *shape), natural.dtype)
    vmem = pl.BlockSpec(memory_space=pltpu.VMEM)
    return pl.pallas_call(
        kernel,
        out_shape=(out, out),
        in_specs=[pl.BlockSpec(memory_space=pltpu.SMEM), vmem],
        out_specs=(vmem, vmem),
    )(jnp.reshape(mine, (1,)).astype(jnp.int32), natural)


def place_in(codes, offset):
    place = 0
    for j, code in enumerate(codes):
        place = place ^ (((offset >> j) & 1) * code)
    return place


def codes_of(offsets, count):
    codes, bit = [], 1
    while bit < count:
        codes.append(offsets.index(bit))
        bit *= 2
    return codes


def split_low(values):
    high = values.astype(LOW)
    return high, (values - high.astype(WIDE)).astype(LOW)


def triple(table):
    high = table.astype(ml_dtypes.bfloat16)
    low = (table - high.astype(np.float32)).astype(ml_dtypes.bfloat16)
    return np.concatenate([high, high, low], axis=1)


def store_triple(target, columns, values):
    high, low = split_low(values)
    size = values.shape[0]
    target[0:size, columns] = high
    target[size : 2 * size, columns] = low
    target[2 * size : 3 * size, columns] = high


def long_range(starts, count, block_len, length):
    begin, end, before = starts[0], jnp.int32(length), jnp.int32(-1)
    for d in range(count):
        begin = jnp.where(starts[d] <= block_len, starts[d], begin)
        before = before + jnp.where(starts[d] <= block_len, 1, 0)
    for d in reversed(range(count)):
        end = jnp.where(starts[d] > block_len, starts[d], end)
    return begin, end, before


def short_range(starts, count, number, before, block_len, length):
    early = number < before
    bounds = [starts[d] for d in range(count)] + [jnp.int32(length)]
    begin = jnp.where(early, bounds[number], bounds[number + 1])
    end = jnp.where(early, bounds[number + 1], bounds[number + 2])
    return begin, end, jnp.where(early, 0, length - block_len)


def rows_from(base, size, lanes):
    return lax.broadcasted_iota(jnp.int32, (size, lanes), 0) + base


def inside_mask(base, size, lanes, begin, end):
    rows = rows_from(base, size, lanes)
    return (rows >= begin) & (rows < end)


def keep_masks(starts, count, base, size, lanes):
    rows = rows_from(base, size, lanes)
    one = rows != starts[0]
    for d in range(1, count):
        one = one & (rows != starts[d])
    two = one
    for d in range(count):
        two = two & (rows != starts[d] + 1)
    return one, two


VMEM_SPACE = pl.BlockSpec(memory_space=pltpu.VMEM)
ANY_SPACE = pl.BlockSpec(memory_space=pl.ANY)
SMEM_SPACE = pl.BlockSpec(memory_space=pltpu.SMEM)
LIMIT = 30 * 1024 * 1024
WHOLE = 56 * 1024 * 1024


def cost(microseconds):
    return pl.CostEstimate(
        flops=int(microseconds * 1e9), bytes_accessed=int(microseconds * 3e6), transcendentals=0
    )


class Copies:
    def __init__(self, sems):
        self.sems, self.used = sems, 0

    def start(self, source, target):
        copy = pltpu.make_async_copy(source, target, self.sems.at[self.used])
        self.used += 1
        copy.start()
        return copy


def filter_kernel(block_len, blocks, table_ref, w1, w2, vec, third_at, f3_ref, spectra):
    length = block_len * blocks
    channels = vec.shape[1]
    one_row = jnp.where(lax.broadcasted_iota(jnp.int32, (8, length), 0) == 0, 1.0, 0.0)

    def turned(left, right):
        return lax.dot_general(
            left, right, (((0,), (0,)), ((), ())), precision=HIGHEST, preferred_element_type=WIDE
        )

    first = jnp.sin(turned(w1[...], table_ref[...]))
    second = jnp.sin(turned(w2[...], jnp.concatenate([first, one_row], axis=0)))
    decay = vec[third_at - 2 : third_at - 1, :]
    third_w = vec[third_at : third_at + second.shape[0], :]
    before = None
    half_rows = lax.broadcasted_iota(jnp.int32, (2 * block_len, channels), 0)
    parity = jnp.where(half_rows % 2 == 0, 1.0, -1.0)
    sign = jnp.where(half_rows == block_len, 1.0, parity)
    for i in range(blocks):
        part = turned(second[:, i * block_len : (i + 1) * block_len], third_w)
        times = rows_from(i * block_len, block_len, channels).astype(WIDE) / (length - 1)
        part = part * (jnp.exp(-times * decay) + MOD_SHIFT)
        high, low = split_low(part)
        stacked = jnp.concatenate([high, low, high], axis=0)
        half = jnp.dot(f3_ref[...], stacked, preferred_element_type=WIDE)
        spectra[i] = sign * half if before is None else before + sign * half
        before = half


def with_bias(weights, bias):
    rows = weights.shape[0]
    return jnp.pad(jnp.concatenate([weights, bias[None]], axis=0), ((0, -(rows + 1) % 8), (0, 0)))


def turned_table(table):
    length, count = table.shape
    rows = [table.T, np.ones((1, length), np.float32)]
    rows.append(np.zeros((-(count + 1) % 8, length), np.float32))
    return np.concatenate(rows, axis=0)


def filter_call(block_len, blocks, table, f3, w1, w2, vec, third_at):
    channels = vec.shape[1]

    def body(table_ref, w1_ref, w2_ref, vec_ref, f3_ref, spectra, mark):
        filter_kernel(
            block_len, blocks, table_ref, w1_ref, w2_ref, vec_ref, third_at, f3_ref, spectra
        )
        mark[...] = w1_ref[...]

    return pl.pallas_call(
        body,
        out_shape=[
            jax.ShapeDtypeStruct((blocks, 2 * block_len, channels), WIDE),
            jax.ShapeDtypeStruct(w1.shape, WIDE),
        ],
        in_specs=[VMEM_SPACE] * 5,
        out_specs=[VMEM_SPACE] * 2,
        compiler_params=pltpu.CompilerParams(vmem_limit_bytes=LIMIT),
        cost_estimate=cost(7),
    )(table, w1, w2, vec, f3)


def gather_in(copies, pieces, mine, offsets, target):
    started, at = [], 0
    for ref in pieces:
        for i in range(ref.shape[0]):
            started.append(copies.start(ref.at[i], target.at[mine ^ offsets[at]]))
            at += 1
    return started


def conv_call(
    block_len, blocks, places, starts, normed_pieces, in_pieces, in_offsets, block_offsets, vec, spectra, f3, i3
):
    length = block_len * blocks
    channels = vec.shape[1]
    docs = starts.shape[0]
    entries = blocks + docs - 1
    width = normed_pieces[0].shape[-1]
    groups = len(in_pieces)
    share = in_pieces[0][0].shape[1]
    count_dp = len(in_offsets[0])
    flat_in = [piece for pieces in in_pieces for piece in pieces]
    n_norm, n_in, n_out = len(normed_pieces), len(flat_in), blocks
    step = 16

    def body(place_ref, starts_ref, vec_ref, f3_ref, i3_ref, spectra_ref, *refs):
        norm_refs, in_refs = refs[:n_norm], refs[n_norm : n_norm + n_in]
        refs = refs[n_norm + n_in :]
        gated_refs, (proj_out, entry_out, mixed_out, rows_out, norm_out) = refs[:n_out], refs[n_out : n_out + 5]
        norm, rows, proj, inner, gate, xs, ent, ys, mixed, spec, sems = refs[n_out + 5 :]
        row, place = place_ref[0], place_ref[1]
        copies = Copies(sems)
        waiting = gather_in(copies, norm_refs, place, block_offsets, norm)
        at = 0
        for g in range(groups):
            count = len(in_pieces[g])
            index = 0
            for ref in in_refs[at : at + count]:
                for i in range(ref.shape[0]):
                    to = row ^ in_offsets[g][index]
                    waiting.append(copies.start(ref.at[i], rows.at[to, g]))
                    index += 1
            at += count
        spec_copy = copies.start(spectra_ref, spec)
        for copy in waiting:
            copy.wait()
        leaving = [copies.start(norm, norm_out), copies.start(rows, rows_out)]

        flat_rows = rows[...].reshape(3 * channels, width)
        for role in range(3):
            weights = flat_rows[role * channels : (role + 1) * channels]
            bias = vec_ref[role : role + 1, :]
            for b in range(blocks):
                proj[b * block_len : (b + 1) * block_len, role * channels : (role + 1) * channels] = (
                    lax.dot_general(
                        norm[b],
                        weights,
                        (((1,), (1,)), ((), ())),
                        preferred_element_type=WIDE,
                    )
                    + bias
                )
        leaving.append(copies.start(proj, proj_out))
        for b in range(blocks):
            base = b * block_len
            one, two = keep_masks(starts_ref, docs, base, block_len, channels)
            parts = []
            for role in range(3):
                lanes = slice(role * channels, (role + 1) * channels)
                here = proj[base : base + block_len, lanes]
                if b:
                    back = proj[base - 8 : base + block_len, lanes]
                    prev_one = pltpu.roll(back, 1, 0)[8:]
                    prev_two = pltpu.roll(back, 2, 0)[8:]
                else:
                    prev_one, prev_two = pltpu.roll(here, 1, 0), pltpu.roll(here, 2, 0)
                tap = [vec_ref[3 + 3 * j + role : 4 + 3 * j + role, :] for j in range(3)]
                short = (
                    vec_ref[12 + role : 13 + role, :]
                    + tap[0] * here
                    + tap[1] * jnp.where(one, prev_one, 0.0)
                    + tap[2] * jnp.where(two, prev_two, 0.0)
                )
                parts.append(short)
            gate[base : base + block_len] = parts[0]
            inner[base : base + block_len] = parts[1] * parts[2]
        begin, end, before = long_range(starts_ref, docs, block_len, length)
        for b in range(blocks):
            mask = inside_mask(b * block_len, block_len, channels, begin, end)
            part = jnp.where(mask, inner[b * block_len : (b + 1) * block_len], 0.0)
            store_triple(xs, slice(b * channels, (b + 1) * channels), part)
        for m in range(docs - 1):
            first, last, base = short_range(starts_ref, docs, m, before, block_len, length)
            base = pl.multiple_of(base, block_len)
            mask = inside_mask(base, block_len, channels, first, last)
            part = jnp.where(mask, inner[pl.ds(base, block_len)], 0.0)
            store_triple(xs, slice((blocks + m) * channels, (blocks + m + 1) * channels), part)
        for e in range(entries):
            ent[e] = jnp.dot(
                f3_ref[...], xs[:, e * channels : (e + 1) * channels], preferred_element_type=WIDE
            )
        leaving.append(copies.start(ent, entry_out))
        spec_copy.wait()

        @pl.loop(0, block_len // step)
        def _(number):
            at_re = pl.multiple_of(number * step, step)
            at_im = pl.multiple_of(number * step + block_len, step)
            edge = jnp.where(rows_from(at_re, step, channels) == 0, 1.0, 0.0)
            inside = 1.0 - edge
            keys = [(spec[k, pl.ds(at_re, step)], spec[k, pl.ds(at_im, step)]) for k in range(blocks)]
            held = [(ent[k, pl.ds(at_re, step)], ent[k, pl.ds(at_im, step)]) for k in range(blocks)]
            for e in range(entries):
                pairs = (
                    [(held[j], keys[e - j]) for j in range(e + 1)]
                    if e < blocks
                    else [((ent[e, pl.ds(at_re, step)], ent[e, pl.ds(at_im, step)]), keys[0])]
                )
                rr = ii = ri = None
                for (a, b), (c, d) in pairs:
                    rr = a * c if rr is None else rr + a * c
                    ii = b * d if ii is None else ii + b * d
                    ri = a * d + b * c if ri is None else ri + (a * d + b * c)
                lanes = slice(e * channels, (e + 1) * channels)
                out_re = rr - inside * ii
                out_im = inside * ri + edge * ii
                for part, at in ((out_re, at_re), (out_im, at_im)):
                    high, low = split_low(part)
                    ys[pl.ds(at, step), lanes] = high
                    ys[pl.ds(at + 2 * block_len, step), lanes] = low
                    ys[pl.ds(at + 4 * block_len, step), lanes] = high

        direct = vec_ref[16:17, :]
        for b in range(blocks):
            back = jnp.dot(
                i3_ref[...], ys[:, b * channels : (b + 1) * channels], preferred_element_type=WIDE
            )
            rows_here = slice(b * block_len, (b + 1) * block_len)
            mask = inside_mask(b * block_len, block_len, channels, begin, end)
            mixed[rows_here] = jnp.where(mask, back, 0.0) + direct * inner[rows_here]
        for m in range(docs - 1):
            lanes = slice((blocks + m) * channels, (blocks + m + 1) * channels)
            back = jnp.dot(i3_ref[...], ys[:, lanes], preferred_element_type=WIDE)
            first, last, base = short_range(starts_ref, docs, m, before, block_len, length)
            base = pl.multiple_of(base, block_len)
            mask = inside_mask(base, block_len, channels, first, last)
            where = pl.ds(base, block_len)
            mixed[where] = mixed[where] + jnp.where(mask, back, 0.0)
        leaving.append(copies.start(mixed, mixed_out))
        for index, offset in enumerate(block_offsets):
            where = pl.ds(pl.multiple_of((place ^ offset) * block_len, block_len), block_len)
            gated_refs[index][...] = (gate[where] * mixed[where]).astype(LOW)
        for copy in leaving:
            copy.wait()

    shape = jax.ShapeDtypeStruct
    sem_count = blocks + groups * count_dp + 6
    return pl.pallas_call(
        body,
        out_shape=[shape((block_len, channels), LOW)] * blocks
        + [
            shape((length, 3 * channels), WIDE),
            shape((entries, 2 * block_len, channels), WIDE),
            shape((length, channels), WIDE),
            shape((count_dp, groups, share, width), LOW),
            shape((blocks, block_len, width), LOW),
        ],
        in_specs=[SMEM_SPACE, SMEM_SPACE, VMEM_SPACE, VMEM_SPACE, VMEM_SPACE, ANY_SPACE]
        + [ANY_SPACE] * (n_norm + n_in),
        out_specs=[VMEM_SPACE] * blocks + [ANY_SPACE] * 5,
        scratch_shapes=[
            pltpu.VMEM((blocks, block_len, width), LOW),
            pltpu.VMEM((count_dp, groups, share, width), LOW),
            pltpu.VMEM((length, 3 * channels), WIDE),
            pltpu.VMEM((length, channels), WIDE),
            pltpu.VMEM((length, channels), WIDE),
            pltpu.VMEM((3 * block_len, entries * channels), LOW),
            pltpu.VMEM((entries, 2 * block_len, channels), WIDE),
            pltpu.VMEM((6 * block_len, entries * channels), LOW),
            pltpu.VMEM((length, channels), WIDE),
            pltpu.VMEM((blocks, 2 * block_len, channels), WIDE),
            pltpu.SemaphoreType.DMA((sem_count,)),
        ],
        compiler_params=pltpu.CompilerParams(vmem_limit_bytes=WHOLE),
        cost_estimate=cost(14),
    )(places, starts, vec, f3, i3, spectra, *normed_pieces, *flat_in)


def back_call(
    block_len,
    blocks,
    places,
    starts,
    grad_pieces,
    block_offsets,
    vec,
    spectra,
    proj,
    entries,
    mixed,
    it3,
    ft3,
):
    length = block_len * blocks
    channels = vec.shape[1]
    docs = starts.shape[0]
    count = entries.shape[0]
    three = 3 * channels
    step = 16

    def body(place_ref, starts_ref, vec_ref, it3_ref, ft3_ref, *refs):
        grad_refs, refs = refs[:blocks], refs[blocks:]
        spectra_ref, proj_ref, entry_ref, mixed_ref, lags, direct_out, gs_out = refs[:7]
        spec, proj, ent, mixed, gg, short, gs, gm, xs, gt, ys, gi, sems = refs[7:]
        place = place_ref[1]
        copies = Copies(sems)
        proj_copy = copies.start(proj_ref, proj)
        mixed_copy = copies.start(mixed_ref, mixed)
        spec_copy = copies.start(spectra_ref, spec)
        entry_copy = copies.start(entry_ref, ent)
        for index, offset in enumerate(block_offsets):
            where = pl.ds(pl.multiple_of((place ^ offset) * block_len, block_len), block_len)
            gg[where] = grad_refs[index][...]
        proj_copy.wait()
        mixed_copy.wait()
        direct = vec_ref[16:17, :]
        direct_sum = jnp.zeros((1, channels), WIDE)
        for b in range(blocks):
            base = b * block_len
            here = slice(base, base + block_len)
            one, two = keep_masks(starts_ref, docs, base, block_len, channels)
            parts = []
            for role in range(3):
                lanes = slice(role * channels, (role + 1) * channels)
                now = proj[here, lanes]
                if b:
                    back = proj[base - 8 : base + block_len, lanes]
                    prev_one, prev_two = pltpu.roll(back, 1, 0)[8:], pltpu.roll(back, 2, 0)[8:]
                else:
                    prev_one, prev_two = pltpu.roll(now, 1, 0), pltpu.roll(now, 2, 0)
                tap = [vec_ref[3 + 3 * j + role : 4 + 3 * j + role, :] for j in range(3)]
                parts.append(
                    vec_ref[12 + role : 13 + role, :]
                    + tap[0] * now
                    + tap[1] * jnp.where(one, prev_one, 0.0)
                    + tap[2] * jnp.where(two, prev_two, 0.0)
                )
            grad = gg[here].astype(WIDE)
            gs[here, :channels] = grad * mixed[here]
            grad = grad * parts[0]
            gm[here] = grad
            short[here, :channels] = parts[1]
            short[here, channels:] = parts[2]
            direct_sum = direct_sum + jnp.sum(
                grad * (parts[1] * parts[2]), axis=0, keepdims=True
            )
        gs[length:, :] = jnp.zeros((8, three), WIDE)
        direct_out[...] = direct_sum
        begin, end, before = long_range(starts_ref, docs, block_len, length)
        ranges = []
        for m in range(docs - 1):
            first, last, base = short_range(starts_ref, docs, m, before, block_len, length)
            base = pl.multiple_of(base, block_len)
            ranges.append((base, inside_mask(base, block_len, channels, first, last)))
        for b in range(blocks):
            mask = inside_mask(b * block_len, block_len, channels, begin, end)
            part = jnp.where(mask, gm[b * block_len : (b + 1) * block_len], 0.0)
            store_triple(xs, slice(b * channels, (b + 1) * channels), part)
        for m, (base, mask) in enumerate(ranges):
            part = jnp.where(mask, gm[pl.ds(base, block_len)], 0.0)
            store_triple(xs, slice((blocks + m) * channels, (blocks + m + 1) * channels), part)
        for e in range(count):
            gt[e] = jnp.dot(
                it3_ref[...], xs[:, e * channels : (e + 1) * channels], preferred_element_type=WIDE
            )
        spec_copy.wait()
        entry_copy.wait()

        @pl.loop(0, block_len // step)
        def _(number):
            at_re = pl.multiple_of(number * step, step)
            at_im = pl.multiple_of(number * step + block_len, step)
            edge = jnp.where(rows_from(at_re, step, channels) == 0, 1.0, 0.0)
            inside = 1.0 - edge

            def load(ref, k):
                return ref[k, pl.ds(at_re, step)], ref[k, pl.ds(at_im, step)]

            def combine(pairs):
                rr = ii = ri = None
                for (a, b), (c, d) in pairs:
                    rr = a * c if rr is None else rr + a * c
                    ii = b * d if ii is None else ii + b * d
                    ri = b * c - a * d if ri is None else ri + (b * c - a * d)
                return rr + inside * ii, inside * ri + edge * ii

            for e in range(count):
                if e < blocks:
                    pairs = [(load(gt, i), load(spec, i - e)) for i in range(e, blocks)]
                else:
                    pairs = [(load(gt, e), load(spec, 0))]
                lanes = slice(e * channels, (e + 1) * channels)
                for part, at in zip(combine(pairs), (at_re, at_im)):
                    high, low = split_low(part)
                    ys[pl.ds(at, step), lanes] = high
                    ys[pl.ds(at + 2 * block_len, step), lanes] = low
                    ys[pl.ds(at + 4 * block_len, step), lanes] = high
            for k in range(blocks):
                pairs = [(load(gt, j + k), load(ent, j)) for j in range(blocks - k)]
                if k == 0:
                    pairs += [(load(gt, e), load(ent, e)) for e in range(blocks, count)]
                out_re, out_im = combine(pairs)
                lags[k, pl.ds(at_re, step)] = out_re
                lags[k, pl.ds(at_im, step)] = out_im

        for b in range(blocks):
            here = slice(b * block_len, (b + 1) * block_len)
            back = jnp.dot(
                ft3_ref[...], ys[:, b * channels : (b + 1) * channels], preferred_element_type=WIDE
            )
            mask = inside_mask(b * block_len, block_len, channels, begin, end)
            gi[here] = jnp.where(mask, back, 0.0) + direct * gm[here]
        for m, (base, mask) in enumerate(ranges):
            lanes = slice((blocks + m) * channels, (blocks + m + 1) * channels)
            back = jnp.dot(ft3_ref[...], ys[:, lanes], preferred_element_type=WIDE)
            where = pl.ds(base, block_len)
            gi[where] = gi[where] + jnp.where(mask, back, 0.0)
        for b in range(blocks):
            here = slice(b * block_len, (b + 1) * block_len)
            gs[here, channels : 2 * channels] = gi[here] * short[here, channels:]
            gs[here, 2 * channels :] = gi[here] * short[here, :channels]
        copies.start(gs, gs_out).wait()

    shape = jax.ShapeDtypeStruct
    return pl.pallas_call(
        body,
        out_shape=[
            shape((blocks, 2 * block_len, channels), WIDE),
            shape((1, channels), WIDE),
            shape((length + 8, three), WIDE),
        ],
        in_specs=[SMEM_SPACE] * 2 + [VMEM_SPACE] * (3 + blocks) + [ANY_SPACE] * 4,
        out_specs=[VMEM_SPACE, VMEM_SPACE, ANY_SPACE],
        scratch_shapes=[
            pltpu.VMEM((blocks, 2 * block_len, channels), WIDE),
            pltpu.VMEM((length, three), WIDE),
            pltpu.VMEM((count, 2 * block_len, channels), WIDE),
            pltpu.VMEM((length, channels), WIDE),
            pltpu.VMEM((length, channels), LOW),
            pltpu.VMEM((length, 2 * channels), WIDE),
            pltpu.VMEM((length + 8, three), WIDE),
            pltpu.VMEM((length, channels), WIDE),
            pltpu.VMEM((3 * block_len, count * channels), LOW),
            pltpu.VMEM((count, 2 * block_len, channels), WIDE),
            pltpu.VMEM((6 * block_len, count * channels), LOW),
            pltpu.VMEM((length, channels), WIDE),
            pltpu.SemaphoreType.DMA((5,)),
        ],
        compiler_params=pltpu.CompilerParams(vmem_limit_bytes=LIMIT),
        cost_estimate=cost(14),
    )(places, starts, vec, it3, ft3, *grad_pieces, spectra, proj, entries, mixed)


def project_back_call(
    block_len,
    blocks,
    places,
    starts,
    in_offsets,
    block_offsets,
    vec,
    norm1,
    direct,
    grad_short,
    proj,
    in_rows,
    normed,
):
    length = block_len * blocks
    channels = vec.shape[1]
    docs = starts.shape[0]
    count_dp, groups, share, width = in_rows.shape
    three = 3 * channels
    half_dp, half_block = count_dp // 2, blocks // 2

    def body(place_ref, starts_ref, vec_ref, gain_ref, shift_ref, direct_ref, *refs):
        gs_ref, proj_ref, rows_ref, norm_ref = refs[:4]
        refs = refs[4:]
        dealt_refs = [(refs[2 * g], refs[2 * g + 1]) for g in range(groups)]
        refs = refs[2 * groups :]
        gn_kept, gn_sent, sums, norm_sums = refs[:4]
        gs, proj, rows, norm, gp, gr, sems = refs[4:]
        row, place = place_ref[0], place_ref[1]
        copies = Copies(sems)
        gs_copy = copies.start(gs_ref, gs)
        proj_copy = copies.start(proj_ref, proj)
        rows_copy = copies.start(rows_ref, rows)
        norm_copy = copies.start(norm_ref, norm)
        sums[15:16, :] = direct_ref[...]
        gs_copy.wait()
        proj_copy.wait()
        for role in range(3):
            lanes = slice(role * channels, (role + 1) * channels)
            tap = [vec_ref[3 + 3 * j + role : 4 + 3 * j + role, :] for j in range(3)]
            totals = [jnp.zeros((1, channels), WIDE) for _ in range(5)]
            for b in range(blocks):
                base = b * block_len
                here = slice(base, base + block_len)
                one, two = keep_masks(starts_ref, docs, base, block_len + 8, channels)
                grad = gs[base : base + block_len + 8, lanes]
                pass_one, pass_two = jnp.where(one, grad, 0.0), jnp.where(two, grad, 0.0)
                size = block_len + 8
                result = (
                    tap[0] * grad[:block_len]
                    + tap[1] * pltpu.roll(pass_one, size - 1, 0)[:block_len]
                    + tap[2] * pltpu.roll(pass_two, size - 2, 0)[:block_len]
                ).astype(LOW)
                gp[here, lanes] = result
                now = proj[here, lanes]
                if b:
                    back = proj[base - 8 : base + block_len, lanes]
                    prev_one, prev_two = pltpu.roll(back, 1, 0)[8:], pltpu.roll(back, 2, 0)[8:]
                else:
                    prev_one, prev_two = pltpu.roll(now, 1, 0), pltpu.roll(now, 2, 0)
                terms = [
                    result.astype(WIDE),
                    grad[:block_len] * now,
                    pass_one[:block_len] * prev_one,
                    pass_two[:block_len] * prev_two,
                    grad[:block_len],
                ]
                totals = [
                    total + jnp.sum(term, axis=0, keepdims=True)
                    for total, term in zip(totals, terms)
                ]
            sums[role : role + 1, :] = totals[0]
            for j in range(3):
                sums[3 + 3 * j + role : 4 + 3 * j + role, :] = totals[1 + j]
            sums[12 + role : 13 + role, :] = totals[4]
        rows_copy.wait()
        norm_copy.wait()
        weights = rows[...].reshape(three, width)
        shift_sum = jnp.zeros((1, width), WIDE)
        scale_sum = jnp.zeros((1, width), WIDE)
        for index, offset in enumerate(block_offsets):
            other = place ^ offset
            where = pl.ds(pl.multiple_of(other * block_len, block_len), block_len)
            part = jnp.dot(gp[where], weights, preferred_element_type=WIDE)
            shift_sum = shift_sum + jnp.sum(part, axis=0, keepdims=True)
            scale_sum = scale_sum + jnp.sum(
                part * norm[other].astype(WIDE), axis=0, keepdims=True
            )
            if index < half_block:
                gn_kept[index] = part.astype(LOW)
            else:
                gn_sent[index - half_block] = part.astype(LOW)
        norm_sums[0:1, :] = (scale_sum - shift_ref[...] * shift_sum) / gain_ref[...]
        norm_sums[1:2, :] = shift_sum
        for c in range(3):
            lanes = slice(c * channels, (c + 1) * channels)
            total = lax.dot_general(
                gp[:, lanes],
                norm[...].reshape(length, width),
                (((0,), (0,)), ((), ())),
                preferred_element_type=WIDE,
            )
            gr[lanes] = total.astype(LOW)
        dealt = gr.reshape(count_dp, groups, share, width)
        leaving = []
        for g in range(groups):
            for index, offset in enumerate(in_offsets[g]):
                target = dealt_refs[g][index // half_dp].at[index % half_dp]
                leaving.append(copies.start(dealt.at[row ^ offset, g], target))
        for copy in leaving:
            copy.wait()

    shape = jax.ShapeDtypeStruct
    half_in = shape((half_dp, share, width), LOW)
    return pl.pallas_call(
        body,
        out_shape=[half_in] * (2 * groups)
        + [
            shape((half_block, block_len, width), LOW),
            shape((half_block, block_len, width), LOW),
            shape((16, channels), WIDE),
            shape((2, width), WIDE),
        ],
        in_specs=[SMEM_SPACE] * 2 + [VMEM_SPACE] * 4 + [ANY_SPACE] * 4,
        out_specs=[ANY_SPACE] * (2 * groups) + [VMEM_SPACE] * 4,
        scratch_shapes=[
            pltpu.VMEM((length + 8, three), WIDE),
            pltpu.VMEM((length, three), WIDE),
            pltpu.VMEM((count_dp, groups, share, width), LOW),
            pltpu.VMEM((blocks, block_len, width), LOW),
            pltpu.VMEM((length, three), LOW),
            pltpu.VMEM((three, width), LOW),
            pltpu.SemaphoreType.DMA((4 + groups * count_dp,)),
        ],
        compiler_params=pltpu.CompilerParams(vmem_limit_bytes=LIMIT),
        cost_estimate=cost(10),
    )(places, starts, vec, *norm1, direct, grad_short, proj, in_rows, normed)


def filter_back_call(block_len, blocks, table, ft3, w1, w2, vec, third_at, lags):
    length = block_len * blocks
    channels = vec.shape[1]
    units = w2.shape[1]

    def body(table_ref, w1_ref, w2_ref, vec_ref, ft3_ref, lags_ref, g1, g2, g3, gd):
        one_row = jnp.where(lax.broadcasted_iota(jnp.int32, (8, length), 0) == 0, 1.0, 0.0)

        def product(left, right, dims):
            return lax.dot_general(
                left, right, (dims, ((), ())), precision=HIGHEST, preferred_element_type=WIDE
            )

        z1 = product(w1_ref[...], table_ref[...], ((0,), (0,)))
        first = jnp.concatenate([jnp.sin(z1), one_row], axis=0)
        z2 = product(w2_ref[...], first, ((0,), (0,)))
        second = jnp.sin(z2)
        decay = vec_ref[third_at - 2 : third_at - 1, :]
        third_w = vec_ref[third_at : third_at + units, :]
        half_rows = lax.broadcasted_iota(jnp.int32, (2 * block_len, channels), 0)
        parity = jnp.where(half_rows % 2 == 0, 1.0, -1.0)
        sign = jnp.where(half_rows == block_len, 1.0, parity)
        third_sum = jnp.zeros((units, channels), WIDE)
        decay_sum = jnp.zeros((1, channels), WIDE)
        back = []
        for i in range(blocks):
            grad = sign * lags_ref[i]
            if i + 1 < blocks:
                grad = grad + lags_ref[i + 1]
            high, low = split_low(grad)
            stacked = jnp.concatenate([high, low, high], axis=0)
            grad = jnp.dot(ft3_ref[...], stacked, preferred_element_type=WIDE)
            here = second[:, i * block_len : (i + 1) * block_len]
            third = product(here, third_w, ((0,), (0,)))
            times = rows_from(i * block_len, block_len, channels).astype(WIDE) / (length - 1)
            fall = jnp.exp(-times * decay)
            decay_sum = decay_sum - jnp.sum(grad * third * fall * times, axis=0, keepdims=True)
            grad = grad * (fall + MOD_SHIFT)
            third_sum = third_sum + product(here, grad, ((1,), (0,)))
            back.append(product(third_w, grad, ((1,), (1,))))
        gz2 = jnp.concatenate(back, axis=1) * jnp.cos(z2)
        g2[...] = product(first, gz2, ((1,), (1,)))
        gz1 = product(w2_ref[:units, :], gz2, ((1,), (0,))) * jnp.cos(z1)
        g1[...] = product(table_ref[...], gz1, ((1,), (1,)))
        g3[...] = third_sum
        gd[...] = decay_sum

    shape = jax.ShapeDtypeStruct
    return pl.pallas_call(
        body,
        out_shape=[
            shape(w1.shape, WIDE),
            shape(w2.shape, WIDE),
            shape((units, channels), WIDE),
            shape((1, channels), WIDE),
        ],
        in_specs=[VMEM_SPACE] * 6,
        out_specs=[VMEM_SPACE] * 4,
        compiler_params=pltpu.CompilerParams(vmem_limit_bytes=LIMIT),
        cost_estimate=cost(9),
    )(table, w1, w2, vec, ft3, lags)


def norm_parts(values):
    mean = jnp.mean(values, axis=-1, keepdims=True)
    centered = values - mean
    variance = jnp.mean(centered * centered, axis=-1, keepdims=True)
    scale = lax.rsqrt(variance + EPSILON)
    return centered * scale, scale


def gather_out(copies, refs, row, dp_offsets, target):
    started, at = [], 0
    for ref in refs:
        for i in range(ref.shape[0]):
            for r, offset in enumerate(dp_offsets):
                started.append(copies.start(ref.at[i, r], target.at[at, row ^ offset]))
            at += 1
    return started


def branch_call(row, inputs, gated_parts, out_pieces, dp_offsets, rows):
    blocks = len(gated_parts)
    tokens, channels = gated_parts[0].shape
    width = inputs.shape[-1]
    shard = out_pieces[0].shape[2]
    count_dp = len(dp_offsets)

    def body(row_ref, in_ref, bias_ref, gain_ref, shift_ref, *refs):
        gated_refs, piece_refs = refs[:blocks], refs[blocks : blocks + len(out_pieces)]
        resid_ref, normed_ref, weights, sems = refs[blocks + len(out_pieces) :]
        copies = Copies(sems)
        waiting = gather_out(copies, piece_refs, row_ref[0], dp_offsets, weights)
        for copy in waiting:
            copy.wait()
        total = in_ref[...].astype(WIDE) + bias_ref[...]
        for i in range(blocks):
            total = total + dot_last(
                gated_refs[i][...], weights[i].reshape(width, channels)
            )
        resid_ref[...] = total
        normal, _ = norm_parts(total)
        normed_ref[...] = (normal * gain_ref[...] + shift_ref[...]).astype(LOW)

    shape = jax.ShapeDtypeStruct
    return pl.pallas_call(
        body,
        out_shape=[shape((tokens, width), WIDE), shape((tokens, width), LOW)],
        in_specs=[SMEM_SPACE] + [VMEM_SPACE] * (4 + blocks) + [ANY_SPACE] * len(out_pieces),
        out_specs=[VMEM_SPACE] * 2,
        scratch_shapes=[
            pltpu.VMEM((blocks, count_dp, shard, channels), LOW),
            pltpu.SemaphoreType.DMA((blocks * count_dp,)),
        ],
        compiler_params=pltpu.CompilerParams(vmem_limit_bytes=LIMIT),
        cost_estimate=cost(5),
    )(row, inputs, *rows, *gated_parts, *out_pieces)


def branch_back_call(row, resid, kept, arrived, cot, out_pieces, dp_offsets, gain):
    tokens, width = resid.shape
    blocks = sum(piece.shape[0] for piece in out_pieces)
    shard, channels = out_pieces[0].shape[2:]
    count_dp = len(dp_offsets)

    def body(row_ref, resid_ref, kept_ref, arrived_ref, cot_ref, gain_ref, *refs):
        piece_refs, refs = refs[: len(out_pieces)], refs[len(out_pieces) :]
        grad_refs, (whole_ref, branch_ref, sums, weights, sems) = refs[:blocks], refs[blocks:]
        copies = Copies(sems)
        waiting = gather_out(copies, piece_refs, row_ref[0], dp_offsets, weights)
        grad = kept_ref[...].astype(WIDE) + arrived_ref[...].astype(WIDE)
        normal, scale = norm_parts(resid_ref[...])
        scaled = grad * gain_ref[...]
        back = scaled - jnp.mean(scaled, axis=-1, keepdims=True)
        back = back - normal * jnp.mean(scaled * normal, axis=-1, keepdims=True)
        whole = cot_ref[...].astype(WIDE) + back * scale
        whole_ref[...] = whole
        low = whole.astype(LOW)
        branch_ref[...] = low
        sums[0:1, :] = jnp.sum(low.astype(WIDE), axis=0, keepdims=True)
        sums[1:2, :] = jnp.sum(grad * normal, axis=0, keepdims=True)
        sums[2:3, :] = jnp.sum(grad, axis=0, keepdims=True)
        sums[3:4, :] = jnp.sum(cot_ref[...].astype(WIDE), axis=0, keepdims=True)
        for copy in waiting:
            copy.wait()
        for i in range(blocks):
            grad_refs[i][...] = dot_plain(low, weights[i].reshape(width, channels)).astype(LOW)

    shape = jax.ShapeDtypeStruct
    return pl.pallas_call(
        body,
        out_shape=[shape((tokens, channels), LOW)] * blocks
        + [shape((tokens, width), WIDE), shape((tokens, width), LOW), shape((4, width), WIDE)],
        in_specs=[SMEM_SPACE] + [VMEM_SPACE] * 5 + [ANY_SPACE] * len(out_pieces),
        out_specs=[VMEM_SPACE] * (blocks + 3),
        scratch_shapes=[
            pltpu.VMEM((blocks, count_dp, shard, channels), LOW),
            pltpu.SemaphoreType.DMA((blocks * count_dp,)),
        ],
        compiler_params=pltpu.CompilerParams(vmem_limit_bytes=LIMIT),
        cost_estimate=cost(5),
    )(row, resid, kept, arrived, cot, gain, *out_pieces)


def out_grad_call(row, grad_branch, gated_parts, dp_offsets):
    blocks = len(gated_parts)
    tokens, channels = gated_parts[0].shape
    width = grad_branch.shape[1]
    count_dp = len(dp_offsets)
    shard = width // count_dp
    half = blocks // 2

    def body(row_ref, grad_ref, *refs):
        gated_refs, (kept, sent, total) = refs[:blocks], refs[blocks:]
        for i in range(blocks):
            total[...] = dot_first(grad_ref[...], gated_refs[i][...]).astype(LOW)
            target, at = (kept, i) if i < half else (sent, i - half)
            for r, offset in enumerate(dp_offsets):
                begin = pl.multiple_of((row_ref[0] ^ offset) * shard, shard)
                target[at * count_dp + r] = total[pl.ds(begin, shard)]

    out = jax.ShapeDtypeStruct((half * count_dp, shard, channels), LOW)
    return pl.pallas_call(
        body,
        out_shape=[out, out],
        in_specs=[SMEM_SPACE] + [VMEM_SPACE] * (1 + blocks),
        out_specs=[VMEM_SPACE] * 2,
        scratch_shapes=[pltpu.VMEM((width, channels), LOW)],
        compiler_params=pltpu.CompilerParams(vmem_limit_bytes=LIMIT),
        cost_estimate=cost(3),
    )(row, grad_branch, *gated_parts)


def forward_call(row, normed_pieces, cot_pieces, up_pieces, down_pieces, up_offsets, down_offsets, bias):
    tokens, width = normed_pieces[0].shape[1:]
    blocks = sum(piece.shape[0] for piece in normed_pieces)
    count_dp = len(up_offsets)
    piece = up_pieces[0].shape[1]
    shard = down_pieces[0].shape[1]
    units = piece * count_dp
    tile = 256 if units % 256 == 0 else units
    half = blocks // 2
    lists = (normed_pieces, cot_pieces, up_pieces, down_pieces)
    counts = [len(part) for part in lists]

    def body(row_ref, bias_ref, *refs):
        taken = []
        for count in counts:
            taken.append(refs[:count])
            refs = refs[count:]
        out_kept, out_sent, grad_kept, grad_sent, act_out, hid_out, norm_out, cot_out, sums = refs[:9]
        norm, cot, up, down, act, hid, sems = refs[9:]
        copies = Copies(sems)
        norm_copies = gather_in(copies, taken[0], 0, range(blocks), norm)
        up_copies = gather_in(copies, taken[2], row_ref[0], up_offsets, up)
        cot_copies = gather_in(copies, taken[1], 0, range(blocks), cot)
        down_copies = gather_in(copies, taken[3], row_ref[0], down_offsets, down)
        for copy in norm_copies + up_copies:
            copy.wait()
        up_rows = up[...].reshape(units, width)
        first = dot_last(norm[0], up_rows[:tile])
        for copy in cot_copies + down_copies:
            copy.wait()
        leaving = [copies.start(norm, norm_out), copies.start(cot, cot_out)]
        down_rows = down[...].reshape(width, units)
        for f in range(units // tile):
            lanes = slice(f * tile, (f + 1) * tile)
            total = jnp.zeros((1, tile), WIDE)
            for t in range(blocks):
                hidden = first if f == t == 0 else dot_last(norm[t], up_rows[lanes])
                hidden = hidden + bias_ref[:, lanes]
                grad = dot_plain(cot[t], down_rows[:, lanes])
                below = 0.5 * (1.0 + lax.erf(hidden * math.sqrt(0.5)))
                slope = below + hidden * (
                    jnp.exp(-0.5 * hidden * hidden) * (1.0 / math.sqrt(2.0 * math.pi))
                )
                act[t, :, lanes] = (hidden * below).astype(LOW)
                grad = (grad * slope).astype(LOW)
                hid[t, :, lanes] = grad
                total = total + jnp.sum(grad.astype(WIDE), axis=0, keepdims=True)
            sums[:, lanes] = total
        leaving += [copies.start(act, act_out), copies.start(hid, hid_out)]
        for t in range(blocks):
            back = dot_plain(hid[t], up_rows).astype(LOW)
            out = dot_last(act[t], down_rows).astype(LOW)
            if t < half:
                grad_kept[t] = back
                out_kept[t] = out
            else:
                grad_sent[t - half] = back
                out_sent[t - half] = out
        for copy in leaving:
            copy.wait()

    shape = jax.ShapeDtypeStruct
    part = shape((half, tokens, width), LOW)
    return pl.pallas_call(
        body,
        out_shape=[part] * 4
        + [shape((blocks, tokens, units), LOW)] * 2
        + [shape((blocks, tokens, width), LOW)] * 2
        + [shape((1, units), WIDE)],
        in_specs=[SMEM_SPACE, VMEM_SPACE] + [ANY_SPACE] * sum(counts),
        out_specs=[VMEM_SPACE] * 4 + [ANY_SPACE] * 4 + [VMEM_SPACE],
        scratch_shapes=[
            pltpu.VMEM((blocks, tokens, width), LOW),
            pltpu.VMEM((blocks, tokens, width), LOW),
            pltpu.VMEM((count_dp, piece, width), LOW),
            pltpu.VMEM((count_dp, shard, units), LOW),
            pltpu.VMEM((blocks, tokens, units), LOW),
            pltpu.VMEM((blocks, tokens, units), LOW),
            pltpu.SemaphoreType.DMA((2 * blocks + 2 * count_dp + 4,)),
        ],
        compiler_params=pltpu.CompilerParams(vmem_limit_bytes=LIMIT),
        cost_estimate=cost(17),
    )(row, bias, *normed_pieces, *cot_pieces, *up_pieces, *down_pieces)


def weight_grad_call(row, pairs, offset_lists):
    blocks, tokens, rows = pairs[0][0].shape
    width = pairs[0][1].shape[2]
    count_dp = len(offset_lists[0])
    quarter, share = count_dp // 4, rows // count_dp
    tile = 256 if rows % 256 == 0 else rows
    count = len(pairs)

    def body(row_ref, *refs):
        sources, targets = refs[: 2 * count], refs[2 * count : 6 * count]
        totals, sems = refs[6 * count : 7 * count], refs[7 * count]
        copies = Copies(sems)
        leaving = []
        for p in range(count):
            left_ref, right_ref, total = sources[2 * p], sources[2 * p + 1], totals[p]
            right_all = right_ref[...].reshape(blocks * tokens, width)
            for c in range(rows // tile):
                lanes = slice(c * tile, (c + 1) * tile)
                total[lanes] = dot_first(
                    left_ref[:, :, lanes].reshape(blocks * tokens, tile), right_all
                ).astype(LOW)
            for index, offset in enumerate(offset_lists[p]):
                begin = pl.multiple_of((row_ref[0] ^ offset) * share, share)
                target = targets[4 * p + index // quarter].at[index % quarter]
                leaving.append(copies.start(total.at[pl.ds(begin, share)], target))
        for copy in leaving:
            copy.wait()

    return pl.pallas_call(
        body,
        out_shape=[jax.ShapeDtypeStruct((quarter, share, width), LOW)] * (4 * count),
        in_specs=[SMEM_SPACE] + [VMEM_SPACE] * (2 * count),
        out_specs=[ANY_SPACE] * (4 * count),
        scratch_shapes=[pltpu.VMEM((rows, width), LOW)] * count
        + [pltpu.SemaphoreType.DMA((count * count_dp,))],
        compiler_params=pltpu.CompilerParams(vmem_limit_bytes=LIMIT),
        cost_estimate=cost(11),
    )(row, *(array for pair in pairs for array in pair))


def iota(shape, dim):
    return lax.broadcasted_iota(jnp.int32, shape, dim)


def eye_low(size):
    return jnp.where(iota((size, size), 0) == iota((size, size), 1), 1.0, 0.0).astype(LOW)


def turn(values):
    return values.astype(WIDE).T


def own_channel(index, place, blocks, share):
    return (index // share) * (share * blocks) + place * share + index % share


def first_call(places, blocks, share, w_in, w_out, inputs, rows, parts):
    width, shard = w_in.shape
    shard_out = w_out.shape[1]
    tokens = inputs.shape[0]
    here = shard // blocks
    size = here // parts
    channels = width // blocks

    def body(place_ref, w_ref, out_ref, in_ref, gain_ref, shift_ref, *refs):
        part_refs, (out_own, normed_ref, picked) = refs[:parts], refs[parts:]
        place = place_ref[1]
        shape = (here, shard)
        chosen = own_channel(iota(shape, 0), place, blocks, share) == iota(shape, 1)
        chosen = jnp.where(chosen, 1.0, 0.0).astype(LOW)
        turned = dot_last(chosen, w_ref[...]).astype(LOW)
        for i in range(parts):
            part_refs[i][0] = turned[i * size : (i + 1) * size]
        for j in range(channels // share):
            begin = pl.multiple_of(j * share * blocks + place * share, share)
            picked[j * share : (j + 1) * share] = out_ref[pl.ds(begin, share)]
        out_own[0] = turn(picked[...]).astype(LOW)
        normal, _ = norm_parts(in_ref[...].astype(WIDE))
        normed_ref[0] = (normal * gain_ref[...] + shift_ref[...]).astype(LOW)

    shape = jax.ShapeDtypeStruct
    return pl.pallas_call(
        body,
        out_shape=[shape((1, size, width), LOW)] * parts
        + [shape((1, shard_out, channels), LOW), shape((1, tokens, width), LOW)],
        in_specs=[SMEM_SPACE] + [VMEM_SPACE] * 5,
        out_specs=[VMEM_SPACE] * (parts + 2),
        scratch_shapes=[pltpu.VMEM((channels, shard_out), LOW)],
        compiler_params=pltpu.CompilerParams(vmem_limit_bytes=WHOLE),
        cost_estimate=cost(3),
    )(places, w_in, w_out, inputs, *rows)


def second_call(places, blocks, share, w_up, w_down, b_up, vectors, layers, third):
    width, shard_up = w_up.shape
    piece = shard_up // blocks
    hidden, shard_down = w_down.shape
    count_dp = hidden // shard_up
    channels = width // blocks
    arrays = [array for array, _ in vectors] + [third]
    spans = [rows for _, rows in vectors] + [third.shape[0]]
    used = sum(spans)
    total = -(-used // 8) * 8
    flat_layers = [array for layer in layers for array in layer]
    heights = [weights.shape[0] for weights, _ in layers]

    def body(place_ref, up_ref, down_ref, bias_ref, *refs):
        vec_refs, refs = refs[: len(arrays)], refs[len(arrays) :]
        layer_refs, refs = refs[: len(flat_layers)], refs[len(flat_layers) :]
        up_own, down_own, bias_own, vec_own = refs[:4]
        aug_refs, (up, down, held, sems) = refs[4 : 4 + len(layers)], refs[4 + len(layers) :]
        place = place_ref[1]
        copies = Copies(sems)
        begin = pl.multiple_of(place * piece, piece)
        waiting = [copies.start(up_ref.at[:, pl.ds(begin, piece)], up)]
        for k in range(count_dp):
            rows = pl.ds(pl.multiple_of(k * shard_up + place * piece, piece), piece)
            waiting.append(copies.start(down_ref.at[rows], down.at[pl.ds(k * piece, piece)]))
        for k in range(count_dp):
            lanes = pl.ds(pl.multiple_of(k * shard_up + place * piece, piece), piece)
            bias_own[:, k * piece : (k + 1) * piece] = bias_ref[:, lanes]
        held[used:, :] = jnp.zeros((total - used, width), WIDE)
        at = 0
        for (ref, span) in zip(vec_refs, spans):
            count = ref.shape[0]
            if ref.shape[1] == width:
                held[at : at + count, :] = ref[...]
            else:
                for i in range(count):
                    for j in range(span // count):
                        row = at + i * (span // count) + j
                        held[row : row + 1, :] = ref[i : i + 1, j * width : (j + 1) * width]
            at += span
        shape = (width, channels)
        chosen = iota(shape, 0) == own_channel(iota(shape, 1), place, blocks, share)
        vec_own[...] = dot_high(held[...], jnp.where(chosen, 1.0, 0.0))
        for i, height in enumerate(heights):
            weights, bias, target = layer_refs[2 * i], layer_refs[2 * i + 1], aug_refs[i]
            target[...] = jnp.zeros(target.shape, WIDE)
            target[:height, :] = weights[...]
            target[height : height + 1, :] = bias[...]
        for copy in waiting:
            copy.wait()
        up_own[0] = turn(up[...]).astype(LOW)
        down_own[0] = turn(down[...]).astype(LOW)

    shape = jax.ShapeDtypeStruct
    return pl.pallas_call(
        body,
        out_shape=[
            shape((1, piece, width), LOW),
            shape((1, shard_down, piece * count_dp), LOW),
            shape((1, piece * count_dp), WIDE),
            shape((total, channels), WIDE),
        ]
        + [shape((-(-(height + 1) // 8) * 8, layer[0].shape[1]), WIDE) for height, layer in zip(heights, layers)],
        in_specs=[SMEM_SPACE, ANY_SPACE, ANY_SPACE]
        + [VMEM_SPACE] * (1 + len(arrays) + len(flat_layers)),
        out_specs=[VMEM_SPACE] * (4 + len(layers)),
        scratch_shapes=[
            pltpu.VMEM((width, piece), LOW),
            pltpu.VMEM((piece * count_dp, shard_down), LOW),
            pltpu.VMEM((total, width), WIDE),
            pltpu.SemaphoreType.DMA((1 + count_dp,)),
        ],
        compiler_params=pltpu.CompilerParams(vmem_limit_bytes=LIMIT),
        cost_estimate=cost(4),
    )(places, w_up, w_down, b_up, *arrays, *flat_layers)


def spread_pieces(refs):
    return [ref.at[i] for ref in refs for i in range(ref.shape[0])]


def wide_call(places, offsets, pieces, piece, count_dp):
    total, width = pieces[0].shape[1:]
    shard = total - piece
    units = piece * count_dp
    blocks = len(offsets)

    def body(place_ref, *refs):
        sources = spread_pieces(refs[: len(pieces)])
        up_out, down_out = refs[len(pieces) :]
        for source, offset in zip(sources, offsets):
            place = place_ref[1] ^ offset
            up_out[:, pl.ds(pl.multiple_of(place * piece, piece), piece)] = turn(source[:piece])
            down = turn(source[piece:])
            for k in range(count_dp):
                rows = pl.ds(pl.multiple_of((k * blocks + place) * piece, piece), piece)
                down_out[rows] = down[k * piece : (k + 1) * piece]

    shape = jax.ShapeDtypeStruct
    return pl.pallas_call(
        body,
        out_shape=[
            shape((width, piece * blocks), WIDE),
            shape((units * blocks, shard), WIDE),
        ],
        in_specs=[SMEM_SPACE] + [VMEM_SPACE] * len(pieces),
        out_specs=[VMEM_SPACE] * 2,
        compiler_params=pltpu.CompilerParams(vmem_limit_bytes=LIMIT),
        cost_estimate=cost(8),
    )(places, *pieces)


def in_wide_call(places, offsets, share, pieces):
    here, width = pieces[0].shape[1:]
    blocks = len(offsets)
    shard = here * blocks

    def body(place_ref, *refs):
        out = refs[-1]
        total = None
        for index, ref in enumerate(spread_pieces(refs[:-1])):
            place = place_ref[1] ^ offsets[index]
            shape = (here, shard)
            chosen = own_channel(iota(shape, 0), place, blocks, share) == iota(shape, 1)
            chosen = jnp.where(chosen, 1.0, 0.0).astype(LOW)
            part = dot_first(ref[...], chosen)
            total = part if total is None else total + part
        out[...] = total

    return pl.pallas_call(
        body,
        out_shape=jax.ShapeDtypeStruct((width, shard), WIDE),
        in_specs=[SMEM_SPACE] + [VMEM_SPACE] * len(pieces),
        out_specs=VMEM_SPACE,
        compiler_params=pltpu.CompilerParams(vmem_limit_bytes=LIMIT),
        cost_estimate=cost(3),
    )(places, *pieces)


def out_wide_call(places, offsets, share, pieces):
    shard, channels = pieces[0].shape[1:]
    blocks = len(offsets)

    def body(place_ref, *refs):
        out = refs[-1]
        for index, ref in enumerate(spread_pieces(refs[:-1])):
            place = place_ref[1] ^ offsets[index]
            whole = turn(ref[...])
            for j in range(channels // share):
                rows = pl.ds(pl.multiple_of((j * blocks + place) * share, share), share)
                out[rows] = whole[j * share : (j + 1) * share]

    return pl.pallas_call(
        body,
        out_shape=jax.ShapeDtypeStruct((channels * blocks, shard), WIDE),
        in_specs=[SMEM_SPACE] + [VMEM_SPACE] * len(pieces),
        out_specs=VMEM_SPACE,
        compiler_params=pltpu.CompilerParams(vmem_limit_bytes=LIMIT),
        cost_estimate=cost(2),
    )(places, *pieces)


def small_pack_call(shared, layers, bias, sums, third, decay):
    channels = third.shape[1]
    width = shared[0].shape[1]
    cuts = width // channels
    arrays = list(shared) + list(layers) + [bias, sums, third, decay]
    rows = cuts * sum(array.shape[0] for array in shared)
    layer_rows = [-(-array.shape[0] // cuts // 8) * 8 for array in layers]
    bias_rows = bias.shape[1] // channels
    plain = rows + sum(layer_rows) + bias_rows + sums.shape[0] + third.shape[0] + 1
    total = -(-plain // 8) * 8

    def body(*refs):
        target = refs[-1]
        target[plain:, :] = jnp.zeros((total - plain, channels), WIDE)
        at = 0
        for ref in refs[: len(shared)]:
            for i in range(ref.shape[0]):
                for j in range(cuts):
                    target[at : at + 1, :] = ref[i : i + 1, j * channels : (j + 1) * channels]
                    at += 1
        for ref, height in zip(refs[len(shared) : len(shared) + len(layers)], layer_rows):
            lanes = ref.shape[1]
            target[at : at + height, :] = jnp.zeros((height, channels), WIDE)
            for j in range(cuts):
                size = min(height, ref.shape[0] - j * height)
                if size > 0:
                    target[at : at + size, j * lanes : (j + 1) * lanes] = ref[
                        j * height : j * height + size, :
                    ]
            at += height
        ref = refs[len(shared) + len(layers)]
        for j in range(bias_rows):
            target[at : at + 1, :] = ref[:, j * channels : (j + 1) * channels]
            at += 1
        for ref in refs[len(shared) + len(layers) + 1 : -1]:
            target[at : at + ref.shape[0], :] = ref[...]
            at += ref.shape[0]

    return pl.pallas_call(
        body,
        out_shape=jax.ShapeDtypeStruct((total, channels), WIDE),
        in_specs=[VMEM_SPACE] * len(arrays),
        out_specs=VMEM_SPACE,
        compiler_params=pltpu.CompilerParams(vmem_limit_bytes=LIMIT),
        cost_estimate=cost(2),
    )(*arrays)


def small_out_call(places, offsets, share, pieces, shared, layer_shapes, bias_width, shard_up):
    height, channels = pieces[0].shape[1:]
    blocks = len(offsets)
    width = channels * blocks
    piece = shard_up // blocks
    augmented = [-(-(shape[0] + 1) // 8) * 8 for shape in layer_shapes]
    layer_rows = [-(-rows // blocks // 8) * 8 for rows in augmented]
    bias_rows = bias_width // channels
    units = layer_shapes[1][1]

    def body(place_ref, *refs):
        sources = spread_pieces(refs[: len(pieces)])
        refs = refs[len(pieces) :]
        shared_refs, refs = refs[:shared], refs[shared:]
        layer_refs, refs = refs[: 2 * len(layer_shapes)], refs[2 * len(layer_shapes) :]
        bias_out, in_out, taps_out, short_out, direct_out, third_out, decay_out, held, placed = refs
        for source, offset in zip(sources, offsets):
            placed[place_ref[1] ^ offset] = source[...]
        total = placed[0]
        for i in range(1, blocks):
            total = total + placed[i]
        held[...] = total
        at = 0
        for ref in shared_refs:
            for j in range(blocks):
                ref[:, j * channels : (j + 1) * channels] = held[at : at + 1, :]
                at += 1
        for i, rows in enumerate(layer_rows):
            weights, bias = layer_refs[2 * i], layer_refs[2 * i + 1]
            lanes = weights.shape[1]
            for j in range(blocks):
                size = min(rows, weights.shape[0] - j * rows)
                if size > 0:
                    weights[j * rows : j * rows + size, :] = held[
                        at : at + size, j * lanes : (j + 1) * lanes
                    ]
                if 0 <= weights.shape[0] - j * rows < rows:
                    row = at + weights.shape[0] - j * rows
                    bias[...] = held[row : row + 1, j * lanes : (j + 1) * lanes]
            at += rows
        whole = None
        first = at
        for index, offset in enumerate(offsets):
            place = place_ref[1] ^ offset
            for j in range(bias_rows):
                line = sources[index][first + j : first + j + 1, :]
                for c in range(channels // piece):
                    k = j * (channels // piece) + c
                    lanes = pl.ds(pl.multiple_of((k * blocks + place) * piece, piece), piece)
                    bias_out[:, lanes] = line[:, c * piece : (c + 1) * piece]
            shape = (channels, width)
            chosen = own_channel(iota(shape, 0), place, blocks, share) == iota(shape, 1)
            part = dot_high(
                sources[index][first + bias_rows :, :], jnp.where(chosen, 1.0, 0.0)
            )
            whole = part if whole is None else whole + part
        for role in range(3):
            lanes = slice(role * width, (role + 1) * width)
            in_out[:, lanes] = whole[role : role + 1]
            for j in range(3):
                taps_out[j : j + 1, lanes] = whole[3 + 3 * j + role : 4 + 3 * j + role]
            short_out[:, lanes] = whole[12 + role : 13 + role]
        direct_out[...] = whole[15:16]
        third_out[...] = whole[16 : 16 + units]
        decay_out[...] = whole[16 + units : 17 + units]

    shape = jax.ShapeDtypeStruct
    layer_out = []
    for rows, lanes in layer_shapes:
        layer_out += [shape((rows, lanes), WIDE), shape((1, lanes), WIDE)]
    return pl.pallas_call(
        body,
        out_shape=[shape((1, width), WIDE)] * shared
        + layer_out
        + [
            shape((1, bias_width * blocks), WIDE),
            shape((1, 3 * width), WIDE),
            shape((3, 3 * width), WIDE),
            shape((1, 3 * width), WIDE),
            shape((1, width), WIDE),
            shape((units, width), WIDE),
            shape((1, width), WIDE),
        ],
        in_specs=[SMEM_SPACE] + [VMEM_SPACE] * len(pieces),
        out_specs=[VMEM_SPACE] * (shared + len(layer_out) + 7),
        scratch_shapes=[
            pltpu.VMEM((height, channels), WIDE),
            pltpu.VMEM((blocks, height, channels), WIDE),
        ],
        compiler_params=pltpu.CompilerParams(vmem_limit_bytes=LIMIT),
        cost_estimate=cost(5),
    )(places, *pieces)


def local_plain(
    block_in,
    doc_starts,
    norm1_gain,
    norm1_bias,
    w_in,
    b_in,
    short_taps,
    short_bias,
    filter_w1,
    filter_b1,
    filter_w2,
    filter_b2,
    filter_w3,
    filter_decay,
    conv_bias,
    w_out,
    b_out,
    norm2_gain,
    norm2_bias,
    w_up,
    b_up,
    w_down,
    b_down,
    cotangent,
):
    count_dp, blocks = lax.axis_size("dp"), lax.axis_size("block")
    grid = Grid(count_dp, blocks)
    row, place = grid.row, grid.place
    _, block_len, width = block_in.shape
    length = block_len * blocks
    hidden_width = w_up.shape[1] * count_dp
    hidden_here = hidden_width // blocks
    dp_steps = grid.dp_steps
    block_steps = grid.chip_steps + [grid.core_step]
    block_offsets = [b for _, b in offsets_of(block_steps)]

    def rotated(turn):
        turn = turn % len(dp_steps)
        return dp_steps[turn:] + dp_steps[:turn]

    def dp_offsets(steps):
        return [a for a, _ in offsets_of(steps)]

    shard_in, shard_out = w_in.shape[1], w_out.shape[1]
    group = math.gcd(width, shard_in)
    groups_here, share = shard_in // group, group // blocks
    channels = width // blocks
    bands = width // group
    vectors = jnp.concatenate(
        [
            b_in.reshape(3, width),
            short_taps.reshape(9, width),
            short_bias.reshape(3, width),
            filter_decay[None],
            conv_bias[None],
            filter_w3,
        ],
        axis=0,
    )
    vectors = lax.dynamic_index_in_dim(
        vectors.reshape(vectors.shape[0], bands, blocks, share), place, 2, keepdims=False
    ).reshape(vectors.shape[0], channels)
    b_in_here = vectors[:3].reshape(-1)
    taps = vectors[3:12].reshape(3, 3 * channels)
    short_shift = vectors[12:15].reshape(-1)
    decay_here, direct, third_here = vectors[15], vectors[16], vectors[17:]

    in_turned = w_in.T.reshape(groups_here, blocks, share, width)
    in_own = lax.dynamic_index_in_dim(in_turned, place, 1, keepdims=False)
    in_orders = [rotated(i) for i in range(groups_here)]
    in_rows = jnp.stack(
        [
            arrange(grid.gather(in_own[i], in_orders[i]), row, dp_offsets(in_orders[i]))
            for i in range(groups_here)
        ],
        axis=1,
    ).reshape(3 * channels, width)

    inputs = block_in.astype(WIDE).reshape(block_len, width)
    normed, norm1_back = jax.vjp(layer_norm, inputs, norm1_gain, norm1_bias)
    normed_low = normed.astype(LOW)
    normed_all = arrange(grid.gather(normed_low, block_steps), place, block_offsets).reshape(
        length, width
    )

    up_order, down_order, out_dp_order = rotated(1), rotated(2), rotated(0)
    piece = w_up.shape[1] // blocks
    up_own = lax.dynamic_slice_in_dim(w_up, place * piece, piece, 1).T
    up_rows = arrange(grid.gather(up_own, up_order), row, dp_offsets(up_order)).reshape(
        hidden_here, width
    )
    b_up_here = lax.dynamic_index_in_dim(
        b_up.reshape(count_dp, blocks, piece), place, 1, keepdims=False
    ).reshape(hidden_here)
    down_own = w_down.reshape(count_dp, blocks, piece, w_down.shape[1])
    down_own = lax.dynamic_index_in_dim(down_own, place, 1, keepdims=False)
    down_own = down_own.reshape(hidden_here, w_down.shape[1]).T
    down_rows = arrange(grid.gather(down_own, down_order), row, dp_offsets(down_order)).reshape(
        width, hidden_here
    )

    out_own = w_out.reshape(bands, blocks, share, shard_out)
    out_own = lax.dynamic_index_in_dim(out_own, place, 1, keepdims=False)
    out_own = out_own.reshape(channels, shard_out).T
    out_dealt = arrange(grid.gather(out_own, out_dp_order), row, dp_offsets(out_dp_order))
    out_rows = jnp.concatenate(grid.gather(out_dealt.reshape(width, channels), block_steps), axis=0)
    cot_flat = cotangent.reshape(block_len, width)
    cot_all = jnp.concatenate(grid.gather(cot_flat, block_steps), axis=0).reshape(length, width)

    forward_table, inverse_table, sign, edge = transform_tables(block_len)
    starts = doc_starts[0]
    positions = jnp.arange(length, dtype=jnp.int32)
    segment = jnp.sum((starts[None, :] <= positions[:, None]).astype(jnp.int32), axis=-1) - 1
    keep_one = jnp.concatenate([jnp.zeros((1,), WIDE), (segment[1:] == segment[:-1]).astype(WIDE)])
    keep_two = jnp.concatenate([jnp.zeros((2,), WIDE), (segment[2:] == segment[:-2]).astype(WIDE)])
    keep_one, keep_two = keep_one[:, None], keep_two[:, None]
    num_docs = doc_starts.shape[1]
    long_doc = jnp.sum((starts <= block_len).astype(jnp.int32)) - 1
    long_mask = (segment == long_doc).astype(WIDE)[:, None]
    first_segment, last_segment = segment[:block_len], segment[length - block_len :]
    short_early, short_masks = [], []
    for number in range(num_docs - 1):
        early = number < long_doc
        doc = jnp.where(early, number, number + 1)
        where = jnp.where(early, first_segment, last_segment)
        short_early.append(early.astype(WIDE))
        short_masks.append((where == doc).astype(WIDE)[:, None])

    def spread(values):
        masked = values * long_mask
        parts = [masked[i * block_len : (i + 1) * block_len] for i in range(blocks)]
        first, last = values[:block_len], values[length - block_len :]
        for early, mask in zip(short_early, short_masks):
            parts.append(mask * (early * first + (1.0 - early) * last))
        return jnp.concatenate(parts, axis=1)

    def collect(values):
        parts = [
            values[:, i * channels : (i + 1) * channels] for i in range(blocks + num_docs - 1)
        ]
        first, last = jnp.zeros_like(parts[0]), jnp.zeros_like(parts[0])
        for early, mask, part in zip(short_early, short_masks, parts[blocks:]):
            first = first + early * mask * part
            last = last + (1.0 - early) * mask * part
        joined = jnp.concatenate(parts[:blocks], axis=0) * long_mask
        middle = jnp.zeros((length - 2 * block_len, channels), WIDE)
        return joined + jnp.concatenate([first, middle, last], axis=0)

    def cut(values, count):
        return [values[:, i * channels : (i + 1) * channels] for i in range(count)]

    table, times = position_table(length, filter_w1.shape[0])

    def filter_spectra(params):
        first = jnp.sin(dot_high(table, params[0]) + params[1])
        second = jnp.sin(dot_high(first, params[2]) + params[3])
        kernel = dot_high(second, params[4]) * (
            jnp.exp(-times[:, None] * params[5][None, :]) + MOD_SHIFT
        )
        pieces = jnp.concatenate(
            [kernel[i * block_len : (i + 1) * block_len] for i in range(blocks)], axis=1
        )
        halves = dot_near(forward_table, pieces)
        earlier = jnp.concatenate(
            [jnp.zeros((2 * block_len, channels), WIDE), halves[:, : (blocks - 1) * channels]],
            axis=1,
        )
        return earlier + sign[:, None] * halves

    spectra_flat, filter_back = jax.vjp(
        filter_spectra,
        (filter_w1, filter_b1, filter_w2, filter_b2, third_here, decay_here),
    )
    spectra = cut(spectra_flat, blocks)

    proj = dot_last(normed_all, in_rows) + b_in_here
    three = 3 * channels
    prev_one = jnp.concatenate([jnp.zeros((1, three), WIDE), proj[:-1]], axis=0) * keep_one
    prev_two = jnp.concatenate([jnp.zeros((2, three), WIDE), proj[:-2]], axis=0) * keep_two
    short = short_shift + taps[0] * proj + taps[1] * prev_one + taps[2] * prev_two
    gate_part, mult, value = cut(short, 3)
    inner = value * mult

    entries = cut(dot_near(forward_table, spread(inner)), blocks + num_docs - 1)
    totals = []
    for i in range(blocks):
        total = spectral_product(entries[i], spectra[0], edge)
        for j in range(i):
            total = total + spectral_product(entries[j], spectra[i - j], edge)
        totals.append(total)
    for entry in entries[blocks:]:
        totals.append(spectral_product(entry, spectra[0], edge))
    mixed = collect(dot_near(inverse_table, jnp.concatenate(totals, axis=1))) + direct * inner
    gated_low = (gate_part * mixed).astype(LOW)

    gated_parts = []
    for offset in block_offsets:
        part = lax.dynamic_slice_in_dim(gated_low, (place ^ offset) * block_len, block_len, 0)
        gated_parts.append(grid.swap(part, (0, offset)) if offset else part)
    branch = b_out
    for part, rows in zip(gated_parts, out_rows):
        branch = branch + dot_last(part, rows)
    resid = inputs + branch
    normed2, norm2_back = jax.vjp(layer_norm, resid, norm2_gain, norm2_bias)
    normed2_low = normed2.astype(LOW)

    normed2_all = jnp.concatenate(grid.gather(normed2_low, block_steps), axis=0)
    normed2_all = normed2_all.reshape(length, width)
    hidden = dot_last(normed2_all, up_rows) + b_up_here
    act, gelu_back = jax.vjp(exact_gelu, hidden)
    act_low = act.astype(LOW)
    grad_act = dot_plain(cot_all, down_rows)
    grad_hidden = gelu_back(grad_act)[0].astype(LOW)

    def to_tokens(partial):
        split = partial.astype(LOW).reshape(blocks, block_len, width)
        return grid.scatter(split[: blocks // 2], split[blocks // 2 :], block_steps).astype(WIDE)

    grad_normed2 = to_tokens(dot_plain(grad_hidden, up_rows))
    output = resid + to_tokens(dot_last(act_low, down_rows)) + b_down
    block_out = output.astype(LOW)[None]
    grad_b_up_here = jnp.sum(grad_hidden.astype(WIDE), axis=0)
    grad_b_down = jnp.sum(cot_flat.astype(WIDE), axis=0)

    def send_home(natural, order):
        natural = natural.astype(LOW).reshape(count_dp, -1, natural.shape[-1])
        return grid.scatter(*deal(natural, row, dp_offsets(order)), order)

    up_grad = send_home(dot_first(grad_hidden, normed2_all), up_order)
    down_grad = send_home(dot_first(cot_all, act_low), down_order)

    resid_part, grad_gain_two, grad_bias_two = norm2_back(grad_normed2)
    grad_resid = cot_flat.astype(WIDE) + resid_part
    grad_branch = grad_resid.astype(LOW)
    grad_b_out = jnp.sum(grad_branch.astype(WIDE), axis=0)
    grad_parts = []
    for index, offset in enumerate(block_offsets):
        part = dot_plain(grad_branch, out_rows[index]).astype(LOW)
        grad_parts.append((grid.swap(part, (0, offset)) if offset else part)[None])
    grad_gated = arrange(grad_parts, place, block_offsets).reshape(length, channels).astype(WIDE)
    out_sums = jnp.stack([dot_first(grad_branch, part).astype(LOW) for part in gated_parts], axis=0)
    out_sums = grid.scatter(out_sums[: blocks // 2], out_sums[blocks // 2 :], block_steps)
    out_grad = send_home(out_sums, out_dp_order)

    grad_gate_part = grad_gated * mixed
    grad_mixed = grad_gated * gate_part
    grad_conv_bias = jnp.sum(grad_mixed * inner, axis=0)
    grad_totals = cut(
        lax.dot_general(
            inverse_table,
            spread(grad_mixed),
            (((0,), (0,)), ((), ())),
            precision=HIGH,
            preferred_element_type=WIDE,
        ),
        blocks + num_docs - 1,
    )
    grad_entries = []
    grad_lags = [None] * blocks
    for i in range(blocks + num_docs - 1):
        lag = spectral_back(grad_totals[i], entries[i], edge)
        grad_lags[0] = lag if grad_lags[0] is None else grad_lags[0] + lag
        grad_entries.append(spectral_back(grad_totals[i], spectra[0], edge))
    for j in range(blocks):
        for i in range(j + 1, blocks):
            grad_entries[j] = grad_entries[j] + spectral_back(
                grad_totals[i], spectra[i - j], edge
            )
            lag = spectral_back(grad_totals[i], entries[j], edge)
            grad_lags[i - j] = lag if grad_lags[i - j] is None else grad_lags[i - j] + lag
    filter_grads = filter_back(jnp.concatenate(grad_lags, axis=1))[0]
    grad_inner = (
        collect(
            lax.dot_general(
                forward_table,
                jnp.concatenate(grad_entries, axis=1),
                (((0,), (0,)), ((), ())),
                precision=HIGH,
                preferred_element_type=WIDE,
            )
        )
        + direct * grad_mixed
    )
    grad_short = jnp.concatenate([grad_gate_part, grad_inner * value, grad_inner * mult], axis=1)
    grad_taps = jnp.stack(
        [
            jnp.sum(grad_short * proj, axis=0),
            jnp.sum(grad_short * prev_one, axis=0),
            jnp.sum(grad_short * prev_two, axis=0),
        ],
        axis=0,
    )
    grad_short_bias = jnp.sum(grad_short, axis=0)
    pass_one = grad_short * keep_one
    pass_two = grad_short * keep_two
    grad_proj = (
        taps[0] * grad_short
        + taps[1] * jnp.concatenate([pass_one[1:], jnp.zeros((1, three), WIDE)], axis=0)
        + taps[2] * jnp.concatenate([pass_two[2:], jnp.zeros((2, three), WIDE)], axis=0)
    )
    grad_proj_low = grad_proj.astype(LOW)
    grad_b_in = jnp.sum(grad_proj_low.astype(WIDE), axis=0)
    grad_in_rows = dot_first(grad_proj_low, normed_all)
    grad_in_split = grad_in_rows.reshape(count_dp, groups_here, share, width)
    in_grads = [send_home(grad_in_split[:, i], in_orders[i]) for i in range(groups_here)]
    grad_normed_part = dot_plain(grad_proj_low, in_rows).astype(LOW)
    grad_normed = grid.scatter(
        *deal(grad_normed_part.reshape(blocks, block_len, width), place, block_offsets), block_steps
    ).astype(WIDE)
    input_part, grad_gain_one, grad_bias_one = norm1_back(grad_normed)
    grad_input = (grad_resid + input_part)[None]

    def all_places(value):
        return arrange(grid.gather(value, block_steps), place, block_offsets)

    in_whole = all_places(jnp.concatenate(in_grads, axis=0))
    in_whole = in_whole.reshape(blocks, groups_here, share, width)
    in_whole = in_whole.transpose(3, 1, 0, 2).reshape(width, shard_in).astype(WIDE)
    if up_grad.shape[1] == down_grad.shape[1]:
        ff_whole = all_places(jnp.concatenate([up_grad, down_grad], axis=0))
        up_whole, down_whole = ff_whole[:, :piece], ff_whole[:, piece:]
    else:
        up_whole, down_whole = all_places(up_grad), all_places(down_grad)
    up_whole = up_whole.reshape(blocks * piece, width).T.astype(WIDE)
    down_whole = down_whole.reshape(blocks, w_down.shape[1], count_dp, piece)
    down_whole = down_whole.transpose(2, 0, 3, 1).reshape(hidden_width, w_down.shape[1])
    down_whole = down_whole.astype(WIDE)
    out_whole = all_places(out_grad).reshape(blocks, shard_out, bands, share)
    out_whole = out_whole.transpose(2, 0, 3, 1).reshape(width, shard_out).astype(WIDE)

    shared = [
        grad_gain_one,
        grad_bias_one,
        grad_b_out,
        grad_gain_two,
        grad_bias_two,
        grad_b_down,
        filter_grads[0],
        filter_grads[1],
        filter_grads[2],
        filter_grads[3],
    ]
    flat = jnp.concatenate([item.reshape(-1) for item in shared])
    unit = blocks * channels
    chunk = -(-flat.shape[0] // unit)
    flat = jnp.pad(flat, (0, chunk * unit - flat.shape[0])).reshape(blocks, chunk, channels)
    dealt = [lax.dynamic_slice_in_dim(flat, place ^ offset, 1, 0) for offset in block_offsets]
    half = blocks // 2
    shared_part = grid.scatter(
        jnp.concatenate(dealt[:half], axis=0), jnp.concatenate(dealt[half:], axis=0), block_steps
    )
    joined = jnp.concatenate(
        [
            shared_part,
            jnp.pad(grad_b_up_here, (0, -hidden_here % channels)).reshape(-1, channels),
            grad_b_in.reshape(3, channels),
            grad_taps.reshape(9, channels),
            grad_short_bias.reshape(3, channels),
            filter_grads[5][None],
            grad_conv_bias[None],
            filter_grads[4],
        ],
        axis=0,
    )
    for step in dp_steps:
        joined = joined + grid.swap(joined, step)
    every = all_places(joined)
    whole_flat = every[:, :chunk].reshape(-1)
    shared_out, at = [], 0
    for item in shared:
        shared_out.append(whole_flat[at : at + item.size].reshape(item.shape))
        at += item.size
    at = chunk + -(-hidden_here // channels)
    grad_b_up = every[:, chunk:at].reshape(blocks, -1)[:, :hidden_here]
    grad_b_up = grad_b_up.reshape(blocks, count_dp, piece)
    grad_b_up = grad_b_up.transpose(1, 0, 2).reshape(hidden_width)
    rest = every[:, at:].reshape(blocks, -1, bands, share).transpose(1, 2, 0, 3)
    rest = rest.reshape(-1, width)
    return (
        block_out,
        grad_input,
        shared_out[0],
        shared_out[1],
        in_whole,
        rest[:3].reshape(3 * width),
        rest[3:12].reshape(3, 3 * width),
        rest[12:15].reshape(3 * width),
        shared_out[6],
        shared_out[7],
        shared_out[8],
        shared_out[9],
        rest[17:],
        rest[15],
        rest[16],
        out_whole,
        shared_out[2],
        shared_out[3],
        shared_out[4],
        up_whole,
        grad_b_up,
        down_whole,
        shared_out[5],
    )


def input_back_call(inputs, kept, arrived, gain, grad_resid):
    tokens, width = inputs.shape

    def body(in_ref, kept_ref, arrived_ref, gain_ref, resid_ref, out_ref):
        grad = kept_ref[...].astype(WIDE) + arrived_ref[...].astype(WIDE)
        normal, scale = norm_parts(in_ref[...].astype(WIDE))
        scaled = grad * gain_ref[...]
        back = scaled - jnp.mean(scaled, axis=-1, keepdims=True)
        back = back - normal * jnp.mean(scaled * normal, axis=-1, keepdims=True)
        out_ref[...] = resid_ref[...] + back * scale

    return pl.pallas_call(
        body,
        out_shape=jax.ShapeDtypeStruct((tokens, width), WIDE),
        in_specs=[VMEM_SPACE] * 5,
        out_specs=VMEM_SPACE,
        compiler_params=pltpu.CompilerParams(vmem_limit_bytes=LIMIT),
        cost_estimate=cost(4),
    )(inputs, kept, arrived, gain, grad_resid)


def mark_call(value):
    def body(in_ref, out_ref):
        out_ref[...] = in_ref[...]

    return pl.pallas_call(
        body,
        out_shape=jax.ShapeDtypeStruct(value.shape, value.dtype),
        in_specs=[VMEM_SPACE],
        out_specs=VMEM_SPACE,
        cost_estimate=cost(15),
    )(value)


def after(value, *others):
    return lax.optimization_barrier((value, *others))[0]


def together(values, *others):
    return lax.optimization_barrier((*values, *others))[: len(values)]


def local_kernels(
    block_in,
    doc_starts,
    norm1_gain,
    norm1_bias,
    w_in,
    b_in,
    short_taps,
    short_bias,
    filter_w1,
    filter_b1,
    filter_w2,
    filter_b2,
    filter_w3,
    filter_decay,
    conv_bias,
    w_out,
    b_out,
    norm2_gain,
    norm2_bias,
    w_up,
    b_up,
    w_down,
    b_down,
    cotangent,
):
    count_dp, blocks = lax.axis_size("dp"), lax.axis_size("block")
    grid = Grid(count_dp, blocks)
    row, place = grid.row, grid.place
    places = jnp.stack([row, place]).astype(jnp.int32)
    _, block_len, width = block_in.shape
    dp_steps = grid.dp_steps
    block_steps = grid.chip_steps + [grid.core_step]
    block_offsets = [b for _, b in offsets_of(block_steps)]
    shard_in = w_in.shape[1]
    share = math.gcd(width, shard_in) // blocks
    shard_up = w_up.shape[1]
    starts = doc_starts[0]
    inputs = block_in.reshape(block_len, width)
    cot = cotangent.reshape(block_len, width)
    forward_table, inverse_table, _, _ = transform_tables(block_len)
    forward_three, inverse_three = triple(forward_table), triple(inverse_table)
    forward_back, inverse_back = triple(forward_table.T), triple(inverse_table.T)
    table = turned_table(position_table(block_len * blocks, filter_w1.shape[0])[0])
    third_at = 17

    order_one = dp_steps[::-1]
    order_two = order_one[:-2] + order_one[:-3:-1]
    core_step = grid.core_step

    def dp_offsets(steps):
        return [a for a, _ in offsets_of(steps)]

    parts = 2
    in_orders = [order_one, order_two]
    in_offsets = [dp_offsets(order) for order in in_orders]
    up_order, down_order, out_order = order_one, order_two, order_one
    up_offsets, down_offsets, out_offsets = map(dp_offsets, (up_order, down_order, out_order))
    core, chip = core_step, block_steps[0]

    def joined(pieces):
        return jnp.concatenate(pieces, axis=0)

    def split(values, *counts):
        parts, at = [], 0
        for count in counts:
            parts.append(list(values[at : at + count]))
            at += count
        return parts

    *in_own, out_own, normed_own = first_call(
        places,
        blocks,
        share,
        w_in,
        w_out,
        inputs,
        (norm1_gain[None], norm1_bias[None]),
        parts,
    )
    in_got = [grid.swap(own, order[0]) for own, order in zip(in_own, in_orders)]
    normed_got = grid.swap(normed_own, chip)
    out_got = grid.swap(out_own, out_order[0])
    second = second_call(
        after(places, normed_own),
        blocks,
        share,
        w_up,
        w_down,
        b_up[None],
        [
            (b_in[None], 3),
            (short_taps, 9),
            (short_bias[None], 3),
            (filter_decay[None], 1),
            (conv_bias[None], 1),
        ],
        [(filter_w1, filter_b1[None]), (filter_w2, filter_b2[None])],
        filter_w3,
    )

    in_got, (out_got,), second = split(together((*in_got, out_got, *second)), parts, 1, 6)
    up_own, down_own, b_up_own, vectors, layer_one, layer_two = second
    in_held = [joined(pair) for pair in zip(in_own, in_got)]
    out_held = joined((out_own, out_got))
    in_got = [grid.swap(held, order[1]) for held, order in zip(in_held, in_orders)]
    out_got = grid.swap(out_held, out_order[1])
    up_got = grid.swap(up_own, up_order[0])
    spectra, layer_one = filter_call(
        block_len, blocks, table, forward_three, layer_one, layer_two, vectors, third_at
    )

    in_got, rest = split(
        together((*in_got, out_got, up_got, normed_got, layer_one, layer_two, down_own)), parts, 6
    )
    out_got, up_got, normed_got, layer_one, layer_two, down_own = rest
    in_last = [joined(pair) for pair in zip(in_held, in_got)]
    out_held = joined((out_held, out_got))
    up_held = joined((up_own, up_got))
    normed_held = joined((normed_own, normed_got))
    in_last_got = [grid.swap(held, order[2]) for held, order in zip(in_last, in_orders)]
    normed_last = grid.swap(normed_held, core)
    out_got = grid.swap(out_held, out_order[2])
    down_got = grid.swap(down_own, down_order[0])
    cot_own = after(cot, normed_got)[None]
    cot_got = grid.swap(cot_own, chip)
    layer_two = mark_call(layer_two)

    in_last_got, rest = split(
        together((*in_last_got, out_got, down_got, normed_last, cot_got, layer_two)), parts, 5
    )
    out_got, down_got, normed_last, cot_got, layer_two = rest
    down_held = joined((down_own, down_got))
    out_whole = joined((out_held, out_got))[None]
    cot_held = joined((cot_own, cot_got))
    up_two = grid.swap(up_held, up_order[1])
    down_two = grid.swap(down_held, down_order[1])
    out_got = grid.swap(out_whole, chip)
    cot_last = grid.swap(cot_held, core)
    made = conv_call(
        block_len,
        blocks,
        places,
        starts,
        [normed_held, normed_last],
        [list(pair) for pair in zip(in_last, in_last_got)],
        in_offsets,
        block_offsets,
        vectors,
        spectra,
        forward_three,
        inverse_three,
    )

    gated_own, (proj, entries, mixed, in_rows, normed) = made[:blocks], made[blocks:]
    gated_own, (up_two, down_two, out_got, cot_last, layer_two) = split(
        together((*gated_own, up_two, down_two, out_got, cot_last, layer_two)), blocks, 5
    )
    gated_got = [
        grid.swap(part, (0, offset)) for part, offset in zip(gated_own[1:], block_offsets[1:])
    ]
    out_held = joined((out_whole, out_got))
    out_last = grid.swap(out_held, core)
    up_three = grid.swap(up_held, up_order[2])
    down_three = grid.swap(down_held, down_order[2])
    layer_two = mark_call(layer_two)

    gated_got, (out_last, up_three, down_three, layer_two) = split(
        together((*gated_got, out_last, up_three, down_three, layer_two)), blocks - 1, 4
    )
    gated_parts = [gated_own[0], *gated_got]
    out_pieces = [out_held, out_last]
    resid, normed2 = branch_call(
        places,
        inputs,
        gated_parts,
        out_pieces,
        out_offsets,
        (b_out[None], norm2_gain[None], norm2_bias[None]),
    )
    normed2_got = grid.swap(normed2[None], chip)
    up_four = grid.swap(up_two, up_order[2])
    down_four = grid.swap(down_two, down_order[2])

    normed2_got, up_four, down_four = together((normed2_got, up_four, down_four))
    normed2_held = joined((normed2[None], normed2_got))
    normed2_last = grid.swap(normed2_held, core)
    made = forward_call(
        places,
        [normed2_held, normed2_last],
        [cot_held, cot_last],
        [up_held, up_two, up_three, up_four],
        [down_held, down_two, down_three, down_four],
        up_offsets,
        down_offsets,
        b_up_own,
    )
    block_kept, block_sent, grad_kept, grad_sent = made[:4]
    act, grad_hidden, normed2_all, cot_all, b_up_sum = made[4:]

    grad_got = grid.swap(grad_sent, core)
    block_got = grid.swap(block_sent, core)

    grad_kept, grad_sent = halves(grad_kept, grad_got)
    grad_got = grid.swap(grad_sent, chip)
    dealt = weight_grad_call(
        after(places, grad_kept),
        [(grad_hidden, normed2_all), (cot_all, act)],
        [up_offsets, down_offsets],
    )

    grad_got, block_got, *dealt = together((grad_got, block_got, *dealt))
    up_dealt, down_dealt = split(dealt, 4, 4)
    made = branch_back_call(
        places, resid, grad_kept[0], grad_got[0], cot, out_pieces, out_offsets, norm2_gain[None]
    )
    grad_resid, grad_branch, norm2_sums = made[blocks:]
    grad_own = made[0]
    grad_got = [
        grid.swap(part, (0, offset))
        for part, offset in zip(made[1:blocks], block_offsets[1:])
    ]
    up_got = grid.swap(after(up_dealt[3], grad_branch), up_order[2])
    down_got = grid.swap(after(down_dealt[3], grad_branch), down_order[2])
    out_kept, out_sent = out_grad_call(places, grad_branch, gated_parts, out_offsets)

    grad_got, rest = split(
        together((*grad_got, up_got, down_got, out_kept, out_sent, block_kept)), blocks - 1, 5
    )
    up_got, down_got, out_kept, out_sent, block_kept = rest
    grad_parts = [grad_own, *grad_got]
    up_high = add_low(up_dealt[1], up_got)
    down_high = add_low(down_dealt[1], down_got)
    up_got = grid.swap(up_dealt[2], up_order[2])
    down_got = grid.swap(down_dealt[2], down_order[2])
    out_got = grid.swap(out_sent, core)
    block_kept, block_sent = halves(block_kept, block_got)
    block_got = grid.swap(block_sent, chip)
    grad_lags, direct_sum, grad_short = back_call(
        block_len,
        blocks,
        places,
        starts,
        grad_parts,
        block_offsets,
        vectors,
        spectra,
        proj,
        entries,
        mixed,
        inverse_back,
        forward_back,
    )

    up_got, down_got, out_got, block_got, direct_sum = together(
        (up_got, down_got, out_got, block_got, direct_sum)
    )
    up_low = add_low(up_dealt[0], up_got)
    down_low = add_low(down_dealt[0], down_got)
    out_kept, out_sent = halves(out_kept, out_got)
    up_got = grid.swap(up_high, up_order[1])
    down_got = grid.swap(down_high, down_order[1])
    out_got = grid.swap(out_sent, chip)
    made = project_back_call(
        block_len,
        blocks,
        places,
        starts,
        in_offsets,
        block_offsets,
        vectors,
        (norm1_gain[None], norm1_bias[None]),
        direct_sum,
        grad_short,
        proj,
        in_rows,
        normed,
    )

    made, (up_got, down_got, out_got, layer_one) = split(
        together((*made, up_got, down_got, out_got, layer_one)), len(made), 4
    )
    in_dealt = [(made[2 * i], made[2 * i + 1]) for i in range(parts)]
    normed_kept, normed_sent, sums, norm1_sums = made[2 * parts :]
    up_kept, up_sent = halves(up_low, up_got)
    down_kept, down_sent = halves(down_low, down_got)
    out_kept, out_sent = halves(out_kept, out_got)
    in_got = [grid.swap(pair[1], order[2]) for pair, order in zip(in_dealt, in_orders)]
    normed_got = grid.swap(normed_sent, core)
    up_got = grid.swap(up_sent, up_order[0])
    out_got = grid.swap(out_sent, out_order[2])
    layer_one_grad, layer_two_grad, third_grad, decay_grad = filter_back_call(
        block_len, blocks, table, forward_back, layer_one, layer_two, vectors, third_at, grad_lags
    )
    small = small_pack_call(
        [norm2_sums, norm1_sums],
        [layer_one_grad, layer_two_grad],
        b_up_sum,
        sums,
        third_grad,
        decay_grad,
    )

    in_got, (normed_got, up_got, out_got, small) = split(
        together((*in_got, normed_got, up_got, out_got, small)), parts, 4
    )
    in_half = [halves(pair[0], got) for pair, got in zip(in_dealt, in_got)]
    normed_kept, normed_sent = halves(normed_kept, normed_got)
    out_kept, out_sent = halves(out_kept, out_got)
    in_got = [grid.swap(pair[1], order[1]) for pair, order in zip(in_half, in_orders)]
    normed_got = grid.swap(normed_sent, chip)
    small_got = grid.swap(small, dp_steps[0])
    down_got = grid.swap(down_sent, down_order[0])
    out_got = grid.swap(out_sent, out_order[1])
    up_grad = add_low(up_kept, up_got)

    in_got, (normed_got, small_got, down_got, out_got) = split(
        together((*in_got, normed_got, small_got, down_got, out_got)), parts, 4
    )
    in_half = [halves(pair[0], got) for pair, got in zip(in_half, in_got)]
    out_kept, out_sent = halves(out_kept, out_got)
    small = small + small_got
    ff_own = jnp.concatenate([up_grad, add_low(down_kept, down_got)], axis=1)
    in_got = [grid.swap(pair[1], order[0]) for pair, order in zip(in_half, in_orders)]
    small_got = grid.swap(small, dp_steps[1])
    ff_got = grid.swap(ff_own, chip)
    out_got = grid.swap(out_sent, out_order[0])
    grad_input = input_back_call(
        inputs, normed_kept[0], normed_got[0], norm1_gain[None], grad_resid
    )[None]

    in_got, (small_got, ff_got, out_got, grad_input) = split(
        together((*in_got, small_got, ff_got, out_got, grad_input)), parts, 4
    )
    in_grad = jnp.concatenate(
        [add_low(pair[0], got) for pair, got in zip(in_half, in_got)], axis=1
    )
    out_grad = add_low(out_kept, out_got)
    small = small + small_got
    ff_held = joined((ff_own, ff_got))
    ff_last = grid.swap(ff_held, core)
    in_got = grid.swap(in_grad, chip)
    out_got = grid.swap(out_grad, chip)
    small_got = grid.swap(small, dp_steps[2])
    output = resid + block_kept[0].astype(WIDE) + block_got[0].astype(WIDE) + b_down
    block_out = output.astype(LOW)[None]

    ff_last, in_got, out_got, small_got, block_out = together(
        (ff_last, in_got, out_got, small_got, block_out)
    )
    in_held, out_held = joined((in_grad, in_got)), joined((out_grad, out_got))
    small = (small + small_got)[None]
    small_got = grid.swap(small, chip)
    in_last = grid.swap(in_held, core)
    out_last = grid.swap(out_held, core)
    up_whole, down_whole = wide_call(
        places, block_offsets, [ff_held, ff_last], up_own.shape[1], count_dp
    )

    small_got, in_last, out_last, up_whole = together((small_got, in_last, out_last, up_whole))
    small_held = joined((small, small_got))
    small_last = grid.swap(small_held, core)
    in_whole = in_wide_call(places, block_offsets, share, [in_held, in_last])
    out_whole = out_wide_call(places, block_offsets, share, [out_held, out_last])
    small_pieces = [small_held, small_last]
    (
        grad_b_out,
        grad_gain_two,
        grad_bias_two,
        grad_b_down,
        grad_gain_one,
        grad_bias_one,
        grad_w1,
        grad_b1,
        grad_w2,
        grad_b2,
        grad_b_up,
        grad_b_in,
        grad_taps,
        grad_short,
        grad_direct,
        grad_w3,
        grad_decay,
    ) = small_out_call(
        places,
        block_offsets,
        share,
        small_pieces,
        norm2_sums.shape[0] + norm1_sums.shape[0],
        [filter_w1.shape, filter_w2.shape],
        b_up_sum.shape[1],
        shard_up,
    )
    return (
        block_out,
        grad_input,
        grad_gain_one[0],
        grad_bias_one[0],
        in_whole,
        grad_b_in[0],
        grad_taps,
        grad_short[0],
        grad_w1,
        grad_b1[0],
        grad_w2,
        grad_b2[0],
        grad_w3,
        grad_decay[0],
        grad_direct[0],
        out_whole,
        grad_b_out[0],
        grad_gain_two[0],
        grad_bias_two[0],
        up_whole,
        grad_b_up[0],
        down_whole,
        grad_b_down[0],
    )


def local(*args):
    blocks, width, shard_in = lax.axis_size("block"), args[0].shape[2], args[4].shape[1]
    channels, group = width // blocks, math.gcd(width, shard_in)
    fits = (
        channels % 128 == 0
        and group // blocks % 32 == 0
        and shard_in // blocks % 32 == 0
        and args[19].shape[1] // blocks % 128 == 0
        and args[15].shape[1] % 128 == 0
        and args[10].shape[1] * blocks == channels
        and lax.axis_size("dp") > 1
    )
    return (local_kernels if fits else local_plain)(*args)


def solution(mesh):
    placed = (
        P("dp", "block", None),
        P("dp", None),
        P(),
        P(),
        P(None, "dp"),
        P(),
        P(),
        P(),
        P(),
        P(),
        P(),
        P(),
        P(),
        P(),
        P(),
        P(None, "dp"),
        P(),
        P(),
        P(),
        P(None, "dp"),
        P(),
        P(None, "dp"),
        P(),
        P("dp", "block", None),
    )
    return jax.shard_map(
        local,
        mesh=mesh,
        in_specs=placed,
        out_specs=(
            P("dp", "block", None),
            P("dp", "block", None),
            P(),
            P(),
            P(None, "dp"),
            P(),
            P(),
            P(),
            P(),
            P(),
            P(),
            P(),
            P(),
            P(),
            P(),
            P(None, "dp"),
            P(),
            P(),
            P(),
            P(None, "dp"),
            P(),
            P(None, "dp"),
            P(),
        ),
        check_vma=False,
    )
```

```python
import math

import jax
import jax.numpy as jnp
import ml_dtypes
import numpy as np
from jax import lax
from jax.experimental import pallas as pl
from jax.experimental.pallas import tpu as pltpu
from jax.sharding import PartitionSpec as P

EPSILON = 1e-05
MOD_SHIFT = 0.05
HIGHEST = lax.Precision.HIGHEST
HIGH = lax.Precision.HIGH
LOW = jnp.bfloat16
WIDE = jnp.float32


def dot_high(left, right):
    return jnp.dot(left, right, precision=HIGHEST, preferred_element_type=WIDE)


def dot_near(left, right):
    return jnp.dot(left, right, precision=HIGH, preferred_element_type=WIDE)


def dot_plain(left, right):
    return jnp.dot(left, right, preferred_element_type=WIDE)


def dot_first(left, right):
    return lax.dot_general(left, right, (((0,), (0,)), ((), ())), preferred_element_type=WIDE)


def dot_last(left, right):
    return lax.dot_general(left, right, (((1,), (1,)), ((), ())), preferred_element_type=WIDE)


def layer_norm(values, gain, bias):
    mean = jnp.mean(values, axis=-1, keepdims=True)
    centered = values - mean
    variance = jnp.mean(centered * centered, axis=-1, keepdims=True)
    return centered * lax.rsqrt(variance + EPSILON) * gain + bias


def exact_gelu(values):
    return jax.nn.gelu(values, approximate=False)


def position_table(length, emb_dim):
    bands = (emb_dim - 1) // 2
    sample = np.arange(length, dtype=np.float32)
    times = sample / np.float32(length - 1)
    frequency = np.linspace(0.0001, bands - 1, bands).astype(np.float32)
    angle = np.float32(2.0 * math.pi) * sample[:, None] * frequency[None, :] / np.float32(length)
    table = np.concatenate([times[:, None], np.cos(angle), -np.sin(angle)], axis=1)
    return (table.astype(np.float32), times)


def transform_tables(block_len):
    span = 2 * block_len
    frequency = np.arange(block_len)
    sample = np.arange(block_len)
    is_zero = (frequency == 0)[:, None]
    angle = 2.0 * math.pi * (frequency[:, None] * sample[None, :] % span) / span
    alternate = np.where(sample % 2 == 0, 1.0, -1.0)
    real_rows = np.cos(angle)
    imag_rows = np.where(is_zero, alternate[None, :], -np.sin(angle))
    forward_table = np.concatenate([real_rows, imag_rows], axis=0)
    outputs = sample + block_len
    out_angle = 2.0 * math.pi * (outputs[:, None] * frequency[None, :] % span) / span
    out_alternate = np.where(outputs % 2 == 0, 1.0, -1.0)
    zero_col = (frequency == 0)[None, :]
    real_cols = np.where(zero_col, 1.0, 2.0) * np.cos(out_angle) / span
    imag_cols = np.where(zero_col, out_alternate[:, None] / span, -2.0 * np.sin(out_angle) / span)
    inverse_table = np.concatenate([real_cols, imag_cols], axis=1)
    parity = np.where(frequency % 2 == 0, 1.0, -1.0)
    sign = np.concatenate([parity, np.where(frequency == 0, 1.0, parity)])
    edge = (frequency == 0).astype(np.float32)[:, None]
    return tuple(item.astype(np.float32) for item in (forward_table, inverse_table, sign, edge))


def spectral_product(left, right, edge):
    half = left.shape[-2] // 2
    left_re, left_im = (left[..., :half, :], left[..., half:, :])
    right_re, right_im = (right[..., :half, :], right[..., half:, :])
    inside = 1.0 - edge
    out_re = left_re * right_re - inside * left_im * right_im
    out_im = inside * (left_re * right_im + left_im * right_re) + edge * left_im * right_im
    return jnp.concatenate([out_re, out_im], axis=-2)


def spectral_back(grad, other, edge):
    half = grad.shape[-2] // 2
    grad_re, grad_im = (grad[..., :half, :], grad[..., half:, :])
    other_re, other_im = (other[..., :half, :], other[..., half:, :])
    inside = 1.0 - edge
    back_re = grad_re * other_re + inside * grad_im * other_im
    back_im = inside * (grad_im * other_re - grad_re * other_im) + edge * grad_im * other_im
    return jnp.concatenate([back_re, back_im], axis=-2)


class Grid:
    def __init__(self, count_dp, count_block):
        self.count_dp = count_dp
        self.count_block = count_block
        self.row = lax.axis_index("dp")
        self.place = lax.axis_index("block")
        self.dp_steps = []
        bit = 1
        while bit < count_dp:
            self.dp_steps.append((bit | (bit >> 1) if bit == 4 else bit, 0))
            bit *= 2
        self.chip_steps = []
        bit = 2
        while bit < count_block:
            self.chip_steps.append((0, bit | (bit >> 1) if bit == 4 else bit))
            bit *= 2
        self.core_step = (0, 1)

    def swap(self, value, step):
        pairs = []
        for row in range(self.count_dp):
            for place in range(self.count_block):
                to = (row ^ step[0]) * self.count_block + (place ^ step[1])
                pairs.append((row * self.count_block + place, to))
        return lax.ppermute(value, ("dp", "block"), pairs)

    def gather(self, value, steps, gates=()):
        held = value[None]
        pieces = [held]
        for number, step in enumerate(steps):
            if number < len(gates):
                held = after(held, *gates[number])
            pieces.append(self.swap(held, step))
            if number + 1 < len(steps):
                held = jnp.concatenate(pieces, axis=0)
        return pieces

    def scatter(self, kept, sent, steps, whole=True, sends=None, adds=None):
        for number, step in enumerate(reversed(steps)):
            if sends and number in sends:
                sent = after(sent, *sends[number])
            arrived = self.swap(sent, step)
            if adds and number in adds:
                arrived = after(arrived, *adds[number])
            half = kept.shape[0] // 2
            if not half and not whole:
                return kept[0], arrived[0]
            if half:
                sent = add_low(kept[half:], arrived[half:])
                kept = add_low(kept[:half], arrived[:half])
            else:
                kept = add_low(kept, arrived)
        return kept[0]

    def halve(self, kept, sent, step):
        return halves(kept, self.swap(sent, step))


def halves(left, right):
    half = left.shape[0] // 2
    return add_low(left[:half], right[:half]), add_low(left[half:], right[half:])


def add_low(left, right):
    return (left.astype(WIDE) + right.astype(WIDE)).astype(left.dtype)


def offsets_of(steps):
    offsets = [(0, 0)]
    for step in steps:
        offsets = offsets + [(a ^ step[0], b ^ step[1]) for a, b in offsets]
    return offsets


def arrange(pieces, mine, offsets):
    shape = pieces[0].shape[1:]
    if shape[-2] % 32 or shape[-1] % 128:
        held = jnp.concatenate(pieces, axis=0)
        codes = codes_of(offsets, len(offsets))
        return jnp.concatenate(
            [
                lax.dynamic_slice_in_dim(held, place_in(codes, k ^ mine), 1, 0)
                for k in range(len(offsets))
            ],
            axis=0,
        )
    count = len(pieces)

    def kernel(mine_ref, *refs):
        source, target = refs[:count], refs[count]
        at = 0
        for ref in source:
            for i in range(ref.shape[0]):
                target[mine_ref[0] ^ offsets[at]] = ref[i]
                at += 1

    return pl.pallas_call(
        kernel,
        out_shape=jax.ShapeDtypeStruct((len(offsets), *shape), pieces[0].dtype),
        in_specs=[pl.BlockSpec(memory_space=pltpu.SMEM)]
        + [pl.BlockSpec(memory_space=pltpu.VMEM)] * count,
        out_specs=pl.BlockSpec(memory_space=pltpu.VMEM),
    )(jnp.reshape(mine, (1,)).astype(jnp.int32), *pieces)


def deal(natural, mine, offsets):
    half = len(offsets) // 2
    shape = natural.shape[1:]
    if shape[-2] % 32 or shape[-1] % 128:
        dealt = [lax.dynamic_slice_in_dim(natural, mine ^ offset, 1, 0) for offset in offsets]
        return jnp.concatenate(dealt[:half], axis=0), jnp.concatenate(dealt[half:], axis=0)

    def kernel(mine_ref, source, kept, sent):
        for at, offset in enumerate(offsets):
            if at < half:
                kept[at] = source[mine_ref[0] ^ offset]
            else:
                sent[at - half] = source[mine_ref[0] ^ offset]

    out = jax.ShapeDtypeStruct((half, *shape), natural.dtype)
    vmem = pl.BlockSpec(memory_space=pltpu.VMEM)
    return pl.pallas_call(
        kernel,
        out_shape=(out, out),
        in_specs=[pl.BlockSpec(memory_space=pltpu.SMEM), vmem],
        out_specs=(vmem, vmem),
    )(jnp.reshape(mine, (1,)).astype(jnp.int32), natural)


def place_in(codes, offset):
    place = 0
    for j, code in enumerate(codes):
        place = place ^ (((offset >> j) & 1) * code)
    return place


def codes_of(offsets, count):
    codes, bit = [], 1
    while bit < count:
        codes.append(offsets.index(bit))
        bit *= 2
    return codes


def split_low(values):
    high = values.astype(LOW)
    return high, (values - high.astype(WIDE)).astype(LOW)


def triple(table):
    high = table.astype(ml_dtypes.bfloat16)
    low = (table - high.astype(np.float32)).astype(ml_dtypes.bfloat16)
    return np.concatenate([high, high, low], axis=1)


def store_triple(target, columns, values):
    high, low = split_low(values)
    size = values.shape[0]
    target[0:size, columns] = high
    target[size : 2 * size, columns] = low
    target[2 * size : 3 * size, columns] = high


def long_range(starts, count, block_len, length):
    begin, end, before = starts[0], jnp.int32(length), jnp.int32(-1)
    for d in range(count):
        begin = jnp.where(starts[d] <= block_len, starts[d], begin)
        before = before + jnp.where(starts[d] <= block_len, 1, 0)
    for d in reversed(range(count)):
        end = jnp.where(starts[d] > block_len, starts[d], end)
    return begin, end, before


def short_range(starts, count, number, before, block_len, length):
    early = number < before
    bounds = [starts[d] for d in range(count)] + [jnp.int32(length)]
    begin = jnp.where(early, bounds[number], bounds[number + 1])
    end = jnp.where(early, bounds[number + 1], bounds[number + 2])
    return begin, end, jnp.where(early, 0, length - block_len)


def rows_from(base, size, lanes):
    return lax.broadcasted_iota(jnp.int32, (size, lanes), 0) + base


def inside_mask(base, size, lanes, begin, end):
    rows = rows_from(base, size, lanes)
    return (rows >= begin) & (rows < end)


def keep_masks(starts, count, base, size, lanes):
    rows = rows_from(base, size, lanes)
    one = rows != starts[0]
    for d in range(1, count):
        one = one & (rows != starts[d])
    two = one
    for d in range(count):
        two = two & (rows != starts[d] + 1)
    return one, two


VMEM_SPACE = pl.BlockSpec(memory_space=pltpu.VMEM)
ANY_SPACE = pl.BlockSpec(memory_space=pl.ANY)
SMEM_SPACE = pl.BlockSpec(memory_space=pltpu.SMEM)
LIMIT = 30 * 1024 * 1024
WHOLE = 56 * 1024 * 1024


def cost(microseconds):
    return pl.CostEstimate(
        flops=int(microseconds * 1e9), bytes_accessed=int(microseconds * 3e6), transcendentals=0
    )


class Copies:
    def __init__(self, sems):
        self.sems, self.used = sems, 0

    def start(self, source, target):
        copy = pltpu.make_async_copy(source, target, self.sems.at[self.used])
        self.used += 1
        copy.start()
        return copy


def filter_kernel(block_len, blocks, table_ref, w1, w2, vec, third_at, f3_ref, spectra):
    length = block_len * blocks
    channels = vec.shape[1]
    one_row = jnp.where(lax.broadcasted_iota(jnp.int32, (8, length), 0) == 0, 1.0, 0.0)

    def turned(left, right):
        return lax.dot_general(
            left, right, (((0,), (0,)), ((), ())), precision=HIGHEST, preferred_element_type=WIDE
        )

    first = jnp.sin(turned(w1[...], table_ref[...]))
    second = jnp.sin(turned(w2[...], jnp.concatenate([first, one_row], axis=0)))
    decay = vec[third_at - 2 : third_at - 1, :]
    third_w = vec[third_at : third_at + second.shape[0], :]
    before = None
    half_rows = lax.broadcasted_iota(jnp.int32, (2 * block_len, channels), 0)
    parity = jnp.where(half_rows % 2 == 0, 1.0, -1.0)
    sign = jnp.where(half_rows == block_len, 1.0, parity)
    for i in range(blocks):
        part = turned(second[:, i * block_len : (i + 1) * block_len], third_w)
        times = rows_from(i * block_len, block_len, channels).astype(WIDE) / (length - 1)
        part = part * (jnp.exp(-times * decay) + MOD_SHIFT)
        high, low = split_low(part)
        stacked = jnp.concatenate([high, low, high], axis=0)
        half = jnp.dot(f3_ref[...], stacked, preferred_element_type=WIDE)
        spectra[i] = sign * half if before is None else before + sign * half
        before = half


def with_bias(weights, bias):
    rows = weights.shape[0]
    return jnp.pad(jnp.concatenate([weights, bias[None]], axis=0), ((0, -(rows + 1) % 8), (0, 0)))


def turned_table(table):
    length, count = table.shape
    rows = [table.T, np.ones((1, length), np.float32)]
    rows.append(np.zeros((-(count + 1) % 8, length), np.float32))
    return np.concatenate(rows, axis=0)


def filter_call(block_len, blocks, table, f3, w1, w2, vec, third_at):
    channels = vec.shape[1]

    def body(table_ref, w1_ref, w2_ref, vec_ref, f3_ref, spectra, mark):
        filter_kernel(
            block_len, blocks, table_ref, w1_ref, w2_ref, vec_ref, third_at, f3_ref, spectra
        )
        mark[...] = w1_ref[...]

    return pl.pallas_call(
        body,
        out_shape=[
            jax.ShapeDtypeStruct((blocks, 2 * block_len, channels), WIDE),
            jax.ShapeDtypeStruct(w1.shape, WIDE),
        ],
        in_specs=[VMEM_SPACE] * 5,
        out_specs=[VMEM_SPACE] * 2,
        compiler_params=pltpu.CompilerParams(vmem_limit_bytes=LIMIT),
        cost_estimate=cost(7),
    )(table, w1, w2, vec, f3)


def gather_in(copies, pieces, mine, offsets, target):
    started, at = [], 0
    for ref in pieces:
        for i in range(ref.shape[0]):
            started.append(copies.start(ref.at[i], target.at[mine ^ offsets[at]]))
            at += 1
    return started


def conv_call(
    block_len, blocks, places, starts, normed_pieces, in_pieces, in_offsets, block_offsets, vec, spectra, f3, i3
):
    length = block_len * blocks
    channels = vec.shape[1]
    docs = starts.shape[0]
    entries = blocks + docs - 1
    width = normed_pieces[0].shape[-1]
    groups = len(in_pieces)
    share = in_pieces[0][0].shape[1]
    count_dp = len(in_offsets[0])
    flat_in = [piece for pieces in in_pieces for piece in pieces]
    n_norm, n_in, n_out = len(normed_pieces), len(flat_in), blocks
    step = 16

    def body(place_ref, starts_ref, vec_ref, f3_ref, i3_ref, spectra_ref, *refs):
        norm_refs, in_refs = refs[:n_norm], refs[n_norm : n_norm + n_in]
        refs = refs[n_norm + n_in :]
        gated_refs, (proj_out, entry_out, mixed_out, rows_out, norm_out) = refs[:n_out], refs[n_out : n_out + 5]
        norm, rows, proj, inner, gate, xs, ent, ys, mixed, spec, sems = refs[n_out + 5 :]
        row, place = place_ref[0], place_ref[1]
        copies = Copies(sems)
        waiting = gather_in(copies, norm_refs, place, block_offsets, norm)
        at = 0
        for g in range(groups):
            count = len(in_pieces[g])
            index = 0
            for ref in in_refs[at : at + count]:
                for i in range(ref.shape[0]):
                    to = row ^ in_offsets[g][index]
                    waiting.append(copies.start(ref.at[i], rows.at[to, g]))
                    index += 1
            at += count
        spec_copy = copies.start(spectra_ref, spec)
        for copy in waiting:
            copy.wait()
        leaving = [copies.start(norm, norm_out), copies.start(rows, rows_out)]

        flat_rows = rows[...].reshape(3 * channels, width)
        for role in range(3):
            weights = flat_rows[role * channels : (role + 1) * channels]
            bias = vec_ref[role : role + 1, :]
            for b in range(blocks):
                proj[b * block_len : (b + 1) * block_len, role * channels : (role + 1) * channels] = (
                    lax.dot_general(
                        norm[b],
                        weights,
                        (((1,), (1,)), ((), ())),
                        preferred_element_type=WIDE,
                    )
                    + bias
                )
        leaving.append(copies.start(proj, proj_out))
        for b in range(blocks):
            base = b * block_len
            one, two = keep_masks(starts_ref, docs, base, block_len, channels)
            parts = []
            for role in range(3):
                lanes = slice(role * channels, (role + 1) * channels)
                here = proj[base : base + block_len, lanes]
                if b:
                    back = proj[base - 8 : base + block_len, lanes]
                    prev_one = pltpu.roll(back, 1, 0)[8:]
                    prev_two = pltpu.roll(back, 2, 0)[8:]
                else:
                    prev_one, prev_two = pltpu.roll(here, 1, 0), pltpu.roll(here, 2, 0)
                tap = [vec_ref[3 + 3 * j + role : 4 + 3 * j + role, :] for j in range(3)]
                short = (
                    vec_ref[12 + role : 13 + role, :]
                    + tap[0] * here
                    + tap[1] * jnp.where(one, prev_one, 0.0)
                    + tap[2] * jnp.where(two, prev_two, 0.0)
                )
                parts.append(short)
            gate[base : base + block_len] = parts[0]
            inner[base : base + block_len] = parts[1] * parts[2]
        begin, end, before = long_range(starts_ref, docs, block_len, length)
        for b in range(blocks):
            mask = inside_mask(b * block_len, block_len, channels, begin, end)
            part = jnp.where(mask, inner[b * block_len : (b + 1) * block_len], 0.0)
            store_triple(xs, slice(b * channels, (b + 1) * channels), part)
        for m in range(docs - 1):
            first, last, base = short_range(starts_ref, docs, m, before, block_len, length)
            base = pl.multiple_of(base, block_len)
            mask = inside_mask(base, block_len, channels, first, last)
            part = jnp.where(mask, inner[pl.ds(base, block_len)], 0.0)
            store_triple(xs, slice((blocks + m) * channels, (blocks + m + 1) * channels), part)
        for e in range(entries):
            ent[e] = jnp.dot(
                f3_ref[...], xs[:, e * channels : (e + 1) * channels], preferred_element_type=WIDE
            )
        leaving.append(copies.start(ent, entry_out))
        spec_copy.wait()

        @pl.loop(0, block_len // step)
        def _(number):
            at_re = pl.multiple_of(number * step, step)
            at_im = pl.multiple_of(number * step + block_len, step)
            edge = jnp.where(rows_from(at_re, step, channels) == 0, 1.0, 0.0)
            inside = 1.0 - edge
            keys = [(spec[k, pl.ds(at_re, step)], spec[k, pl.ds(at_im, step)]) for k in range(blocks)]
            held = [(ent[k, pl.ds(at_re, step)], ent[k, pl.ds(at_im, step)]) for k in range(blocks)]
            for e in range(entries):
                pairs = (
                    [(held[j], keys[e - j]) for j in range(e + 1)]
                    if e < blocks
                    else [((ent[e, pl.ds(at_re, step)], ent[e, pl.ds(at_im, step)]), keys[0])]
                )
                rr = ii = ri = None
                for (a, b), (c, d) in pairs:
                    rr = a * c if rr is None else rr + a * c
                    ii = b * d if ii is None else ii + b * d
                    ri = a * d + b * c if ri is None else ri + (a * d + b * c)
                lanes = slice(e * channels, (e + 1) * channels)
                out_re = rr - inside * ii
                out_im = inside * ri + edge * ii
                for part, at in ((out_re, at_re), (out_im, at_im)):
                    high, low = split_low(part)
                    ys[pl.ds(at, step), lanes] = high
                    ys[pl.ds(at + 2 * block_len, step), lanes] = low
                    ys[pl.ds(at + 4 * block_len, step), lanes] = high

        direct = vec_ref[16:17, :]
        for b in range(blocks):
            back = jnp.dot(
                i3_ref[...], ys[:, b * channels : (b + 1) * channels], preferred_element_type=WIDE
            )
            rows_here = slice(b * block_len, (b + 1) * block_len)
            mask = inside_mask(b * block_len, block_len, channels, begin, end)
            mixed[rows_here] = jnp.where(mask, back, 0.0) + direct * inner[rows_here]
        for m in range(docs - 1):
            lanes = slice((blocks + m) * channels, (blocks + m + 1) * channels)
            back = jnp.dot(i3_ref[...], ys[:, lanes], preferred_element_type=WIDE)
            first, last, base = short_range(starts_ref, docs, m, before, block_len, length)
            base = pl.multiple_of(base, block_len)
            mask = inside_mask(base, block_len, channels, first, last)
            where = pl.ds(base, block_len)
            mixed[where] = mixed[where] + jnp.where(mask, back, 0.0)
        leaving.append(copies.start(mixed, mixed_out))
        for index, offset in enumerate(block_offsets):
            where = pl.ds(pl.multiple_of((place ^ offset) * block_len, block_len), block_len)
            gated_refs[index][...] = (gate[where] * mixed[where]).astype(LOW)
        for copy in leaving:
            copy.wait()

    shape = jax.ShapeDtypeStruct
    sem_count = blocks + groups * count_dp + 6
    return pl.pallas_call(
        body,
        out_shape=[shape((block_len, channels), LOW)] * blocks
        + [
            shape((length, 3 * channels), WIDE),
            shape((entries, 2 * block_len, channels), WIDE),
            shape((length, channels), WIDE),
            shape((count_dp, groups, share, width), LOW),
            shape((blocks, block_len, width), LOW),
        ],
        in_specs=[SMEM_SPACE, SMEM_SPACE, VMEM_SPACE, VMEM_SPACE, VMEM_SPACE, ANY_SPACE]
        + [ANY_SPACE] * (n_norm + n_in),
        out_specs=[VMEM_SPACE] * blocks + [ANY_SPACE] * 5,
        scratch_shapes=[
            pltpu.VMEM((blocks, block_len, width), LOW),
            pltpu.VMEM((count_dp, groups, share, width), LOW),
            pltpu.VMEM((length, 3 * channels), WIDE),
            pltpu.VMEM((length, channels), WIDE),
            pltpu.VMEM((length, channels), WIDE),
            pltpu.VMEM((3 * block_len, entries * channels), LOW),
            pltpu.VMEM((entries, 2 * block_len, channels), WIDE),
            pltpu.VMEM((6 * block_len, entries * channels), LOW),
            pltpu.VMEM((length, channels), WIDE),
            pltpu.VMEM((blocks, 2 * block_len, channels), WIDE),
            pltpu.SemaphoreType.DMA((sem_count,)),
        ],
        compiler_params=pltpu.CompilerParams(vmem_limit_bytes=WHOLE),
        cost_estimate=cost(14),
    )(places, starts, vec, f3, i3, spectra, *normed_pieces, *flat_in)


def back_call(
    block_len,
    blocks,
    places,
    starts,
    grad_pieces,
    block_offsets,
    vec,
    spectra,
    proj,
    entries,
    mixed,
    it3,
    ft3,
):
    length = block_len * blocks
    channels = vec.shape[1]
    docs = starts.shape[0]
    count = entries.shape[0]
    three = 3 * channels
    step = 16

    def body(place_ref, starts_ref, vec_ref, it3_ref, ft3_ref, *refs):
        grad_refs, refs = refs[:blocks], refs[blocks:]
        spectra_ref, proj_ref, entry_ref, mixed_ref, lags, direct_out, gs_out = refs[:7]
        spec, proj, ent, mixed, gg, short, gs, gm, xs, gt, ys, gi, sems = refs[7:]
        place = place_ref[1]
        copies = Copies(sems)
        proj_copy = copies.start(proj_ref, proj)
        mixed_copy = copies.start(mixed_ref, mixed)
        spec_copy = copies.start(spectra_ref, spec)
        entry_copy = copies.start(entry_ref, ent)
        for index, offset in enumerate(block_offsets):
            where = pl.ds(pl.multiple_of((place ^ offset) * block_len, block_len), block_len)
            gg[where] = grad_refs[index][...]
        proj_copy.wait()
        mixed_copy.wait()
        direct = vec_ref[16:17, :]
        direct_sum = jnp.zeros((1, channels), WIDE)
        for b in range(blocks):
            base = b * block_len
            here = slice(base, base + block_len)
            one, two = keep_masks(starts_ref, docs, base, block_len, channels)
            parts = []
            for role in range(3):
                lanes = slice(role * channels, (role + 1) * channels)
                now = proj[here, lanes]
                if b:
                    back = proj[base - 8 : base + block_len, lanes]
                    prev_one, prev_two = pltpu.roll(back, 1, 0)[8:], pltpu.roll(back, 2, 0)[8:]
                else:
                    prev_one, prev_two = pltpu.roll(now, 1, 0), pltpu.roll(now, 2, 0)
                tap = [vec_ref[3 + 3 * j + role : 4 + 3 * j + role, :] for j in range(3)]
                parts.append(
                    vec_ref[12 + role : 13 + role, :]
                    + tap[0] * now
                    + tap[1] * jnp.where(one, prev_one, 0.0)
                    + tap[2] * jnp.where(two, prev_two, 0.0)
                )
            grad = gg[here].astype(WIDE)
            gs[here, :channels] = grad * mixed[here]
            grad = grad * parts[0]
            gm[here] = grad
            short[here, :channels] = parts[1]
            short[here, channels:] = parts[2]
            direct_sum = direct_sum + jnp.sum(
                grad * (parts[1] * parts[2]), axis=0, keepdims=True
            )
        gs[length:, :] = jnp.zeros((8, three), WIDE)
        direct_out[...] = direct_sum
        begin, end, before = long_range(starts_ref, docs, block_len, length)
        ranges = []
        for m in range(docs - 1):
            first, last, base = short_range(starts_ref, docs, m, before, block_len, length)
            base = pl.multiple_of(base, block_len)
            ranges.append((base, inside_mask(base, block_len, channels, first, last)))
        for b in range(blocks):
            mask = inside_mask(b * block_len, block_len, channels, begin, end)
            part = jnp.where(mask, gm[b * block_len : (b + 1) * block_len], 0.0)
            store_triple(xs, slice(b * channels, (b + 1) * channels), part)
        for m, (base, mask) in enumerate(ranges):
            part = jnp.where(mask, gm[pl.ds(base, block_len)], 0.0)
            store_triple(xs, slice((blocks + m) * channels, (blocks + m + 1) * channels), part)
        for e in range(count):
            gt[e] = jnp.dot(
                it3_ref[...], xs[:, e * channels : (e + 1) * channels], preferred_element_type=WIDE
            )
        spec_copy.wait()
        entry_copy.wait()

        @pl.loop(0, block_len // step)
        def _(number):
            at_re = pl.multiple_of(number * step, step)
            at_im = pl.multiple_of(number * step + block_len, step)
            edge = jnp.where(rows_from(at_re, step, channels) == 0, 1.0, 0.0)
            inside = 1.0 - edge

            def load(ref, k):
                return ref[k, pl.ds(at_re, step)], ref[k, pl.ds(at_im, step)]

            def combine(pairs):
                rr = ii = ri = None
                for (a, b), (c, d) in pairs:
                    rr = a * c if rr is None else rr + a * c
                    ii = b * d if ii is None else ii + b * d
                    ri = b * c - a * d if ri is None else ri + (b * c - a * d)
                return rr + inside * ii, inside * ri + edge * ii

            for e in range(count):
                if e < blocks:
                    pairs = [(load(gt, i), load(spec, i - e)) for i in range(e, blocks)]
                else:
                    pairs = [(load(gt, e), load(spec, 0))]
                lanes = slice(e * channels, (e + 1) * channels)
                for part, at in zip(combine(pairs), (at_re, at_im)):
                    high, low = split_low(part)
                    ys[pl.ds(at, step), lanes] = high
                    ys[pl.ds(at + 2 * block_len, step), lanes] = low
                    ys[pl.ds(at + 4 * block_len, step), lanes] = high
            for k in range(blocks):
                pairs = [(load(gt, j + k), load(ent, j)) for j in range(blocks - k)]
                if k == 0:
                    pairs += [(load(gt, e), load(ent, e)) for e in range(blocks, count)]
                out_re, out_im = combine(pairs)
                lags[k, pl.ds(at_re, step)] = out_re
                lags[k, pl.ds(at_im, step)] = out_im

        for b in range(blocks):
            here = slice(b * block_len, (b + 1) * block_len)
            back = jnp.dot(
                ft3_ref[...], ys[:, b * channels : (b + 1) * channels], preferred_element_type=WIDE
            )
            mask = inside_mask(b * block_len, block_len, channels, begin, end)
            gi[here] = jnp.where(mask, back, 0.0) + direct * gm[here]
        for m, (base, mask) in enumerate(ranges):
            lanes = slice((blocks + m) * channels, (blocks + m + 1) * channels)
            back = jnp.dot(ft3_ref[...], ys[:, lanes], preferred_element_type=WIDE)
            where = pl.ds(base, block_len)
            gi[where] = gi[where] + jnp.where(mask, back, 0.0)
        for b in range(blocks):
            here = slice(b * block_len, (b + 1) * block_len)
            gs[here, channels : 2 * channels] = gi[here] * short[here, channels:]
            gs[here, 2 * channels :] = gi[here] * short[here, :channels]
        copies.start(gs, gs_out).wait()

    shape = jax.ShapeDtypeStruct
    return pl.pallas_call(
        body,
        out_shape=[
            shape((blocks, 2 * block_len, channels), WIDE),
            shape((1, channels), WIDE),
            shape((length + 8, three), WIDE),
        ],
        in_specs=[SMEM_SPACE] * 2 + [VMEM_SPACE] * (3 + blocks) + [ANY_SPACE] * 4,
        out_specs=[VMEM_SPACE, VMEM_SPACE, ANY_SPACE],
        scratch_shapes=[
            pltpu.VMEM((blocks, 2 * block_len, channels), WIDE),
            pltpu.VMEM((length, three), WIDE),
            pltpu.VMEM((count, 2 * block_len, channels), WIDE),
            pltpu.VMEM((length, channels), WIDE),
            pltpu.VMEM((length, channels), LOW),
            pltpu.VMEM((length, 2 * channels), WIDE),
            pltpu.VMEM((length + 8, three), WIDE),
            pltpu.VMEM((length, channels), WIDE),
            pltpu.VMEM((3 * block_len, count * channels), LOW),
            pltpu.VMEM((count, 2 * block_len, channels), WIDE),
            pltpu.VMEM((6 * block_len, count * channels), LOW),
            pltpu.VMEM((length, channels), WIDE),
            pltpu.SemaphoreType.DMA((5,)),
        ],
        compiler_params=pltpu.CompilerParams(vmem_limit_bytes=LIMIT),
        cost_estimate=cost(14),
    )(places, starts, vec, it3, ft3, *grad_pieces, spectra, proj, entries, mixed)


def project_back_call(
    block_len,
    blocks,
    places,
    starts,
    in_offsets,
    block_offsets,
    vec,
    norm1,
    direct,
    grad_short,
    proj,
    in_rows,
    normed,
):
    length = block_len * blocks
    channels = vec.shape[1]
    docs = starts.shape[0]
    count_dp, groups, share, width = in_rows.shape
    three = 3 * channels
    half_dp, half_block = count_dp // 2, blocks // 2

    def body(place_ref, starts_ref, vec_ref, gain_ref, shift_ref, direct_ref, *refs):
        gs_ref, proj_ref, rows_ref, norm_ref = refs[:4]
        refs = refs[4:]
        dealt_refs = [(refs[2 * g], refs[2 * g + 1]) for g in range(groups)]
        refs = refs[2 * groups :]
        gn_kept, gn_sent, sums, norm_sums = refs[:4]
        gs, proj, rows, norm, gp, gr, sems = refs[4:]
        row, place = place_ref[0], place_ref[1]
        copies = Copies(sems)
        gs_copy = copies.start(gs_ref, gs)
        proj_copy = copies.start(proj_ref, proj)
        rows_copy = copies.start(rows_ref, rows)
        norm_copy = copies.start(norm_ref, norm)
        sums[15:16, :] = direct_ref[...]
        gs_copy.wait()
        proj_copy.wait()
        for role in range(3):
            lanes = slice(role * channels, (role + 1) * channels)
            tap = [vec_ref[3 + 3 * j + role : 4 + 3 * j + role, :] for j in range(3)]
            totals = [jnp.zeros((1, channels), WIDE) for _ in range(5)]
            for b in range(blocks):
                base = b * block_len
                here = slice(base, base + block_len)
                one, two = keep_masks(starts_ref, docs, base, block_len + 8, channels)
                grad = gs[base : base + block_len + 8, lanes]
                pass_one, pass_two = jnp.where(one, grad, 0.0), jnp.where(two, grad, 0.0)
                size = block_len + 8
                result = (
                    tap[0] * grad[:block_len]
                    + tap[1] * pltpu.roll(pass_one, size - 1, 0)[:block_len]
                    + tap[2] * pltpu.roll(pass_two, size - 2, 0)[:block_len]
                ).astype(LOW)
                gp[here, lanes] = result
                now = proj[here, lanes]
                if b:
                    back = proj[base - 8 : base + block_len, lanes]
                    prev_one, prev_two = pltpu.roll(back, 1, 0)[8:], pltpu.roll(back, 2, 0)[8:]
                else:
                    prev_one, prev_two = pltpu.roll(now, 1, 0), pltpu.roll(now, 2, 0)
                terms = [
                    result.astype(WIDE),
                    grad[:block_len] * now,
                    pass_one[:block_len] * prev_one,
                    pass_two[:block_len] * prev_two,
                    grad[:block_len],
                ]
                totals = [
                    total + jnp.sum(term, axis=0, keepdims=True)
                    for total, term in zip(totals, terms)
                ]
            sums[role : role + 1, :] = totals[0]
            for j in range(3):
                sums[3 + 3 * j + role : 4 + 3 * j + role, :] = totals[1 + j]
            sums[12 + role : 13 + role, :] = totals[4]
        rows_copy.wait()
        norm_copy.wait()
        weights = rows[...].reshape(three, width)
        shift_sum = jnp.zeros((1, width), WIDE)
        scale_sum = jnp.zeros((1, width), WIDE)
        for index, offset in enumerate(block_offsets):
            other = place ^ offset
            where = pl.ds(pl.multiple_of(other * block_len, block_len), block_len)
            part = jnp.dot(gp[where], weights, preferred_element_type=WIDE)
            shift_sum = shift_sum + jnp.sum(part, axis=0, keepdims=True)
            scale_sum = scale_sum + jnp.sum(
                part * norm[other].astype(WIDE), axis=0, keepdims=True
            )
            if index < half_block:
                gn_kept[index] = part.astype(LOW)
            else:
                gn_sent[index - half_block] = part.astype(LOW)
        norm_sums[0:1, :] = (scale_sum - shift_ref[...] * shift_sum) / gain_ref[...]
        norm_sums[1:2, :] = shift_sum
        for c in range(3):
            lanes = slice(c * channels, (c + 1) * channels)
            total = lax.dot_general(
                gp[:, lanes],
                norm[...].reshape(length, width),
                (((0,), (0,)), ((), ())),
                preferred_element_type=WIDE,
            )
            gr[lanes] = total.astype(LOW)
        dealt = gr.reshape(count_dp, groups, share, width)
        leaving = []
        for g in range(groups):
            for index, offset in enumerate(in_offsets[g]):
                target = dealt_refs[g][index // half_dp].at[index % half_dp]
                leaving.append(copies.start(dealt.at[row ^ offset, g], target))
        for copy in leaving:
            copy.wait()

    shape = jax.ShapeDtypeStruct
    half_in = shape((half_dp, share, width), LOW)
    return pl.pallas_call(
        body,
        out_shape=[half_in] * (2 * groups)
        + [
            shape((half_block, block_len, width), LOW),
            shape((half_block, block_len, width), LOW),
            shape((16, channels), WIDE),
            shape((2, width), WIDE),
        ],
        in_specs=[SMEM_SPACE] * 2 + [VMEM_SPACE] * 4 + [ANY_SPACE] * 4,
        out_specs=[ANY_SPACE] * (2 * groups) + [VMEM_SPACE] * 4,
        scratch_shapes=[
            pltpu.VMEM((length + 8, three), WIDE),
            pltpu.VMEM((length, three), WIDE),
            pltpu.VMEM((count_dp, groups, share, width), LOW),
            pltpu.VMEM((blocks, block_len, width), LOW),
            pltpu.VMEM((length, three), LOW),
            pltpu.VMEM((three, width), LOW),
            pltpu.SemaphoreType.DMA((4 + groups * count_dp,)),
        ],
        compiler_params=pltpu.CompilerParams(vmem_limit_bytes=LIMIT),
        cost_estimate=cost(10),
    )(places, starts, vec, *norm1, direct, grad_short, proj, in_rows, normed)


def filter_back_call(block_len, blocks, table, ft3, w1, w2, vec, third_at, lags):
    length = block_len * blocks
    channels = vec.shape[1]
    units = w2.shape[1]

    def body(table_ref, w1_ref, w2_ref, vec_ref, ft3_ref, lags_ref, g1, g2, g3, gd):
        one_row = jnp.where(lax.broadcasted_iota(jnp.int32, (8, length), 0) == 0, 1.0, 0.0)

        def product(left, right, dims):
            return lax.dot_general(
                left, right, (dims, ((), ())), precision=HIGHEST, preferred_element_type=WIDE
            )

        z1 = product(w1_ref[...], table_ref[...], ((0,), (0,)))
        first = jnp.concatenate([jnp.sin(z1), one_row], axis=0)
        z2 = product(w2_ref[...], first, ((0,), (0,)))
        second = jnp.sin(z2)
        decay = vec_ref[third_at - 2 : third_at - 1, :]
        third_w = vec_ref[third_at : third_at + units, :]
        half_rows = lax.broadcasted_iota(jnp.int32, (2 * block_len, channels), 0)
        parity = jnp.where(half_rows % 2 == 0, 1.0, -1.0)
        sign = jnp.where(half_rows == block_len, 1.0, parity)
        third_sum = jnp.zeros((units, channels), WIDE)
        decay_sum = jnp.zeros((1, channels), WIDE)
        back = []
        for i in range(blocks):
            grad = sign * lags_ref[i]
            if i + 1 < blocks:
                grad = grad + lags_ref[i + 1]
            high, low = split_low(grad)
            stacked = jnp.concatenate([high, low, high], axis=0)
            grad = jnp.dot(ft3_ref[...], stacked, preferred_element_type=WIDE)
            here = second[:, i * block_len : (i + 1) * block_len]
            third = product(here, third_w, ((0,), (0,)))
            times = rows_from(i * block_len, block_len, channels).astype(WIDE) / (length - 1)
            fall = jnp.exp(-times * decay)
            decay_sum = decay_sum - jnp.sum(grad * third * fall * times, axis=0, keepdims=True)
            grad = grad * (fall + MOD_SHIFT)
            third_sum = third_sum + product(here, grad, ((1,), (0,)))
            back.append(product(third_w, grad, ((1,), (1,))))
        gz2 = jnp.concatenate(back, axis=1) * jnp.cos(z2)
        g2[...] = product(first, gz2, ((1,), (1,)))
        gz1 = product(w2_ref[:units, :], gz2, ((1,), (0,))) * jnp.cos(z1)
        g1[...] = product(table_ref[...], gz1, ((1,), (1,)))
        g3[...] = third_sum
        gd[...] = decay_sum

    shape = jax.ShapeDtypeStruct
    return pl.pallas_call(
        body,
        out_shape=[
            shape(w1.shape, WIDE),
            shape(w2.shape, WIDE),
            shape((units, channels), WIDE),
            shape((1, channels), WIDE),
        ],
        in_specs=[VMEM_SPACE] * 6,
        out_specs=[VMEM_SPACE] * 4,
        compiler_params=pltpu.CompilerParams(vmem_limit_bytes=LIMIT),
        cost_estimate=cost(9),
    )(table, w1, w2, vec, ft3, lags)


def norm_parts(values):
    mean = jnp.mean(values, axis=-1, keepdims=True)
    centered = values - mean
    variance = jnp.mean(centered * centered, axis=-1, keepdims=True)
    scale = lax.rsqrt(variance + EPSILON)
    return centered * scale, scale


def gather_out(copies, refs, row, dp_offsets, target):
    started, at = [], 0
    for ref in refs:
        for i in range(ref.shape[0]):
            for r, offset in enumerate(dp_offsets):
                started.append(copies.start(ref.at[i, r], target.at[at, row ^ offset]))
            at += 1
    return started


def branch_call(row, inputs, gated_parts, out_pieces, dp_offsets, rows):
    blocks = len(gated_parts)
    tokens, channels = gated_parts[0].shape
    width = inputs.shape[-1]
    shard = out_pieces[0].shape[2]
    count_dp = len(dp_offsets)

    def body(row_ref, in_ref, bias_ref, gain_ref, shift_ref, *refs):
        gated_refs, piece_refs = refs[:blocks], refs[blocks : blocks + len(out_pieces)]
        resid_ref, normed_ref, weights, sems = refs[blocks + len(out_pieces) :]
        copies = Copies(sems)
        waiting = gather_out(copies, piece_refs, row_ref[0], dp_offsets, weights)
        for copy in waiting:
            copy.wait()
        total = in_ref[...].astype(WIDE) + bias_ref[...]
        for i in range(blocks):
            total = total + dot_last(
                gated_refs[i][...], weights[i].reshape(width, channels)
            )
        resid_ref[...] = total
        normal, _ = norm_parts(total)
        normed_ref[...] = (normal * gain_ref[...] + shift_ref[...]).astype(LOW)

    shape = jax.ShapeDtypeStruct
    return pl.pallas_call(
        body,
        out_shape=[shape((tokens, width), WIDE), shape((tokens, width), LOW)],
        in_specs=[SMEM_SPACE] + [VMEM_SPACE] * (4 + blocks) + [ANY_SPACE] * len(out_pieces),
        out_specs=[VMEM_SPACE] * 2,
        scratch_shapes=[
            pltpu.VMEM((blocks, count_dp, shard, channels), LOW),
            pltpu.SemaphoreType.DMA((blocks * count_dp,)),
        ],
        compiler_params=pltpu.CompilerParams(vmem_limit_bytes=LIMIT),
        cost_estimate=cost(1),
    )(row, inputs, *rows, *gated_parts, *out_pieces)


def branch_back_call(row, resid, kept, arrived, cot, out_pieces, dp_offsets, gain):
    tokens, width = resid.shape
    blocks = sum(piece.shape[0] for piece in out_pieces)
    shard, channels = out_pieces[0].shape[2:]
    count_dp = len(dp_offsets)

    def body(row_ref, resid_ref, kept_ref, arrived_ref, cot_ref, gain_ref, *refs):
        piece_refs, refs = refs[: len(out_pieces)], refs[len(out_pieces) :]
        grad_refs, (whole_ref, branch_ref, sums, weights, sems) = refs[:blocks], refs[blocks:]
        copies = Copies(sems)
        waiting = gather_out(copies, piece_refs, row_ref[0], dp_offsets, weights)
        grad = kept_ref[...].astype(WIDE) + arrived_ref[...].astype(WIDE)
        normal, scale = norm_parts(resid_ref[...])
        scaled = grad * gain_ref[...]
        back = scaled - jnp.mean(scaled, axis=-1, keepdims=True)
        back = back - normal * jnp.mean(scaled * normal, axis=-1, keepdims=True)
        whole = cot_ref[...].astype(WIDE) + back * scale
        whole_ref[...] = whole
        low = whole.astype(LOW)
        branch_ref[...] = low
        sums[0:1, :] = jnp.sum(low.astype(WIDE), axis=0, keepdims=True)
        sums[1:2, :] = jnp.sum(grad * normal, axis=0, keepdims=True)
        sums[2:3, :] = jnp.sum(grad, axis=0, keepdims=True)
        sums[3:4, :] = jnp.sum(cot_ref[...].astype(WIDE), axis=0, keepdims=True)
        for copy in waiting:
            copy.wait()
        for i in range(blocks):
            grad_refs[i][...] = dot_plain(low, weights[i].reshape(width, channels)).astype(LOW)

    shape = jax.ShapeDtypeStruct
    return pl.pallas_call(
        body,
        out_shape=[shape((tokens, channels), LOW)] * blocks
        + [shape((tokens, width), WIDE), shape((tokens, width), LOW), shape((4, width), WIDE)],
        in_specs=[SMEM_SPACE] + [VMEM_SPACE] * 5 + [ANY_SPACE] * len(out_pieces),
        out_specs=[VMEM_SPACE] * (blocks + 3),
        scratch_shapes=[
            pltpu.VMEM((blocks, count_dp, shard, channels), LOW),
            pltpu.SemaphoreType.DMA((blocks * count_dp,)),
        ],
        compiler_params=pltpu.CompilerParams(vmem_limit_bytes=LIMIT),
        cost_estimate=cost(1),
    )(row, resid, kept, arrived, cot, gain, *out_pieces)


def out_grad_call(row, grad_branch, gated_parts, dp_offsets):
    blocks = len(gated_parts)
    tokens, channels = gated_parts[0].shape
    width = grad_branch.shape[1]
    count_dp = len(dp_offsets)
    shard = width // count_dp
    half = blocks // 2

    def body(row_ref, grad_ref, *refs):
        gated_refs, (kept, sent, total) = refs[:blocks], refs[blocks:]
        for i in range(blocks):
            total[...] = dot_first(grad_ref[...], gated_refs[i][...]).astype(LOW)
            target, at = (kept, i) if i < half else (sent, i - half)
            for r, offset in enumerate(dp_offsets):
                begin = pl.multiple_of((row_ref[0] ^ offset) * shard, shard)
                target[at * count_dp + r] = total[pl.ds(begin, shard)]

    out = jax.ShapeDtypeStruct((half * count_dp, shard, channels), LOW)
    return pl.pallas_call(
        body,
        out_shape=[out, out],
        in_specs=[SMEM_SPACE] + [VMEM_SPACE] * (1 + blocks),
        out_specs=[VMEM_SPACE] * 2,
        scratch_shapes=[pltpu.VMEM((width, channels), LOW)],
        compiler_params=pltpu.CompilerParams(vmem_limit_bytes=LIMIT),
        cost_estimate=cost(3),
    )(row, grad_branch, *gated_parts)


def forward_call(row, normed_pieces, cot_pieces, up_pieces, down_pieces, up_offsets, down_offsets, bias):
    tokens, width = normed_pieces[0].shape[1:]
    blocks = sum(piece.shape[0] for piece in normed_pieces)
    count_dp = len(up_offsets)
    piece = up_pieces[0].shape[1]
    shard = down_pieces[0].shape[1]
    units = piece * count_dp
    tile = 256 if units % 256 == 0 else units
    half = blocks // 2
    lists = (normed_pieces, cot_pieces, up_pieces, down_pieces)
    counts = [len(part) for part in lists]

    def body(row_ref, bias_ref, *refs):
        taken = []
        for count in counts:
            taken.append(refs[:count])
            refs = refs[count:]
        out_kept, out_sent, grad_kept, grad_sent, act_out, hid_out, norm_out, cot_out, sums = refs[:9]
        norm, cot, up, down, act, hid, sems = refs[9:]
        copies = Copies(sems)
        norm_copies = gather_in(copies, taken[0], 0, range(blocks), norm)
        up_copies = gather_in(copies, taken[2], row_ref[0], up_offsets, up)
        cot_copies = gather_in(copies, taken[1], 0, range(blocks), cot)
        down_copies = gather_in(copies, taken[3], row_ref[0], down_offsets, down)
        for copy in norm_copies + up_copies:
            copy.wait()
        up_rows = up[...].reshape(units, width)
        first = dot_last(norm[0], up_rows[:tile])
        for copy in cot_copies + down_copies:
            copy.wait()
        leaving = [copies.start(norm, norm_out), copies.start(cot, cot_out)]
        down_rows = down[...].reshape(width, units)
        for f in range(units // tile):
            lanes = slice(f * tile, (f + 1) * tile)
            total = jnp.zeros((1, tile), WIDE)
            for t in range(blocks):
                hidden = first if f == t == 0 else dot_last(norm[t], up_rows[lanes])
                hidden = hidden + bias_ref[:, lanes]
                grad = dot_plain(cot[t], down_rows[:, lanes])
                below = 0.5 * (1.0 + lax.erf(hidden * math.sqrt(0.5)))
                slope = below + hidden * (
                    jnp.exp(-0.5 * hidden * hidden) * (1.0 / math.sqrt(2.0 * math.pi))
                )
                act[t, :, lanes] = (hidden * below).astype(LOW)
                grad = (grad * slope).astype(LOW)
                hid[t, :, lanes] = grad
                total = total + jnp.sum(grad.astype(WIDE), axis=0, keepdims=True)
            sums[:, lanes] = total
        leaving += [copies.start(act, act_out), copies.start(hid, hid_out)]
        for t in range(blocks):
            back = dot_plain(hid[t], up_rows).astype(LOW)
            out = dot_last(act[t], down_rows).astype(LOW)
            if t < half:
                grad_kept[t] = back
                out_kept[t] = out
            else:
                grad_sent[t - half] = back
                out_sent[t - half] = out
        for copy in leaving:
            copy.wait()

    shape = jax.ShapeDtypeStruct
    part = shape((half, tokens, width), LOW)
    return pl.pallas_call(
        body,
        out_shape=[part] * 4
        + [shape((blocks, tokens, units), LOW)] * 2
        + [shape((blocks, tokens, width), LOW)] * 2
        + [shape((1, units), WIDE)],
        in_specs=[SMEM_SPACE, VMEM_SPACE] + [ANY_SPACE] * sum(counts),
        out_specs=[VMEM_SPACE] * 4 + [ANY_SPACE] * 4 + [VMEM_SPACE],
        scratch_shapes=[
            pltpu.VMEM((blocks, tokens, width), LOW),
            pltpu.VMEM((blocks, tokens, width), LOW),
            pltpu.VMEM((count_dp, piece, width), LOW),
            pltpu.VMEM((count_dp, shard, units), LOW),
            pltpu.VMEM((blocks, tokens, units), LOW),
            pltpu.VMEM((blocks, tokens, units), LOW),
            pltpu.SemaphoreType.DMA((2 * blocks + 2 * count_dp + 4,)),
        ],
        compiler_params=pltpu.CompilerParams(vmem_limit_bytes=LIMIT),
        cost_estimate=cost(17),
    )(row, bias, *normed_pieces, *cot_pieces, *up_pieces, *down_pieces)


def weight_grad_call(row, pairs, offset_lists):
    blocks, tokens, rows = pairs[0][0].shape
    width = pairs[0][1].shape[2]
    count_dp = len(offset_lists[0])
    quarter, share = count_dp // 4, rows // count_dp
    tile = 256 if rows % 256 == 0 else rows
    count = len(pairs)

    def body(row_ref, *refs):
        sources, targets = refs[: 2 * count], refs[2 * count : 6 * count]
        totals, sems = refs[6 * count : 7 * count], refs[7 * count]
        copies = Copies(sems)
        leaving = []
        for p in range(count):
            left_ref, right_ref, total = sources[2 * p], sources[2 * p + 1], totals[p]
            right_all = right_ref[...].reshape(blocks * tokens, width)
            for c in range(rows // tile):
                lanes = slice(c * tile, (c + 1) * tile)
                total[lanes] = dot_first(
                    left_ref[:, :, lanes].reshape(blocks * tokens, tile), right_all
                ).astype(LOW)
            for index, offset in enumerate(offset_lists[p]):
                begin = pl.multiple_of((row_ref[0] ^ offset) * share, share)
                target = targets[4 * p + index // quarter].at[index % quarter]
                leaving.append(copies.start(total.at[pl.ds(begin, share)], target))
        for copy in leaving:
            copy.wait()

    return pl.pallas_call(
        body,
        out_shape=[jax.ShapeDtypeStruct((quarter, share, width), LOW)] * (4 * count),
        in_specs=[SMEM_SPACE] + [VMEM_SPACE] * (2 * count),
        out_specs=[ANY_SPACE] * (4 * count),
        scratch_shapes=[pltpu.VMEM((rows, width), LOW)] * count
        + [pltpu.SemaphoreType.DMA((count * count_dp,))],
        compiler_params=pltpu.CompilerParams(vmem_limit_bytes=LIMIT),
        cost_estimate=cost(11),
    )(row, *(array for pair in pairs for array in pair))


def iota(shape, dim):
    return lax.broadcasted_iota(jnp.int32, shape, dim)


def eye_low(size):
    return jnp.where(iota((size, size), 0) == iota((size, size), 1), 1.0, 0.0).astype(LOW)


def turn(values):
    return values.astype(WIDE).T


def own_channel(index, place, blocks, share):
    return (index // share) * (share * blocks) + place * share + index % share


def first_call(places, blocks, share, w_in, w_out, inputs, rows, parts):
    width, shard = w_in.shape
    shard_out = w_out.shape[1]
    tokens = inputs.shape[0]
    here = shard // blocks
    size = here // parts
    channels = width // blocks

    def body(place_ref, w_ref, out_ref, in_ref, gain_ref, shift_ref, *refs):
        part_refs, (out_own, normed_ref, picked) = refs[:parts], refs[parts:]
        place = place_ref[1]
        shape = (here, shard)
        chosen = own_channel(iota(shape, 0), place, blocks, share) == iota(shape, 1)
        chosen = jnp.where(chosen, 1.0, 0.0).astype(LOW)
        turned = dot_last(chosen, w_ref[...]).astype(LOW)
        for i in range(parts):
            part_refs[i][0] = turned[i * size : (i + 1) * size]
        for j in range(channels // share):
            begin = pl.multiple_of(j * share * blocks + place * share, share)
            picked[j * share : (j + 1) * share] = out_ref[pl.ds(begin, share)]
        out_own[0] = turn(picked[...]).astype(LOW)
        normal, _ = norm_parts(in_ref[...].astype(WIDE))
        normed_ref[0] = (normal * gain_ref[...] + shift_ref[...]).astype(LOW)

    shape = jax.ShapeDtypeStruct
    return pl.pallas_call(
        body,
        out_shape=[shape((1, size, width), LOW)] * parts
        + [shape((1, shard_out, channels), LOW), shape((1, tokens, width), LOW)],
        in_specs=[SMEM_SPACE] + [VMEM_SPACE] * 5,
        out_specs=[VMEM_SPACE] * (parts + 2),
        scratch_shapes=[pltpu.VMEM((channels, shard_out), LOW)],
        compiler_params=pltpu.CompilerParams(vmem_limit_bytes=WHOLE),
        cost_estimate=cost(3),
    )(places, w_in, w_out, inputs, *rows)


def second_call(places, blocks, share, w_up, w_down, b_up, vectors, layers, third):
    width, shard_up = w_up.shape
    piece = shard_up // blocks
    hidden, shard_down = w_down.shape
    count_dp = hidden // shard_up
    channels = width // blocks
    arrays = [array for array, _ in vectors] + [third]
    spans = [rows for _, rows in vectors] + [third.shape[0]]
    used = sum(spans)
    total = -(-used // 8) * 8
    flat_layers = [array for layer in layers for array in layer]
    heights = [weights.shape[0] for weights, _ in layers]

    def body(place_ref, up_ref, down_ref, bias_ref, *refs):
        vec_refs, refs = refs[: len(arrays)], refs[len(arrays) :]
        layer_refs, refs = refs[: len(flat_layers)], refs[len(flat_layers) :]
        up_own, down_own, bias_own, vec_own = refs[:4]
        aug_refs, (up, down, held, sems) = refs[4 : 4 + len(layers)], refs[4 + len(layers) :]
        place = place_ref[1]
        copies = Copies(sems)
        begin = pl.multiple_of(place * piece, piece)
        waiting = [copies.start(up_ref.at[:, pl.ds(begin, piece)], up)]
        for k in range(count_dp):
            rows = pl.ds(pl.multiple_of(k * shard_up + place * piece, piece), piece)
            waiting.append(copies.start(down_ref.at[rows], down.at[pl.ds(k * piece, piece)]))
        for k in range(count_dp):
            lanes = pl.ds(pl.multiple_of(k * shard_up + place * piece, piece), piece)
            bias_own[:, k * piece : (k + 1) * piece] = bias_ref[:, lanes]
        held[used:, :] = jnp.zeros((total - used, width), WIDE)
        at = 0
        for (ref, span) in zip(vec_refs, spans):
            count = ref.shape[0]
            if ref.shape[1] == width:
                held[at : at + count, :] = ref[...]
            else:
                for i in range(count):
                    for j in range(span // count):
                        row = at + i * (span // count) + j
                        held[row : row + 1, :] = ref[i : i + 1, j * width : (j + 1) * width]
            at += span
        shape = (width, channels)
        chosen = iota(shape, 0) == own_channel(iota(shape, 1), place, blocks, share)
        vec_own[...] = dot_high(held[...], jnp.where(chosen, 1.0, 0.0))
        for i, height in enumerate(heights):
            weights, bias, target = layer_refs[2 * i], layer_refs[2 * i + 1], aug_refs[i]
            target[...] = jnp.zeros(target.shape, WIDE)
            target[:height, :] = weights[...]
            target[height : height + 1, :] = bias[...]
        for copy in waiting:
            copy.wait()
        up_own[0] = turn(up[...]).astype(LOW)
        down_own[0] = turn(down[...]).astype(LOW)

    shape = jax.ShapeDtypeStruct
    return pl.pallas_call(
        body,
        out_shape=[
            shape((1, piece, width), LOW),
            shape((1, shard_down, piece * count_dp), LOW),
            shape((1, piece * count_dp), WIDE),
            shape((total, channels), WIDE),
        ]
        + [shape((-(-(height + 1) // 8) * 8, layer[0].shape[1]), WIDE) for height, layer in zip(heights, layers)],
        in_specs=[SMEM_SPACE, ANY_SPACE, ANY_SPACE]
        + [VMEM_SPACE] * (1 + len(arrays) + len(flat_layers)),
        out_specs=[VMEM_SPACE] * (4 + len(layers)),
        scratch_shapes=[
            pltpu.VMEM((width, piece), LOW),
            pltpu.VMEM((piece * count_dp, shard_down), LOW),
            pltpu.VMEM((total, width), WIDE),
            pltpu.SemaphoreType.DMA((1 + count_dp,)),
        ],
        compiler_params=pltpu.CompilerParams(vmem_limit_bytes=LIMIT),
        cost_estimate=cost(4),
    )(places, w_up, w_down, b_up, *arrays, *flat_layers)


def spread_pieces(refs):
    return [ref.at[i] for ref in refs for i in range(ref.shape[0])]


def wide_call(places, offsets, pieces, piece, count_dp):
    total, width = pieces[0].shape[1:]
    shard = total - piece
    units = piece * count_dp
    blocks = len(offsets)

    def body(place_ref, *refs):
        sources = spread_pieces(refs[: len(pieces)])
        up_out, down_out = refs[len(pieces) :]
        for source, offset in zip(sources, offsets):
            place = place_ref[1] ^ offset
            up_out[:, pl.ds(pl.multiple_of(place * piece, piece), piece)] = turn(source[:piece])
            down = turn(source[piece:])
            for k in range(count_dp):
                rows = pl.ds(pl.multiple_of((k * blocks + place) * piece, piece), piece)
                down_out[rows] = down[k * piece : (k + 1) * piece]

    shape = jax.ShapeDtypeStruct
    return pl.pallas_call(
        body,
        out_shape=[
            shape((width, piece * blocks), WIDE),
            shape((units * blocks, shard), WIDE),
        ],
        in_specs=[SMEM_SPACE] + [VMEM_SPACE] * len(pieces),
        out_specs=[VMEM_SPACE] * 2,
        compiler_params=pltpu.CompilerParams(vmem_limit_bytes=LIMIT),
        cost_estimate=cost(8),
    )(places, *pieces)


def in_wide_call(places, offsets, share, pieces):
    here, width = pieces[0].shape[1:]
    blocks = len(offsets)
    shard = here * blocks

    def body(place_ref, *refs):
        out = refs[-1]
        total = None
        for index, ref in enumerate(spread_pieces(refs[:-1])):
            place = place_ref[1] ^ offsets[index]
            shape = (here, shard)
            chosen = own_channel(iota(shape, 0), place, blocks, share) == iota(shape, 1)
            chosen = jnp.where(chosen, 1.0, 0.0).astype(LOW)
            part = dot_first(ref[...], chosen)
            total = part if total is None else total + part
        out[...] = total

    return pl.pallas_call(
        body,
        out_shape=jax.ShapeDtypeStruct((width, shard), WIDE),
        in_specs=[SMEM_SPACE] + [VMEM_SPACE] * len(pieces),
        out_specs=VMEM_SPACE,
        compiler_params=pltpu.CompilerParams(vmem_limit_bytes=LIMIT),
        cost_estimate=cost(3),
    )(places, *pieces)


def out_wide_call(places, offsets, share, pieces):
    shard, channels = pieces[0].shape[1:]
    blocks = len(offsets)

    def body(place_ref, *refs):
        out = refs[-1]
        for index, ref in enumerate(spread_pieces(refs[:-1])):
            place = place_ref[1] ^ offsets[index]
            whole = turn(ref[...])
            for j in range(channels // share):
                rows = pl.ds(pl.multiple_of((j * blocks + place) * share, share), share)
                out[rows] = whole[j * share : (j + 1) * share]

    return pl.pallas_call(
        body,
        out_shape=jax.ShapeDtypeStruct((channels * blocks, shard), WIDE),
        in_specs=[SMEM_SPACE] + [VMEM_SPACE] * len(pieces),
        out_specs=VMEM_SPACE,
        compiler_params=pltpu.CompilerParams(vmem_limit_bytes=LIMIT),
        cost_estimate=cost(2),
    )(places, *pieces)


def small_pack_call(shared, layers, bias, sums, third, decay):
    channels = third.shape[1]
    width = shared[0].shape[1]
    cuts = width // channels
    arrays = list(shared) + list(layers) + [bias, sums, third, decay]
    rows = cuts * sum(array.shape[0] for array in shared)
    layer_rows = [-(-array.shape[0] // cuts // 8) * 8 for array in layers]
    bias_rows = bias.shape[1] // channels
    plain = rows + sum(layer_rows) + bias_rows + sums.shape[0] + third.shape[0] + 1
    total = -(-plain // 8) * 8

    def body(*refs):
        target = refs[-1]
        target[plain:, :] = jnp.zeros((total - plain, channels), WIDE)
        at = 0
        for ref in refs[: len(shared)]:
            for i in range(ref.shape[0]):
                for j in range(cuts):
                    target[at : at + 1, :] = ref[i : i + 1, j * channels : (j + 1) * channels]
                    at += 1
        for ref, height in zip(refs[len(shared) : len(shared) + len(layers)], layer_rows):
            lanes = ref.shape[1]
            target[at : at + height, :] = jnp.zeros((height, channels), WIDE)
            for j in range(cuts):
                size = min(height, ref.shape[0] - j * height)
                if size > 0:
                    target[at : at + size, j * lanes : (j + 1) * lanes] = ref[
                        j * height : j * height + size, :
                    ]
            at += height
        ref = refs[len(shared) + len(layers)]
        for j in range(bias_rows):
            target[at : at + 1, :] = ref[:, j * channels : (j + 1) * channels]
            at += 1
        for ref in refs[len(shared) + len(layers) + 1 : -1]:
            target[at : at + ref.shape[0], :] = ref[...]
            at += ref.shape[0]

    return pl.pallas_call(
        body,
        out_shape=jax.ShapeDtypeStruct((total, channels), WIDE),
        in_specs=[VMEM_SPACE] * len(arrays),
        out_specs=VMEM_SPACE,
        compiler_params=pltpu.CompilerParams(vmem_limit_bytes=LIMIT),
        cost_estimate=cost(2),
    )(*arrays)


def small_out_call(places, offsets, share, pieces, shared, layer_shapes, bias_width, shard_up):
    height, channels = pieces[0].shape[1:]
    blocks = len(offsets)
    width = channels * blocks
    piece = shard_up // blocks
    augmented = [-(-(shape[0] + 1) // 8) * 8 for shape in layer_shapes]
    layer_rows = [-(-rows // blocks // 8) * 8 for rows in augmented]
    bias_rows = bias_width // channels
    units = layer_shapes[1][1]

    def body(place_ref, *refs):
        sources = spread_pieces(refs[: len(pieces)])
        refs = refs[len(pieces) :]
        shared_refs, refs = refs[:shared], refs[shared:]
        layer_refs, refs = refs[: 2 * len(layer_shapes)], refs[2 * len(layer_shapes) :]
        bias_out, in_out, taps_out, short_out, direct_out, third_out, decay_out, held, placed = refs
        for source, offset in zip(sources, offsets):
            placed[place_ref[1] ^ offset] = source[...]
        total = placed[0]
        for i in range(1, blocks):
            total = total + placed[i]
        held[...] = total
        at = 0
        for ref in shared_refs:
            for j in range(blocks):
                ref[:, j * channels : (j + 1) * channels] = held[at : at + 1, :]
                at += 1
        for i, rows in enumerate(layer_rows):
            weights, bias = layer_refs[2 * i], layer_refs[2 * i + 1]
            lanes = weights.shape[1]
            for j in range(blocks):
                size = min(rows, weights.shape[0] - j * rows)
                if size > 0:
                    weights[j * rows : j * rows + size, :] = held[
                        at : at + size, j * lanes : (j + 1) * lanes
                    ]
                if 0 <= weights.shape[0] - j * rows < rows:
                    row = at + weights.shape[0] - j * rows
                    bias[...] = held[row : row + 1, j * lanes : (j + 1) * lanes]
            at += rows
        whole = None
        first = at
        for index, offset in enumerate(offsets):
            place = place_ref[1] ^ offset
            for j in range(bias_rows):
                line = sources[index][first + j : first + j + 1, :]
                for c in range(channels // piece):
                    k = j * (channels // piece) + c
                    lanes = pl.ds(pl.multiple_of((k * blocks + place) * piece, piece), piece)
                    bias_out[:, lanes] = line[:, c * piece : (c + 1) * piece]
            shape = (channels, width)
            chosen = own_channel(iota(shape, 0), place, blocks, share) == iota(shape, 1)
            part = dot_high(
                sources[index][first + bias_rows :, :], jnp.where(chosen, 1.0, 0.0)
            )
            whole = part if whole is None else whole + part
        for role in range(3):
            lanes = slice(role * width, (role + 1) * width)
            in_out[:, lanes] = whole[role : role + 1]
            for j in range(3):
                taps_out[j : j + 1, lanes] = whole[3 + 3 * j + role : 4 + 3 * j + role]
            short_out[:, lanes] = whole[12 + role : 13 + role]
        direct_out[...] = whole[15:16]
        third_out[...] = whole[16 : 16 + units]
        decay_out[...] = whole[16 + units : 17 + units]

    shape = jax.ShapeDtypeStruct
    layer_out = []
    for rows, lanes in layer_shapes:
        layer_out += [shape((rows, lanes), WIDE), shape((1, lanes), WIDE)]
    return pl.pallas_call(
        body,
        out_shape=[shape((1, width), WIDE)] * shared
        + layer_out
        + [
            shape((1, bias_width * blocks), WIDE),
            shape((1, 3 * width), WIDE),
            shape((3, 3 * width), WIDE),
            shape((1, 3 * width), WIDE),
            shape((1, width), WIDE),
            shape((units, width), WIDE),
            shape((1, width), WIDE),
        ],
        in_specs=[SMEM_SPACE] + [VMEM_SPACE] * len(pieces),
        out_specs=[VMEM_SPACE] * (shared + len(layer_out) + 7),
        scratch_shapes=[
            pltpu.VMEM((height, channels), WIDE),
            pltpu.VMEM((blocks, height, channels), WIDE),
        ],
        compiler_params=pltpu.CompilerParams(vmem_limit_bytes=LIMIT),
        cost_estimate=cost(5),
    )(places, *pieces)


def local_plain(
    block_in,
    doc_starts,
    norm1_gain,
    norm1_bias,
    w_in,
    b_in,
    short_taps,
    short_bias,
    filter_w1,
    filter_b1,
    filter_w2,
    filter_b2,
    filter_w3,
    filter_decay,
    conv_bias,
    w_out,
    b_out,
    norm2_gain,
    norm2_bias,
    w_up,
    b_up,
    w_down,
    b_down,
    cotangent,
):
    count_dp, blocks = lax.axis_size("dp"), lax.axis_size("block")
    grid = Grid(count_dp, blocks)
    row, place = grid.row, grid.place
    _, block_len, width = block_in.shape
    length = block_len * blocks
    hidden_width = w_up.shape[1] * count_dp
    hidden_here = hidden_width // blocks
    dp_steps = grid.dp_steps
    block_steps = grid.chip_steps + [grid.core_step]
    block_offsets = [b for _, b in offsets_of(block_steps)]

    def rotated(turn):
        turn = turn % len(dp_steps)
        return dp_steps[turn:] + dp_steps[:turn]

    def dp_offsets(steps):
        return [a for a, _ in offsets_of(steps)]

    shard_in, shard_out = w_in.shape[1], w_out.shape[1]
    group = math.gcd(width, shard_in)
    groups_here, share = shard_in // group, group // blocks
    channels = width // blocks
    bands = width // group
    vectors = jnp.concatenate(
        [
            b_in.reshape(3, width),
            short_taps.reshape(9, width),
            short_bias.reshape(3, width),
            filter_decay[None],
            conv_bias[None],
            filter_w3,
        ],
        axis=0,
    )
    vectors = lax.dynamic_index_in_dim(
        vectors.reshape(vectors.shape[0], bands, blocks, share), place, 2, keepdims=False
    ).reshape(vectors.shape[0], channels)
    b_in_here = vectors[:3].reshape(-1)
    taps = vectors[3:12].reshape(3, 3 * channels)
    short_shift = vectors[12:15].reshape(-1)
    decay_here, direct, third_here = vectors[15], vectors[16], vectors[17:]

    in_turned = w_in.T.reshape(groups_here, blocks, share, width)
    in_own = lax.dynamic_index_in_dim(in_turned, place, 1, keepdims=False)
    in_orders = [rotated(i) for i in range(groups_here)]
    in_rows = jnp.stack(
        [
            arrange(grid.gather(in_own[i], in_orders[i]), row, dp_offsets(in_orders[i]))
            for i in range(groups_here)
        ],
        axis=1,
    ).reshape(3 * channels, width)

    inputs = block_in.astype(WIDE).reshape(block_len, width)
    normed, norm1_back = jax.vjp(layer_norm, inputs, norm1_gain, norm1_bias)
    normed_low = normed.astype(LOW)
    normed_all = arrange(grid.gather(normed_low, block_steps), place, block_offsets).reshape(
        length, width
    )

    up_order, down_order, out_dp_order = rotated(1), rotated(2), rotated(0)
    piece = w_up.shape[1] // blocks
    up_own = lax.dynamic_slice_in_dim(w_up, place * piece, piece, 1).T
    up_rows = arrange(grid.gather(up_own, up_order), row, dp_offsets(up_order)).reshape(
        hidden_here, width
    )
    b_up_here = lax.dynamic_index_in_dim(
        b_up.reshape(count_dp, blocks, piece), place, 1, keepdims=False
    ).reshape(hidden_here)
    down_own = w_down.reshape(count_dp, blocks, piece, w_down.shape[1])
    down_own = lax.dynamic_index_in_dim(down_own, place, 1, keepdims=False)
    down_own = down_own.reshape(hidden_here, w_down.shape[1]).T
    down_rows = arrange(grid.gather(down_own, down_order), row, dp_offsets(down_order)).reshape(
        width, hidden_here
    )

    out_own = w_out.reshape(bands, blocks, share, shard_out)
    out_own = lax.dynamic_index_in_dim(out_own, place, 1, keepdims=False)
    out_own = out_own.reshape(channels, shard_out).T
    out_dealt = arrange(grid.gather(out_own, out_dp_order), row, dp_offsets(out_dp_order))
    out_rows = jnp.concatenate(grid.gather(out_dealt.reshape(width, channels), block_steps), axis=0)
    cot_flat = cotangent.reshape(block_len, width)
    cot_all = jnp.concatenate(grid.gather(cot_flat, block_steps), axis=0).reshape(length, width)

    forward_table, inverse_table, sign, edge = transform_tables(block_len)
    starts = doc_starts[0]
    positions = jnp.arange(length, dtype=jnp.int32)
    segment = jnp.sum((starts[None, :] <= positions[:, None]).astype(jnp.int32), axis=-1) - 1
    keep_one = jnp.concatenate([jnp.zeros((1,), WIDE), (segment[1:] == segment[:-1]).astype(WIDE)])
    keep_two = jnp.concatenate([jnp.zeros((2,), WIDE), (segment[2:] == segment[:-2]).astype(WIDE)])
    keep_one, keep_two = keep_one[:, None], keep_two[:, None]
    num_docs = doc_starts.shape[1]
    long_doc = jnp.sum((starts <= block_len).astype(jnp.int32)) - 1
    long_mask = (segment == long_doc).astype(WIDE)[:, None]
    first_segment, last_segment = segment[:block_len], segment[length - block_len :]
    short_early, short_masks = [], []
    for number in range(num_docs - 1):
        early = number < long_doc
        doc = jnp.where(early, number, number + 1)
        where = jnp.where(early, first_segment, last_segment)
        short_early.append(early.astype(WIDE))
        short_masks.append((where == doc).astype(WIDE)[:, None])

    def spread(values):
        masked = values * long_mask
        parts = [masked[i * block_len : (i + 1) * block_len] for i in range(blocks)]
        first, last = values[:block_len], values[length - block_len :]
        for early, mask in zip(short_early, short_masks):
            parts.append(mask * (early * first + (1.0 - early) * last))
        return jnp.concatenate(parts, axis=1)

    def collect(values):
        parts = [
            values[:, i * channels : (i + 1) * channels] for i in range(blocks + num_docs - 1)
        ]
        first, last = jnp.zeros_like(parts[0]), jnp.zeros_like(parts[0])
        for early, mask, part in zip(short_early, short_masks, parts[blocks:]):
            first = first + early * mask * part
            last = last + (1.0 - early) * mask * part
        joined = jnp.concatenate(parts[:blocks], axis=0) * long_mask
        middle = jnp.zeros((length - 2 * block_len, channels), WIDE)
        return joined + jnp.concatenate([first, middle, last], axis=0)

    def cut(values, count):
        return [values[:, i * channels : (i + 1) * channels] for i in range(count)]

    table, times = position_table(length, filter_w1.shape[0])

    def filter_spectra(params):
        first = jnp.sin(dot_high(table, params[0]) + params[1])
        second = jnp.sin(dot_high(first, params[2]) + params[3])
        kernel = dot_high(second, params[4]) * (
            jnp.exp(-times[:, None] * params[5][None, :]) + MOD_SHIFT
        )
        pieces = jnp.concatenate(
            [kernel[i * block_len : (i + 1) * block_len] for i in range(blocks)], axis=1
        )
        halves = dot_near(forward_table, pieces)
        earlier = jnp.concatenate(
            [jnp.zeros((2 * block_len, channels), WIDE), halves[:, : (blocks - 1) * channels]],
            axis=1,
        )
        return earlier + sign[:, None] * halves

    spectra_flat, filter_back = jax.vjp(
        filter_spectra,
        (filter_w1, filter_b1, filter_w2, filter_b2, third_here, decay_here),
    )
    spectra = cut(spectra_flat, blocks)

    proj = dot_last(normed_all, in_rows) + b_in_here
    three = 3 * channels
    prev_one = jnp.concatenate([jnp.zeros((1, three), WIDE), proj[:-1]], axis=0) * keep_one
    prev_two = jnp.concatenate([jnp.zeros((2, three), WIDE), proj[:-2]], axis=0) * keep_two
    short = short_shift + taps[0] * proj + taps[1] * prev_one + taps[2] * prev_two
    gate_part, mult, value = cut(short, 3)
    inner = value * mult

    entries = cut(dot_near(forward_table, spread(inner)), blocks + num_docs - 1)
    totals = []
    for i in range(blocks):
        total = spectral_product(entries[i], spectra[0], edge)
        for j in range(i):
            total = total + spectral_product(entries[j], spectra[i - j], edge)
        totals.append(total)
    for entry in entries[blocks:]:
        totals.append(spectral_product(entry, spectra[0], edge))
    mixed = collect(dot_near(inverse_table, jnp.concatenate(totals, axis=1))) + direct * inner
    gated_low = (gate_part * mixed).astype(LOW)

    gated_parts = []
    for offset in block_offsets:
        part = lax.dynamic_slice_in_dim(gated_low, (place ^ offset) * block_len, block_len, 0)
        gated_parts.append(grid.swap(part, (0, offset)) if offset else part)
    branch = b_out
    for part, rows in zip(gated_parts, out_rows):
        branch = branch + dot_last(part, rows)
    resid = inputs + branch
    normed2, norm2_back = jax.vjp(layer_norm, resid, norm2_gain, norm2_bias)
    normed2_low = normed2.astype(LOW)

    normed2_all = jnp.concatenate(grid.gather(normed2_low, block_steps), axis=0)
    normed2_all = normed2_all.reshape(length, width)
    hidden = dot_last(normed2_all, up_rows) + b_up_here
    act, gelu_back = jax.vjp(exact_gelu, hidden)
    act_low = act.astype(LOW)
    grad_act = dot_plain(cot_all, down_rows)
    grad_hidden = gelu_back(grad_act)[0].astype(LOW)

    def to_tokens(partial):
        split = partial.astype(LOW).reshape(blocks, block_len, width)
        return grid.scatter(split[: blocks // 2], split[blocks // 2 :], block_steps).astype(WIDE)

    grad_normed2 = to_tokens(dot_plain(grad_hidden, up_rows))
    output = resid + to_tokens(dot_last(act_low, down_rows)) + b_down
    block_out = output.astype(LOW)[None]
    grad_b_up_here = jnp.sum(grad_hidden.astype(WIDE), axis=0)
    grad_b_down = jnp.sum(cot_flat.astype(WIDE), axis=0)

    def send_home(natural, order):
        natural = natural.astype(LOW).reshape(count_dp, -1, natural.shape[-1])
        return grid.scatter(*deal(natural, row, dp_offsets(order)), order)

    up_grad = send_home(dot_first(grad_hidden, normed2_all), up_order)
    down_grad = send_home(dot_first(cot_all, act_low), down_order)

    resid_part, grad_gain_two, grad_bias_two = norm2_back(grad_normed2)
    grad_resid = cot_flat.astype(WIDE) + resid_part
    grad_branch = grad_resid.astype(LOW)
    grad_b_out = jnp.sum(grad_branch.astype(WIDE), axis=0)
    grad_parts = []
    for index, offset in enumerate(block_offsets):
        part = dot_plain(grad_branch, out_rows[index]).astype(LOW)
        grad_parts.append((grid.swap(part, (0, offset)) if offset else part)[None])
    grad_gated = arrange(grad_parts, place, block_offsets).reshape(length, channels).astype(WIDE)
    out_sums = jnp.stack([dot_first(grad_branch, part).astype(LOW) for part in gated_parts], axis=0)
    out_sums = grid.scatter(out_sums[: blocks // 2], out_sums[blocks // 2 :], block_steps)
    out_grad = send_home(out_sums, out_dp_order)

    grad_gate_part = grad_gated * mixed
    grad_mixed = grad_gated * gate_part
    grad_conv_bias = jnp.sum(grad_mixed * inner, axis=0)
    grad_totals = cut(
        lax.dot_general(
            inverse_table,
            spread(grad_mixed),
            (((0,), (0,)), ((), ())),
            precision=HIGH,
            preferred_element_type=WIDE,
        ),
        blocks + num_docs - 1,
    )
    grad_entries = []
    grad_lags = [None] * blocks
    for i in range(blocks + num_docs - 1):
        lag = spectral_back(grad_totals[i], entries[i], edge)
        grad_lags[0] = lag if grad_lags[0] is None else grad_lags[0] + lag
        grad_entries.append(spectral_back(grad_totals[i], spectra[0], edge))
    for j in range(blocks):
        for i in range(j + 1, blocks):
            grad_entries[j] = grad_entries[j] + spectral_back(
                grad_totals[i], spectra[i - j], edge
            )
            lag = spectral_back(grad_totals[i], entries[j], edge)
            grad_lags[i - j] = lag if grad_lags[i - j] is None else grad_lags[i - j] + lag
    filter_grads = filter_back(jnp.concatenate(grad_lags, axis=1))[0]
    grad_inner = (
        collect(
            lax.dot_general(
                forward_table,
                jnp.concatenate(grad_entries, axis=1),
                (((0,), (0,)), ((), ())),
                precision=HIGH,
                preferred_element_type=WIDE,
            )
        )
        + direct * grad_mixed
    )
    grad_short = jnp.concatenate([grad_gate_part, grad_inner * value, grad_inner * mult], axis=1)
    grad_taps = jnp.stack(
        [
            jnp.sum(grad_short * proj, axis=0),
            jnp.sum(grad_short * prev_one, axis=0),
            jnp.sum(grad_short * prev_two, axis=0),
        ],
        axis=0,
    )
    grad_short_bias = jnp.sum(grad_short, axis=0)
    pass_one = grad_short * keep_one
    pass_two = grad_short * keep_two
    grad_proj = (
        taps[0] * grad_short
        + taps[1] * jnp.concatenate([pass_one[1:], jnp.zeros((1, three), WIDE)], axis=0)
        + taps[2] * jnp.concatenate([pass_two[2:], jnp.zeros((2, three), WIDE)], axis=0)
    )
    grad_proj_low = grad_proj.astype(LOW)
    grad_b_in = jnp.sum(grad_proj_low.astype(WIDE), axis=0)
    grad_in_rows = dot_first(grad_proj_low, normed_all)
    grad_in_split = grad_in_rows.reshape(count_dp, groups_here, share, width)
    in_grads = [send_home(grad_in_split[:, i], in_orders[i]) for i in range(groups_here)]
    grad_normed_part = dot_plain(grad_proj_low, in_rows).astype(LOW)
    grad_normed = grid.scatter(
        *deal(grad_normed_part.reshape(blocks, block_len, width), place, block_offsets), block_steps
    ).astype(WIDE)
    input_part, grad_gain_one, grad_bias_one = norm1_back(grad_normed)
    grad_input = (grad_resid + input_part)[None]

    def all_places(value):
        return arrange(grid.gather(value, block_steps), place, block_offsets)

    in_whole = all_places(jnp.concatenate(in_grads, axis=0))
    in_whole = in_whole.reshape(blocks, groups_here, share, width)
    in_whole = in_whole.transpose(3, 1, 0, 2).reshape(width, shard_in).astype(WIDE)
    if up_grad.shape[1] == down_grad.shape[1]:
        ff_whole = all_places(jnp.concatenate([up_grad, down_grad], axis=0))
        up_whole, down_whole = ff_whole[:, :piece], ff_whole[:, piece:]
    else:
        up_whole, down_whole = all_places(up_grad), all_places(down_grad)
    up_whole = up_whole.reshape(blocks * piece, width).T.astype(WIDE)
    down_whole = down_whole.reshape(blocks, w_down.shape[1], count_dp, piece)
    down_whole = down_whole.transpose(2, 0, 3, 1).reshape(hidden_width, w_down.shape[1])
    down_whole = down_whole.astype(WIDE)
    out_whole = all_places(out_grad).reshape(blocks, shard_out, bands, share)
    out_whole = out_whole.transpose(2, 0, 3, 1).reshape(width, shard_out).astype(WIDE)

    shared = [
        grad_gain_one,
        grad_bias_one,
        grad_b_out,
        grad_gain_two,
        grad_bias_two,
        grad_b_down,
        filter_grads[0],
        filter_grads[1],
        filter_grads[2],
        filter_grads[3],
    ]
    flat = jnp.concatenate([item.reshape(-1) for item in shared])
    unit = blocks * channels
    chunk = -(-flat.shape[0] // unit)
    flat = jnp.pad(flat, (0, chunk * unit - flat.shape[0])).reshape(blocks, chunk, channels)
    dealt = [lax.dynamic_slice_in_dim(flat, place ^ offset, 1, 0) for offset in block_offsets]
    half = blocks // 2
    shared_part = grid.scatter(
        jnp.concatenate(dealt[:half], axis=0), jnp.concatenate(dealt[half:], axis=0), block_steps
    )
    joined = jnp.concatenate(
        [
            shared_part,
            jnp.pad(grad_b_up_here, (0, -hidden_here % channels)).reshape(-1, channels),
            grad_b_in.reshape(3, channels),
            grad_taps.reshape(9, channels),
            grad_short_bias.reshape(3, channels),
            filter_grads[5][None],
            grad_conv_bias[None],
            filter_grads[4],
        ],
        axis=0,
    )
    for step in dp_steps:
        joined = joined + grid.swap(joined, step)
    every = all_places(joined)
    whole_flat = every[:, :chunk].reshape(-1)
    shared_out, at = [], 0
    for item in shared:
        shared_out.append(whole_flat[at : at + item.size].reshape(item.shape))
        at += item.size
    at = chunk + -(-hidden_here // channels)
    grad_b_up = every[:, chunk:at].reshape(blocks, -1)[:, :hidden_here]
    grad_b_up = grad_b_up.reshape(blocks, count_dp, piece)
    grad_b_up = grad_b_up.transpose(1, 0, 2).reshape(hidden_width)
    rest = every[:, at:].reshape(blocks, -1, bands, share).transpose(1, 2, 0, 3)
    rest = rest.reshape(-1, width)
    return (
        block_out,
        grad_input,
        shared_out[0],
        shared_out[1],
        in_whole,
        rest[:3].reshape(3 * width),
        rest[3:12].reshape(3, 3 * width),
        rest[12:15].reshape(3 * width),
        shared_out[6],
        shared_out[7],
        shared_out[8],
        shared_out[9],
        rest[17:],
        rest[15],
        rest[16],
        out_whole,
        shared_out[2],
        shared_out[3],
        shared_out[4],
        up_whole,
        grad_b_up,
        down_whole,
        shared_out[5],
    )


def input_back_call(inputs, kept, arrived, gain, grad_resid):
    tokens, width = inputs.shape

    def body(in_ref, kept_ref, arrived_ref, gain_ref, resid_ref, out_ref):
        grad = kept_ref[...].astype(WIDE) + arrived_ref[...].astype(WIDE)
        normal, scale = norm_parts(in_ref[...].astype(WIDE))
        scaled = grad * gain_ref[...]
        back = scaled - jnp.mean(scaled, axis=-1, keepdims=True)
        back = back - normal * jnp.mean(scaled * normal, axis=-1, keepdims=True)
        out_ref[...] = resid_ref[...] + back * scale

    return pl.pallas_call(
        body,
        out_shape=jax.ShapeDtypeStruct((tokens, width), WIDE),
        in_specs=[VMEM_SPACE] * 5,
        out_specs=VMEM_SPACE,
        compiler_params=pltpu.CompilerParams(vmem_limit_bytes=LIMIT),
        cost_estimate=cost(4),
    )(inputs, kept, arrived, gain, grad_resid)


def mark_call(value):
    def body(in_ref, out_ref):
        out_ref[...] = in_ref[...]

    return pl.pallas_call(
        body,
        out_shape=jax.ShapeDtypeStruct(value.shape, value.dtype),
        in_specs=[VMEM_SPACE],
        out_specs=VMEM_SPACE,
        cost_estimate=cost(15),
    )(value)


def after(value, *others):
    return lax.optimization_barrier((value, *others))[0]


def together(values, *others):
    return lax.optimization_barrier((*values, *others))[: len(values)]


def local_kernels(
    block_in,
    doc_starts,
    norm1_gain,
    norm1_bias,
    w_in,
    b_in,
    short_taps,
    short_bias,
    filter_w1,
    filter_b1,
    filter_w2,
    filter_b2,
    filter_w3,
    filter_decay,
    conv_bias,
    w_out,
    b_out,
    norm2_gain,
    norm2_bias,
    w_up,
    b_up,
    w_down,
    b_down,
    cotangent,
):
    count_dp, blocks = lax.axis_size("dp"), lax.axis_size("block")
    grid = Grid(count_dp, blocks)
    row, place = grid.row, grid.place
    places = jnp.stack([row, place]).astype(jnp.int32)
    _, block_len, width = block_in.shape
    dp_steps = grid.dp_steps
    block_steps = grid.chip_steps + [grid.core_step]
    block_offsets = [b for _, b in offsets_of(block_steps)]
    shard_in = w_in.shape[1]
    share = math.gcd(width, shard_in) // blocks
    shard_up = w_up.shape[1]
    starts = doc_starts[0]
    inputs = block_in.reshape(block_len, width)
    cot = cotangent.reshape(block_len, width)
    forward_table, inverse_table, _, _ = transform_tables(block_len)
    forward_three, inverse_three = triple(forward_table), triple(inverse_table)
    forward_back, inverse_back = triple(forward_table.T), triple(inverse_table.T)
    table = turned_table(position_table(block_len * blocks, filter_w1.shape[0])[0])
    third_at = 17

    order_one = dp_steps[::-1]
    order_two = order_one[:-2] + order_one[:-3:-1]
    core_step = grid.core_step

    def dp_offsets(steps):
        return [a for a, _ in offsets_of(steps)]

    parts = 2
    in_orders = [order_one, order_two]
    in_offsets = [dp_offsets(order) for order in in_orders]
    up_order, down_order, out_order = order_one, order_two, order_one
    up_offsets, down_offsets, out_offsets = map(dp_offsets, (up_order, down_order, out_order))
    core, chip = core_step, block_steps[0]

    def joined(pieces):
        return jnp.concatenate(pieces, axis=0)

    def split(values, *counts):
        parts, at = [], 0
        for count in counts:
            parts.append(list(values[at : at + count]))
            at += count
        return parts

    *in_own, out_own, normed_own = first_call(
        places,
        blocks,
        share,
        w_in,
        w_out,
        inputs,
        (norm1_gain[None], norm1_bias[None]),
        parts,
    )
    in_got = [grid.swap(own, order[0]) for own, order in zip(in_own, in_orders)]
    normed_got = grid.swap(normed_own, chip)
    out_got = grid.swap(out_own, out_order[0])
    second = second_call(
        after(places, normed_own),
        blocks,
        share,
        w_up,
        w_down,
        b_up[None],
        [
            (b_in[None], 3),
            (short_taps, 9),
            (short_bias[None], 3),
            (filter_decay[None], 1),
            (conv_bias[None], 1),
        ],
        [(filter_w1, filter_b1[None]), (filter_w2, filter_b2[None])],
        filter_w3,
    )

    in_got, (out_got,), second = split(together((*in_got, out_got, *second)), parts, 1, 6)
    up_own, down_own, b_up_own, vectors, layer_one, layer_two = second
    in_held = [joined(pair) for pair in zip(in_own, in_got)]
    out_held = joined((out_own, out_got))
    in_got = [grid.swap(held, order[1]) for held, order in zip(in_held, in_orders)]
    out_got = grid.swap(out_held, out_order[1])
    up_got = grid.swap(up_own, up_order[0])
    spectra, layer_one = filter_call(
        block_len, blocks, table, forward_three, layer_one, layer_two, vectors, third_at
    )

    in_got, rest = split(
        together((*in_got, out_got, up_got, normed_got, layer_one, layer_two, down_own)), parts, 6
    )
    out_got, up_got, normed_got, layer_one, layer_two, down_own = rest
    in_last = [joined(pair) for pair in zip(in_held, in_got)]
    out_held = joined((out_held, out_got))
    up_held = joined((up_own, up_got))
    normed_held = joined((normed_own, normed_got))
    in_last_got = [grid.swap(held, order[2]) for held, order in zip(in_last, in_orders)]
    normed_last = grid.swap(normed_held, core)
    out_got = grid.swap(out_held, out_order[2])
    down_got = grid.swap(down_own, down_order[0])
    cot_own = after(cot, normed_got)[None]
    cot_got = grid.swap(cot_own, chip)
    layer_two = mark_call(layer_two)

    in_last_got, rest = split(
        together((*in_last_got, out_got, down_got, normed_last, cot_got, layer_two)), parts, 5
    )
    out_got, down_got, normed_last, cot_got, layer_two = rest
    down_held = joined((down_own, down_got))
    out_whole = joined((out_held, out_got))[None]
    cot_held = joined((cot_own, cot_got))
    up_two = grid.swap(up_held, up_order[1])
    down_two = grid.swap(down_held, down_order[1])
    out_got = grid.swap(out_whole, chip)
    cot_last = grid.swap(cot_held, core)
    made = conv_call(
        block_len,
        blocks,
        places,
        starts,
        [normed_held, normed_last],
        [list(pair) for pair in zip(in_last, in_last_got)],
        in_offsets,
        block_offsets,
        vectors,
        spectra,
        forward_three,
        inverse_three,
    )

    gated_own, (proj, entries, mixed, in_rows, normed) = made[:blocks], made[blocks:]
    gated_own, (up_two, down_two, out_got, cot_last, layer_two) = split(
        together((*gated_own, up_two, down_two, out_got, cot_last, layer_two)), blocks, 5
    )
    gated_got = [
        grid.swap(part, (0, offset)) for part, offset in zip(gated_own[1:], block_offsets[1:])
    ]
    out_held = joined((out_whole, out_got))
    out_last = grid.swap(out_held, core)
    up_three = grid.swap(up_held, up_order[2])
    down_three = grid.swap(down_held, down_order[2])
    layer_two = mark_call(layer_two)

    gated_got, (out_last, layer_two) = split(
        together((*gated_got, out_last, layer_two)), blocks - 1, 2
    )
    gated_parts = [gated_own[0], *gated_got]
    out_pieces = [out_held, out_last]
    resid, normed2 = branch_call(
        places,
        inputs,
        gated_parts,
        out_pieces,
        out_offsets,
        (b_out[None], norm2_gain[None], norm2_bias[None]),
    )
    normed2, up_three, down_three = together((normed2, up_three, down_three))
    normed2_got = grid.swap(normed2[None], chip)
    up_four = grid.swap(up_two, up_order[2])
    down_four = grid.swap(down_two, down_order[2])

    normed2_got, up_four, down_four = together((normed2_got, up_four, down_four))
    normed2_held = joined((normed2[None], normed2_got))
    normed2_last = grid.swap(normed2_held, core)
    made = forward_call(
        places,
        [normed2_held, normed2_last],
        [cot_held, cot_last],
        [up_held, up_two, up_three, up_four],
        [down_held, down_two, down_three, down_four],
        up_offsets,
        down_offsets,
        b_up_own,
    )
    block_kept, block_sent, grad_kept, grad_sent = made[:4]
    act, grad_hidden, normed2_all, cot_all, b_up_sum = made[4:]

    grad_got = grid.swap(grad_sent, core)
    block_got = grid.swap(block_sent, core)

    grad_kept, grad_sent = halves(grad_kept, grad_got)
    grad_got = grid.swap(grad_sent, chip)
    dealt = weight_grad_call(
        after(places, grad_kept),
        [(grad_hidden, normed2_all), (cot_all, act)],
        [up_offsets, down_offsets],
    )

    up_dealt, down_dealt = split(dealt, 4, 4)
    up_got = grid.swap(up_dealt[3], up_order[2])
    down_got = grid.swap(down_dealt[3], down_order[2])

    grad_got, block_got, *dealt = together(
        (grad_got, block_got, *up_dealt[:3], *down_dealt[:3])
    )
    up_dealt, down_dealt = split(dealt, 3, 3)
    made = branch_back_call(
        places, resid, grad_kept[0], grad_got[0], cot, out_pieces, out_offsets, norm2_gain[None]
    )
    grad_resid, grad_branch, norm2_sums = made[blocks:]
    made, (up_got, down_got, grad_branch) = split(
        together((*made[:blocks], up_got, down_got, grad_branch)), blocks, 3
    )
    grad_own = made[0]
    grad_got = [
        grid.swap(part, (0, offset)) for part, offset in zip(made[1:], block_offsets[1:])
    ]
    up_high = add_low(up_dealt[1], up_got)
    down_high = add_low(down_dealt[1], down_got)
    out_kept, out_sent = out_grad_call(places, grad_branch, gated_parts, out_offsets)

    grad_got, rest = split(
        together((*grad_got, out_kept, out_sent, block_kept, up_high, down_high)), blocks - 1, 5
    )
    out_kept, out_sent, block_kept, up_high, down_high = rest
    grad_parts = [grad_own, *grad_got]
    up_got = grid.swap(up_dealt[2], up_order[2])
    down_got = grid.swap(down_dealt[2], down_order[2])
    out_got = grid.swap(out_sent, core)
    block_kept, block_sent = halves(block_kept, block_got)
    block_got = grid.swap(block_sent, chip)
    grad_lags, direct_sum, grad_short = back_call(
        block_len,
        blocks,
        places,
        starts,
        grad_parts,
        block_offsets,
        vectors,
        spectra,
        proj,
        entries,
        mixed,
        inverse_back,
        forward_back,
    )

    up_got, down_got, out_got, block_got, direct_sum = together(
        (up_got, down_got, out_got, block_got, direct_sum)
    )
    up_low = add_low(up_dealt[0], up_got)
    down_low = add_low(down_dealt[0], down_got)
    out_kept, out_sent = halves(out_kept, out_got)
    up_got = grid.swap(up_high, up_order[1])
    down_got = grid.swap(down_high, down_order[1])
    out_got = grid.swap(out_sent, chip)
    made = project_back_call(
        block_len,
        blocks,
        places,
        starts,
        in_offsets,
        block_offsets,
        vectors,
        (norm1_gain[None], norm1_bias[None]),
        direct_sum,
        grad_short,
        proj,
        in_rows,
        normed,
    )

    made, (up_got, down_got, out_got, layer_one) = split(
        together((*made, up_got, down_got, out_got, layer_one)), len(made), 4
    )
    in_dealt = [(made[2 * i], made[2 * i + 1]) for i in range(parts)]
    normed_kept, normed_sent, sums, norm1_sums = made[2 * parts :]
    up_kept, up_sent = halves(up_low, up_got)
    down_kept, down_sent = halves(down_low, down_got)
    out_kept, out_sent = halves(out_kept, out_got)
    in_got = [grid.swap(pair[1], order[2]) for pair, order in zip(in_dealt, in_orders)]
    normed_got = grid.swap(normed_sent, core)
    up_got = grid.swap(up_sent, up_order[0])
    out_got = grid.swap(out_sent, out_order[2])
    layer_one_grad, layer_two_grad, third_grad, decay_grad = filter_back_call(
        block_len, blocks, table, forward_back, layer_one, layer_two, vectors, third_at, grad_lags
    )
    small = small_pack_call(
        [norm2_sums, norm1_sums],
        [layer_one_grad, layer_two_grad],
        b_up_sum,
        sums,
        third_grad,
        decay_grad,
    )

    in_got, (normed_got, up_got, out_got, small) = split(
        together((*in_got, normed_got, up_got, out_got, small)), parts, 4
    )
    in_half = [halves(pair[0], got) for pair, got in zip(in_dealt, in_got)]
    normed_kept, normed_sent = halves(normed_kept, normed_got)
    out_kept, out_sent = halves(out_kept, out_got)
    in_got = [grid.swap(pair[1], order[1]) for pair, order in zip(in_half, in_orders)]
    normed_got = grid.swap(normed_sent, chip)
    small_got = grid.swap(small, dp_steps[0])
    out_got = grid.swap(out_sent, out_order[1])
    down_got = grid.swap(down_sent, down_order[0])
    up_grad = add_low(up_kept, up_got)

    in_got, (normed_got, small_got, out_got, down_got) = split(
        together((*in_got, normed_got, small_got, out_got, down_got)), parts, 4
    )
    ff_own = jnp.concatenate([up_grad, add_low(down_kept, down_got)], axis=1)
    in_half = [halves(pair[0], got) for pair, got in zip(in_half, in_got)]
    out_kept, out_sent = halves(out_kept, out_got)
    small = small + small_got
    in_got = [grid.swap(pair[1], order[0]) for pair, order in zip(in_half, in_orders)]
    small_got = grid.swap(small, dp_steps[1])
    ff_got = grid.swap(ff_own, chip)
    out_got = grid.swap(out_sent, out_order[0])
    grad_input = input_back_call(
        inputs, normed_kept[0], normed_got[0], norm1_gain[None], grad_resid
    )[None]

    in_got, (small_got, ff_got, out_got, grad_input) = split(
        together((*in_got, small_got, ff_got, out_got, grad_input)), parts, 4
    )
    in_grad = jnp.concatenate(
        [add_low(pair[0], got) for pair, got in zip(in_half, in_got)], axis=1
    )
    out_grad = add_low(out_kept, out_got)
    small = small + small_got
    ff_held = joined((ff_own, ff_got))
    ff_last = grid.swap(ff_held, core)
    in_got = grid.swap(in_grad, chip)
    out_got = grid.swap(out_grad, chip)
    small_got = grid.swap(small, dp_steps[2])
    output = resid + block_kept[0].astype(WIDE) + block_got[0].astype(WIDE) + b_down
    block_out = output.astype(LOW)[None]

    ff_last, in_got, out_got, small_got, block_out = together(
        (ff_last, in_got, out_got, small_got, block_out)
    )
    in_held, out_held = joined((in_grad, in_got)), joined((out_grad, out_got))
    small = (small + small_got)[None]
    small_got = grid.swap(small, chip)
    in_last = grid.swap(in_held, core)
    out_last = grid.swap(out_held, core)
    up_whole, down_whole = wide_call(
        places, block_offsets, [ff_held, ff_last], up_own.shape[1], count_dp
    )

    small_got, in_last, out_last, up_whole = together((small_got, in_last, out_last, up_whole))
    small_held = joined((small, small_got))
    small_last = grid.swap(small_held, core)
    in_whole = in_wide_call(places, block_offsets, share, [in_held, in_last])
    out_whole = out_wide_call(places, block_offsets, share, [out_held, out_last])
    small_pieces = [small_held, small_last]
    (
        grad_b_out,
        grad_gain_two,
        grad_bias_two,
        grad_b_down,
        grad_gain_one,
        grad_bias_one,
        grad_w1,
        grad_b1,
        grad_w2,
        grad_b2,
        grad_b_up,
        grad_b_in,
        grad_taps,
        grad_short,
        grad_direct,
        grad_w3,
        grad_decay,
    ) = small_out_call(
        places,
        block_offsets,
        share,
        small_pieces,
        norm2_sums.shape[0] + norm1_sums.shape[0],
        [filter_w1.shape, filter_w2.shape],
        b_up_sum.shape[1],
        shard_up,
    )
    return (
        block_out,
        grad_input,
        grad_gain_one[0],
        grad_bias_one[0],
        in_whole,
        grad_b_in[0],
        grad_taps,
        grad_short[0],
        grad_w1,
        grad_b1[0],
        grad_w2,
        grad_b2[0],
        grad_w3,
        grad_decay[0],
        grad_direct[0],
        out_whole,
        grad_b_out[0],
        grad_gain_two[0],
        grad_bias_two[0],
        up_whole,
        grad_b_up[0],
        down_whole,
        grad_b_down[0],
    )


def local(*args):
    blocks, width, shard_in = lax.axis_size("block"), args[0].shape[2], args[4].shape[1]
    channels, group = width // blocks, math.gcd(width, shard_in)
    fits = (
        channels % 128 == 0
        and group // blocks % 32 == 0
        and shard_in // blocks % 32 == 0
        and args[19].shape[1] // blocks % 128 == 0
        and args[15].shape[1] % 128 == 0
        and args[10].shape[1] * blocks == channels
        and lax.axis_size("dp") > 1
    )
    return (local_kernels if fits else local_plain)(*args)


def solution(mesh):
    placed = (
        P("dp", "block", None),
        P("dp", None),
        P(),
        P(),
        P(None, "dp"),
        P(),
        P(),
        P(),
        P(),
        P(),
        P(),
        P(),
        P(),
        P(),
        P(),
        P(None, "dp"),
        P(),
        P(),
        P(),
        P(None, "dp"),
        P(),
        P(None, "dp"),
        P(),
        P("dp", "block", None),
    )
    return jax.shard_map(
        local,
        mesh=mesh,
        in_specs=placed,
        out_specs=(
            P("dp", "block", None),
            P("dp", "block", None),
            P(),
            P(),
            P(None, "dp"),
            P(),
            P(),
            P(),
            P(),
            P(),
            P(),
            P(),
            P(),
            P(),
            P(),
            P(None, "dp"),
            P(),
            P(),
            P(),
            P(None, "dp"),
            P(),
            P(None, "dp"),
            P(),
        ),
        check_vma=False,
    )
```

```python
import math

import jax
import jax.numpy as jnp
import ml_dtypes
import numpy as np
from jax import lax
from jax.experimental import pallas as pl
from jax.experimental.pallas import tpu as pltpu
from jax.sharding import PartitionSpec as P

EPSILON = 1e-05
MOD_SHIFT = 0.05
HIGHEST = lax.Precision.HIGHEST
HIGH = lax.Precision.HIGH
LOW = jnp.bfloat16
WIDE = jnp.float32


def dot_high(left, right):
    return jnp.dot(left, right, precision=HIGHEST, preferred_element_type=WIDE)


def dot_near(left, right):
    return jnp.dot(left, right, precision=HIGH, preferred_element_type=WIDE)


def dot_plain(left, right):
    return jnp.dot(left, right, preferred_element_type=WIDE)


def dot_first(left, right):
    return lax.dot_general(left, right, (((0,), (0,)), ((), ())), preferred_element_type=WIDE)


def dot_last(left, right):
    return lax.dot_general(left, right, (((1,), (1,)), ((), ())), preferred_element_type=WIDE)


def layer_norm(values, gain, bias):
    mean = jnp.mean(values, axis=-1, keepdims=True)
    centered = values - mean
    variance = jnp.mean(centered * centered, axis=-1, keepdims=True)
    return centered * lax.rsqrt(variance + EPSILON) * gain + bias


def exact_gelu(values):
    return jax.nn.gelu(values, approximate=False)


def position_table(length, emb_dim):
    bands = (emb_dim - 1) // 2
    sample = np.arange(length, dtype=np.float32)
    times = sample / np.float32(length - 1)
    frequency = np.linspace(0.0001, bands - 1, bands).astype(np.float32)
    angle = np.float32(2.0 * math.pi) * sample[:, None] * frequency[None, :] / np.float32(length)
    table = np.concatenate([times[:, None], np.cos(angle), -np.sin(angle)], axis=1)
    return (table.astype(np.float32), times)


def transform_tables(block_len):
    span = 2 * block_len
    frequency = np.arange(block_len)
    sample = np.arange(block_len)
    is_zero = (frequency == 0)[:, None]
    angle = 2.0 * math.pi * (frequency[:, None] * sample[None, :] % span) / span
    alternate = np.where(sample % 2 == 0, 1.0, -1.0)
    real_rows = np.cos(angle)
    imag_rows = np.where(is_zero, alternate[None, :], -np.sin(angle))
    forward_table = np.concatenate([real_rows, imag_rows], axis=0)
    outputs = sample + block_len
    out_angle = 2.0 * math.pi * (outputs[:, None] * frequency[None, :] % span) / span
    out_alternate = np.where(outputs % 2 == 0, 1.0, -1.0)
    zero_col = (frequency == 0)[None, :]
    real_cols = np.where(zero_col, 1.0, 2.0) * np.cos(out_angle) / span
    imag_cols = np.where(zero_col, out_alternate[:, None] / span, -2.0 * np.sin(out_angle) / span)
    inverse_table = np.concatenate([real_cols, imag_cols], axis=1)
    parity = np.where(frequency % 2 == 0, 1.0, -1.0)
    sign = np.concatenate([parity, np.where(frequency == 0, 1.0, parity)])
    edge = (frequency == 0).astype(np.float32)[:, None]
    return tuple(item.astype(np.float32) for item in (forward_table, inverse_table, sign, edge))


def spectral_product(left, right, edge):
    half = left.shape[-2] // 2
    left_re, left_im = (left[..., :half, :], left[..., half:, :])
    right_re, right_im = (right[..., :half, :], right[..., half:, :])
    inside = 1.0 - edge
    out_re = left_re * right_re - inside * left_im * right_im
    out_im = inside * (left_re * right_im + left_im * right_re) + edge * left_im * right_im
    return jnp.concatenate([out_re, out_im], axis=-2)


def spectral_back(grad, other, edge):
    half = grad.shape[-2] // 2
    grad_re, grad_im = (grad[..., :half, :], grad[..., half:, :])
    other_re, other_im = (other[..., :half, :], other[..., half:, :])
    inside = 1.0 - edge
    back_re = grad_re * other_re + inside * grad_im * other_im
    back_im = inside * (grad_im * other_re - grad_re * other_im) + edge * grad_im * other_im
    return jnp.concatenate([back_re, back_im], axis=-2)


class Grid:
    def __init__(self, count_dp, count_block):
        self.count_dp = count_dp
        self.count_block = count_block
        self.row = lax.axis_index("dp")
        self.place = lax.axis_index("block")
        self.dp_steps = []
        bit = 1
        while bit < count_dp:
            self.dp_steps.append((bit | (bit >> 1) if bit == 4 else bit, 0))
            bit *= 2
        self.chip_steps = []
        bit = 2
        while bit < count_block:
            self.chip_steps.append((0, bit | (bit >> 1) if bit == 4 else bit))
            bit *= 2
        self.core_step = (0, 1)

    def swap(self, value, step):
        pairs = []
        for row in range(self.count_dp):
            for place in range(self.count_block):
                to = (row ^ step[0]) * self.count_block + (place ^ step[1])
                pairs.append((row * self.count_block + place, to))
        return lax.ppermute(value, ("dp", "block"), pairs)

    def gather(self, value, steps, gates=()):
        held = value[None]
        pieces = [held]
        for number, step in enumerate(steps):
            if number < len(gates):
                held = after(held, *gates[number])
            pieces.append(self.swap(held, step))
            if number + 1 < len(steps):
                held = jnp.concatenate(pieces, axis=0)
        return pieces

    def scatter(self, kept, sent, steps, whole=True, sends=None, adds=None):
        for number, step in enumerate(reversed(steps)):
            if sends and number in sends:
                sent = after(sent, *sends[number])
            arrived = self.swap(sent, step)
            if adds and number in adds:
                arrived = after(arrived, *adds[number])
            half = kept.shape[0] // 2
            if not half and not whole:
                return kept[0], arrived[0]
            if half:
                sent = add_low(kept[half:], arrived[half:])
                kept = add_low(kept[:half], arrived[:half])
            else:
                kept = add_low(kept, arrived)
        return kept[0]

    def halve(self, kept, sent, step):
        return halves(kept, self.swap(sent, step))


def halves(left, right):
    half = left.shape[0] // 2
    return add_low(left[:half], right[:half]), add_low(left[half:], right[half:])


def add_low(left, right):
    return (left.astype(WIDE) + right.astype(WIDE)).astype(left.dtype)


def offsets_of(steps):
    offsets = [(0, 0)]
    for step in steps:
        offsets = offsets + [(a ^ step[0], b ^ step[1]) for a, b in offsets]
    return offsets


def arrange(pieces, mine, offsets):
    shape = pieces[0].shape[1:]
    if shape[-2] % 32 or shape[-1] % 128:
        held = jnp.concatenate(pieces, axis=0)
        codes = codes_of(offsets, len(offsets))
        return jnp.concatenate(
            [
                lax.dynamic_slice_in_dim(held, place_in(codes, k ^ mine), 1, 0)
                for k in range(len(offsets))
            ],
            axis=0,
        )
    count = len(pieces)

    def kernel(mine_ref, *refs):
        source, target = refs[:count], refs[count]
        at = 0
        for ref in source:
            for i in range(ref.shape[0]):
                target[mine_ref[0] ^ offsets[at]] = ref[i]
                at += 1

    return pl.pallas_call(
        kernel,
        out_shape=jax.ShapeDtypeStruct((len(offsets), *shape), pieces[0].dtype),
        in_specs=[pl.BlockSpec(memory_space=pltpu.SMEM)]
        + [pl.BlockSpec(memory_space=pltpu.VMEM)] * count,
        out_specs=pl.BlockSpec(memory_space=pltpu.VMEM),
    )(jnp.reshape(mine, (1,)).astype(jnp.int32), *pieces)


def deal(natural, mine, offsets):
    half = len(offsets) // 2
    shape = natural.shape[1:]
    if shape[-2] % 32 or shape[-1] % 128:
        dealt = [lax.dynamic_slice_in_dim(natural, mine ^ offset, 1, 0) for offset in offsets]
        return jnp.concatenate(dealt[:half], axis=0), jnp.concatenate(dealt[half:], axis=0)

    def kernel(mine_ref, source, kept, sent):
        for at, offset in enumerate(offsets):
            if at < half:
                kept[at] = source[mine_ref[0] ^ offset]
            else:
                sent[at - half] = source[mine_ref[0] ^ offset]

    out = jax.ShapeDtypeStruct((half, *shape), natural.dtype)
    vmem = pl.BlockSpec(memory_space=pltpu.VMEM)
    return pl.pallas_call(
        kernel,
        out_shape=(out, out),
        in_specs=[pl.BlockSpec(memory_space=pltpu.SMEM), vmem],
        out_specs=(vmem, vmem),
    )(jnp.reshape(mine, (1,)).astype(jnp.int32), natural)


def place_in(codes, offset):
    place = 0
    for j, code in enumerate(codes):
        place = place ^ (((offset >> j) & 1) * code)
    return place


def codes_of(offsets, count):
    codes, bit = [], 1
    while bit < count:
        codes.append(offsets.index(bit))
        bit *= 2
    return codes


def split_low(values):
    high = values.astype(LOW)
    return high, (values - high.astype(WIDE)).astype(LOW)


def triple(table):
    high = table.astype(ml_dtypes.bfloat16)
    low = (table - high.astype(np.float32)).astype(ml_dtypes.bfloat16)
    return np.concatenate([high, high, low], axis=1)


def store_triple(target, columns, values):
    high, low = split_low(values)
    size = values.shape[0]
    target[0:size, columns] = high
    target[size : 2 * size, columns] = low
    target[2 * size : 3 * size, columns] = high


def long_range(starts, count, block_len, length):
    begin, end, before = starts[0], jnp.int32(length), jnp.int32(-1)
    for d in range(count):
        begin = jnp.where(starts[d] <= block_len, starts[d], begin)
        before = before + jnp.where(starts[d] <= block_len, 1, 0)
    for d in reversed(range(count)):
        end = jnp.where(starts[d] > block_len, starts[d], end)
    return begin, end, before


def short_range(starts, count, number, before, block_len, length):
    early = number < before
    bounds = [starts[d] for d in range(count)] + [jnp.int32(length)]
    begin = jnp.where(early, bounds[number], bounds[number + 1])
    end = jnp.where(early, bounds[number + 1], bounds[number + 2])
    return begin, end, jnp.where(early, 0, length - block_len)


def rows_from(base, size, lanes):
    return lax.broadcasted_iota(jnp.int32, (size, lanes), 0) + base


def inside_mask(base, size, lanes, begin, end):
    rows = rows_from(base, size, lanes)
    return (rows >= begin) & (rows < end)


def keep_masks(starts, count, base, size, lanes):
    rows = rows_from(base, size, lanes)
    one = rows != starts[0]
    for d in range(1, count):
        one = one & (rows != starts[d])
    two = one
    for d in range(count):
        two = two & (rows != starts[d] + 1)
    return one, two


VMEM_SPACE = pl.BlockSpec(memory_space=pltpu.VMEM)
ANY_SPACE = pl.BlockSpec(memory_space=pl.ANY)
SMEM_SPACE = pl.BlockSpec(memory_space=pltpu.SMEM)
LIMIT = 30 * 1024 * 1024
WHOLE = 56 * 1024 * 1024


def cost(microseconds):
    return pl.CostEstimate(
        flops=int(microseconds * 1e9), bytes_accessed=int(microseconds * 3e6), transcendentals=0
    )


class Copies:
    def __init__(self, sems):
        self.sems, self.used = sems, 0

    def start(self, source, target):
        copy = pltpu.make_async_copy(source, target, self.sems.at[self.used])
        self.used += 1
        copy.start()
        return copy


def filter_kernel(block_len, blocks, table_ref, w1, w2, vec, third_at, f3_ref, spectra):
    length = block_len * blocks
    channels = vec.shape[1]
    one_row = jnp.where(lax.broadcasted_iota(jnp.int32, (8, length), 0) == 0, 1.0, 0.0)

    def turned(left, right):
        return lax.dot_general(
            left, right, (((0,), (0,)), ((), ())), precision=HIGHEST, preferred_element_type=WIDE
        )

    first = jnp.sin(turned(w1[...], table_ref[...]))
    second = jnp.sin(turned(w2[...], jnp.concatenate([first, one_row], axis=0)))
    decay = vec[third_at - 2 : third_at - 1, :]
    third_w = vec[third_at : third_at + second.shape[0], :]
    before = None
    half_rows = lax.broadcasted_iota(jnp.int32, (2 * block_len, channels), 0)
    parity = jnp.where(half_rows % 2 == 0, 1.0, -1.0)
    sign = jnp.where(half_rows == block_len, 1.0, parity)
    for i in range(blocks):
        part = turned(second[:, i * block_len : (i + 1) * block_len], third_w)
        times = rows_from(i * block_len, block_len, channels).astype(WIDE) / (length - 1)
        part = part * (jnp.exp(-times * decay) + MOD_SHIFT)
        high, low = split_low(part)
        stacked = jnp.concatenate([high, low, high], axis=0)
        half = jnp.dot(f3_ref[...], stacked, preferred_element_type=WIDE)
        spectra[i] = sign * half if before is None else before + sign * half
        before = half


def with_bias(weights, bias):
    rows = weights.shape[0]
    return jnp.pad(jnp.concatenate([weights, bias[None]], axis=0), ((0, -(rows + 1) % 8), (0, 0)))


def turned_table(table):
    length, count = table.shape
    rows = [table.T, np.ones((1, length), np.float32)]
    rows.append(np.zeros((-(count + 1) % 8, length), np.float32))
    return np.concatenate(rows, axis=0)


def filter_call(block_len, blocks, table, f3, w1, w2, vec, third_at):
    channels = vec.shape[1]

    def body(table_ref, w1_ref, w2_ref, vec_ref, f3_ref, spectra, mark):
        filter_kernel(
            block_len, blocks, table_ref, w1_ref, w2_ref, vec_ref, third_at, f3_ref, spectra
        )
        mark[...] = w1_ref[...]

    return pl.pallas_call(
        body,
        out_shape=[
            jax.ShapeDtypeStruct((blocks, 2 * block_len, channels), WIDE),
            jax.ShapeDtypeStruct(w1.shape, WIDE),
        ],
        in_specs=[VMEM_SPACE] * 5,
        out_specs=[VMEM_SPACE] * 2,
        compiler_params=pltpu.CompilerParams(vmem_limit_bytes=LIMIT),
        cost_estimate=cost(7),
    )(table, w1, w2, vec, f3)


def gather_in(copies, pieces, mine, offsets, target):
    started, at = [], 0
    for ref in pieces:
        for i in range(ref.shape[0]):
            started.append(copies.start(ref.at[i], target.at[mine ^ offsets[at]]))
            at += 1
    return started


def conv_call(
    block_len, blocks, places, starts, normed_pieces, in_pieces, in_offsets, block_offsets, vec, spectra, f3, i3
):
    length = block_len * blocks
    channels = vec.shape[1]
    docs = starts.shape[0]
    entries = blocks + docs - 1
    width = normed_pieces[0].shape[-1]
    groups = len(in_pieces)
    share = in_pieces[0][0].shape[1]
    count_dp = len(in_offsets[0])
    flat_in = [piece for pieces in in_pieces for piece in pieces]
    n_norm, n_in, n_out = len(normed_pieces), len(flat_in), blocks
    step = 16

    def body(place_ref, starts_ref, vec_ref, f3_ref, i3_ref, spectra_ref, *refs):
        norm_refs, in_refs = refs[:n_norm], refs[n_norm : n_norm + n_in]
        refs = refs[n_norm + n_in :]
        gated_refs, (proj_out, entry_out, mixed_out, rows_out, norm_out) = refs[:n_out], refs[n_out : n_out + 5]
        norm, rows, proj, inner, gate, xs, ent, ys, mixed, spec, sems = refs[n_out + 5 :]
        row, place = place_ref[0], place_ref[1]
        copies = Copies(sems)
        waiting = gather_in(copies, norm_refs, place, block_offsets, norm)
        at = 0
        for g in range(groups):
            count = len(in_pieces[g])
            index = 0
            for ref in in_refs[at : at + count]:
                for i in range(ref.shape[0]):
                    to = row ^ in_offsets[g][index]
                    waiting.append(copies.start(ref.at[i], rows.at[to, g]))
                    index += 1
            at += count
        spec_copy = copies.start(spectra_ref, spec)
        for copy in waiting:
            copy.wait()
        leaving = [copies.start(norm, norm_out), copies.start(rows, rows_out)]

        flat_rows = rows[...].reshape(3 * channels, width)
        for role in range(3):
            weights = flat_rows[role * channels : (role + 1) * channels]
            bias = vec_ref[role : role + 1, :]
            for b in range(blocks):
                proj[b * block_len : (b + 1) * block_len, role * channels : (role + 1) * channels] = (
                    lax.dot_general(
                        norm[b],
                        weights,
                        (((1,), (1,)), ((), ())),
                        preferred_element_type=WIDE,
                    )
                    + bias
                )
        leaving.append(copies.start(proj, proj_out))
        for b in range(blocks):
            base = b * block_len
            one, two = keep_masks(starts_ref, docs, base, block_len, channels)
            parts = []
            for role in range(3):
                lanes = slice(role * channels, (role + 1) * channels)
                here = proj[base : base + block_len, lanes]
                if b:
                    back = proj[base - 8 : base + block_len, lanes]
                    prev_one = pltpu.roll(back, 1, 0)[8:]
                    prev_two = pltpu.roll(back, 2, 0)[8:]
                else:
                    prev_one, prev_two = pltpu.roll(here, 1, 0), pltpu.roll(here, 2, 0)
                tap = [vec_ref[3 + 3 * j + role : 4 + 3 * j + role, :] for j in range(3)]
                short = (
                    vec_ref[12 + role : 13 + role, :]
                    + tap[0] * here
                    + tap[1] * jnp.where(one, prev_one, 0.0)
                    + tap[2] * jnp.where(two, prev_two, 0.0)
                )
                parts.append(short)
            gate[base : base + block_len] = parts[0]
            inner[base : base + block_len] = parts[1] * parts[2]
        begin, end, before = long_range(starts_ref, docs, block_len, length)
        for b in range(blocks):
            mask = inside_mask(b * block_len, block_len, channels, begin, end)
            part = jnp.where(mask, inner[b * block_len : (b + 1) * block_len], 0.0)
            store_triple(xs, slice(b * channels, (b + 1) * channels), part)
        for m in range(docs - 1):
            first, last, base = short_range(starts_ref, docs, m, before, block_len, length)
            base = pl.multiple_of(base, block_len)
            mask = inside_mask(base, block_len, channels, first, last)
            part = jnp.where(mask, inner[pl.ds(base, block_len)], 0.0)
            store_triple(xs, slice((blocks + m) * channels, (blocks + m + 1) * channels), part)
        for e in range(entries):
            ent[e] = jnp.dot(
                f3_ref[...], xs[:, e * channels : (e + 1) * channels], preferred_element_type=WIDE
            )
        leaving.append(copies.start(ent, entry_out))
        spec_copy.wait()

        @pl.loop(0, block_len // step)
        def _(number):
            at_re = pl.multiple_of(number * step, step)
            at_im = pl.multiple_of(number * step + block_len, step)
            edge = jnp.where(rows_from(at_re, step, channels) == 0, 1.0, 0.0)
            inside = 1.0 - edge
            keys = [(spec[k, pl.ds(at_re, step)], spec[k, pl.ds(at_im, step)]) for k in range(blocks)]
            held = [(ent[k, pl.ds(at_re, step)], ent[k, pl.ds(at_im, step)]) for k in range(blocks)]
            for e in range(entries):
                pairs = (
                    [(held[j], keys[e - j]) for j in range(e + 1)]
                    if e < blocks
                    else [((ent[e, pl.ds(at_re, step)], ent[e, pl.ds(at_im, step)]), keys[0])]
                )
                rr = ii = ri = None
                for (a, b), (c, d) in pairs:
                    rr = a * c if rr is None else rr + a * c
                    ii = b * d if ii is None else ii + b * d
                    ri = a * d + b * c if ri is None else ri + (a * d + b * c)
                lanes = slice(e * channels, (e + 1) * channels)
                out_re = rr - inside * ii
                out_im = inside * ri + edge * ii
                for part, at in ((out_re, at_re), (out_im, at_im)):
                    high, low = split_low(part)
                    ys[pl.ds(at, step), lanes] = high
                    ys[pl.ds(at + 2 * block_len, step), lanes] = low
                    ys[pl.ds(at + 4 * block_len, step), lanes] = high

        direct = vec_ref[16:17, :]
        for b in range(blocks):
            back = jnp.dot(
                i3_ref[...], ys[:, b * channels : (b + 1) * channels], preferred_element_type=WIDE
            )
            rows_here = slice(b * block_len, (b + 1) * block_len)
            mask = inside_mask(b * block_len, block_len, channels, begin, end)
            mixed[rows_here] = jnp.where(mask, back, 0.0) + direct * inner[rows_here]
        for m in range(docs - 1):
            lanes = slice((blocks + m) * channels, (blocks + m + 1) * channels)
            back = jnp.dot(i3_ref[...], ys[:, lanes], preferred_element_type=WIDE)
            first, last, base = short_range(starts_ref, docs, m, before, block_len, length)
            base = pl.multiple_of(base, block_len)
            mask = inside_mask(base, block_len, channels, first, last)
            where = pl.ds(base, block_len)
            mixed[where] = mixed[where] + jnp.where(mask, back, 0.0)
        leaving.append(copies.start(mixed, mixed_out))
        for index, offset in enumerate(block_offsets):
            where = pl.ds(pl.multiple_of((place ^ offset) * block_len, block_len), block_len)
            gated_refs[index][...] = (gate[where] * mixed[where]).astype(LOW)
        for copy in leaving:
            copy.wait()

    shape = jax.ShapeDtypeStruct
    sem_count = blocks + groups * count_dp + 6
    return pl.pallas_call(
        body,
        out_shape=[shape((block_len, channels), LOW)] * blocks
        + [
            shape((length, 3 * channels), WIDE),
            shape((entries, 2 * block_len, channels), WIDE),
            shape((length, channels), WIDE),
            shape((count_dp, groups, share, width), LOW),
            shape((blocks, block_len, width), LOW),
        ],
        in_specs=[SMEM_SPACE, SMEM_SPACE, VMEM_SPACE, VMEM_SPACE, VMEM_SPACE, ANY_SPACE]
        + [ANY_SPACE] * (n_norm + n_in),
        out_specs=[VMEM_SPACE] * blocks + [ANY_SPACE] * 5,
        scratch_shapes=[
            pltpu.VMEM((blocks, block_len, width), LOW),
            pltpu.VMEM((count_dp, groups, share, width), LOW),
            pltpu.VMEM((length, 3 * channels), WIDE),
            pltpu.VMEM((length, channels), WIDE),
            pltpu.VMEM((length, channels), WIDE),
            pltpu.VMEM((3 * block_len, entries * channels), LOW),
            pltpu.VMEM((entries, 2 * block_len, channels), WIDE),
            pltpu.VMEM((6 * block_len, entries * channels), LOW),
            pltpu.VMEM((length, channels), WIDE),
            pltpu.VMEM((blocks, 2 * block_len, channels), WIDE),
            pltpu.SemaphoreType.DMA((sem_count,)),
        ],
        compiler_params=pltpu.CompilerParams(vmem_limit_bytes=WHOLE),
        cost_estimate=cost(14),
    )(places, starts, vec, f3, i3, spectra, *normed_pieces, *flat_in)


def back_call(
    block_len,
    blocks,
    places,
    starts,
    grad_pieces,
    block_offsets,
    vec,
    spectra,
    proj,
    entries,
    mixed,
    it3,
    ft3,
):
    length = block_len * blocks
    channels = vec.shape[1]
    docs = starts.shape[0]
    count = entries.shape[0]
    three = 3 * channels
    step = 16

    def body(place_ref, starts_ref, vec_ref, it3_ref, ft3_ref, *refs):
        grad_refs, refs = refs[:blocks], refs[blocks:]
        spectra_ref, proj_ref, entry_ref, mixed_ref, lags, direct_out, gs_out = refs[:7]
        spec, proj, ent, mixed, gg, short, gs, gm, xs, gt, ys, gi, sems = refs[7:]
        place = place_ref[1]
        copies = Copies(sems)
        proj_copy = copies.start(proj_ref, proj)
        mixed_copy = copies.start(mixed_ref, mixed)
        spec_copy = copies.start(spectra_ref, spec)
        entry_copy = copies.start(entry_ref, ent)
        for index, offset in enumerate(block_offsets):
            where = pl.ds(pl.multiple_of((place ^ offset) * block_len, block_len), block_len)
            gg[where] = grad_refs[index][...]
        proj_copy.wait()
        mixed_copy.wait()
        direct = vec_ref[16:17, :]
        direct_sum = jnp.zeros((1, channels), WIDE)
        for b in range(blocks):
            base = b * block_len
            here = slice(base, base + block_len)
            one, two = keep_masks(starts_ref, docs, base, block_len, channels)
            parts = []
            for role in range(3):
                lanes = slice(role * channels, (role + 1) * channels)
                now = proj[here, lanes]
                if b:
                    back = proj[base - 8 : base + block_len, lanes]
                    prev_one, prev_two = pltpu.roll(back, 1, 0)[8:], pltpu.roll(back, 2, 0)[8:]
                else:
                    prev_one, prev_two = pltpu.roll(now, 1, 0), pltpu.roll(now, 2, 0)
                tap = [vec_ref[3 + 3 * j + role : 4 + 3 * j + role, :] for j in range(3)]
                parts.append(
                    vec_ref[12 + role : 13 + role, :]
                    + tap[0] * now
                    + tap[1] * jnp.where(one, prev_one, 0.0)
                    + tap[2] * jnp.where(two, prev_two, 0.0)
                )
            grad = gg[here].astype(WIDE)
            gs[here, :channels] = grad * mixed[here]
            grad = grad * parts[0]
            gm[here] = grad
            short[here, :channels] = parts[1]
            short[here, channels:] = parts[2]
            direct_sum = direct_sum + jnp.sum(
                grad * (parts[1] * parts[2]), axis=0, keepdims=True
            )
        gs[length:, :] = jnp.zeros((8, three), WIDE)
        direct_out[...] = direct_sum
        begin, end, before = long_range(starts_ref, docs, block_len, length)
        ranges = []
        for m in range(docs - 1):
            first, last, base = short_range(starts_ref, docs, m, before, block_len, length)
            base = pl.multiple_of(base, block_len)
            ranges.append((base, inside_mask(base, block_len, channels, first, last)))
        for b in range(blocks):
            mask = inside_mask(b * block_len, block_len, channels, begin, end)
            part = jnp.where(mask, gm[b * block_len : (b + 1) * block_len], 0.0)
            store_triple(xs, slice(b * channels, (b + 1) * channels), part)
        for m, (base, mask) in enumerate(ranges):
            part = jnp.where(mask, gm[pl.ds(base, block_len)], 0.0)
            store_triple(xs, slice((blocks + m) * channels, (blocks + m + 1) * channels), part)
        for e in range(count):
            gt[e] = jnp.dot(
                it3_ref[...], xs[:, e * channels : (e + 1) * channels], preferred_element_type=WIDE
            )
        spec_copy.wait()
        entry_copy.wait()

        @pl.loop(0, block_len // step)
        def _(number):
            at_re = pl.multiple_of(number * step, step)
            at_im = pl.multiple_of(number * step + block_len, step)
            edge = jnp.where(rows_from(at_re, step, channels) == 0, 1.0, 0.0)
            inside = 1.0 - edge

            def load(ref, k):
                return ref[k, pl.ds(at_re, step)], ref[k, pl.ds(at_im, step)]

            def combine(pairs):
                rr = ii = ri = None
                for (a, b), (c, d) in pairs:
                    rr = a * c if rr is None else rr + a * c
                    ii = b * d if ii is None else ii + b * d
                    ri = b * c - a * d if ri is None else ri + (b * c - a * d)
                return rr + inside * ii, inside * ri + edge * ii

            for e in range(count):
                if e < blocks:
                    pairs = [(load(gt, i), load(spec, i - e)) for i in range(e, blocks)]
                else:
                    pairs = [(load(gt, e), load(spec, 0))]
                lanes = slice(e * channels, (e + 1) * channels)
                for part, at in zip(combine(pairs), (at_re, at_im)):
                    high, low = split_low(part)
                    ys[pl.ds(at, step), lanes] = high
                    ys[pl.ds(at + 2 * block_len, step), lanes] = low
                    ys[pl.ds(at + 4 * block_len, step), lanes] = high
            for k in range(blocks):
                pairs = [(load(gt, j + k), load(ent, j)) for j in range(blocks - k)]
                if k == 0:
                    pairs += [(load(gt, e), load(ent, e)) for e in range(blocks, count)]
                out_re, out_im = combine(pairs)
                lags[k, pl.ds(at_re, step)] = out_re
                lags[k, pl.ds(at_im, step)] = out_im

        for b in range(blocks):
            here = slice(b * block_len, (b + 1) * block_len)
            back = jnp.dot(
                ft3_ref[...], ys[:, b * channels : (b + 1) * channels], preferred_element_type=WIDE
            )
            mask = inside_mask(b * block_len, block_len, channels, begin, end)
            gi[here] = jnp.where(mask, back, 0.0) + direct * gm[here]
        for m, (base, mask) in enumerate(ranges):
            lanes = slice((blocks + m) * channels, (blocks + m + 1) * channels)
            back = jnp.dot(ft3_ref[...], ys[:, lanes], preferred_element_type=WIDE)
            where = pl.ds(base, block_len)
            gi[where] = gi[where] + jnp.where(mask, back, 0.0)
        for b in range(blocks):
            here = slice(b * block_len, (b + 1) * block_len)
            gs[here, channels : 2 * channels] = gi[here] * short[here, channels:]
            gs[here, 2 * channels :] = gi[here] * short[here, :channels]
        copies.start(gs, gs_out).wait()

    shape = jax.ShapeDtypeStruct
    return pl.pallas_call(
        body,
        out_shape=[
            shape((blocks, 2 * block_len, channels), WIDE),
            shape((1, channels), WIDE),
            shape((length + 8, three), WIDE),
        ],
        in_specs=[SMEM_SPACE] * 2 + [VMEM_SPACE] * (3 + blocks) + [ANY_SPACE] * 4,
        out_specs=[VMEM_SPACE, VMEM_SPACE, ANY_SPACE],
        scratch_shapes=[
            pltpu.VMEM((blocks, 2 * block_len, channels), WIDE),
            pltpu.VMEM((length, three), WIDE),
            pltpu.VMEM((count, 2 * block_len, channels), WIDE),
            pltpu.VMEM((length, channels), WIDE),
            pltpu.VMEM((length, channels), LOW),
            pltpu.VMEM((length, 2 * channels), WIDE),
            pltpu.VMEM((length + 8, three), WIDE),
            pltpu.VMEM((length, channels), WIDE),
            pltpu.VMEM((3 * block_len, count * channels), LOW),
            pltpu.VMEM((count, 2 * block_len, channels), WIDE),
            pltpu.VMEM((6 * block_len, count * channels), LOW),
            pltpu.VMEM((length, channels), WIDE),
            pltpu.SemaphoreType.DMA((5,)),
        ],
        compiler_params=pltpu.CompilerParams(vmem_limit_bytes=LIMIT),
        cost_estimate=cost(14),
    )(places, starts, vec, it3, ft3, *grad_pieces, spectra, proj, entries, mixed)


def project_back_call(
    block_len,
    blocks,
    places,
    starts,
    in_offsets,
    block_offsets,
    vec,
    norm1,
    direct,
    grad_short,
    proj,
    in_rows,
    normed,
):
    length = block_len * blocks
    channels = vec.shape[1]
    docs = starts.shape[0]
    count_dp, groups, share, width = in_rows.shape
    three = 3 * channels
    half_dp, half_block = count_dp // 2, blocks // 2

    def body(place_ref, starts_ref, vec_ref, gain_ref, shift_ref, direct_ref, *refs):
        gs_ref, proj_ref, rows_ref, norm_ref = refs[:4]
        refs = refs[4:]
        dealt_refs = [(refs[2 * g], refs[2 * g + 1]) for g in range(groups)]
        refs = refs[2 * groups :]
        gn_kept, gn_sent, sums, norm_sums = refs[:4]
        gs, proj, rows, norm, gp, gr, sems = refs[4:]
        row, place = place_ref[0], place_ref[1]
        copies = Copies(sems)
        gs_copy = copies.start(gs_ref, gs)
        proj_copy = copies.start(proj_ref, proj)
        rows_copy = copies.start(rows_ref, rows)
        norm_copy = copies.start(norm_ref, norm)
        sums[15:16, :] = direct_ref[...]
        gs_copy.wait()
        proj_copy.wait()
        for role in range(3):
            lanes = slice(role * channels, (role + 1) * channels)
            tap = [vec_ref[3 + 3 * j + role : 4 + 3 * j + role, :] for j in range(3)]
            totals = [jnp.zeros((1, channels), WIDE) for _ in range(5)]
            for b in range(blocks):
                base = b * block_len
                here = slice(base, base + block_len)
                one, two = keep_masks(starts_ref, docs, base, block_len + 8, channels)
                grad = gs[base : base + block_len + 8, lanes]
                pass_one, pass_two = jnp.where(one, grad, 0.0), jnp.where(two, grad, 0.0)
                size = block_len + 8
                result = (
                    tap[0] * grad[:block_len]
                    + tap[1] * pltpu.roll(pass_one, size - 1, 0)[:block_len]
                    + tap[2] * pltpu.roll(pass_two, size - 2, 0)[:block_len]
                ).astype(LOW)
                gp[here, lanes] = result
                now = proj[here, lanes]
                if b:
                    back = proj[base - 8 : base + block_len, lanes]
                    prev_one, prev_two = pltpu.roll(back, 1, 0)[8:], pltpu.roll(back, 2, 0)[8:]
                else:
                    prev_one, prev_two = pltpu.roll(now, 1, 0), pltpu.roll(now, 2, 0)
                terms = [
                    result.astype(WIDE),
                    grad[:block_len] * now,
                    pass_one[:block_len] * prev_one,
                    pass_two[:block_len] * prev_two,
                    grad[:block_len],
                ]
                totals = [
                    total + jnp.sum(term, axis=0, keepdims=True)
                    for total, term in zip(totals, terms)
                ]
            sums[role : role + 1, :] = totals[0]
            for j in range(3):
                sums[3 + 3 * j + role : 4 + 3 * j + role, :] = totals[1 + j]
            sums[12 + role : 13 + role, :] = totals[4]
        rows_copy.wait()
        norm_copy.wait()
        weights = rows[...].reshape(three, width)
        shift_sum = jnp.zeros((1, width), WIDE)
        scale_sum = jnp.zeros((1, width), WIDE)
        for index, offset in enumerate(block_offsets):
            other = place ^ offset
            where = pl.ds(pl.multiple_of(other * block_len, block_len), block_len)
            part = jnp.dot(gp[where], weights, preferred_element_type=WIDE)
            shift_sum = shift_sum + jnp.sum(part, axis=0, keepdims=True)
            scale_sum = scale_sum + jnp.sum(
                part * norm[other].astype(WIDE), axis=0, keepdims=True
            )
            if index < half_block:
                gn_kept[index] = part.astype(LOW)
            else:
                gn_sent[index - half_block] = part.astype(LOW)
        norm_sums[0:1, :] = (scale_sum - shift_ref[...] * shift_sum) / gain_ref[...]
        norm_sums[1:2, :] = shift_sum
        for c in range(3):
            lanes = slice(c * channels, (c + 1) * channels)
            total = lax.dot_general(
                gp[:, lanes],
                norm[...].reshape(length, width),
                (((0,), (0,)), ((), ())),
                preferred_element_type=WIDE,
            )
            gr[lanes] = total.astype(LOW)
        dealt = gr.reshape(count_dp, groups, share, width)
        leaving = []
        for g in range(groups):
            for index, offset in enumerate(in_offsets[g]):
                target = dealt_refs[g][index // half_dp].at[index % half_dp]
                leaving.append(copies.start(dealt.at[row ^ offset, g], target))
        for copy in leaving:
            copy.wait()

    shape = jax.ShapeDtypeStruct
    half_in = shape((half_dp, share, width), LOW)
    return pl.pallas_call(
        body,
        out_shape=[half_in] * (2 * groups)
        + [
            shape((half_block, block_len, width), LOW),
            shape((half_block, block_len, width), LOW),
            shape((16, channels), WIDE),
            shape((2, width), WIDE),
        ],
        in_specs=[SMEM_SPACE] * 2 + [VMEM_SPACE] * 4 + [ANY_SPACE] * 4,
        out_specs=[ANY_SPACE] * (2 * groups) + [VMEM_SPACE] * 4,
        scratch_shapes=[
            pltpu.VMEM((length + 8, three), WIDE),
            pltpu.VMEM((length, three), WIDE),
            pltpu.VMEM((count_dp, groups, share, width), LOW),
            pltpu.VMEM((blocks, block_len, width), LOW),
            pltpu.VMEM((length, three), LOW),
            pltpu.VMEM((three, width), LOW),
            pltpu.SemaphoreType.DMA((4 + groups * count_dp,)),
        ],
        compiler_params=pltpu.CompilerParams(vmem_limit_bytes=LIMIT),
        cost_estimate=cost(10),
    )(places, starts, vec, *norm1, direct, grad_short, proj, in_rows, normed)


def filter_back_call(block_len, blocks, table, ft3, w1, w2, vec, third_at, lags):
    length = block_len * blocks
    channels = vec.shape[1]
    units = w2.shape[1]

    def body(table_ref, w1_ref, w2_ref, vec_ref, ft3_ref, lags_ref, g1, g2, g3, gd):
        one_row = jnp.where(lax.broadcasted_iota(jnp.int32, (8, length), 0) == 0, 1.0, 0.0)

        def product(left, right, dims):
            return lax.dot_general(
                left, right, (dims, ((), ())), precision=HIGHEST, preferred_element_type=WIDE
            )

        z1 = product(w1_ref[...], table_ref[...], ((0,), (0,)))
        first = jnp.concatenate([jnp.sin(z1), one_row], axis=0)
        z2 = product(w2_ref[...], first, ((0,), (0,)))
        second = jnp.sin(z2)
        decay = vec_ref[third_at - 2 : third_at - 1, :]
        third_w = vec_ref[third_at : third_at + units, :]
        half_rows = lax.broadcasted_iota(jnp.int32, (2 * block_len, channels), 0)
        parity = jnp.where(half_rows % 2 == 0, 1.0, -1.0)
        sign = jnp.where(half_rows == block_len, 1.0, parity)
        third_sum = jnp.zeros((units, channels), WIDE)
        decay_sum = jnp.zeros((1, channels), WIDE)
        back = []
        for i in range(blocks):
            grad = sign * lags_ref[i]
            if i + 1 < blocks:
                grad = grad + lags_ref[i + 1]
            high, low = split_low(grad)
            stacked = jnp.concatenate([high, low, high], axis=0)
            grad = jnp.dot(ft3_ref[...], stacked, preferred_element_type=WIDE)
            here = second[:, i * block_len : (i + 1) * block_len]
            third = product(here, third_w, ((0,), (0,)))
            times = rows_from(i * block_len, block_len, channels).astype(WIDE) / (length - 1)
            fall = jnp.exp(-times * decay)
            decay_sum = decay_sum - jnp.sum(grad * third * fall * times, axis=0, keepdims=True)
            grad = grad * (fall + MOD_SHIFT)
            third_sum = third_sum + product(here, grad, ((1,), (0,)))
            back.append(product(third_w, grad, ((1,), (1,))))
        gz2 = jnp.concatenate(back, axis=1) * jnp.cos(z2)
        g2[...] = product(first, gz2, ((1,), (1,)))
        gz1 = product(w2_ref[:units, :], gz2, ((1,), (0,))) * jnp.cos(z1)
        g1[...] = product(table_ref[...], gz1, ((1,), (1,)))
        g3[...] = third_sum
        gd[...] = decay_sum

    shape = jax.ShapeDtypeStruct
    return pl.pallas_call(
        body,
        out_shape=[
            shape(w1.shape, WIDE),
            shape(w2.shape, WIDE),
            shape((units, channels), WIDE),
            shape((1, channels), WIDE),
        ],
        in_specs=[VMEM_SPACE] * 6,
        out_specs=[VMEM_SPACE] * 4,
        compiler_params=pltpu.CompilerParams(vmem_limit_bytes=LIMIT),
        cost_estimate=cost(9),
    )(table, w1, w2, vec, ft3, lags)


def norm_parts(values):
    mean = jnp.mean(values, axis=-1, keepdims=True)
    centered = values - mean
    variance = jnp.mean(centered * centered, axis=-1, keepdims=True)
    scale = lax.rsqrt(variance + EPSILON)
    return centered * scale, scale


def gather_out(copies, refs, row, dp_offsets, target):
    started, at = [], 0
    for ref in refs:
        for i in range(ref.shape[0]):
            for r, offset in enumerate(dp_offsets):
                started.append(copies.start(ref.at[i, r], target.at[at, row ^ offset]))
            at += 1
    return started


def branch_call(row, inputs, gated_parts, out_pieces, dp_offsets, rows):
    blocks = len(gated_parts)
    tokens, channels = gated_parts[0].shape
    width = inputs.shape[-1]
    shard = out_pieces[0].shape[2]
    count_dp = len(dp_offsets)

    def body(row_ref, in_ref, bias_ref, gain_ref, shift_ref, *refs):
        gated_refs, piece_refs = refs[:blocks], refs[blocks : blocks + len(out_pieces)]
        resid_ref, normed_ref, weights, sems = refs[blocks + len(out_pieces) :]
        copies = Copies(sems)
        waiting = gather_out(copies, piece_refs, row_ref[0], dp_offsets, weights)
        for copy in waiting:
            copy.wait()
        total = in_ref[...].astype(WIDE) + bias_ref[...]
        for i in range(blocks):
            total = total + dot_last(
                gated_refs[i][...], weights[i].reshape(width, channels)
            )
        resid_ref[...] = total
        normal, _ = norm_parts(total)
        normed_ref[...] = (normal * gain_ref[...] + shift_ref[...]).astype(LOW)

    shape = jax.ShapeDtypeStruct
    return pl.pallas_call(
        body,
        out_shape=[shape((tokens, width), WIDE), shape((tokens, width), LOW)],
        in_specs=[SMEM_SPACE] + [VMEM_SPACE] * (4 + blocks) + [ANY_SPACE] * len(out_pieces),
        out_specs=[VMEM_SPACE] * 2,
        scratch_shapes=[
            pltpu.VMEM((blocks, count_dp, shard, channels), LOW),
            pltpu.SemaphoreType.DMA((blocks * count_dp,)),
        ],
        compiler_params=pltpu.CompilerParams(vmem_limit_bytes=LIMIT),
        cost_estimate=cost(1),
    )(row, inputs, *rows, *gated_parts, *out_pieces)


def branch_back_call(row, resid, kept, arrived, cot, out_pieces, dp_offsets, gain):
    tokens, width = resid.shape
    blocks = sum(piece.shape[0] for piece in out_pieces)
    shard, channels = out_pieces[0].shape[2:]
    count_dp = len(dp_offsets)

    def body(row_ref, resid_ref, kept_ref, arrived_ref, cot_ref, gain_ref, *refs):
        piece_refs, refs = refs[: len(out_pieces)], refs[len(out_pieces) :]
        grad_refs, (whole_ref, branch_ref, sums, weights, sems) = refs[:blocks], refs[blocks:]
        copies = Copies(sems)
        waiting = gather_out(copies, piece_refs, row_ref[0], dp_offsets, weights)
        grad = kept_ref[...].astype(WIDE) + arrived_ref[...].astype(WIDE)
        normal, scale = norm_parts(resid_ref[...])
        scaled = grad * gain_ref[...]
        back = scaled - jnp.mean(scaled, axis=-1, keepdims=True)
        back = back - normal * jnp.mean(scaled * normal, axis=-1, keepdims=True)
        whole = cot_ref[...].astype(WIDE) + back * scale
        whole_ref[...] = whole
        low = whole.astype(LOW)
        branch_ref[...] = low
        sums[0:1, :] = jnp.sum(low.astype(WIDE), axis=0, keepdims=True)
        sums[1:2, :] = jnp.sum(grad * normal, axis=0, keepdims=True)
        sums[2:3, :] = jnp.sum(grad, axis=0, keepdims=True)
        sums[3:4, :] = jnp.sum(cot_ref[...].astype(WIDE), axis=0, keepdims=True)
        for copy in waiting:
            copy.wait()
        for i in range(blocks):
            grad_refs[i][...] = dot_plain(low, weights[i].reshape(width, channels)).astype(LOW)

    shape = jax.ShapeDtypeStruct
    return pl.pallas_call(
        body,
        out_shape=[shape((tokens, channels), LOW)] * blocks
        + [shape((tokens, width), WIDE), shape((tokens, width), LOW), shape((4, width), WIDE)],
        in_specs=[SMEM_SPACE] + [VMEM_SPACE] * 5 + [ANY_SPACE] * len(out_pieces),
        out_specs=[VMEM_SPACE] * (blocks + 3),
        scratch_shapes=[
            pltpu.VMEM((blocks, count_dp, shard, channels), LOW),
            pltpu.SemaphoreType.DMA((blocks * count_dp,)),
        ],
        compiler_params=pltpu.CompilerParams(vmem_limit_bytes=LIMIT),
        cost_estimate=cost(1),
    )(row, resid, kept, arrived, cot, gain, *out_pieces)


def out_grad_call(row, grad_branch, gated_parts, dp_offsets):
    blocks = len(gated_parts)
    tokens, channels = gated_parts[0].shape
    width = grad_branch.shape[1]
    count_dp = len(dp_offsets)
    shard = width // count_dp
    half = blocks // 2

    def body(row_ref, grad_ref, *refs):
        gated_refs, (kept, sent, total) = refs[:blocks], refs[blocks:]
        for i in range(blocks):
            total[...] = dot_first(grad_ref[...], gated_refs[i][...]).astype(LOW)
            target, at = (kept, i) if i < half else (sent, i - half)
            for r, offset in enumerate(dp_offsets):
                begin = pl.multiple_of((row_ref[0] ^ offset) * shard, shard)
                target[at * count_dp + r] = total[pl.ds(begin, shard)]

    out = jax.ShapeDtypeStruct((half * count_dp, shard, channels), LOW)
    return pl.pallas_call(
        body,
        out_shape=[out, out],
        in_specs=[SMEM_SPACE] + [VMEM_SPACE] * (1 + blocks),
        out_specs=[VMEM_SPACE] * 2,
        scratch_shapes=[pltpu.VMEM((width, channels), LOW)],
        compiler_params=pltpu.CompilerParams(vmem_limit_bytes=LIMIT),
        cost_estimate=cost(3),
    )(row, grad_branch, *gated_parts)


def forward_call(row, normed_pieces, cot_pieces, up_pieces, down_pieces, up_offsets, down_offsets, bias):
    tokens, width = normed_pieces[0].shape[1:]
    blocks = sum(piece.shape[0] for piece in normed_pieces)
    count_dp = len(up_offsets)
    piece = up_pieces[0].shape[1]
    shard = down_pieces[0].shape[1]
    units = piece * count_dp
    tile = 256 if units % 256 == 0 else units
    half = blocks // 2
    lists = (normed_pieces, cot_pieces, up_pieces, down_pieces)
    counts = [len(part) for part in lists]

    def body(row_ref, bias_ref, *refs):
        taken = []
        for count in counts:
            taken.append(refs[:count])
            refs = refs[count:]
        out_kept, out_sent, grad_kept, grad_sent, act_out, hid_out, sums = refs[:7]
        norm, cot, up, down, act, hid, sems = refs[7:]
        copies = Copies(sems)
        norm_copies = gather_in(copies, taken[0], 0, range(blocks), norm)
        up_copies = gather_in(copies, taken[2], row_ref[0], up_offsets, up)
        cot_copies = gather_in(copies, taken[1], 0, range(blocks), cot)
        down_copies = gather_in(copies, taken[3], row_ref[0], down_offsets, down)
        for copy in norm_copies + up_copies:
            copy.wait()
        up_rows = up[...].reshape(units, width)
        first = dot_last(norm[0], up_rows[:tile])
        for copy in cot_copies + down_copies:
            copy.wait()
        down_rows = down[...].reshape(width, units)
        for f in range(units // tile):
            lanes = slice(f * tile, (f + 1) * tile)
            total = jnp.zeros((1, tile), WIDE)
            for t in range(blocks):
                hidden = first if f == t == 0 else dot_last(norm[t], up_rows[lanes])
                hidden = hidden + bias_ref[:, lanes]
                grad = dot_plain(cot[t], down_rows[:, lanes])
                below = 0.5 * (1.0 + lax.erf(hidden * math.sqrt(0.5)))
                slope = below + hidden * (
                    jnp.exp(-0.5 * hidden * hidden) * (1.0 / math.sqrt(2.0 * math.pi))
                )
                act[t, :, lanes] = (hidden * below).astype(LOW)
                grad = (grad * slope).astype(LOW)
                hid[t, :, lanes] = grad
                total = total + jnp.sum(grad.astype(WIDE), axis=0, keepdims=True)
            sums[:, lanes] = total
        leaving = [copies.start(act, act_out), copies.start(hid, hid_out)]
        for t in range(blocks):
            back = dot_plain(hid[t], up_rows).astype(LOW)
            out = dot_last(act[t], down_rows).astype(LOW)
            if t < half:
                grad_kept[t] = back
                out_kept[t] = out
            else:
                grad_sent[t - half] = back
                out_sent[t - half] = out
        for copy in leaving:
            copy.wait()

    shape = jax.ShapeDtypeStruct
    part = shape((half, tokens, width), LOW)
    return pl.pallas_call(
        body,
        out_shape=[part] * 4
        + [shape((blocks, tokens, units), LOW)] * 2
        + [shape((1, units), WIDE)],
        in_specs=[SMEM_SPACE, VMEM_SPACE] + [ANY_SPACE] * sum(counts),
        out_specs=[VMEM_SPACE] * 4 + [ANY_SPACE] * 2 + [VMEM_SPACE],
        scratch_shapes=[
            pltpu.VMEM((blocks, tokens, width), LOW),
            pltpu.VMEM((blocks, tokens, width), LOW),
            pltpu.VMEM((count_dp, piece, width), LOW),
            pltpu.VMEM((count_dp, shard, units), LOW),
            pltpu.VMEM((blocks, tokens, units), LOW),
            pltpu.VMEM((blocks, tokens, units), LOW),
            pltpu.SemaphoreType.DMA((2 * blocks + 2 * count_dp + 2,)),
        ],
        compiler_params=pltpu.CompilerParams(vmem_limit_bytes=LIMIT),
        cost_estimate=cost(17),
    )(row, bias, *normed_pieces, *cot_pieces, *up_pieces, *down_pieces)


def weight_grad_call(row, pairs, offset_lists):
    blocks = sum(array.shape[0] for array in pairs[0][0])
    _, tokens, rows = pairs[0][0][0].shape
    width = pairs[0][1][0].shape[2]
    count_dp = len(offset_lists[0])
    quarter, share = count_dp // 4, rows // count_dp
    half = blocks // 2
    tile = 256 if rows % 256 == 0 else rows
    count = len(pairs)
    arrays = [array for pair in pairs for side in pair for array in side]

    def body(row_ref, *refs):
        sources, targets = list(refs[: len(arrays)]), refs[len(arrays) : len(arrays) + 4 * count]
        refs = refs[len(arrays) + 4 * count :]
        totals, sems = refs[:count], refs[count]
        copies = Copies(sems)
        leaving = []

        def part(side, number, lanes):
            ref, at = (side[0], number * half) if len(side) == 1 else (side[number], 0)
            return ref[at : at + half, :, lanes].reshape(half * tokens, -1)

        for p, pair in enumerate(pairs):
            left, right = ([sources.pop(0) for _ in side] for side in pair)
            total = totals[p]
            rights = [part(right, number, slice(0, width)) for number in range(2)]
            for c in range(rows // tile):
                lanes = slice(c * tile, (c + 1) * tile)
                total[lanes] = (
                    dot_first(part(left, 0, lanes), rights[0])
                    + dot_first(part(left, 1, lanes), rights[1])
                ).astype(LOW)
            for index, offset in enumerate(offset_lists[p]):
                begin = pl.multiple_of((row_ref[0] ^ offset) * share, share)
                target = targets[4 * p + index // quarter].at[index % quarter]
                leaving.append(copies.start(total.at[pl.ds(begin, share)], target))
        for copy in leaving:
            copy.wait()

    return pl.pallas_call(
        body,
        out_shape=[jax.ShapeDtypeStruct((quarter, share, width), LOW)] * (4 * count),
        in_specs=[SMEM_SPACE] + [VMEM_SPACE] * len(arrays),
        out_specs=[ANY_SPACE] * (4 * count),
        scratch_shapes=[pltpu.VMEM((rows, width), LOW)] * count
        + [pltpu.SemaphoreType.DMA((count * count_dp,))],
        compiler_params=pltpu.CompilerParams(vmem_limit_bytes=LIMIT),
        cost_estimate=cost(11),
    )(row, *arrays)


def iota(shape, dim):
    return lax.broadcasted_iota(jnp.int32, shape, dim)


def eye_low(size):
    return jnp.where(iota((size, size), 0) == iota((size, size), 1), 1.0, 0.0).astype(LOW)


def turn(values):
    return values.astype(WIDE).T


def own_channel(index, place, blocks, share):
    return (index // share) * (share * blocks) + place * share + index % share


def first_call(places, blocks, share, w_in, w_out, inputs, rows, parts):
    width, shard = w_in.shape
    shard_out = w_out.shape[1]
    tokens = inputs.shape[0]
    here = shard // blocks
    size = here // parts
    channels = width // blocks

    def body(place_ref, w_ref, out_ref, in_ref, gain_ref, shift_ref, *refs):
        part_refs, (out_own, normed_ref, picked) = refs[:parts], refs[parts:]
        place = place_ref[1]
        shape = (here, shard)
        chosen = own_channel(iota(shape, 0), place, blocks, share) == iota(shape, 1)
        chosen = jnp.where(chosen, 1.0, 0.0).astype(LOW)
        turned = dot_last(chosen, w_ref[...]).astype(LOW)
        for i in range(parts):
            part_refs[i][0] = turned[i * size : (i + 1) * size]
        for j in range(channels // share):
            begin = pl.multiple_of(j * share * blocks + place * share, share)
            picked[j * share : (j + 1) * share] = out_ref[pl.ds(begin, share)]
        out_own[0] = turn(picked[...]).astype(LOW)
        normal, _ = norm_parts(in_ref[...].astype(WIDE))
        normed_ref[0] = (normal * gain_ref[...] + shift_ref[...]).astype(LOW)

    shape = jax.ShapeDtypeStruct
    return pl.pallas_call(
        body,
        out_shape=[shape((1, size, width), LOW)] * parts
        + [shape((1, shard_out, channels), LOW), shape((1, tokens, width), LOW)],
        in_specs=[SMEM_SPACE] + [VMEM_SPACE] * 5,
        out_specs=[VMEM_SPACE] * (parts + 2),
        scratch_shapes=[pltpu.VMEM((channels, shard_out), LOW)],
        compiler_params=pltpu.CompilerParams(vmem_limit_bytes=WHOLE),
        cost_estimate=cost(3),
    )(places, w_in, w_out, inputs, *rows)


def second_call(places, blocks, share, w_up, w_down, b_up, vectors, layers, third):
    width, shard_up = w_up.shape
    piece = shard_up // blocks
    hidden, shard_down = w_down.shape
    count_dp = hidden // shard_up
    channels = width // blocks
    arrays = [array for array, _ in vectors] + [third]
    spans = [rows for _, rows in vectors] + [third.shape[0]]
    used = sum(spans)
    total = -(-used // 8) * 8
    flat_layers = [array for layer in layers for array in layer]
    heights = [weights.shape[0] for weights, _ in layers]

    def body(place_ref, up_ref, down_ref, bias_ref, *refs):
        vec_refs, refs = refs[: len(arrays)], refs[len(arrays) :]
        layer_refs, refs = refs[: len(flat_layers)], refs[len(flat_layers) :]
        up_own, down_own, bias_own, vec_own = refs[:4]
        aug_refs, (up, down, held, sems) = refs[4 : 4 + len(layers)], refs[4 + len(layers) :]
        place = place_ref[1]
        copies = Copies(sems)
        begin = pl.multiple_of(place * piece, piece)
        waiting = [copies.start(up_ref.at[:, pl.ds(begin, piece)], up)]
        for k in range(count_dp):
            rows = pl.ds(pl.multiple_of(k * shard_up + place * piece, piece), piece)
            waiting.append(copies.start(down_ref.at[rows], down.at[pl.ds(k * piece, piece)]))
        for k in range(count_dp):
            lanes = pl.ds(pl.multiple_of(k * shard_up + place * piece, piece), piece)
            bias_own[:, k * piece : (k + 1) * piece] = bias_ref[:, lanes]
        held[used:, :] = jnp.zeros((total - used, width), WIDE)
        at = 0
        for (ref, span) in zip(vec_refs, spans):
            count = ref.shape[0]
            if ref.shape[1] == width:
                held[at : at + count, :] = ref[...]
            else:
                for i in range(count):
                    for j in range(span // count):
                        row = at + i * (span // count) + j
                        held[row : row + 1, :] = ref[i : i + 1, j * width : (j + 1) * width]
            at += span
        shape = (width, channels)
        chosen = iota(shape, 0) == own_channel(iota(shape, 1), place, blocks, share)
        vec_own[...] = dot_high(held[...], jnp.where(chosen, 1.0, 0.0))
        for i, height in enumerate(heights):
            weights, bias, target = layer_refs[2 * i], layer_refs[2 * i + 1], aug_refs[i]
            target[...] = jnp.zeros(target.shape, WIDE)
            target[:height, :] = weights[...]
            target[height : height + 1, :] = bias[...]
        for copy in waiting:
            copy.wait()
        up_own[0] = turn(up[...]).astype(LOW)
        down_own[0] = turn(down[...]).astype(LOW)

    shape = jax.ShapeDtypeStruct
    return pl.pallas_call(
        body,
        out_shape=[
            shape((1, piece, width), LOW),
            shape((1, shard_down, piece * count_dp), LOW),
            shape((1, piece * count_dp), WIDE),
            shape((total, channels), WIDE),
        ]
        + [shape((-(-(height + 1) // 8) * 8, layer[0].shape[1]), WIDE) for height, layer in zip(heights, layers)],
        in_specs=[SMEM_SPACE, ANY_SPACE, ANY_SPACE]
        + [VMEM_SPACE] * (1 + len(arrays) + len(flat_layers)),
        out_specs=[VMEM_SPACE] * (4 + len(layers)),
        scratch_shapes=[
            pltpu.VMEM((width, piece), LOW),
            pltpu.VMEM((piece * count_dp, shard_down), LOW),
            pltpu.VMEM((total, width), WIDE),
            pltpu.SemaphoreType.DMA((1 + count_dp,)),
        ],
        compiler_params=pltpu.CompilerParams(vmem_limit_bytes=LIMIT),
        cost_estimate=cost(4),
    )(places, w_up, w_down, b_up, *arrays, *flat_layers)


def spread_pieces(refs):
    return [ref.at[i] for ref in refs for i in range(ref.shape[0])]


def wide_call(places, offsets, pieces, piece, count_dp):
    total, width = pieces[0].shape[1:]
    shard = total - piece
    units = piece * count_dp
    blocks = len(offsets)

    def body(place_ref, *refs):
        sources = spread_pieces(refs[: len(pieces)])
        up_out, down_out = refs[len(pieces) :]
        for source, offset in zip(sources, offsets):
            place = place_ref[1] ^ offset
            up_out[:, pl.ds(pl.multiple_of(place * piece, piece), piece)] = turn(source[:piece])
            down = turn(source[piece:])
            for k in range(count_dp):
                rows = pl.ds(pl.multiple_of((k * blocks + place) * piece, piece), piece)
                down_out[rows] = down[k * piece : (k + 1) * piece]

    shape = jax.ShapeDtypeStruct
    return pl.pallas_call(
        body,
        out_shape=[
            shape((width, piece * blocks), WIDE),
            shape((units * blocks, shard), WIDE),
        ],
        in_specs=[SMEM_SPACE] + [VMEM_SPACE] * len(pieces),
        out_specs=[VMEM_SPACE] * 2,
        compiler_params=pltpu.CompilerParams(vmem_limit_bytes=LIMIT),
        cost_estimate=cost(8),
    )(places, *pieces)


def in_wide_call(places, offsets, share, pieces):
    here, width = pieces[0].shape[1:]
    blocks = len(offsets)
    shard = here * blocks

    def body(place_ref, *refs):
        out = refs[-1]
        total = None
        for index, ref in enumerate(spread_pieces(refs[:-1])):
            place = place_ref[1] ^ offsets[index]
            shape = (here, shard)
            chosen = own_channel(iota(shape, 0), place, blocks, share) == iota(shape, 1)
            chosen = jnp.where(chosen, 1.0, 0.0).astype(LOW)
            part = dot_first(ref[...], chosen)
            total = part if total is None else total + part
        out[...] = total

    return pl.pallas_call(
        body,
        out_shape=jax.ShapeDtypeStruct((width, shard), WIDE),
        in_specs=[SMEM_SPACE] + [VMEM_SPACE] * len(pieces),
        out_specs=VMEM_SPACE,
        compiler_params=pltpu.CompilerParams(vmem_limit_bytes=LIMIT),
        cost_estimate=cost(3),
    )(places, *pieces)


def out_wide_call(places, offsets, share, pieces):
    shard, channels = pieces[0].shape[1:]
    blocks = len(offsets)

    def body(place_ref, *refs):
        out = refs[-1]
        for index, ref in enumerate(spread_pieces(refs[:-1])):
            place = place_ref[1] ^ offsets[index]
            whole = turn(ref[...])
            for j in range(channels // share):
                rows = pl.ds(pl.multiple_of((j * blocks + place) * share, share), share)
                out[rows] = whole[j * share : (j + 1) * share]

    return pl.pallas_call(
        body,
        out_shape=jax.ShapeDtypeStruct((channels * blocks, shard), WIDE),
        in_specs=[SMEM_SPACE] + [VMEM_SPACE] * len(pieces),
        out_specs=VMEM_SPACE,
        compiler_params=pltpu.CompilerParams(vmem_limit_bytes=LIMIT),
        cost_estimate=cost(2),
    )(places, *pieces)


def small_pack_call(shared, layers, bias, sums, third, decay):
    channels = third.shape[1]
    width = shared[0].shape[1]
    cuts = width // channels
    arrays = list(shared) + list(layers) + [bias, sums, third, decay]
    rows = cuts * sum(array.shape[0] for array in shared)
    layer_rows = [-(-array.shape[0] // cuts // 8) * 8 for array in layers]
    bias_rows = bias.shape[1] // channels
    plain = rows + sum(layer_rows) + bias_rows + sums.shape[0] + third.shape[0] + 1
    total = -(-plain // 8) * 8

    def body(*refs):
        target = refs[-1]
        target[plain:, :] = jnp.zeros((total - plain, channels), WIDE)
        at = 0
        for ref in refs[: len(shared)]:
            for i in range(ref.shape[0]):
                for j in range(cuts):
                    target[at : at + 1, :] = ref[i : i + 1, j * channels : (j + 1) * channels]
                    at += 1
        for ref, height in zip(refs[len(shared) : len(shared) + len(layers)], layer_rows):
            lanes = ref.shape[1]
            target[at : at + height, :] = jnp.zeros((height, channels), WIDE)
            for j in range(cuts):
                size = min(height, ref.shape[0] - j * height)
                if size > 0:
                    target[at : at + size, j * lanes : (j + 1) * lanes] = ref[
                        j * height : j * height + size, :
                    ]
            at += height
        ref = refs[len(shared) + len(layers)]
        for j in range(bias_rows):
            target[at : at + 1, :] = ref[:, j * channels : (j + 1) * channels]
            at += 1
        for ref in refs[len(shared) + len(layers) + 1 : -1]:
            target[at : at + ref.shape[0], :] = ref[...]
            at += ref.shape[0]

    return pl.pallas_call(
        body,
        out_shape=jax.ShapeDtypeStruct((total, channels), WIDE),
        in_specs=[VMEM_SPACE] * len(arrays),
        out_specs=VMEM_SPACE,
        compiler_params=pltpu.CompilerParams(vmem_limit_bytes=LIMIT),
        cost_estimate=cost(2),
    )(*arrays)


def small_out_call(places, offsets, share, pieces, shared, layer_shapes, bias_width, shard_up):
    height, channels = pieces[0].shape[1:]
    blocks = len(offsets)
    width = channels * blocks
    piece = shard_up // blocks
    augmented = [-(-(shape[0] + 1) // 8) * 8 for shape in layer_shapes]
    layer_rows = [-(-rows // blocks // 8) * 8 for rows in augmented]
    bias_rows = bias_width // channels
    units = layer_shapes[1][1]

    def body(place_ref, *refs):
        sources = spread_pieces(refs[: len(pieces)])
        refs = refs[len(pieces) :]
        shared_refs, refs = refs[:shared], refs[shared:]
        layer_refs, refs = refs[: 2 * len(layer_shapes)], refs[2 * len(layer_shapes) :]
        bias_out, in_out, taps_out, short_out, direct_out, third_out, decay_out, held, placed = refs
        for source, offset in zip(sources, offsets):
            placed[place_ref[1] ^ offset] = source[...]
        total = placed[0]
        for i in range(1, blocks):
            total = total + placed[i]
        held[...] = total
        at = 0
        for ref in shared_refs:
            for j in range(blocks):
                ref[:, j * channels : (j + 1) * channels] = held[at : at + 1, :]
                at += 1
        for i, rows in enumerate(layer_rows):
            weights, bias = layer_refs[2 * i], layer_refs[2 * i + 1]
            lanes = weights.shape[1]
            for j in range(blocks):
                size = min(rows, weights.shape[0] - j * rows)
                if size > 0:
                    weights[j * rows : j * rows + size, :] = held[
                        at : at + size, j * lanes : (j + 1) * lanes
                    ]
                if 0 <= weights.shape[0] - j * rows < rows:
                    row = at + weights.shape[0] - j * rows
                    bias[...] = held[row : row + 1, j * lanes : (j + 1) * lanes]
            at += rows
        whole = None
        first = at
        for index, offset in enumerate(offsets):
            place = place_ref[1] ^ offset
            for j in range(bias_rows):
                line = sources[index][first + j : first + j + 1, :]
                for c in range(channels // piece):
                    k = j * (channels // piece) + c
                    lanes = pl.ds(pl.multiple_of((k * blocks + place) * piece, piece), piece)
                    bias_out[:, lanes] = line[:, c * piece : (c + 1) * piece]
            shape = (channels, width)
            chosen = own_channel(iota(shape, 0), place, blocks, share) == iota(shape, 1)
            part = dot_high(
                sources[index][first + bias_rows :, :], jnp.where(chosen, 1.0, 0.0)
            )
            whole = part if whole is None else whole + part
        for role in range(3):
            lanes = slice(role * width, (role + 1) * width)
            in_out[:, lanes] = whole[role : role + 1]
            for j in range(3):
                taps_out[j : j + 1, lanes] = whole[3 + 3 * j + role : 4 + 3 * j + role]
            short_out[:, lanes] = whole[12 + role : 13 + role]
        direct_out[...] = whole[15:16]
        third_out[...] = whole[16 : 16 + units]
        decay_out[...] = whole[16 + units : 17 + units]

    shape = jax.ShapeDtypeStruct
    layer_out = []
    for rows, lanes in layer_shapes:
        layer_out += [shape((rows, lanes), WIDE), shape((1, lanes), WIDE)]
    return pl.pallas_call(
        body,
        out_shape=[shape((1, width), WIDE)] * shared
        + layer_out
        + [
            shape((1, bias_width * blocks), WIDE),
            shape((1, 3 * width), WIDE),
            shape((3, 3 * width), WIDE),
            shape((1, 3 * width), WIDE),
            shape((1, width), WIDE),
            shape((units, width), WIDE),
            shape((1, width), WIDE),
        ],
        in_specs=[SMEM_SPACE] + [VMEM_SPACE] * len(pieces),
        out_specs=[VMEM_SPACE] * (shared + len(layer_out) + 7),
        scratch_shapes=[
            pltpu.VMEM((height, channels), WIDE),
            pltpu.VMEM((blocks, height, channels), WIDE),
        ],
        compiler_params=pltpu.CompilerParams(vmem_limit_bytes=LIMIT),
        cost_estimate=cost(5),
    )(places, *pieces)


def local_plain(
    block_in,
    doc_starts,
    norm1_gain,
    norm1_bias,
    w_in,
    b_in,
    short_taps,
    short_bias,
    filter_w1,
    filter_b1,
    filter_w2,
    filter_b2,
    filter_w3,
    filter_decay,
    conv_bias,
    w_out,
    b_out,
    norm2_gain,
    norm2_bias,
    w_up,
    b_up,
    w_down,
    b_down,
    cotangent,
):
    count_dp, blocks = lax.axis_size("dp"), lax.axis_size("block")
    grid = Grid(count_dp, blocks)
    row, place = grid.row, grid.place
    _, block_len, width = block_in.shape
    length = block_len * blocks
    hidden_width = w_up.shape[1] * count_dp
    hidden_here = hidden_width // blocks
    dp_steps = grid.dp_steps
    block_steps = grid.chip_steps + [grid.core_step]
    block_offsets = [b for _, b in offsets_of(block_steps)]

    def rotated(turn):
        turn = turn % len(dp_steps)
        return dp_steps[turn:] + dp_steps[:turn]

    def dp_offsets(steps):
        return [a for a, _ in offsets_of(steps)]

    shard_in, shard_out = w_in.shape[1], w_out.shape[1]
    group = math.gcd(width, shard_in)
    groups_here, share = shard_in // group, group // blocks
    channels = width // blocks
    bands = width // group
    vectors = jnp.concatenate(
        [
            b_in.reshape(3, width),
            short_taps.reshape(9, width),
            short_bias.reshape(3, width),
            filter_decay[None],
            conv_bias[None],
            filter_w3,
        ],
        axis=0,
    )
    vectors = lax.dynamic_index_in_dim(
        vectors.reshape(vectors.shape[0], bands, blocks, share), place, 2, keepdims=False
    ).reshape(vectors.shape[0], channels)
    b_in_here = vectors[:3].reshape(-1)
    taps = vectors[3:12].reshape(3, 3 * channels)
    short_shift = vectors[12:15].reshape(-1)
    decay_here, direct, third_here = vectors[15], vectors[16], vectors[17:]

    in_turned = w_in.T.reshape(groups_here, blocks, share, width)
    in_own = lax.dynamic_index_in_dim(in_turned, place, 1, keepdims=False)
    in_orders = [rotated(i) for i in range(groups_here)]
    in_rows = jnp.stack(
        [
            arrange(grid.gather(in_own[i], in_orders[i]), row, dp_offsets(in_orders[i]))
            for i in range(groups_here)
        ],
        axis=1,
    ).reshape(3 * channels, width)

    inputs = block_in.astype(WIDE).reshape(block_len, width)
    normed, norm1_back = jax.vjp(layer_norm, inputs, norm1_gain, norm1_bias)
    normed_low = normed.astype(LOW)
    normed_all = arrange(grid.gather(normed_low, block_steps), place, block_offsets).reshape(
        length, width
    )

    up_order, down_order, out_dp_order = rotated(1), rotated(2), rotated(0)
    piece = w_up.shape[1] // blocks
    up_own = lax.dynamic_slice_in_dim(w_up, place * piece, piece, 1).T
    up_rows = arrange(grid.gather(up_own, up_order), row, dp_offsets(up_order)).reshape(
        hidden_here, width
    )
    b_up_here = lax.dynamic_index_in_dim(
        b_up.reshape(count_dp, blocks, piece), place, 1, keepdims=False
    ).reshape(hidden_here)
    down_own = w_down.reshape(count_dp, blocks, piece, w_down.shape[1])
    down_own = lax.dynamic_index_in_dim(down_own, place, 1, keepdims=False)
    down_own = down_own.reshape(hidden_here, w_down.shape[1]).T
    down_rows = arrange(grid.gather(down_own, down_order), row, dp_offsets(down_order)).reshape(
        width, hidden_here
    )

    out_own = w_out.reshape(bands, blocks, share, shard_out)
    out_own = lax.dynamic_index_in_dim(out_own, place, 1, keepdims=False)
    out_own = out_own.reshape(channels, shard_out).T
    out_dealt = arrange(grid.gather(out_own, out_dp_order), row, dp_offsets(out_dp_order))
    out_rows = jnp.concatenate(grid.gather(out_dealt.reshape(width, channels), block_steps), axis=0)
    cot_flat = cotangent.reshape(block_len, width)
    cot_all = jnp.concatenate(grid.gather(cot_flat, block_steps), axis=0).reshape(length, width)

    forward_table, inverse_table, sign, edge = transform_tables(block_len)
    starts = doc_starts[0]
    positions = jnp.arange(length, dtype=jnp.int32)
    segment = jnp.sum((starts[None, :] <= positions[:, None]).astype(jnp.int32), axis=-1) - 1
    keep_one = jnp.concatenate([jnp.zeros((1,), WIDE), (segment[1:] == segment[:-1]).astype(WIDE)])
    keep_two = jnp.concatenate([jnp.zeros((2,), WIDE), (segment[2:] == segment[:-2]).astype(WIDE)])
    keep_one, keep_two = keep_one[:, None], keep_two[:, None]
    num_docs = doc_starts.shape[1]
    long_doc = jnp.sum((starts <= block_len).astype(jnp.int32)) - 1
    long_mask = (segment == long_doc).astype(WIDE)[:, None]
    first_segment, last_segment = segment[:block_len], segment[length - block_len :]
    short_early, short_masks = [], []
    for number in range(num_docs - 1):
        early = number < long_doc
        doc = jnp.where(early, number, number + 1)
        where = jnp.where(early, first_segment, last_segment)
        short_early.append(early.astype(WIDE))
        short_masks.append((where == doc).astype(WIDE)[:, None])

    def spread(values):
        masked = values * long_mask
        parts = [masked[i * block_len : (i + 1) * block_len] for i in range(blocks)]
        first, last = values[:block_len], values[length - block_len :]
        for early, mask in zip(short_early, short_masks):
            parts.append(mask * (early * first + (1.0 - early) * last))
        return jnp.concatenate(parts, axis=1)

    def collect(values):
        parts = [
            values[:, i * channels : (i + 1) * channels] for i in range(blocks + num_docs - 1)
        ]
        first, last = jnp.zeros_like(parts[0]), jnp.zeros_like(parts[0])
        for early, mask, part in zip(short_early, short_masks, parts[blocks:]):
            first = first + early * mask * part
            last = last + (1.0 - early) * mask * part
        joined = jnp.concatenate(parts[:blocks], axis=0) * long_mask
        middle = jnp.zeros((length - 2 * block_len, channels), WIDE)
        return joined + jnp.concatenate([first, middle, last], axis=0)

    def cut(values, count):
        return [values[:, i * channels : (i + 1) * channels] for i in range(count)]

    table, times = position_table(length, filter_w1.shape[0])

    def filter_spectra(params):
        first = jnp.sin(dot_high(table, params[0]) + params[1])
        second = jnp.sin(dot_high(first, params[2]) + params[3])
        kernel = dot_high(second, params[4]) * (
            jnp.exp(-times[:, None] * params[5][None, :]) + MOD_SHIFT
        )
        pieces = jnp.concatenate(
            [kernel[i * block_len : (i + 1) * block_len] for i in range(blocks)], axis=1
        )
        halves = dot_near(forward_table, pieces)
        earlier = jnp.concatenate(
            [jnp.zeros((2 * block_len, channels), WIDE), halves[:, : (blocks - 1) * channels]],
            axis=1,
        )
        return earlier + sign[:, None] * halves

    spectra_flat, filter_back = jax.vjp(
        filter_spectra,
        (filter_w1, filter_b1, filter_w2, filter_b2, third_here, decay_here),
    )
    spectra = cut(spectra_flat, blocks)

    proj = dot_last(normed_all, in_rows) + b_in_here
    three = 3 * channels
    prev_one = jnp.concatenate([jnp.zeros((1, three), WIDE), proj[:-1]], axis=0) * keep_one
    prev_two = jnp.concatenate([jnp.zeros((2, three), WIDE), proj[:-2]], axis=0) * keep_two
    short = short_shift + taps[0] * proj + taps[1] * prev_one + taps[2] * prev_two
    gate_part, mult, value = cut(short, 3)
    inner = value * mult

    entries = cut(dot_near(forward_table, spread(inner)), blocks + num_docs - 1)
    totals = []
    for i in range(blocks):
        total = spectral_product(entries[i], spectra[0], edge)
        for j in range(i):
            total = total + spectral_product(entries[j], spectra[i - j], edge)
        totals.append(total)
    for entry in entries[blocks:]:
        totals.append(spectral_product(entry, spectra[0], edge))
    mixed = collect(dot_near(inverse_table, jnp.concatenate(totals, axis=1))) + direct * inner
    gated_low = (gate_part * mixed).astype(LOW)

    gated_parts = []
    for offset in block_offsets:
        part = lax.dynamic_slice_in_dim(gated_low, (place ^ offset) * block_len, block_len, 0)
        gated_parts.append(grid.swap(part, (0, offset)) if offset else part)
    branch = b_out
    for part, rows in zip(gated_parts, out_rows):
        branch = branch + dot_last(part, rows)
    resid = inputs + branch
    normed2, norm2_back = jax.vjp(layer_norm, resid, norm2_gain, norm2_bias)
    normed2_low = normed2.astype(LOW)

    normed2_all = jnp.concatenate(grid.gather(normed2_low, block_steps), axis=0)
    normed2_all = normed2_all.reshape(length, width)
    hidden = dot_last(normed2_all, up_rows) + b_up_here
    act, gelu_back = jax.vjp(exact_gelu, hidden)
    act_low = act.astype(LOW)
    grad_act = dot_plain(cot_all, down_rows)
    grad_hidden = gelu_back(grad_act)[0].astype(LOW)

    def to_tokens(partial):
        split = partial.astype(LOW).reshape(blocks, block_len, width)
        return grid.scatter(split[: blocks // 2], split[blocks // 2 :], block_steps).astype(WIDE)

    grad_normed2 = to_tokens(dot_plain(grad_hidden, up_rows))
    output = resid + to_tokens(dot_last(act_low, down_rows)) + b_down
    block_out = output.astype(LOW)[None]
    grad_b_up_here = jnp.sum(grad_hidden.astype(WIDE), axis=0)
    grad_b_down = jnp.sum(cot_flat.astype(WIDE), axis=0)

    def send_home(natural, order):
        natural = natural.astype(LOW).reshape(count_dp, -1, natural.shape[-1])
        return grid.scatter(*deal(natural, row, dp_offsets(order)), order)

    up_grad = send_home(dot_first(grad_hidden, normed2_all), up_order)
    down_grad = send_home(dot_first(cot_all, act_low), down_order)

    resid_part, grad_gain_two, grad_bias_two = norm2_back(grad_normed2)
    grad_resid = cot_flat.astype(WIDE) + resid_part
    grad_branch = grad_resid.astype(LOW)
    grad_b_out = jnp.sum(grad_branch.astype(WIDE), axis=0)
    grad_parts = []
    for index, offset in enumerate(block_offsets):
        part = dot_plain(grad_branch, out_rows[index]).astype(LOW)
        grad_parts.append((grid.swap(part, (0, offset)) if offset else part)[None])
    grad_gated = arrange(grad_parts, place, block_offsets).reshape(length, channels).astype(WIDE)
    out_sums = jnp.stack([dot_first(grad_branch, part).astype(LOW) for part in gated_parts], axis=0)
    out_sums = grid.scatter(out_sums[: blocks // 2], out_sums[blocks // 2 :], block_steps)
    out_grad = send_home(out_sums, out_dp_order)

    grad_gate_part = grad_gated * mixed
    grad_mixed = grad_gated * gate_part
    grad_conv_bias = jnp.sum(grad_mixed * inner, axis=0)
    grad_totals = cut(
        lax.dot_general(
            inverse_table,
            spread(grad_mixed),
            (((0,), (0,)), ((), ())),
            precision=HIGH,
            preferred_element_type=WIDE,
        ),
        blocks + num_docs - 1,
    )
    grad_entries = []
    grad_lags = [None] * blocks
    for i in range(blocks + num_docs - 1):
        lag = spectral_back(grad_totals[i], entries[i], edge)
        grad_lags[0] = lag if grad_lags[0] is None else grad_lags[0] + lag
        grad_entries.append(spectral_back(grad_totals[i], spectra[0], edge))
    for j in range(blocks):
        for i in range(j + 1, blocks):
            grad_entries[j] = grad_entries[j] + spectral_back(
                grad_totals[i], spectra[i - j], edge
            )
            lag = spectral_back(grad_totals[i], entries[j], edge)
            grad_lags[i - j] = lag if grad_lags[i - j] is None else grad_lags[i - j] + lag
    filter_grads = filter_back(jnp.concatenate(grad_lags, axis=1))[0]
    grad_inner = (
        collect(
            lax.dot_general(
                forward_table,
                jnp.concatenate(grad_entries, axis=1),
                (((0,), (0,)), ((), ())),
                precision=HIGH,
                preferred_element_type=WIDE,
            )
        )
        + direct * grad_mixed
    )
    grad_short = jnp.concatenate([grad_gate_part, grad_inner * value, grad_inner * mult], axis=1)
    grad_taps = jnp.stack(
        [
            jnp.sum(grad_short * proj, axis=0),
            jnp.sum(grad_short * prev_one, axis=0),
            jnp.sum(grad_short * prev_two, axis=0),
        ],
        axis=0,
    )
    grad_short_bias = jnp.sum(grad_short, axis=0)
    pass_one = grad_short * keep_one
    pass_two = grad_short * keep_two
    grad_proj = (
        taps[0] * grad_short
        + taps[1] * jnp.concatenate([pass_one[1:], jnp.zeros((1, three), WIDE)], axis=0)
        + taps[2] * jnp.concatenate([pass_two[2:], jnp.zeros((2, three), WIDE)], axis=0)
    )
    grad_proj_low = grad_proj.astype(LOW)
    grad_b_in = jnp.sum(grad_proj_low.astype(WIDE), axis=0)
    grad_in_rows = dot_first(grad_proj_low, normed_all)
    grad_in_split = grad_in_rows.reshape(count_dp, groups_here, share, width)
    in_grads = [send_home(grad_in_split[:, i], in_orders[i]) for i in range(groups_here)]
    grad_normed_part = dot_plain(grad_proj_low, in_rows).astype(LOW)
    grad_normed = grid.scatter(
        *deal(grad_normed_part.reshape(blocks, block_len, width), place, block_offsets), block_steps
    ).astype(WIDE)
    input_part, grad_gain_one, grad_bias_one = norm1_back(grad_normed)
    grad_input = (grad_resid + input_part)[None]

    def all_places(value):
        return arrange(grid.gather(value, block_steps), place, block_offsets)

    in_whole = all_places(jnp.concatenate(in_grads, axis=0))
    in_whole = in_whole.reshape(blocks, groups_here, share, width)
    in_whole = in_whole.transpose(3, 1, 0, 2).reshape(width, shard_in).astype(WIDE)
    if up_grad.shape[1] == down_grad.shape[1]:
        ff_whole = all_places(jnp.concatenate([up_grad, down_grad], axis=0))
        up_whole, down_whole = ff_whole[:, :piece], ff_whole[:, piece:]
    else:
        up_whole, down_whole = all_places(up_grad), all_places(down_grad)
    up_whole = up_whole.reshape(blocks * piece, width).T.astype(WIDE)
    down_whole = down_whole.reshape(blocks, w_down.shape[1], count_dp, piece)
    down_whole = down_whole.transpose(2, 0, 3, 1).reshape(hidden_width, w_down.shape[1])
    down_whole = down_whole.astype(WIDE)
    out_whole = all_places(out_grad).reshape(blocks, shard_out, bands, share)
    out_whole = out_whole.transpose(2, 0, 3, 1).reshape(width, shard_out).astype(WIDE)

    shared = [
        grad_gain_one,
        grad_bias_one,
        grad_b_out,
        grad_gain_two,
        grad_bias_two,
        grad_b_down,
        filter_grads[0],
        filter_grads[1],
        filter_grads[2],
        filter_grads[3],
    ]
    flat = jnp.concatenate([item.reshape(-1) for item in shared])
    unit = blocks * channels
    chunk = -(-flat.shape[0] // unit)
    flat = jnp.pad(flat, (0, chunk * unit - flat.shape[0])).reshape(blocks, chunk, channels)
    dealt = [lax.dynamic_slice_in_dim(flat, place ^ offset, 1, 0) for offset in block_offsets]
    half = blocks // 2
    shared_part = grid.scatter(
        jnp.concatenate(dealt[:half], axis=0), jnp.concatenate(dealt[half:], axis=0), block_steps
    )
    joined = jnp.concatenate(
        [
            shared_part,
            jnp.pad(grad_b_up_here, (0, -hidden_here % channels)).reshape(-1, channels),
            grad_b_in.reshape(3, channels),
            grad_taps.reshape(9, channels),
            grad_short_bias.reshape(3, channels),
            filter_grads[5][None],
            grad_conv_bias[None],
            filter_grads[4],
        ],
        axis=0,
    )
    for step in dp_steps:
        joined = joined + grid.swap(joined, step)
    every = all_places(joined)
    whole_flat = every[:, :chunk].reshape(-1)
    shared_out, at = [], 0
    for item in shared:
        shared_out.append(whole_flat[at : at + item.size].reshape(item.shape))
        at += item.size
    at = chunk + -(-hidden_here // channels)
    grad_b_up = every[:, chunk:at].reshape(blocks, -1)[:, :hidden_here]
    grad_b_up = grad_b_up.reshape(blocks, count_dp, piece)
    grad_b_up = grad_b_up.transpose(1, 0, 2).reshape(hidden_width)
    rest = every[:, at:].reshape(blocks, -1, bands, share).transpose(1, 2, 0, 3)
    rest = rest.reshape(-1, width)
    return (
        block_out,
        grad_input,
        shared_out[0],
        shared_out[1],
        in_whole,
        rest[:3].reshape(3 * width),
        rest[3:12].reshape(3, 3 * width),
        rest[12:15].reshape(3 * width),
        shared_out[6],
        shared_out[7],
        shared_out[8],
        shared_out[9],
        rest[17:],
        rest[15],
        rest[16],
        out_whole,
        shared_out[2],
        shared_out[3],
        shared_out[4],
        up_whole,
        grad_b_up,
        down_whole,
        shared_out[5],
    )


def input_back_call(inputs, kept, arrived, gain, grad_resid):
    tokens, width = inputs.shape

    def body(in_ref, kept_ref, arrived_ref, gain_ref, resid_ref, out_ref):
        grad = kept_ref[...].astype(WIDE) + arrived_ref[...].astype(WIDE)
        normal, scale = norm_parts(in_ref[...].astype(WIDE))
        scaled = grad * gain_ref[...]
        back = scaled - jnp.mean(scaled, axis=-1, keepdims=True)
        back = back - normal * jnp.mean(scaled * normal, axis=-1, keepdims=True)
        out_ref[...] = resid_ref[...] + back * scale

    return pl.pallas_call(
        body,
        out_shape=jax.ShapeDtypeStruct((tokens, width), WIDE),
        in_specs=[VMEM_SPACE] * 5,
        out_specs=VMEM_SPACE,
        compiler_params=pltpu.CompilerParams(vmem_limit_bytes=LIMIT),
        cost_estimate=cost(4),
    )(inputs, kept, arrived, gain, grad_resid)


def mark_call(value):
    def body(in_ref, out_ref):
        out_ref[...] = in_ref[...]

    return pl.pallas_call(
        body,
        out_shape=jax.ShapeDtypeStruct(value.shape, value.dtype),
        in_specs=[VMEM_SPACE],
        out_specs=VMEM_SPACE,
        compiler_params=pltpu.CompilerParams(vmem_limit_bytes=LIMIT // 8),
        cost_estimate=cost(15),
    )(value)


def after(value, *others):
    return lax.optimization_barrier((value, *others))[0]


def together(values, *others):
    return lax.optimization_barrier((*values, *others))[: len(values)]


def local_kernels(
    block_in,
    doc_starts,
    norm1_gain,
    norm1_bias,
    w_in,
    b_in,
    short_taps,
    short_bias,
    filter_w1,
    filter_b1,
    filter_w2,
    filter_b2,
    filter_w3,
    filter_decay,
    conv_bias,
    w_out,
    b_out,
    norm2_gain,
    norm2_bias,
    w_up,
    b_up,
    w_down,
    b_down,
    cotangent,
):
    count_dp, blocks = lax.axis_size("dp"), lax.axis_size("block")
    grid = Grid(count_dp, blocks)
    row, place = grid.row, grid.place
    places = jnp.stack([row, place]).astype(jnp.int32)
    _, block_len, width = block_in.shape
    dp_steps = grid.dp_steps
    block_steps = grid.chip_steps + [grid.core_step]
    block_offsets = [b for _, b in offsets_of(block_steps)]
    shard_in = w_in.shape[1]
    share = math.gcd(width, shard_in) // blocks
    shard_up = w_up.shape[1]
    starts = doc_starts[0]
    inputs = block_in.reshape(block_len, width)
    cot = cotangent.reshape(block_len, width)
    forward_table, inverse_table, _, _ = transform_tables(block_len)
    forward_three, inverse_three = triple(forward_table), triple(inverse_table)
    forward_back, inverse_back = triple(forward_table.T), triple(inverse_table.T)
    table = turned_table(position_table(block_len * blocks, filter_w1.shape[0])[0])
    third_at = 17

    order_one = dp_steps[::-1]
    order_two = order_one[:-2] + order_one[:-3:-1]
    core_step = grid.core_step

    def dp_offsets(steps):
        return [a for a, _ in offsets_of(steps)]

    parts = 2
    in_orders = [order_one, order_two]
    in_offsets = [dp_offsets(order) for order in in_orders]
    up_order, down_order, out_order = order_one, order_two, order_one
    up_offsets, down_offsets, out_offsets = map(dp_offsets, (up_order, down_order, out_order))
    core, chip = core_step, block_steps[0]

    def joined(pieces):
        return jnp.concatenate(pieces, axis=0)

    def split(values, *counts):
        parts, at = [], 0
        for count in counts:
            parts.append(list(values[at : at + count]))
            at += count
        return parts

    *in_own, out_own, normed_own = first_call(
        places,
        blocks,
        share,
        w_in,
        w_out,
        inputs,
        (norm1_gain[None], norm1_bias[None]),
        parts,
    )
    in_got = [grid.swap(own, order[0]) for own, order in zip(in_own, in_orders)]
    normed_got = grid.swap(normed_own, chip)
    out_got = grid.swap(out_own, out_order[0])
    second = second_call(
        after(places, normed_own),
        blocks,
        share,
        w_up,
        w_down,
        b_up[None],
        [
            (b_in[None], 3),
            (short_taps, 9),
            (short_bias[None], 3),
            (filter_decay[None], 1),
            (conv_bias[None], 1),
        ],
        [(filter_w1, filter_b1[None]), (filter_w2, filter_b2[None])],
        filter_w3,
    )

    in_got, (out_got,), second = split(together((*in_got, out_got, *second)), parts, 1, 6)
    up_own, down_own, b_up_own, vectors, layer_one, layer_two = second
    in_held = [joined(pair) for pair in zip(in_own, in_got)]
    out_held = joined((out_own, out_got))
    in_got = [grid.swap(held, order[1]) for held, order in zip(in_held, in_orders)]
    out_got = grid.swap(out_held, out_order[1])
    up_got = grid.swap(up_own, up_order[0])
    spectra, layer_one = filter_call(
        block_len, blocks, table, forward_three, layer_one, layer_two, vectors, third_at
    )

    in_got, rest = split(
        together((*in_got, out_got, up_got, normed_got, layer_one, layer_two, down_own)), parts, 6
    )
    out_got, up_got, normed_got, layer_one, layer_two, down_own = rest
    in_last = [joined(pair) for pair in zip(in_held, in_got)]
    out_held = joined((out_held, out_got))
    up_held = joined((up_own, up_got))
    normed_held = joined((normed_own, normed_got))
    in_last_got = [grid.swap(held, order[2]) for held, order in zip(in_last, in_orders)]
    normed_last = grid.swap(normed_held, core)
    out_got = grid.swap(out_held, out_order[2])
    down_got = grid.swap(down_own, down_order[0])
    cot_own = after(cot, normed_got)[None]
    cot_got = grid.swap(cot_own, chip)
    layer_two = mark_call(layer_two)

    in_last_got, rest = split(
        together((*in_last_got, out_got, down_got, normed_last, cot_got, layer_two)), parts, 5
    )
    out_got, down_got, normed_last, cot_got, layer_two = rest
    down_held = joined((down_own, down_got))
    out_whole = joined((out_held, out_got))[None]
    cot_held = joined((cot_own, cot_got))
    up_two = grid.swap(up_held, up_order[1])
    down_two = grid.swap(down_held, down_order[1])
    out_got = grid.swap(out_whole, chip)
    cot_last = grid.swap(cot_held, core)
    made = conv_call(
        block_len,
        blocks,
        places,
        starts,
        [normed_held, normed_last],
        [list(pair) for pair in zip(in_last, in_last_got)],
        in_offsets,
        block_offsets,
        vectors,
        spectra,
        forward_three,
        inverse_three,
    )

    gated_own, (proj, entries, mixed, in_rows, normed) = made[:blocks], made[blocks:]
    gated_own, (up_two, down_two, out_got, cot_last, layer_two) = split(
        together((*gated_own, up_two, down_two, out_got, cot_last, layer_two)), blocks, 5
    )
    gated_got = [
        grid.swap(part, (0, offset)) for part, offset in zip(gated_own[1:], block_offsets[1:])
    ]
    out_held = joined((out_whole, out_got))
    out_last = grid.swap(out_held, core)
    up_three = grid.swap(up_held, up_order[2])
    down_three = grid.swap(down_held, down_order[2])
    layer_two = mark_call(layer_two)

    gated_got, (out_last, layer_two) = split(
        together((*gated_got, out_last, layer_two)), blocks - 1, 2
    )
    gated_parts = [gated_own[0], *gated_got]
    out_pieces = [out_held, out_last]
    resid, normed2 = branch_call(
        places,
        inputs,
        gated_parts,
        out_pieces,
        out_offsets,
        (b_out[None], norm2_gain[None], norm2_bias[None]),
    )
    normed2, up_three, down_three = together((normed2, up_three, down_three))
    normed2_got = grid.swap(normed2[None], chip)
    up_four = grid.swap(up_two, up_order[2])
    down_four = grid.swap(down_two, down_order[2])

    normed2_got, up_four, down_four = together((normed2_got, up_four, down_four))
    normed2_held = joined((normed2[None], normed2_got))
    normed2_last = grid.swap(normed2_held, core)
    made = forward_call(
        places,
        [normed2_held, normed2_last],
        [cot_held, cot_last],
        [up_held, up_two, up_three, up_four],
        [down_held, down_two, down_three, down_four],
        up_offsets,
        down_offsets,
        b_up_own,
    )
    block_kept, block_sent, grad_kept, grad_sent = made[:4]
    act, grad_hidden, b_up_sum = made[4:]

    grad_got = grid.swap(grad_sent, core)
    block_got = grid.swap(block_sent, core)

    grad_kept, grad_sent = halves(grad_kept, grad_got)
    grad_got = grid.swap(grad_sent, chip)
    dealt = weight_grad_call(
        after(places, grad_kept),
        [([grad_hidden], [normed2_held, normed2_last]), ([cot_held, cot_last], [act])],
        [up_offsets, down_offsets],
    )

    up_dealt, down_dealt = split(dealt, 4, 4)
    up_got = grid.swap(up_dealt[3], up_order[2])
    down_got = grid.swap(down_dealt[3], down_order[2])

    grad_got, block_got, *dealt = together(
        (grad_got, block_got, *up_dealt[:3], *down_dealt[:3])
    )
    up_dealt, down_dealt = split(dealt, 3, 3)
    made = branch_back_call(
        places, resid, grad_kept[0], grad_got[0], cot, out_pieces, out_offsets, norm2_gain[None]
    )
    grad_resid, grad_branch, norm2_sums = made[blocks:]
    made, (up_got, down_got, grad_branch) = split(
        together((*made[:blocks], up_got, down_got, grad_branch)), blocks, 3
    )
    grad_own = made[0]
    grad_got = [
        grid.swap(part, (0, offset)) for part, offset in zip(made[1:], block_offsets[1:])
    ]
    up_high = add_low(up_dealt[1], up_got)
    down_high = add_low(down_dealt[1], down_got)
    out_kept, out_sent = out_grad_call(places, grad_branch, gated_parts, out_offsets)

    grad_got, rest = split(
        together((*grad_got, out_kept, out_sent, block_kept, up_high, down_high)), blocks - 1, 5
    )
    out_kept, out_sent, block_kept, up_high, down_high = rest
    grad_parts = [grad_own, *grad_got]
    up_got = grid.swap(up_dealt[2], up_order[2])
    down_got = grid.swap(down_dealt[2], down_order[2])
    out_got = grid.swap(out_sent, core)
    block_kept, block_sent = halves(block_kept, block_got)
    block_got = grid.swap(block_sent, chip)
    grad_lags, direct_sum, grad_short = back_call(
        block_len,
        blocks,
        places,
        starts,
        grad_parts,
        block_offsets,
        vectors,
        spectra,
        proj,
        entries,
        mixed,
        inverse_back,
        forward_back,
    )

    up_got, down_got, out_got, block_got, direct_sum = together(
        (up_got, down_got, out_got, block_got, direct_sum)
    )
    up_low = add_low(up_dealt[0], up_got)
    down_low = add_low(down_dealt[0], down_got)
    out_kept, out_sent = halves(out_kept, out_got)
    up_got = grid.swap(up_high, up_order[1])
    down_got = grid.swap(down_high, down_order[1])
    out_got = grid.swap(out_sent, chip)
    made = project_back_call(
        block_len,
        blocks,
        places,
        starts,
        in_offsets,
        block_offsets,
        vectors,
        (norm1_gain[None], norm1_bias[None]),
        direct_sum,
        grad_short,
        proj,
        in_rows,
        normed,
    )

    made, (up_got, down_got, out_got, layer_one) = split(
        together((*made, up_got, down_got, out_got, layer_one)), len(made), 4
    )
    in_dealt = [(made[2 * i], made[2 * i + 1]) for i in range(parts)]
    normed_kept, normed_sent, sums, norm1_sums = made[2 * parts :]
    up_kept, up_sent = halves(up_low, up_got)
    down_kept, down_sent = halves(down_low, down_got)
    out_kept, out_sent = halves(out_kept, out_got)
    in_got = [grid.swap(pair[1], order[2]) for pair, order in zip(in_dealt, in_orders)]
    normed_got = grid.swap(normed_sent, core)
    up_got = grid.swap(up_sent, up_order[0])
    out_got = grid.swap(out_sent, out_order[2])
    layer_one_grad, layer_two_grad, third_grad, decay_grad = filter_back_call(
        block_len, blocks, table, forward_back, layer_one, layer_two, vectors, third_at, grad_lags
    )
    small = small_pack_call(
        [norm2_sums, norm1_sums],
        [layer_one_grad, layer_two_grad],
        b_up_sum,
        sums,
        third_grad,
        decay_grad,
    )

    in_got, (normed_got, up_got, out_got, small) = split(
        together((*in_got, normed_got, up_got, out_got, small)), parts, 4
    )
    in_half = [halves(pair[0], got) for pair, got in zip(in_dealt, in_got)]
    normed_kept, normed_sent = halves(normed_kept, normed_got)
    out_kept, out_sent = halves(out_kept, out_got)
    in_got = [grid.swap(pair[1], order[1]) for pair, order in zip(in_half, in_orders)]
    normed_got = grid.swap(normed_sent, chip)
    small_got = grid.swap(small, dp_steps[0])
    out_got = grid.swap(out_sent, out_order[1])
    down_got = grid.swap(down_sent, down_order[0])
    up_grad = add_low(up_kept, up_got)

    in_got, (normed_got, small_got, out_got, down_got) = split(
        together((*in_got, normed_got, small_got, out_got, down_got)), parts, 4
    )
    ff_own = jnp.concatenate([up_grad, add_low(down_kept, down_got)], axis=1)
    in_half = [halves(pair[0], got) for pair, got in zip(in_half, in_got)]
    out_kept, out_sent = halves(out_kept, out_got)
    small = small + small_got
    in_got = [grid.swap(pair[1], order[0]) for pair, order in zip(in_half, in_orders)]
    small_got = grid.swap(small, dp_steps[1])
    ff_got = grid.swap(ff_own, chip)
    out_got = grid.swap(out_sent, out_order[0])
    grad_input = input_back_call(
        inputs, normed_kept[0], normed_got[0], norm1_gain[None], grad_resid
    )[None]

    in_got, (small_got, ff_got, out_got, grad_input) = split(
        together((*in_got, small_got, ff_got, out_got, grad_input)), parts, 4
    )
    in_grad = jnp.concatenate(
        [add_low(pair[0], got) for pair, got in zip(in_half, in_got)], axis=1
    )
    out_grad = add_low(out_kept, out_got)
    small = small + small_got
    ff_held = joined((ff_own, ff_got))
    ff_last = grid.swap(ff_held, core)
    in_got = grid.swap(in_grad, chip)
    out_got = grid.swap(out_grad, chip)
    small_got = grid.swap(small, dp_steps[2])
    output = resid + block_kept[0].astype(WIDE) + block_got[0].astype(WIDE) + b_down
    block_out = output.astype(LOW)[None]

    ff_last, in_got, out_got, small_got, block_out = together(
        (ff_last, in_got, out_got, small_got, block_out)
    )
    in_held, out_held = joined((in_grad, in_got)), joined((out_grad, out_got))
    small = (small + small_got)[None]
    small_got = grid.swap(small, chip)
    in_last = grid.swap(in_held, core)
    out_last = grid.swap(out_held, core)
    up_whole, down_whole = wide_call(
        places, block_offsets, [ff_held, ff_last], up_own.shape[1], count_dp
    )

    small_got, in_last, out_last, up_whole = together((small_got, in_last, out_last, up_whole))
    small_held = joined((small, small_got))
    small_last = grid.swap(small_held, core)
    in_whole = in_wide_call(places, block_offsets, share, [in_held, in_last])
    out_whole = out_wide_call(places, block_offsets, share, [out_held, out_last])
    small_pieces = [small_held, small_last]
    (
        grad_b_out,
        grad_gain_two,
        grad_bias_two,
        grad_b_down,
        grad_gain_one,
        grad_bias_one,
        grad_w1,
        grad_b1,
        grad_w2,
        grad_b2,
        grad_b_up,
        grad_b_in,
        grad_taps,
        grad_short,
        grad_direct,
        grad_w3,
        grad_decay,
    ) = small_out_call(
        places,
        block_offsets,
        share,
        small_pieces,
        norm2_sums.shape[0] + norm1_sums.shape[0],
        [filter_w1.shape, filter_w2.shape],
        b_up_sum.shape[1],
        shard_up,
    )
    return (
        block_out,
        grad_input,
        grad_gain_one[0],
        grad_bias_one[0],
        in_whole,
        grad_b_in[0],
        grad_taps,
        grad_short[0],
        grad_w1,
        grad_b1[0],
        grad_w2,
        grad_b2[0],
        grad_w3,
        grad_decay[0],
        grad_direct[0],
        out_whole,
        grad_b_out[0],
        grad_gain_two[0],
        grad_bias_two[0],
        up_whole,
        grad_b_up[0],
        down_whole,
        grad_b_down[0],
    )


def local(*args):
    blocks, width, shard_in = lax.axis_size("block"), args[0].shape[2], args[4].shape[1]
    channels, group = width // blocks, math.gcd(width, shard_in)
    fits = (
        channels % 128 == 0
        and group // blocks % 32 == 0
        and shard_in // blocks % 32 == 0
        and args[19].shape[1] // blocks % 128 == 0
        and args[15].shape[1] % 128 == 0
        and args[10].shape[1] * blocks == channels
        and lax.axis_size("dp") > 1
    )
    return (local_kernels if fits else local_plain)(*args)


def solution(mesh):
    placed = (
        P("dp", "block", None),
        P("dp", None),
        P(),
        P(),
        P(None, "dp"),
        P(),
        P(),
        P(),
        P(),
        P(),
        P(),
        P(),
        P(),
        P(),
        P(),
        P(None, "dp"),
        P(),
        P(),
        P(),
        P(None, "dp"),
        P(),
        P(None, "dp"),
        P(),
        P("dp", "block", None),
    )
    return jax.shard_map(
        local,
        mesh=mesh,
        in_specs=placed,
        out_specs=(
            P("dp", "block", None),
            P("dp", "block", None),
            P(),
            P(),
            P(None, "dp"),
            P(),
            P(),
            P(),
            P(),
            P(),
            P(),
            P(),
            P(),
            P(),
            P(),
            P(None, "dp"),
            P(),
            P(),
            P(),
            P(None, "dp"),
            P(),
            P(None, "dp"),
            P(),
        ),
        check_vma=False,
    )
```

```python
import math

import jax
import jax.numpy as jnp
import ml_dtypes
import numpy as np
from jax import lax
from jax.experimental import pallas as pl
from jax.experimental.pallas import tpu as pltpu
from jax.sharding import PartitionSpec as P

EPSILON = 1e-05
MOD_SHIFT = 0.05
HIGHEST = lax.Precision.HIGHEST
HIGH = lax.Precision.HIGH
LOW = jnp.bfloat16
WIDE = jnp.float32


def dot_high(left, right):
    return jnp.dot(left, right, precision=HIGHEST, preferred_element_type=WIDE)


def dot_near(left, right):
    return jnp.dot(left, right, precision=HIGH, preferred_element_type=WIDE)


def dot_plain(left, right):
    return jnp.dot(left, right, preferred_element_type=WIDE)


def dot_first(left, right):
    return lax.dot_general(left, right, (((0,), (0,)), ((), ())), preferred_element_type=WIDE)


def dot_last(left, right):
    return lax.dot_general(left, right, (((1,), (1,)), ((), ())), preferred_element_type=WIDE)


def layer_norm(values, gain, bias):
    mean = jnp.mean(values, axis=-1, keepdims=True)
    centered = values - mean
    variance = jnp.mean(centered * centered, axis=-1, keepdims=True)
    return centered * lax.rsqrt(variance + EPSILON) * gain + bias


def exact_gelu(values):
    return jax.nn.gelu(values, approximate=False)


def position_table(length, emb_dim):
    bands = (emb_dim - 1) // 2
    sample = np.arange(length, dtype=np.float32)
    times = sample / np.float32(length - 1)
    frequency = np.linspace(0.0001, bands - 1, bands).astype(np.float32)
    angle = np.float32(2.0 * math.pi) * sample[:, None] * frequency[None, :] / np.float32(length)
    table = np.concatenate([times[:, None], np.cos(angle), -np.sin(angle)], axis=1)
    return (table.astype(np.float32), times)


def transform_tables(block_len):
    span = 2 * block_len
    frequency = np.arange(block_len)
    sample = np.arange(block_len)
    is_zero = (frequency == 0)[:, None]
    angle = 2.0 * math.pi * (frequency[:, None] * sample[None, :] % span) / span
    alternate = np.where(sample % 2 == 0, 1.0, -1.0)
    real_rows = np.cos(angle)
    imag_rows = np.where(is_zero, alternate[None, :], -np.sin(angle))
    forward_table = np.concatenate([real_rows, imag_rows], axis=0)
    outputs = sample + block_len
    out_angle = 2.0 * math.pi * (outputs[:, None] * frequency[None, :] % span) / span
    out_alternate = np.where(outputs % 2 == 0, 1.0, -1.0)
    zero_col = (frequency == 0)[None, :]
    real_cols = np.where(zero_col, 1.0, 2.0) * np.cos(out_angle) / span
    imag_cols = np.where(zero_col, out_alternate[:, None] / span, -2.0 * np.sin(out_angle) / span)
    inverse_table = np.concatenate([real_cols, imag_cols], axis=1)
    parity = np.where(frequency % 2 == 0, 1.0, -1.0)
    sign = np.concatenate([parity, np.where(frequency == 0, 1.0, parity)])
    edge = (frequency == 0).astype(np.float32)[:, None]
    return tuple(item.astype(np.float32) for item in (forward_table, inverse_table, sign, edge))


def spectral_product(left, right, edge):
    half = left.shape[-2] // 2
    left_re, left_im = (left[..., :half, :], left[..., half:, :])
    right_re, right_im = (right[..., :half, :], right[..., half:, :])
    inside = 1.0 - edge
    out_re = left_re * right_re - inside * left_im * right_im
    out_im = inside * (left_re * right_im + left_im * right_re) + edge * left_im * right_im
    return jnp.concatenate([out_re, out_im], axis=-2)


def spectral_back(grad, other, edge):
    half = grad.shape[-2] // 2
    grad_re, grad_im = (grad[..., :half, :], grad[..., half:, :])
    other_re, other_im = (other[..., :half, :], other[..., half:, :])
    inside = 1.0 - edge
    back_re = grad_re * other_re + inside * grad_im * other_im
    back_im = inside * (grad_im * other_re - grad_re * other_im) + edge * grad_im * other_im
    return jnp.concatenate([back_re, back_im], axis=-2)


class Grid:
    def __init__(self, count_dp, count_block):
        self.count_dp = count_dp
        self.count_block = count_block
        self.row = lax.axis_index("dp")
        self.place = lax.axis_index("block")
        self.dp_steps = []
        bit = 1
        while bit < count_dp:
            self.dp_steps.append((bit | (bit >> 1) if bit == 4 else bit, 0))
            bit *= 2
        self.chip_steps = []
        bit = 2
        while bit < count_block:
            self.chip_steps.append((0, bit | (bit >> 1) if bit == 4 else bit))
            bit *= 2
        self.core_step = (0, 1)

    def swap(self, value, step):
        pairs = []
        for row in range(self.count_dp):
            for place in range(self.count_block):
                to = (row ^ step[0]) * self.count_block + (place ^ step[1])
                pairs.append((row * self.count_block + place, to))
        return lax.ppermute(value, ("dp", "block"), pairs)

    def gather(self, value, steps, gates=()):
        held = value[None]
        pieces = [held]
        for number, step in enumerate(steps):
            if number < len(gates):
                held = after(held, *gates[number])
            pieces.append(self.swap(held, step))
            if number + 1 < len(steps):
                held = jnp.concatenate(pieces, axis=0)
        return pieces

    def scatter(self, kept, sent, steps, whole=True, sends=None, adds=None):
        for number, step in enumerate(reversed(steps)):
            if sends and number in sends:
                sent = after(sent, *sends[number])
            arrived = self.swap(sent, step)
            if adds and number in adds:
                arrived = after(arrived, *adds[number])
            half = kept.shape[0] // 2
            if not half and not whole:
                return kept[0], arrived[0]
            if half:
                sent = add_low(kept[half:], arrived[half:])
                kept = add_low(kept[:half], arrived[:half])
            else:
                kept = add_low(kept, arrived)
        return kept[0]

    def halve(self, kept, sent, step):
        return halves(kept, self.swap(sent, step))


def halves(left, right):
    half = left.shape[0] // 2
    return add_low(left[:half], right[:half]), add_low(left[half:], right[half:])


def add_low(left, right):
    return (left.astype(WIDE) + right.astype(WIDE)).astype(left.dtype)


def offsets_of(steps):
    offsets = [(0, 0)]
    for step in steps:
        offsets = offsets + [(a ^ step[0], b ^ step[1]) for a, b in offsets]
    return offsets


def arrange(pieces, mine, offsets):
    shape = pieces[0].shape[1:]
    if shape[-2] % 32 or shape[-1] % 128:
        held = jnp.concatenate(pieces, axis=0)
        codes = codes_of(offsets, len(offsets))
        return jnp.concatenate(
            [
                lax.dynamic_slice_in_dim(held, place_in(codes, k ^ mine), 1, 0)
                for k in range(len(offsets))
            ],
            axis=0,
        )
    count = len(pieces)

    def kernel(mine_ref, *refs):
        source, target = refs[:count], refs[count]
        at = 0
        for ref in source:
            for i in range(ref.shape[0]):
                target[mine_ref[0] ^ offsets[at]] = ref[i]
                at += 1

    return pl.pallas_call(
        kernel,
        out_shape=jax.ShapeDtypeStruct((len(offsets), *shape), pieces[0].dtype),
        in_specs=[pl.BlockSpec(memory_space=pltpu.SMEM)]
        + [pl.BlockSpec(memory_space=pltpu.VMEM)] * count,
        out_specs=pl.BlockSpec(memory_space=pltpu.VMEM),
    )(jnp.reshape(mine, (1,)).astype(jnp.int32), *pieces)


def deal(natural, mine, offsets):
    half = len(offsets) // 2
    shape = natural.shape[1:]
    if shape[-2] % 32 or shape[-1] % 128:
        dealt = [lax.dynamic_slice_in_dim(natural, mine ^ offset, 1, 0) for offset in offsets]
        return jnp.concatenate(dealt[:half], axis=0), jnp.concatenate(dealt[half:], axis=0)

    def kernel(mine_ref, source, kept, sent):
        for at, offset in enumerate(offsets):
            if at < half:
                kept[at] = source[mine_ref[0] ^ offset]
            else:
                sent[at - half] = source[mine_ref[0] ^ offset]

    out = jax.ShapeDtypeStruct((half, *shape), natural.dtype)
    vmem = pl.BlockSpec(memory_space=pltpu.VMEM)
    return pl.pallas_call(
        kernel,
        out_shape=(out, out),
        in_specs=[pl.BlockSpec(memory_space=pltpu.SMEM), vmem],
        out_specs=(vmem, vmem),
    )(jnp.reshape(mine, (1,)).astype(jnp.int32), natural)


def place_in(codes, offset):
    place = 0
    for j, code in enumerate(codes):
        place = place ^ (((offset >> j) & 1) * code)
    return place


def codes_of(offsets, count):
    codes, bit = [], 1
    while bit < count:
        codes.append(offsets.index(bit))
        bit *= 2
    return codes


def split_low(values):
    high = values.astype(LOW)
    return high, (values - high.astype(WIDE)).astype(LOW)


def triple(table):
    high = table.astype(ml_dtypes.bfloat16)
    low = (table - high.astype(np.float32)).astype(ml_dtypes.bfloat16)
    return np.concatenate([high, high, low], axis=1)


def store_triple(target, columns, values):
    high, low = split_low(values)
    size = values.shape[0]
    target[0:size, columns] = high
    target[size : 2 * size, columns] = low
    target[2 * size : 3 * size, columns] = high


def long_range(starts, count, block_len, length):
    begin, end, before = starts[0], jnp.int32(length), jnp.int32(-1)
    for d in range(count):
        begin = jnp.where(starts[d] <= block_len, starts[d], begin)
        before = before + jnp.where(starts[d] <= block_len, 1, 0)
    for d in reversed(range(count)):
        end = jnp.where(starts[d] > block_len, starts[d], end)
    return begin, end, before


def short_range(starts, count, number, before, block_len, length):
    early = number < before
    bounds = [starts[d] for d in range(count)] + [jnp.int32(length)]
    begin = jnp.where(early, bounds[number], bounds[number + 1])
    end = jnp.where(early, bounds[number + 1], bounds[number + 2])
    return begin, end, jnp.where(early, 0, length - block_len)


def rows_from(base, size, lanes):
    return lax.broadcasted_iota(jnp.int32, (size, lanes), 0) + base


def inside_mask(base, size, lanes, begin, end):
    rows = rows_from(base, size, lanes)
    return (rows >= begin) & (rows < end)


def keep_masks(starts, count, base, size, lanes):
    rows = rows_from(base, size, lanes)
    one = rows != starts[0]
    for d in range(1, count):
        one = one & (rows != starts[d])
    two = one
    for d in range(count):
        two = two & (rows != starts[d] + 1)
    return one, two


VMEM_SPACE = pl.BlockSpec(memory_space=pltpu.VMEM)
ANY_SPACE = pl.BlockSpec(memory_space=pl.ANY)
SMEM_SPACE = pl.BlockSpec(memory_space=pltpu.SMEM)
LIMIT = 30 * 1024 * 1024
WHOLE = 56 * 1024 * 1024


def cost(microseconds):
    return pl.CostEstimate(
        flops=int(microseconds * 1e9), bytes_accessed=int(microseconds * 3e6), transcendentals=0
    )


class Copies:
    def __init__(self, sems):
        self.sems, self.used = sems, 0

    def start(self, source, target):
        copy = pltpu.make_async_copy(source, target, self.sems.at[self.used])
        self.used += 1
        copy.start()
        return copy


def filter_kernel(block_len, blocks, table_ref, w1, w2, vec, third_at, f3_ref, spectra):
    length = block_len * blocks
    channels = vec.shape[1]
    one_row = jnp.where(lax.broadcasted_iota(jnp.int32, (8, length), 0) == 0, 1.0, 0.0)

    def turned(left, right):
        return lax.dot_general(
            left, right, (((0,), (0,)), ((), ())), precision=HIGHEST, preferred_element_type=WIDE
        )

    first = jnp.sin(turned(w1[...], table_ref[...]))
    second = jnp.sin(turned(w2[...], jnp.concatenate([first, one_row], axis=0)))
    decay = vec[third_at - 2 : third_at - 1, :]
    third_w = vec[third_at : third_at + second.shape[0], :]
    before = None
    half_rows = lax.broadcasted_iota(jnp.int32, (2 * block_len, channels), 0)
    parity = jnp.where(half_rows % 2 == 0, 1.0, -1.0)
    sign = jnp.where(half_rows == block_len, 1.0, parity)
    for i in range(blocks):
        part = turned(second[:, i * block_len : (i + 1) * block_len], third_w)
        times = rows_from(i * block_len, block_len, channels).astype(WIDE) / (length - 1)
        part = part * (jnp.exp(-times * decay) + MOD_SHIFT)
        high, low = split_low(part)
        stacked = jnp.concatenate([high, low, high], axis=0)
        half = jnp.dot(f3_ref[...], stacked, preferred_element_type=WIDE)
        spectra[i] = sign * half if before is None else before + sign * half
        before = half


def with_bias(weights, bias):
    rows = weights.shape[0]
    return jnp.pad(jnp.concatenate([weights, bias[None]], axis=0), ((0, -(rows + 1) % 8), (0, 0)))


def turned_table(table):
    length, count = table.shape
    rows = [table.T, np.ones((1, length), np.float32)]
    rows.append(np.zeros((-(count + 1) % 8, length), np.float32))
    return np.concatenate(rows, axis=0)


def filter_call(block_len, blocks, table, f3, w1, w2, vec, third_at):
    channels = vec.shape[1]

    def body(table_ref, w1_ref, w2_ref, vec_ref, f3_ref, spectra, mark):
        filter_kernel(
            block_len, blocks, table_ref, w1_ref, w2_ref, vec_ref, third_at, f3_ref, spectra
        )
        mark[...] = w1_ref[...]

    return pl.pallas_call(
        body,
        out_shape=[
            jax.ShapeDtypeStruct((blocks, 2 * block_len, channels), WIDE),
            jax.ShapeDtypeStruct(w1.shape, WIDE),
        ],
        in_specs=[VMEM_SPACE] * 5,
        out_specs=[VMEM_SPACE] * 2,
        compiler_params=pltpu.CompilerParams(vmem_limit_bytes=LIMIT),
        cost_estimate=cost(7),
    )(table, w1, w2, vec, f3)


def gather_in(copies, pieces, mine, offsets, target):
    started, at = [], 0
    for ref in pieces:
        for i in range(ref.shape[0]):
            started.append(copies.start(ref.at[i], target.at[mine ^ offsets[at]]))
            at += 1
    return started


def conv_call(
    block_len, blocks, places, starts, normed_pieces, in_pieces, in_offsets, block_offsets, vec, spectra, f3, i3
):
    length = block_len * blocks
    channels = vec.shape[1]
    docs = starts.shape[0]
    entries = blocks + docs - 1
    width = normed_pieces[0].shape[-1]
    groups = len(in_pieces)
    share = in_pieces[0][0].shape[1]
    count_dp = len(in_offsets[0])
    flat_in = [piece for pieces in in_pieces for piece in pieces]
    n_norm, n_in, n_out = len(normed_pieces), len(flat_in), blocks
    step = 16

    def body(place_ref, starts_ref, vec_ref, f3_ref, i3_ref, spectra_ref, *refs):
        norm_refs, in_refs = refs[:n_norm], refs[n_norm : n_norm + n_in]
        refs = refs[n_norm + n_in :]
        gated_refs, (proj_out, entry_out, mixed_out, rows_out, norm_out) = refs[:n_out], refs[n_out : n_out + 5]
        norm, rows, proj, inner, gate, xs, ent, ys, mixed, spec, sems = refs[n_out + 5 :]
        row, place = place_ref[0], place_ref[1]
        copies = Copies(sems)
        waiting = gather_in(copies, norm_refs, place, block_offsets, norm)
        at = 0
        for g in range(groups):
            count = len(in_pieces[g])
            index = 0
            for ref in in_refs[at : at + count]:
                for i in range(ref.shape[0]):
                    to = row ^ in_offsets[g][index]
                    waiting.append(copies.start(ref.at[i], rows.at[to, g]))
                    index += 1
            at += count
        spec_copy = copies.start(spectra_ref, spec)
        for copy in waiting:
            copy.wait()
        leaving = [copies.start(norm, norm_out), copies.start(rows, rows_out)]

        flat_rows = rows[...].reshape(3 * channels, width)
        for role in range(3):
            weights = flat_rows[role * channels : (role + 1) * channels]
            bias = vec_ref[role : role + 1, :]
            for b in range(blocks):
                proj[b * block_len : (b + 1) * block_len, role * channels : (role + 1) * channels] = (
                    lax.dot_general(
                        norm[b],
                        weights,
                        (((1,), (1,)), ((), ())),
                        preferred_element_type=WIDE,
                    )
                    + bias
                )
        leaving.append(copies.start(proj, proj_out))
        for b in range(blocks):
            base = b * block_len
            one, two = keep_masks(starts_ref, docs, base, block_len, channels)
            parts = []
            for role in range(3):
                lanes = slice(role * channels, (role + 1) * channels)
                here = proj[base : base + block_len, lanes]
                if b:
                    back = proj[base - 8 : base + block_len, lanes]
                    prev_one = pltpu.roll(back, 1, 0)[8:]
                    prev_two = pltpu.roll(back, 2, 0)[8:]
                else:
                    prev_one, prev_two = pltpu.roll(here, 1, 0), pltpu.roll(here, 2, 0)
                tap = [vec_ref[3 + 3 * j + role : 4 + 3 * j + role, :] for j in range(3)]
                short = (
                    vec_ref[12 + role : 13 + role, :]
                    + tap[0] * here
                    + tap[1] * jnp.where(one, prev_one, 0.0)
                    + tap[2] * jnp.where(two, prev_two, 0.0)
                )
                parts.append(short)
            gate[base : base + block_len] = parts[0]
            inner[base : base + block_len] = parts[1] * parts[2]
        begin, end, before = long_range(starts_ref, docs, block_len, length)
        for b in range(blocks):
            mask = inside_mask(b * block_len, block_len, channels, begin, end)
            part = jnp.where(mask, inner[b * block_len : (b + 1) * block_len], 0.0)
            store_triple(xs, slice(b * channels, (b + 1) * channels), part)
        for m in range(docs - 1):
            first, last, base = short_range(starts_ref, docs, m, before, block_len, length)
            base = pl.multiple_of(base, block_len)
            mask = inside_mask(base, block_len, channels, first, last)
            part = jnp.where(mask, inner[pl.ds(base, block_len)], 0.0)
            store_triple(xs, slice((blocks + m) * channels, (blocks + m + 1) * channels), part)
        for e in range(entries):
            ent[e] = jnp.dot(
                f3_ref[...], xs[:, e * channels : (e + 1) * channels], preferred_element_type=WIDE
            )
        leaving.append(copies.start(ent, entry_out))
        spec_copy.wait()

        @pl.loop(0, block_len // step)
        def _(number):
            at_re = pl.multiple_of(number * step, step)
            at_im = pl.multiple_of(number * step + block_len, step)
            edge = jnp.where(rows_from(at_re, step, channels) == 0, 1.0, 0.0)
            inside = 1.0 - edge
            keys = [(spec[k, pl.ds(at_re, step)], spec[k, pl.ds(at_im, step)]) for k in range(blocks)]
            held = [(ent[k, pl.ds(at_re, step)], ent[k, pl.ds(at_im, step)]) for k in range(blocks)]
            for e in range(entries):
                pairs = (
                    [(held[j], keys[e - j]) for j in range(e + 1)]
                    if e < blocks
                    else [((ent[e, pl.ds(at_re, step)], ent[e, pl.ds(at_im, step)]), keys[0])]
                )
                rr = ii = ri = None
                for (a, b), (c, d) in pairs:
                    rr = a * c if rr is None else rr + a * c
                    ii = b * d if ii is None else ii + b * d
                    ri = a * d + b * c if ri is None else ri + (a * d + b * c)
                lanes = slice(e * channels, (e + 1) * channels)
                out_re = rr - inside * ii
                out_im = inside * ri + edge * ii
                for part, at in ((out_re, at_re), (out_im, at_im)):
                    high, low = split_low(part)
                    ys[pl.ds(at, step), lanes] = high
                    ys[pl.ds(at + 2 * block_len, step), lanes] = low
                    ys[pl.ds(at + 4 * block_len, step), lanes] = high

        direct = vec_ref[16:17, :]
        for b in range(blocks):
            back = jnp.dot(
                i3_ref[...], ys[:, b * channels : (b + 1) * channels], preferred_element_type=WIDE
            )
            rows_here = slice(b * block_len, (b + 1) * block_len)
            mask = inside_mask(b * block_len, block_len, channels, begin, end)
            mixed[rows_here] = jnp.where(mask, back, 0.0) + direct * inner[rows_here]
        for m in range(docs - 1):
            lanes = slice((blocks + m) * channels, (blocks + m + 1) * channels)
            back = jnp.dot(i3_ref[...], ys[:, lanes], preferred_element_type=WIDE)
            first, last, base = short_range(starts_ref, docs, m, before, block_len, length)
            base = pl.multiple_of(base, block_len)
            mask = inside_mask(base, block_len, channels, first, last)
            where = pl.ds(base, block_len)
            mixed[where] = mixed[where] + jnp.where(mask, back, 0.0)
        leaving.append(copies.start(mixed, mixed_out))
        for index, offset in enumerate(block_offsets):
            where = pl.ds(pl.multiple_of((place ^ offset) * block_len, block_len), block_len)
            gated_refs[index][...] = (gate[where] * mixed[where]).astype(LOW)
        for copy in leaving:
            copy.wait()

    shape = jax.ShapeDtypeStruct
    sem_count = blocks + groups * count_dp + 6
    return pl.pallas_call(
        body,
        out_shape=[shape((block_len, channels), LOW)] * blocks
        + [
            shape((length, 3 * channels), WIDE),
            shape((entries, 2 * block_len, channels), WIDE),
            shape((length, channels), WIDE),
            shape((count_dp, groups, share, width), LOW),
            shape((blocks, block_len, width), LOW),
        ],
        in_specs=[SMEM_SPACE, SMEM_SPACE, VMEM_SPACE, VMEM_SPACE, VMEM_SPACE, ANY_SPACE]
        + [ANY_SPACE] * (n_norm + n_in),
        out_specs=[VMEM_SPACE] * blocks + [ANY_SPACE] * 5,
        scratch_shapes=[
            pltpu.VMEM((blocks, block_len, width), LOW),
            pltpu.VMEM((count_dp, groups, share, width), LOW),
            pltpu.VMEM((length, 3 * channels), WIDE),
            pltpu.VMEM((length, channels), WIDE),
            pltpu.VMEM((length, channels), WIDE),
            pltpu.VMEM((3 * block_len, entries * channels), LOW),
            pltpu.VMEM((entries, 2 * block_len, channels), WIDE),
            pltpu.VMEM((6 * block_len, entries * channels), LOW),
            pltpu.VMEM((length, channels), WIDE),
            pltpu.VMEM((blocks, 2 * block_len, channels), WIDE),
            pltpu.SemaphoreType.DMA((sem_count,)),
        ],
        compiler_params=pltpu.CompilerParams(vmem_limit_bytes=WHOLE),
        cost_estimate=cost(14),
    )(places, starts, vec, f3, i3, spectra, *normed_pieces, *flat_in)


def back_call(
    block_len,
    blocks,
    places,
    starts,
    grad_pieces,
    block_offsets,
    vec,
    spectra,
    proj,
    entries,
    mixed,
    it3,
    ft3,
):
    length = block_len * blocks
    channels = vec.shape[1]
    docs = starts.shape[0]
    count = entries.shape[0]
    three = 3 * channels
    step = 16

    def body(place_ref, starts_ref, vec_ref, it3_ref, ft3_ref, *refs):
        grad_refs, refs = refs[:blocks], refs[blocks:]
        spectra_ref, proj_ref, entry_ref, mixed_ref, lags, direct_out, gs_out = refs[:7]
        spec, proj, ent, mixed, gg, short, gs, gm, xs, gt, ys, gi, sems = refs[7:]
        place = place_ref[1]
        copies = Copies(sems)
        proj_copy = copies.start(proj_ref, proj)
        mixed_copy = copies.start(mixed_ref, mixed)
        spec_copy = copies.start(spectra_ref, spec)
        entry_copy = copies.start(entry_ref, ent)
        for index, offset in enumerate(block_offsets):
            where = pl.ds(pl.multiple_of((place ^ offset) * block_len, block_len), block_len)
            gg[where] = grad_refs[index][...]
        proj_copy.wait()
        mixed_copy.wait()
        direct = vec_ref[16:17, :]
        direct_sum = jnp.zeros((1, channels), WIDE)
        for b in range(blocks):
            base = b * block_len
            here = slice(base, base + block_len)
            one, two = keep_masks(starts_ref, docs, base, block_len, channels)
            parts = []
            for role in range(3):
                lanes = slice(role * channels, (role + 1) * channels)
                now = proj[here, lanes]
                if b:
                    back = proj[base - 8 : base + block_len, lanes]
                    prev_one, prev_two = pltpu.roll(back, 1, 0)[8:], pltpu.roll(back, 2, 0)[8:]
                else:
                    prev_one, prev_two = pltpu.roll(now, 1, 0), pltpu.roll(now, 2, 0)
                tap = [vec_ref[3 + 3 * j + role : 4 + 3 * j + role, :] for j in range(3)]
                parts.append(
                    vec_ref[12 + role : 13 + role, :]
                    + tap[0] * now
                    + tap[1] * jnp.where(one, prev_one, 0.0)
                    + tap[2] * jnp.where(two, prev_two, 0.0)
                )
            grad = gg[here].astype(WIDE)
            gs[here, :channels] = grad * mixed[here]
            grad = grad * parts[0]
            gm[here] = grad
            short[here, :channels] = parts[1]
            short[here, channels:] = parts[2]
            direct_sum = direct_sum + jnp.sum(
                grad * (parts[1] * parts[2]), axis=0, keepdims=True
            )
        gs[length:, :] = jnp.zeros((8, three), WIDE)
        direct_out[...] = direct_sum
        begin, end, before = long_range(starts_ref, docs, block_len, length)
        ranges = []
        for m in range(docs - 1):
            first, last, base = short_range(starts_ref, docs, m, before, block_len, length)
            base = pl.multiple_of(base, block_len)
            ranges.append((base, inside_mask(base, block_len, channels, first, last)))
        for b in range(blocks):
            mask = inside_mask(b * block_len, block_len, channels, begin, end)
            part = jnp.where(mask, gm[b * block_len : (b + 1) * block_len], 0.0)
            store_triple(xs, slice(b * channels, (b + 1) * channels), part)
        for m, (base, mask) in enumerate(ranges):
            part = jnp.where(mask, gm[pl.ds(base, block_len)], 0.0)
            store_triple(xs, slice((blocks + m) * channels, (blocks + m + 1) * channels), part)
        for e in range(count):
            gt[e] = jnp.dot(
                it3_ref[...], xs[:, e * channels : (e + 1) * channels], preferred_element_type=WIDE
            )
        spec_copy.wait()
        entry_copy.wait()

        @pl.loop(0, block_len // step)
        def _(number):
            at_re = pl.multiple_of(number * step, step)
            at_im = pl.multiple_of(number * step + block_len, step)
            edge = jnp.where(rows_from(at_re, step, channels) == 0, 1.0, 0.0)
            inside = 1.0 - edge

            def load(ref, k):
                return ref[k, pl.ds(at_re, step)], ref[k, pl.ds(at_im, step)]

            def combine(pairs):
                rr = ii = ri = None
                for (a, b), (c, d) in pairs:
                    rr = a * c if rr is None else rr + a * c
                    ii = b * d if ii is None else ii + b * d
                    ri = b * c - a * d if ri is None else ri + (b * c - a * d)
                return rr + inside * ii, inside * ri + edge * ii

            for e in range(count):
                if e < blocks:
                    pairs = [(load(gt, i), load(spec, i - e)) for i in range(e, blocks)]
                else:
                    pairs = [(load(gt, e), load(spec, 0))]
                lanes = slice(e * channels, (e + 1) * channels)
                for part, at in zip(combine(pairs), (at_re, at_im)):
                    high, low = split_low(part)
                    ys[pl.ds(at, step), lanes] = high
                    ys[pl.ds(at + 2 * block_len, step), lanes] = low
                    ys[pl.ds(at + 4 * block_len, step), lanes] = high
            for k in range(blocks):
                pairs = [(load(gt, j + k), load(ent, j)) for j in range(blocks - k)]
                if k == 0:
                    pairs += [(load(gt, e), load(ent, e)) for e in range(blocks, count)]
                out_re, out_im = combine(pairs)
                lags[k, pl.ds(at_re, step)] = out_re
                lags[k, pl.ds(at_im, step)] = out_im

        for b in range(blocks):
            here = slice(b * block_len, (b + 1) * block_len)
            back = jnp.dot(
                ft3_ref[...], ys[:, b * channels : (b + 1) * channels], preferred_element_type=WIDE
            )
            mask = inside_mask(b * block_len, block_len, channels, begin, end)
            gi[here] = jnp.where(mask, back, 0.0) + direct * gm[here]
        for m, (base, mask) in enumerate(ranges):
            lanes = slice((blocks + m) * channels, (blocks + m + 1) * channels)
            back = jnp.dot(ft3_ref[...], ys[:, lanes], preferred_element_type=WIDE)
            where = pl.ds(base, block_len)
            gi[where] = gi[where] + jnp.where(mask, back, 0.0)
        for b in range(blocks):
            here = slice(b * block_len, (b + 1) * block_len)
            gs[here, channels : 2 * channels] = gi[here] * short[here, channels:]
            gs[here, 2 * channels :] = gi[here] * short[here, :channels]
        copies.start(gs, gs_out).wait()

    shape = jax.ShapeDtypeStruct
    return pl.pallas_call(
        body,
        out_shape=[
            shape((blocks, 2 * block_len, channels), WIDE),
            shape((1, channels), WIDE),
            shape((length + 8, three), WIDE),
        ],
        in_specs=[SMEM_SPACE] * 2 + [VMEM_SPACE] * (3 + blocks) + [ANY_SPACE] * 4,
        out_specs=[VMEM_SPACE, VMEM_SPACE, ANY_SPACE],
        scratch_shapes=[
            pltpu.VMEM((blocks, 2 * block_len, channels), WIDE),
            pltpu.VMEM((length, three), WIDE),
            pltpu.VMEM((count, 2 * block_len, channels), WIDE),
            pltpu.VMEM((length, channels), WIDE),
            pltpu.VMEM((length, channels), LOW),
            pltpu.VMEM((length, 2 * channels), WIDE),
            pltpu.VMEM((length + 8, three), WIDE),
            pltpu.VMEM((length, channels), WIDE),
            pltpu.VMEM((3 * block_len, count * channels), LOW),
            pltpu.VMEM((count, 2 * block_len, channels), WIDE),
            pltpu.VMEM((6 * block_len, count * channels), LOW),
            pltpu.VMEM((length, channels), WIDE),
            pltpu.SemaphoreType.DMA((5,)),
        ],
        compiler_params=pltpu.CompilerParams(vmem_limit_bytes=LIMIT),
        cost_estimate=cost(14),
    )(places, starts, vec, it3, ft3, *grad_pieces, spectra, proj, entries, mixed)


def project_back_call(
    block_len,
    blocks,
    places,
    starts,
    in_offsets,
    block_offsets,
    vec,
    norm1,
    direct,
    grad_short,
    proj,
    in_rows,
    normed,
):
    length = block_len * blocks
    channels = vec.shape[1]
    docs = starts.shape[0]
    count_dp, groups, share, width = in_rows.shape
    three = 3 * channels
    half_dp, half_block = count_dp // 2, blocks // 2

    def body(place_ref, starts_ref, vec_ref, gain_ref, shift_ref, direct_ref, *refs):
        gs_ref, proj_ref, rows_ref, norm_ref = refs[:4]
        refs = refs[4:]
        dealt_refs = [(refs[2 * g], refs[2 * g + 1]) for g in range(groups)]
        refs = refs[2 * groups :]
        gn_kept, gn_sent, sums, norm_sums = refs[:4]
        gs, proj, rows, norm, gp, gr, sems = refs[4:]
        row, place = place_ref[0], place_ref[1]
        copies = Copies(sems)
        gs_copy = copies.start(gs_ref, gs)
        proj_copy = copies.start(proj_ref, proj)
        rows_copy = copies.start(rows_ref, rows)
        norm_copy = copies.start(norm_ref, norm)
        sums[15:16, :] = direct_ref[...]
        gs_copy.wait()
        proj_copy.wait()
        for role in range(3):
            lanes = slice(role * channels, (role + 1) * channels)
            tap = [vec_ref[3 + 3 * j + role : 4 + 3 * j + role, :] for j in range(3)]
            totals = [jnp.zeros((1, channels), WIDE) for _ in range(5)]
            for b in range(blocks):
                base = b * block_len
                here = slice(base, base + block_len)
                one, two = keep_masks(starts_ref, docs, base, block_len + 8, channels)
                grad = gs[base : base + block_len + 8, lanes]
                pass_one, pass_two = jnp.where(one, grad, 0.0), jnp.where(two, grad, 0.0)
                size = block_len + 8
                result = (
                    tap[0] * grad[:block_len]
                    + tap[1] * pltpu.roll(pass_one, size - 1, 0)[:block_len]
                    + tap[2] * pltpu.roll(pass_two, size - 2, 0)[:block_len]
                ).astype(LOW)
                gp[here, lanes] = result
                now = proj[here, lanes]
                if b:
                    back = proj[base - 8 : base + block_len, lanes]
                    prev_one, prev_two = pltpu.roll(back, 1, 0)[8:], pltpu.roll(back, 2, 0)[8:]
                else:
                    prev_one, prev_two = pltpu.roll(now, 1, 0), pltpu.roll(now, 2, 0)
                terms = [
                    result.astype(WIDE),
                    grad[:block_len] * now,
                    pass_one[:block_len] * prev_one,
                    pass_two[:block_len] * prev_two,
                    grad[:block_len],
                ]
                totals = [
                    total + jnp.sum(term, axis=0, keepdims=True)
                    for total, term in zip(totals, terms)
                ]
            sums[role : role + 1, :] = totals[0]
            for j in range(3):
                sums[3 + 3 * j + role : 4 + 3 * j + role, :] = totals[1 + j]
            sums[12 + role : 13 + role, :] = totals[4]
        rows_copy.wait()
        norm_copy.wait()
        weights = rows[...].reshape(three, width)
        shift_sum = jnp.zeros((1, width), WIDE)
        scale_sum = jnp.zeros((1, width), WIDE)
        for index, offset in enumerate(block_offsets):
            other = place ^ offset
            where = pl.ds(pl.multiple_of(other * block_len, block_len), block_len)
            part = jnp.dot(gp[where], weights, preferred_element_type=WIDE)
            shift_sum = shift_sum + jnp.sum(part, axis=0, keepdims=True)
            scale_sum = scale_sum + jnp.sum(
                part * norm[other].astype(WIDE), axis=0, keepdims=True
            )
            if index < half_block:
                gn_kept[index] = part.astype(LOW)
            else:
                gn_sent[index - half_block] = part.astype(LOW)
        norm_sums[0:1, :] = (scale_sum - shift_ref[...] * shift_sum) / gain_ref[...]
        norm_sums[1:2, :] = shift_sum
        for c in range(3):
            lanes = slice(c * channels, (c + 1) * channels)
            total = lax.dot_general(
                gp[:, lanes],
                norm[...].reshape(length, width),
                (((0,), (0,)), ((), ())),
                preferred_element_type=WIDE,
            )
            gr[lanes] = total.astype(LOW)
        dealt = gr.reshape(count_dp, groups, share, width)
        leaving = []
        for g in range(groups):
            for index, offset in enumerate(in_offsets[g]):
                target = dealt_refs[g][index // half_dp].at[index % half_dp]
                leaving.append(copies.start(dealt.at[row ^ offset, g], target))
        for copy in leaving:
            copy.wait()

    shape = jax.ShapeDtypeStruct
    half_in = shape((half_dp, share, width), LOW)
    return pl.pallas_call(
        body,
        out_shape=[half_in] * (2 * groups)
        + [
            shape((half_block, block_len, width), LOW),
            shape((half_block, block_len, width), LOW),
            shape((16, channels), WIDE),
            shape((2, width), WIDE),
        ],
        in_specs=[SMEM_SPACE] * 2 + [VMEM_SPACE] * 4 + [ANY_SPACE] * 4,
        out_specs=[ANY_SPACE] * (2 * groups) + [VMEM_SPACE] * 4,
        scratch_shapes=[
            pltpu.VMEM((length + 8, three), WIDE),
            pltpu.VMEM((length, three), WIDE),
            pltpu.VMEM((count_dp, groups, share, width), LOW),
            pltpu.VMEM((blocks, block_len, width), LOW),
            pltpu.VMEM((length, three), LOW),
            pltpu.VMEM((three, width), LOW),
            pltpu.SemaphoreType.DMA((4 + groups * count_dp,)),
        ],
        compiler_params=pltpu.CompilerParams(vmem_limit_bytes=LIMIT),
        cost_estimate=cost(10),
    )(places, starts, vec, *norm1, direct, grad_short, proj, in_rows, normed)


def filter_back_call(block_len, blocks, table, ft3, w1, w2, vec, third_at, lags):
    length = block_len * blocks
    channels = vec.shape[1]
    units = w2.shape[1]

    def body(table_ref, w1_ref, w2_ref, vec_ref, ft3_ref, lags_ref, g1, g2, g3, gd):
        one_row = jnp.where(lax.broadcasted_iota(jnp.int32, (8, length), 0) == 0, 1.0, 0.0)

        def product(left, right, dims):
            return lax.dot_general(
                left, right, (dims, ((), ())), precision=HIGHEST, preferred_element_type=WIDE
            )

        z1 = product(w1_ref[...], table_ref[...], ((0,), (0,)))
        first = jnp.concatenate([jnp.sin(z1), one_row], axis=0)
        z2 = product(w2_ref[...], first, ((0,), (0,)))
        second = jnp.sin(z2)
        decay = vec_ref[third_at - 2 : third_at - 1, :]
        third_w = vec_ref[third_at : third_at + units, :]
        half_rows = lax.broadcasted_iota(jnp.int32, (2 * block_len, channels), 0)
        parity = jnp.where(half_rows % 2 == 0, 1.0, -1.0)
        sign = jnp.where(half_rows == block_len, 1.0, parity)
        third_sum = jnp.zeros((units, channels), WIDE)
        decay_sum = jnp.zeros((1, channels), WIDE)
        back = []
        for i in range(blocks):
            grad = sign * lags_ref[i]
            if i + 1 < blocks:
                grad = grad + lags_ref[i + 1]
            high, low = split_low(grad)
            stacked = jnp.concatenate([high, low, high], axis=0)
            grad = jnp.dot(ft3_ref[...], stacked, preferred_element_type=WIDE)
            here = second[:, i * block_len : (i + 1) * block_len]
            third = product(here, third_w, ((0,), (0,)))
            times = rows_from(i * block_len, block_len, channels).astype(WIDE) / (length - 1)
            fall = jnp.exp(-times * decay)
            decay_sum = decay_sum - jnp.sum(grad * third * fall * times, axis=0, keepdims=True)
            grad = grad * (fall + MOD_SHIFT)
            third_sum = third_sum + product(here, grad, ((1,), (0,)))
            back.append(product(third_w, grad, ((1,), (1,))))
        gz2 = jnp.concatenate(back, axis=1) * jnp.cos(z2)
        g2[...] = product(first, gz2, ((1,), (1,)))
        gz1 = product(w2_ref[:units, :], gz2, ((1,), (0,))) * jnp.cos(z1)
        g1[...] = product(table_ref[...], gz1, ((1,), (1,)))
        g3[...] = third_sum
        gd[...] = decay_sum

    shape = jax.ShapeDtypeStruct
    return pl.pallas_call(
        body,
        out_shape=[
            shape(w1.shape, WIDE),
            shape(w2.shape, WIDE),
            shape((units, channels), WIDE),
            shape((1, channels), WIDE),
        ],
        in_specs=[VMEM_SPACE] * 6,
        out_specs=[VMEM_SPACE] * 4,
        compiler_params=pltpu.CompilerParams(vmem_limit_bytes=LIMIT),
        cost_estimate=cost(9),
    )(table, w1, w2, vec, ft3, lags)


def norm_parts(values):
    mean = jnp.mean(values, axis=-1, keepdims=True)
    centered = values - mean
    variance = jnp.mean(centered * centered, axis=-1, keepdims=True)
    scale = lax.rsqrt(variance + EPSILON)
    return centered * scale, scale


def gather_out(copies, refs, row, dp_offsets, target):
    started, at = [], 0
    for ref in refs:
        for i in range(ref.shape[0]):
            for r, offset in enumerate(dp_offsets):
                started.append(copies.start(ref.at[i, r], target.at[at, row ^ offset]))
            at += 1
    return started


def branch_call(row, inputs, gated_parts, out_pieces, dp_offsets, rows):
    blocks = len(gated_parts)
    tokens, channels = gated_parts[0].shape
    width = inputs.shape[-1]
    shard = out_pieces[0].shape[2]
    count_dp = len(dp_offsets)

    def body(row_ref, in_ref, bias_ref, gain_ref, shift_ref, *refs):
        gated_refs, piece_refs = refs[:blocks], refs[blocks : blocks + len(out_pieces)]
        resid_ref, normed_ref, weights, sems = refs[blocks + len(out_pieces) :]
        copies = Copies(sems)
        waiting = gather_out(copies, piece_refs, row_ref[0], dp_offsets, weights)
        for copy in waiting:
            copy.wait()
        total = in_ref[...].astype(WIDE) + bias_ref[...]
        for i in range(blocks):
            total = total + dot_last(
                gated_refs[i][...], weights[i].reshape(width, channels)
            )
        resid_ref[...] = total
        normal, _ = norm_parts(total)
        normed_ref[...] = (normal * gain_ref[...] + shift_ref[...]).astype(LOW)

    shape = jax.ShapeDtypeStruct
    return pl.pallas_call(
        body,
        out_shape=[shape((tokens, width), WIDE), shape((tokens, width), LOW)],
        in_specs=[SMEM_SPACE] + [VMEM_SPACE] * (4 + blocks) + [ANY_SPACE] * len(out_pieces),
        out_specs=[VMEM_SPACE] * 2,
        scratch_shapes=[
            pltpu.VMEM((blocks, count_dp, shard, channels), LOW),
            pltpu.SemaphoreType.DMA((blocks * count_dp,)),
        ],
        compiler_params=pltpu.CompilerParams(vmem_limit_bytes=LIMIT),
        cost_estimate=cost(1),
    )(row, inputs, *rows, *gated_parts, *out_pieces)


def branch_back_call(row, resid, kept, arrived, cot, out_pieces, dp_offsets, gain):
    tokens, width = resid.shape
    blocks = sum(piece.shape[0] for piece in out_pieces)
    shard, channels = out_pieces[0].shape[2:]
    count_dp = len(dp_offsets)

    def body(row_ref, resid_ref, kept_ref, arrived_ref, cot_ref, gain_ref, *refs):
        piece_refs, refs = refs[: len(out_pieces)], refs[len(out_pieces) :]
        grad_refs, (whole_ref, branch_ref, sums, weights, sems) = refs[:blocks], refs[blocks:]
        copies = Copies(sems)
        waiting = gather_out(copies, piece_refs, row_ref[0], dp_offsets, weights)
        grad = kept_ref[...].astype(WIDE) + arrived_ref[...].astype(WIDE)
        normal, scale = norm_parts(resid_ref[...])
        scaled = grad * gain_ref[...]
        back = scaled - jnp.mean(scaled, axis=-1, keepdims=True)
        back = back - normal * jnp.mean(scaled * normal, axis=-1, keepdims=True)
        whole = cot_ref[...].astype(WIDE) + back * scale
        whole_ref[...] = whole
        low = whole.astype(LOW)
        branch_ref[...] = low
        sums[0:1, :] = jnp.sum(low.astype(WIDE), axis=0, keepdims=True)
        sums[1:2, :] = jnp.sum(grad * normal, axis=0, keepdims=True)
        sums[2:3, :] = jnp.sum(grad, axis=0, keepdims=True)
        sums[3:4, :] = jnp.sum(cot_ref[...].astype(WIDE), axis=0, keepdims=True)
        for copy in waiting:
            copy.wait()
        for i in range(blocks):
            grad_refs[i][...] = dot_plain(low, weights[i].reshape(width, channels)).astype(LOW)

    shape = jax.ShapeDtypeStruct
    return pl.pallas_call(
        body,
        out_shape=[shape((tokens, channels), LOW)] * blocks
        + [shape((tokens, width), WIDE), shape((tokens, width), LOW), shape((4, width), WIDE)],
        in_specs=[SMEM_SPACE] + [VMEM_SPACE] * 5 + [ANY_SPACE] * len(out_pieces),
        out_specs=[VMEM_SPACE] * (blocks + 3),
        scratch_shapes=[
            pltpu.VMEM((blocks, count_dp, shard, channels), LOW),
            pltpu.SemaphoreType.DMA((blocks * count_dp,)),
        ],
        compiler_params=pltpu.CompilerParams(vmem_limit_bytes=LIMIT),
        cost_estimate=cost(1),
    )(row, resid, kept, arrived, cot, gain, *out_pieces)


def out_grad_call(row, grad_branch, gated_parts, dp_offsets):
    blocks = len(gated_parts)
    tokens, channels = gated_parts[0].shape
    width = grad_branch.shape[1]
    count_dp = len(dp_offsets)
    shard = width // count_dp
    half = blocks // 2

    def body(row_ref, grad_ref, *refs):
        gated_refs, (kept, sent, total) = refs[:blocks], refs[blocks:]
        for i in range(blocks):
            total[...] = dot_first(grad_ref[...], gated_refs[i][...]).astype(LOW)
            target, at = (kept, i) if i < half else (sent, i - half)
            for r, offset in enumerate(dp_offsets):
                begin = pl.multiple_of((row_ref[0] ^ offset) * shard, shard)
                target[at * count_dp + r] = total[pl.ds(begin, shard)]

    out = jax.ShapeDtypeStruct((half * count_dp, shard, channels), LOW)
    return pl.pallas_call(
        body,
        out_shape=[out, out],
        in_specs=[SMEM_SPACE] + [VMEM_SPACE] * (1 + blocks),
        out_specs=[VMEM_SPACE] * 2,
        scratch_shapes=[pltpu.VMEM((width, channels), LOW)],
        compiler_params=pltpu.CompilerParams(vmem_limit_bytes=LIMIT),
        cost_estimate=cost(3),
    )(row, grad_branch, *gated_parts)


def forward_call(row, normed_pieces, cot_pieces, up_pieces, down_pieces, up_offsets, down_offsets, bias):
    tokens, width = normed_pieces[0].shape[1:]
    blocks = sum(piece.shape[0] for piece in normed_pieces)
    count_dp = len(up_offsets)
    piece = up_pieces[0].shape[1]
    shard = down_pieces[0].shape[1]
    units = piece * count_dp
    tile = 256 if units % 256 == 0 else units
    half = blocks // 2
    lists = (normed_pieces, cot_pieces, up_pieces, down_pieces)
    counts = [len(part) for part in lists]

    def body(row_ref, bias_ref, *refs):
        taken = []
        for count in counts:
            taken.append(refs[:count])
            refs = refs[count:]
        out_kept, out_sent, grad_kept, grad_sent, act_out, hid_out, sums = refs[:7]
        norm, cot, up, down, act, hid, sems = refs[7:]
        copies = Copies(sems)
        norm_copies = gather_in(copies, taken[0], 0, range(blocks), norm)
        up_copies = gather_in(copies, taken[2], row_ref[0], up_offsets, up)
        cot_copies = gather_in(copies, taken[1], 0, range(blocks), cot)
        down_copies = gather_in(copies, taken[3], row_ref[0], down_offsets, down)
        for copy in norm_copies + up_copies:
            copy.wait()
        up_rows = up[...].reshape(units, width)
        first = dot_last(norm[0], up_rows[:tile])
        for copy in cot_copies + down_copies:
            copy.wait()
        down_rows = down[...].reshape(width, units)
        for f in range(units // tile):
            lanes = slice(f * tile, (f + 1) * tile)
            total = jnp.zeros((1, tile), WIDE)
            for t in range(blocks):
                hidden = first if f == t == 0 else dot_last(norm[t], up_rows[lanes])
                hidden = hidden + bias_ref[:, lanes]
                grad = dot_plain(cot[t], down_rows[:, lanes])
                below = 0.5 * (1.0 + lax.erf(hidden * math.sqrt(0.5)))
                slope = below + hidden * (
                    jnp.exp(-0.5 * hidden * hidden) * (1.0 / math.sqrt(2.0 * math.pi))
                )
                act[t, :, lanes] = (hidden * below).astype(LOW)
                grad = (grad * slope).astype(LOW)
                hid[t, :, lanes] = grad
                total = total + jnp.sum(grad.astype(WIDE), axis=0, keepdims=True)
            sums[:, lanes] = total
        leaving = [copies.start(act, act_out), copies.start(hid, hid_out)]
        for t in range(blocks):
            back = dot_plain(hid[t], up_rows).astype(LOW)
            out = dot_last(act[t], down_rows).astype(LOW)
            if t < half:
                grad_kept[t] = back
                out_kept[t] = out
            else:
                grad_sent[t - half] = back
                out_sent[t - half] = out
        for copy in leaving:
            copy.wait()

    shape = jax.ShapeDtypeStruct
    part = shape((half, tokens, width), LOW)
    return pl.pallas_call(
        body,
        out_shape=[part] * 4
        + [shape((blocks, tokens, units), LOW)] * 2
        + [shape((1, units), WIDE)],
        in_specs=[SMEM_SPACE, VMEM_SPACE] + [ANY_SPACE] * sum(counts),
        out_specs=[VMEM_SPACE] * 4 + [ANY_SPACE] * 2 + [VMEM_SPACE],
        scratch_shapes=[
            pltpu.VMEM((blocks, tokens, width), LOW),
            pltpu.VMEM((blocks, tokens, width), LOW),
            pltpu.VMEM((count_dp, piece, width), LOW),
            pltpu.VMEM((count_dp, shard, units), LOW),
            pltpu.VMEM((blocks, tokens, units), LOW),
            pltpu.VMEM((blocks, tokens, units), LOW),
            pltpu.SemaphoreType.DMA((2 * blocks + 2 * count_dp + 2,)),
        ],
        compiler_params=pltpu.CompilerParams(vmem_limit_bytes=LIMIT),
        cost_estimate=cost(17),
    )(row, bias, *normed_pieces, *cot_pieces, *up_pieces, *down_pieces)


def weight_grad_call(row, pairs, offset_lists):
    blocks = sum(array.shape[0] for array in pairs[0][0])
    _, tokens, rows = pairs[0][0][0].shape
    width = pairs[0][1][0].shape[2]
    count_dp = len(offset_lists[0])
    quarter, share = count_dp // 4, rows // count_dp
    half = blocks // 2
    tile = 256 if rows % 256 == 0 else rows
    count = len(pairs)
    arrays = [array for pair in pairs for side in pair for array in side]

    def body(row_ref, *refs):
        sources, targets = list(refs[: len(arrays)]), refs[len(arrays) : len(arrays) + 4 * count]
        refs = refs[len(arrays) + 4 * count :]
        totals, sems = refs[:count], refs[count]
        copies = Copies(sems)
        leaving = []

        def part(side, number, lanes):
            ref, at = (side[0], number * half) if len(side) == 1 else (side[number], 0)
            return ref[at : at + half, :, lanes].reshape(half * tokens, -1)

        for p, pair in enumerate(pairs):
            left, right = ([sources.pop(0) for _ in side] for side in pair)
            total = totals[p]
            rights = [part(right, number, slice(0, width)) for number in range(2)]
            for c in range(rows // tile):
                lanes = slice(c * tile, (c + 1) * tile)
                total[lanes] = (
                    dot_first(part(left, 0, lanes), rights[0])
                    + dot_first(part(left, 1, lanes), rights[1])
                ).astype(LOW)
            for index, offset in enumerate(offset_lists[p]):
                begin = pl.multiple_of((row_ref[0] ^ offset) * share, share)
                target = targets[4 * p + index // quarter].at[index % quarter]
                leaving.append(copies.start(total.at[pl.ds(begin, share)], target))
        for copy in leaving:
            copy.wait()

    return pl.pallas_call(
        body,
        out_shape=[jax.ShapeDtypeStruct((quarter, share, width), LOW)] * (4 * count),
        in_specs=[SMEM_SPACE] + [VMEM_SPACE] * len(arrays),
        out_specs=[ANY_SPACE] * (4 * count),
        scratch_shapes=[pltpu.VMEM((rows, width), LOW)] * count
        + [pltpu.SemaphoreType.DMA((count * count_dp,))],
        compiler_params=pltpu.CompilerParams(vmem_limit_bytes=LIMIT),
        cost_estimate=cost(11),
    )(row, *arrays)


def iota(shape, dim):
    return lax.broadcasted_iota(jnp.int32, shape, dim)


def eye_low(size):
    return jnp.where(iota((size, size), 0) == iota((size, size), 1), 1.0, 0.0).astype(LOW)


def turn(values):
    return values.astype(WIDE).T


def own_channel(index, place, blocks, share):
    return (index // share) * (share * blocks) + place * share + index % share


def first_call(places, blocks, share, w_in, w_out, inputs, rows, parts):
    width, shard = w_in.shape
    shard_out = w_out.shape[1]
    tokens = inputs.shape[0]
    here = shard // blocks
    size = here // parts
    channels = width // blocks

    def body(place_ref, w_ref, out_ref, in_ref, gain_ref, shift_ref, *refs):
        part_refs, (out_own, normed_ref, picked) = refs[:parts], refs[parts:]
        place = place_ref[1]
        shape = (here, shard)
        chosen = own_channel(iota(shape, 0), place, blocks, share) == iota(shape, 1)
        chosen = jnp.where(chosen, 1.0, 0.0).astype(LOW)
        turned = dot_last(chosen, w_ref[...]).astype(LOW)
        for i in range(parts):
            part_refs[i][0] = turned[i * size : (i + 1) * size]
        for j in range(channels // share):
            begin = pl.multiple_of(j * share * blocks + place * share, share)
            picked[j * share : (j + 1) * share] = out_ref[pl.ds(begin, share)]
        out_own[0] = turn(picked[...]).astype(LOW)
        normal, _ = norm_parts(in_ref[...].astype(WIDE))
        normed_ref[0] = (normal * gain_ref[...] + shift_ref[...]).astype(LOW)

    shape = jax.ShapeDtypeStruct
    return pl.pallas_call(
        body,
        out_shape=[shape((1, size, width), LOW)] * parts
        + [shape((1, shard_out, channels), LOW), shape((1, tokens, width), LOW)],
        in_specs=[SMEM_SPACE] + [VMEM_SPACE] * 5,
        out_specs=[VMEM_SPACE] * (parts + 2),
        scratch_shapes=[pltpu.VMEM((channels, shard_out), LOW)],
        compiler_params=pltpu.CompilerParams(vmem_limit_bytes=WHOLE),
        cost_estimate=cost(3),
    )(places, w_in, w_out, inputs, *rows)


def second_call(places, blocks, share, w_up, w_down, b_up, vectors, layers, third):
    width, shard_up = w_up.shape
    piece = shard_up // blocks
    hidden, shard_down = w_down.shape
    count_dp = hidden // shard_up
    channels = width // blocks
    arrays = [array for array, _ in vectors] + [third]
    spans = [rows for _, rows in vectors] + [third.shape[0]]
    used = sum(spans)
    total = -(-used // 8) * 8
    flat_layers = [array for layer in layers for array in layer]
    heights = [weights.shape[0] for weights, _ in layers]

    def body(place_ref, up_ref, down_ref, bias_ref, *refs):
        vec_refs, refs = refs[: len(arrays)], refs[len(arrays) :]
        layer_refs, refs = refs[: len(flat_layers)], refs[len(flat_layers) :]
        up_own, down_own, bias_own, vec_own = refs[:4]
        aug_refs, (up, down, held, sems) = refs[4 : 4 + len(layers)], refs[4 + len(layers) :]
        place = place_ref[1]
        copies = Copies(sems)
        begin = pl.multiple_of(place * piece, piece)
        waiting = [copies.start(up_ref.at[:, pl.ds(begin, piece)], up)]
        for k in range(count_dp):
            rows = pl.ds(pl.multiple_of(k * shard_up + place * piece, piece), piece)
            waiting.append(copies.start(down_ref.at[rows], down.at[pl.ds(k * piece, piece)]))
        for k in range(count_dp):
            lanes = pl.ds(pl.multiple_of(k * shard_up + place * piece, piece), piece)
            bias_own[:, k * piece : (k + 1) * piece] = bias_ref[:, lanes]
        held[used:, :] = jnp.zeros((total - used, width), WIDE)
        at = 0
        for (ref, span) in zip(vec_refs, spans):
            count = ref.shape[0]
            if ref.shape[1] == width:
                held[at : at + count, :] = ref[...]
            else:
                for i in range(count):
                    for j in range(span // count):
                        row = at + i * (span // count) + j
                        held[row : row + 1, :] = ref[i : i + 1, j * width : (j + 1) * width]
            at += span
        shape = (width, channels)
        chosen = iota(shape, 0) == own_channel(iota(shape, 1), place, blocks, share)
        vec_own[...] = dot_high(held[...], jnp.where(chosen, 1.0, 0.0))
        for i, height in enumerate(heights):
            weights, bias, target = layer_refs[2 * i], layer_refs[2 * i + 1], aug_refs[i]
            target[...] = jnp.zeros(target.shape, WIDE)
            target[:height, :] = weights[...]
            target[height : height + 1, :] = bias[...]
        for copy in waiting:
            copy.wait()
        up_own[0] = turn(up[...]).astype(LOW)
        down_own[0] = turn(down[...]).astype(LOW)

    shape = jax.ShapeDtypeStruct
    return pl.pallas_call(
        body,
        out_shape=[
            shape((1, piece, width), LOW),
            shape((1, shard_down, piece * count_dp), LOW),
            shape((1, piece * count_dp), WIDE),
            shape((total, channels), WIDE),
        ]
        + [shape((-(-(height + 1) // 8) * 8, layer[0].shape[1]), WIDE) for height, layer in zip(heights, layers)],
        in_specs=[SMEM_SPACE, ANY_SPACE, ANY_SPACE]
        + [VMEM_SPACE] * (1 + len(arrays) + len(flat_layers)),
        out_specs=[VMEM_SPACE] * (4 + len(layers)),
        scratch_shapes=[
            pltpu.VMEM((width, piece), LOW),
            pltpu.VMEM((piece * count_dp, shard_down), LOW),
            pltpu.VMEM((total, width), WIDE),
            pltpu.SemaphoreType.DMA((1 + count_dp,)),
        ],
        compiler_params=pltpu.CompilerParams(vmem_limit_bytes=LIMIT),
        cost_estimate=cost(4),
    )(places, w_up, w_down, b_up, *arrays, *flat_layers)


def spread_pieces(refs):
    return [ref.at[i] for ref in refs for i in range(ref.shape[0])]


def wide_call(places, offsets, pieces, piece, count_dp):
    total, width = pieces[0].shape[1:]
    shard = total - piece
    units = piece * count_dp
    blocks = len(offsets)

    def body(place_ref, *refs):
        sources = spread_pieces(refs[: len(pieces)])
        up_out, down_out = refs[len(pieces) :]
        for source, offset in zip(sources, offsets):
            place = place_ref[1] ^ offset
            up_out[:, pl.ds(pl.multiple_of(place * piece, piece), piece)] = turn(source[:piece])
            down = turn(source[piece:])
            for k in range(count_dp):
                rows = pl.ds(pl.multiple_of((k * blocks + place) * piece, piece), piece)
                down_out[rows] = down[k * piece : (k + 1) * piece]

    shape = jax.ShapeDtypeStruct
    return pl.pallas_call(
        body,
        out_shape=[
            shape((width, piece * blocks), WIDE),
            shape((units * blocks, shard), WIDE),
        ],
        in_specs=[SMEM_SPACE] + [VMEM_SPACE] * len(pieces),
        out_specs=[VMEM_SPACE] * 2,
        compiler_params=pltpu.CompilerParams(vmem_limit_bytes=LIMIT),
        cost_estimate=cost(8),
    )(places, *pieces)


def in_wide_call(places, offsets, share, pieces):
    here, width = pieces[0].shape[1:]
    blocks = len(offsets)
    shard = here * blocks

    def body(place_ref, *refs):
        out = refs[-1]
        total = None
        for index, ref in enumerate(spread_pieces(refs[:-1])):
            place = place_ref[1] ^ offsets[index]
            shape = (here, shard)
            chosen = own_channel(iota(shape, 0), place, blocks, share) == iota(shape, 1)
            chosen = jnp.where(chosen, 1.0, 0.0).astype(LOW)
            part = dot_first(ref[...], chosen)
            total = part if total is None else total + part
        out[...] = total

    return pl.pallas_call(
        body,
        out_shape=jax.ShapeDtypeStruct((width, shard), WIDE),
        in_specs=[SMEM_SPACE] + [VMEM_SPACE] * len(pieces),
        out_specs=VMEM_SPACE,
        compiler_params=pltpu.CompilerParams(vmem_limit_bytes=LIMIT),
        cost_estimate=cost(3),
    )(places, *pieces)


def out_wide_call(places, offsets, share, pieces):
    shard, channels = pieces[0].shape[1:]
    blocks = len(offsets)

    def body(place_ref, *refs):
        out = refs[-1]
        for index, ref in enumerate(spread_pieces(refs[:-1])):
            place = place_ref[1] ^ offsets[index]
            whole = turn(ref[...])
            for j in range(channels // share):
                rows = pl.ds(pl.multiple_of((j * blocks + place) * share, share), share)
                out[rows] = whole[j * share : (j + 1) * share]

    return pl.pallas_call(
        body,
        out_shape=jax.ShapeDtypeStruct((channels * blocks, shard), WIDE),
        in_specs=[SMEM_SPACE] + [VMEM_SPACE] * len(pieces),
        out_specs=VMEM_SPACE,
        compiler_params=pltpu.CompilerParams(vmem_limit_bytes=LIMIT),
        cost_estimate=cost(2),
    )(places, *pieces)


def small_pack_call(shared, layers, bias, sums, third, decay):
    channels = third.shape[1]
    width = shared[0].shape[1]
    cuts = width // channels
    arrays = list(shared) + list(layers) + [bias, sums, third, decay]
    rows = cuts * sum(array.shape[0] for array in shared)
    layer_rows = [-(-array.shape[0] // cuts // 8) * 8 for array in layers]
    bias_rows = bias.shape[1] // channels
    plain = rows + sum(layer_rows) + bias_rows + sums.shape[0] + third.shape[0] + 1
    total = -(-plain // 16) * 16

    def body(*refs):
        target = refs[-1]
        target[plain:, :] = jnp.zeros((total - plain, channels), WIDE)
        at = 0
        for ref in refs[: len(shared)]:
            for i in range(ref.shape[0]):
                for j in range(cuts):
                    target[at : at + 1, :] = ref[i : i + 1, j * channels : (j + 1) * channels]
                    at += 1
        for ref, height in zip(refs[len(shared) : len(shared) + len(layers)], layer_rows):
            lanes = ref.shape[1]
            target[at : at + height, :] = jnp.zeros((height, channels), WIDE)
            for j in range(cuts):
                size = min(height, ref.shape[0] - j * height)
                if size > 0:
                    target[at : at + size, j * lanes : (j + 1) * lanes] = ref[
                        j * height : j * height + size, :
                    ]
            at += height
        ref = refs[len(shared) + len(layers)]
        for j in range(bias_rows):
            target[at : at + 1, :] = ref[:, j * channels : (j + 1) * channels]
            at += 1
        for ref in refs[len(shared) + len(layers) + 1 : -1]:
            target[at : at + ref.shape[0], :] = ref[...]
            at += ref.shape[0]

    return pl.pallas_call(
        body,
        out_shape=jax.ShapeDtypeStruct((total, channels), WIDE),
        in_specs=[VMEM_SPACE] * len(arrays),
        out_specs=VMEM_SPACE,
        compiler_params=pltpu.CompilerParams(vmem_limit_bytes=LIMIT),
        cost_estimate=cost(2),
    )(*arrays)


def small_out_call(places, offsets, share, pieces, shared, layer_shapes, bias_width, shard_up):
    height, channels = pieces[0].shape[1:]
    blocks = len(offsets)
    width = channels * blocks
    piece = shard_up // blocks
    augmented = [-(-(shape[0] + 1) // 8) * 8 for shape in layer_shapes]
    layer_rows = [-(-rows // blocks // 8) * 8 for rows in augmented]
    bias_rows = bias_width // channels
    units = layer_shapes[1][1]

    def body(place_ref, *refs):
        sources = spread_pieces(refs[: len(pieces)])
        refs = refs[len(pieces) :]
        shared_refs, refs = refs[:shared], refs[shared:]
        layer_refs, refs = refs[: 2 * len(layer_shapes)], refs[2 * len(layer_shapes) :]
        bias_out, in_out, taps_out, short_out, direct_out, third_out, decay_out, held, placed = refs
        for source, offset in zip(sources, offsets):
            placed[place_ref[1] ^ offset] = source[...].astype(WIDE)
        total = placed[0]
        for i in range(1, blocks):
            total = total + placed[i]
        held[...] = total
        at = 0
        for ref in shared_refs:
            for j in range(blocks):
                ref[:, j * channels : (j + 1) * channels] = held[at : at + 1, :]
                at += 1
        for i, rows in enumerate(layer_rows):
            weights, bias = layer_refs[2 * i], layer_refs[2 * i + 1]
            lanes = weights.shape[1]
            for j in range(blocks):
                size = min(rows, weights.shape[0] - j * rows)
                if size > 0:
                    weights[j * rows : j * rows + size, :] = held[
                        at : at + size, j * lanes : (j + 1) * lanes
                    ]
                if 0 <= weights.shape[0] - j * rows < rows:
                    row = at + weights.shape[0] - j * rows
                    bias[...] = held[row : row + 1, j * lanes : (j + 1) * lanes]
            at += rows
        whole = None
        first = at
        for index, offset in enumerate(offsets):
            place = place_ref[1] ^ offset
            for j in range(bias_rows):
                line = placed[place, first + j : first + j + 1, :]
                for c in range(channels // piece):
                    k = j * (channels // piece) + c
                    lanes = pl.ds(pl.multiple_of((k * blocks + place) * piece, piece), piece)
                    bias_out[:, lanes] = line[:, c * piece : (c + 1) * piece]
            shape = (channels, width)
            chosen = own_channel(iota(shape, 0), place, blocks, share) == iota(shape, 1)
            part = dot_high(
                placed[place, first + bias_rows :, :], jnp.where(chosen, 1.0, 0.0)
            )
            whole = part if whole is None else whole + part
        for role in range(3):
            lanes = slice(role * width, (role + 1) * width)
            in_out[:, lanes] = whole[role : role + 1]
            for j in range(3):
                taps_out[j : j + 1, lanes] = whole[3 + 3 * j + role : 4 + 3 * j + role]
            short_out[:, lanes] = whole[12 + role : 13 + role]
        direct_out[...] = whole[15:16]
        third_out[...] = whole[16 : 16 + units]
        decay_out[...] = whole[16 + units : 17 + units]

    shape = jax.ShapeDtypeStruct
    layer_out = []
    for rows, lanes in layer_shapes:
        layer_out += [shape((rows, lanes), WIDE), shape((1, lanes), WIDE)]
    return pl.pallas_call(
        body,
        out_shape=[shape((1, width), WIDE)] * shared
        + layer_out
        + [
            shape((1, bias_width * blocks), WIDE),
            shape((1, 3 * width), WIDE),
            shape((3, 3 * width), WIDE),
            shape((1, 3 * width), WIDE),
            shape((1, width), WIDE),
            shape((units, width), WIDE),
            shape((1, width), WIDE),
        ],
        in_specs=[SMEM_SPACE] + [VMEM_SPACE] * len(pieces),
        out_specs=[VMEM_SPACE] * (shared + len(layer_out) + 7),
        scratch_shapes=[
            pltpu.VMEM((height, channels), WIDE),
            pltpu.VMEM((blocks, height, channels), WIDE),
        ],
        compiler_params=pltpu.CompilerParams(vmem_limit_bytes=LIMIT),
        cost_estimate=cost(5),
    )(places, *pieces)


def local_plain(
    block_in,
    doc_starts,
    norm1_gain,
    norm1_bias,
    w_in,
    b_in,
    short_taps,
    short_bias,
    filter_w1,
    filter_b1,
    filter_w2,
    filter_b2,
    filter_w3,
    filter_decay,
    conv_bias,
    w_out,
    b_out,
    norm2_gain,
    norm2_bias,
    w_up,
    b_up,
    w_down,
    b_down,
    cotangent,
):
    count_dp, blocks = lax.axis_size("dp"), lax.axis_size("block")
    grid = Grid(count_dp, blocks)
    row, place = grid.row, grid.place
    _, block_len, width = block_in.shape
    length = block_len * blocks
    hidden_width = w_up.shape[1] * count_dp
    hidden_here = hidden_width // blocks
    dp_steps = grid.dp_steps
    block_steps = grid.chip_steps + [grid.core_step]
    block_offsets = [b for _, b in offsets_of(block_steps)]

    def rotated(turn):
        turn = turn % len(dp_steps)
        return dp_steps[turn:] + dp_steps[:turn]

    def dp_offsets(steps):
        return [a for a, _ in offsets_of(steps)]

    shard_in, shard_out = w_in.shape[1], w_out.shape[1]
    group = math.gcd(width, shard_in)
    groups_here, share = shard_in // group, group // blocks
    channels = width // blocks
    bands = width // group
    vectors = jnp.concatenate(
        [
            b_in.reshape(3, width),
            short_taps.reshape(9, width),
            short_bias.reshape(3, width),
            filter_decay[None],
            conv_bias[None],
            filter_w3,
        ],
        axis=0,
    )
    vectors = lax.dynamic_index_in_dim(
        vectors.reshape(vectors.shape[0], bands, blocks, share), place, 2, keepdims=False
    ).reshape(vectors.shape[0], channels)
    b_in_here = vectors[:3].reshape(-1)
    taps = vectors[3:12].reshape(3, 3 * channels)
    short_shift = vectors[12:15].reshape(-1)
    decay_here, direct, third_here = vectors[15], vectors[16], vectors[17:]

    in_turned = w_in.T.reshape(groups_here, blocks, share, width)
    in_own = lax.dynamic_index_in_dim(in_turned, place, 1, keepdims=False)
    in_orders = [rotated(i) for i in range(groups_here)]
    in_rows = jnp.stack(
        [
            arrange(grid.gather(in_own[i], in_orders[i]), row, dp_offsets(in_orders[i]))
            for i in range(groups_here)
        ],
        axis=1,
    ).reshape(3 * channels, width)

    inputs = block_in.astype(WIDE).reshape(block_len, width)
    normed, norm1_back = jax.vjp(layer_norm, inputs, norm1_gain, norm1_bias)
    normed_low = normed.astype(LOW)
    normed_all = arrange(grid.gather(normed_low, block_steps), place, block_offsets).reshape(
        length, width
    )

    up_order, down_order, out_dp_order = rotated(1), rotated(2), rotated(0)
    piece = w_up.shape[1] // blocks
    up_own = lax.dynamic_slice_in_dim(w_up, place * piece, piece, 1).T
    up_rows = arrange(grid.gather(up_own, up_order), row, dp_offsets(up_order)).reshape(
        hidden_here, width
    )
    b_up_here = lax.dynamic_index_in_dim(
        b_up.reshape(count_dp, blocks, piece), place, 1, keepdims=False
    ).reshape(hidden_here)
    down_own = w_down.reshape(count_dp, blocks, piece, w_down.shape[1])
    down_own = lax.dynamic_index_in_dim(down_own, place, 1, keepdims=False)
    down_own = down_own.reshape(hidden_here, w_down.shape[1]).T
    down_rows = arrange(grid.gather(down_own, down_order), row, dp_offsets(down_order)).reshape(
        width, hidden_here
    )

    out_own = w_out.reshape(bands, blocks, share, shard_out)
    out_own = lax.dynamic_index_in_dim(out_own, place, 1, keepdims=False)
    out_own = out_own.reshape(channels, shard_out).T
    out_dealt = arrange(grid.gather(out_own, out_dp_order), row, dp_offsets(out_dp_order))
    out_rows = jnp.concatenate(grid.gather(out_dealt.reshape(width, channels), block_steps), axis=0)
    cot_flat = cotangent.reshape(block_len, width)
    cot_all = jnp.concatenate(grid.gather(cot_flat, block_steps), axis=0).reshape(length, width)

    forward_table, inverse_table, sign, edge = transform_tables(block_len)
    starts = doc_starts[0]
    positions = jnp.arange(length, dtype=jnp.int32)
    segment = jnp.sum((starts[None, :] <= positions[:, None]).astype(jnp.int32), axis=-1) - 1
    keep_one = jnp.concatenate([jnp.zeros((1,), WIDE), (segment[1:] == segment[:-1]).astype(WIDE)])
    keep_two = jnp.concatenate([jnp.zeros((2,), WIDE), (segment[2:] == segment[:-2]).astype(WIDE)])
    keep_one, keep_two = keep_one[:, None], keep_two[:, None]
    num_docs = doc_starts.shape[1]
    long_doc = jnp.sum((starts <= block_len).astype(jnp.int32)) - 1
    long_mask = (segment == long_doc).astype(WIDE)[:, None]
    first_segment, last_segment = segment[:block_len], segment[length - block_len :]
    short_early, short_masks = [], []
    for number in range(num_docs - 1):
        early = number < long_doc
        doc = jnp.where(early, number, number + 1)
        where = jnp.where(early, first_segment, last_segment)
        short_early.append(early.astype(WIDE))
        short_masks.append((where == doc).astype(WIDE)[:, None])

    def spread(values):
        masked = values * long_mask
        parts = [masked[i * block_len : (i + 1) * block_len] for i in range(blocks)]
        first, last = values[:block_len], values[length - block_len :]
        for early, mask in zip(short_early, short_masks):
            parts.append(mask * (early * first + (1.0 - early) * last))
        return jnp.concatenate(parts, axis=1)

    def collect(values):
        parts = [
            values[:, i * channels : (i + 1) * channels] for i in range(blocks + num_docs - 1)
        ]
        first, last = jnp.zeros_like(parts[0]), jnp.zeros_like(parts[0])
        for early, mask, part in zip(short_early, short_masks, parts[blocks:]):
            first = first + early * mask * part
            last = last + (1.0 - early) * mask * part
        joined = jnp.concatenate(parts[:blocks], axis=0) * long_mask
        middle = jnp.zeros((length - 2 * block_len, channels), WIDE)
        return joined + jnp.concatenate([first, middle, last], axis=0)

    def cut(values, count):
        return [values[:, i * channels : (i + 1) * channels] for i in range(count)]

    table, times = position_table(length, filter_w1.shape[0])

    def filter_spectra(params):
        first = jnp.sin(dot_high(table, params[0]) + params[1])
        second = jnp.sin(dot_high(first, params[2]) + params[3])
        kernel = dot_high(second, params[4]) * (
            jnp.exp(-times[:, None] * params[5][None, :]) + MOD_SHIFT
        )
        pieces = jnp.concatenate(
            [kernel[i * block_len : (i + 1) * block_len] for i in range(blocks)], axis=1
        )
        halves = dot_near(forward_table, pieces)
        earlier = jnp.concatenate(
            [jnp.zeros((2 * block_len, channels), WIDE), halves[:, : (blocks - 1) * channels]],
            axis=1,
        )
        return earlier + sign[:, None] * halves

    spectra_flat, filter_back = jax.vjp(
        filter_spectra,
        (filter_w1, filter_b1, filter_w2, filter_b2, third_here, decay_here),
    )
    spectra = cut(spectra_flat, blocks)

    proj = dot_last(normed_all, in_rows) + b_in_here
    three = 3 * channels
    prev_one = jnp.concatenate([jnp.zeros((1, three), WIDE), proj[:-1]], axis=0) * keep_one
    prev_two = jnp.concatenate([jnp.zeros((2, three), WIDE), proj[:-2]], axis=0) * keep_two
    short = short_shift + taps[0] * proj + taps[1] * prev_one + taps[2] * prev_two
    gate_part, mult, value = cut(short, 3)
    inner = value * mult

    entries = cut(dot_near(forward_table, spread(inner)), blocks + num_docs - 1)
    totals = []
    for i in range(blocks):
        total = spectral_product(entries[i], spectra[0], edge)
        for j in range(i):
            total = total + spectral_product(entries[j], spectra[i - j], edge)
        totals.append(total)
    for entry in entries[blocks:]:
        totals.append(spectral_product(entry, spectra[0], edge))
    mixed = collect(dot_near(inverse_table, jnp.concatenate(totals, axis=1))) + direct * inner
    gated_low = (gate_part * mixed).astype(LOW)

    gated_parts = []
    for offset in block_offsets:
        part = lax.dynamic_slice_in_dim(gated_low, (place ^ offset) * block_len, block_len, 0)
        gated_parts.append(grid.swap(part, (0, offset)) if offset else part)
    branch = b_out
    for part, rows in zip(gated_parts, out_rows):
        branch = branch + dot_last(part, rows)
    resid = inputs + branch
    normed2, norm2_back = jax.vjp(layer_norm, resid, norm2_gain, norm2_bias)
    normed2_low = normed2.astype(LOW)

    normed2_all = jnp.concatenate(grid.gather(normed2_low, block_steps), axis=0)
    normed2_all = normed2_all.reshape(length, width)
    hidden = dot_last(normed2_all, up_rows) + b_up_here
    act, gelu_back = jax.vjp(exact_gelu, hidden)
    act_low = act.astype(LOW)
    grad_act = dot_plain(cot_all, down_rows)
    grad_hidden = gelu_back(grad_act)[0].astype(LOW)

    def to_tokens(partial):
        split = partial.astype(LOW).reshape(blocks, block_len, width)
        return grid.scatter(split[: blocks // 2], split[blocks // 2 :], block_steps).astype(WIDE)

    grad_normed2 = to_tokens(dot_plain(grad_hidden, up_rows))
    output = resid + to_tokens(dot_last(act_low, down_rows)) + b_down
    block_out = output.astype(LOW)[None]
    grad_b_up_here = jnp.sum(grad_hidden.astype(WIDE), axis=0)
    grad_b_down = jnp.sum(cot_flat.astype(WIDE), axis=0)

    def send_home(natural, order):
        natural = natural.astype(LOW).reshape(count_dp, -1, natural.shape[-1])
        return grid.scatter(*deal(natural, row, dp_offsets(order)), order)

    up_grad = send_home(dot_first(grad_hidden, normed2_all), up_order)
    down_grad = send_home(dot_first(cot_all, act_low), down_order)

    resid_part, grad_gain_two, grad_bias_two = norm2_back(grad_normed2)
    grad_resid = cot_flat.astype(WIDE) + resid_part
    grad_branch = grad_resid.astype(LOW)
    grad_b_out = jnp.sum(grad_branch.astype(WIDE), axis=0)
    grad_parts = []
    for index, offset in enumerate(block_offsets):
        part = dot_plain(grad_branch, out_rows[index]).astype(LOW)
        grad_parts.append((grid.swap(part, (0, offset)) if offset else part)[None])
    grad_gated = arrange(grad_parts, place, block_offsets).reshape(length, channels).astype(WIDE)
    out_sums = jnp.stack([dot_first(grad_branch, part).astype(LOW) for part in gated_parts], axis=0)
    out_sums = grid.scatter(out_sums[: blocks // 2], out_sums[blocks // 2 :], block_steps)
    out_grad = send_home(out_sums, out_dp_order)

    grad_gate_part = grad_gated * mixed
    grad_mixed = grad_gated * gate_part
    grad_conv_bias = jnp.sum(grad_mixed * inner, axis=0)
    grad_totals = cut(
        lax.dot_general(
            inverse_table,
            spread(grad_mixed),
            (((0,), (0,)), ((), ())),
            precision=HIGH,
            preferred_element_type=WIDE,
        ),
        blocks + num_docs - 1,
    )
    grad_entries = []
    grad_lags = [None] * blocks
    for i in range(blocks + num_docs - 1):
        lag = spectral_back(grad_totals[i], entries[i], edge)
        grad_lags[0] = lag if grad_lags[0] is None else grad_lags[0] + lag
        grad_entries.append(spectral_back(grad_totals[i], spectra[0], edge))
    for j in range(blocks):
        for i in range(j + 1, blocks):
            grad_entries[j] = grad_entries[j] + spectral_back(
                grad_totals[i], spectra[i - j], edge
            )
            lag = spectral_back(grad_totals[i], entries[j], edge)
            grad_lags[i - j] = lag if grad_lags[i - j] is None else grad_lags[i - j] + lag
    filter_grads = filter_back(jnp.concatenate(grad_lags, axis=1))[0]
    grad_inner = (
        collect(
            lax.dot_general(
                forward_table,
                jnp.concatenate(grad_entries, axis=1),
                (((0,), (0,)), ((), ())),
                precision=HIGH,
                preferred_element_type=WIDE,
            )
        )
        + direct * grad_mixed
    )
    grad_short = jnp.concatenate([grad_gate_part, grad_inner * value, grad_inner * mult], axis=1)
    grad_taps = jnp.stack(
        [
            jnp.sum(grad_short * proj, axis=0),
            jnp.sum(grad_short * prev_one, axis=0),
            jnp.sum(grad_short * prev_two, axis=0),
        ],
        axis=0,
    )
    grad_short_bias = jnp.sum(grad_short, axis=0)
    pass_one = grad_short * keep_one
    pass_two = grad_short * keep_two
    grad_proj = (
        taps[0] * grad_short
        + taps[1] * jnp.concatenate([pass_one[1:], jnp.zeros((1, three), WIDE)], axis=0)
        + taps[2] * jnp.concatenate([pass_two[2:], jnp.zeros((2, three), WIDE)], axis=0)
    )
    grad_proj_low = grad_proj.astype(LOW)
    grad_b_in = jnp.sum(grad_proj_low.astype(WIDE), axis=0)
    grad_in_rows = dot_first(grad_proj_low, normed_all)
    grad_in_split = grad_in_rows.reshape(count_dp, groups_here, share, width)
    in_grads = [send_home(grad_in_split[:, i], in_orders[i]) for i in range(groups_here)]
    grad_normed_part = dot_plain(grad_proj_low, in_rows).astype(LOW)
    grad_normed = grid.scatter(
        *deal(grad_normed_part.reshape(blocks, block_len, width), place, block_offsets), block_steps
    ).astype(WIDE)
    input_part, grad_gain_one, grad_bias_one = norm1_back(grad_normed)
    grad_input = (grad_resid + input_part)[None]

    def all_places(value):
        return arrange(grid.gather(value, block_steps), place, block_offsets)

    in_whole = all_places(jnp.concatenate(in_grads, axis=0))
    in_whole = in_whole.reshape(blocks, groups_here, share, width)
    in_whole = in_whole.transpose(3, 1, 0, 2).reshape(width, shard_in).astype(WIDE)
    if up_grad.shape[1] == down_grad.shape[1]:
        ff_whole = all_places(jnp.concatenate([up_grad, down_grad], axis=0))
        up_whole, down_whole = ff_whole[:, :piece], ff_whole[:, piece:]
    else:
        up_whole, down_whole = all_places(up_grad), all_places(down_grad)
    up_whole = up_whole.reshape(blocks * piece, width).T.astype(WIDE)
    down_whole = down_whole.reshape(blocks, w_down.shape[1], count_dp, piece)
    down_whole = down_whole.transpose(2, 0, 3, 1).reshape(hidden_width, w_down.shape[1])
    down_whole = down_whole.astype(WIDE)
    out_whole = all_places(out_grad).reshape(blocks, shard_out, bands, share)
    out_whole = out_whole.transpose(2, 0, 3, 1).reshape(width, shard_out).astype(WIDE)

    shared = [
        grad_gain_one,
        grad_bias_one,
        grad_b_out,
        grad_gain_two,
        grad_bias_two,
        grad_b_down,
        filter_grads[0],
        filter_grads[1],
        filter_grads[2],
        filter_grads[3],
    ]
    flat = jnp.concatenate([item.reshape(-1) for item in shared])
    unit = blocks * channels
    chunk = -(-flat.shape[0] // unit)
    flat = jnp.pad(flat, (0, chunk * unit - flat.shape[0])).reshape(blocks, chunk, channels)
    dealt = [lax.dynamic_slice_in_dim(flat, place ^ offset, 1, 0) for offset in block_offsets]
    half = blocks // 2
    shared_part = grid.scatter(
        jnp.concatenate(dealt[:half], axis=0), jnp.concatenate(dealt[half:], axis=0), block_steps
    )
    joined = jnp.concatenate(
        [
            shared_part,
            jnp.pad(grad_b_up_here, (0, -hidden_here % channels)).reshape(-1, channels),
            grad_b_in.reshape(3, channels),
            grad_taps.reshape(9, channels),
            grad_short_bias.reshape(3, channels),
            filter_grads[5][None],
            grad_conv_bias[None],
            filter_grads[4],
        ],
        axis=0,
    )
    for step in dp_steps:
        joined = joined + grid.swap(joined, step)
    every = all_places(joined)
    whole_flat = every[:, :chunk].reshape(-1)
    shared_out, at = [], 0
    for item in shared:
        shared_out.append(whole_flat[at : at + item.size].reshape(item.shape))
        at += item.size
    at = chunk + -(-hidden_here // channels)
    grad_b_up = every[:, chunk:at].reshape(blocks, -1)[:, :hidden_here]
    grad_b_up = grad_b_up.reshape(blocks, count_dp, piece)
    grad_b_up = grad_b_up.transpose(1, 0, 2).reshape(hidden_width)
    rest = every[:, at:].reshape(blocks, -1, bands, share).transpose(1, 2, 0, 3)
    rest = rest.reshape(-1, width)
    return (
        block_out,
        grad_input,
        shared_out[0],
        shared_out[1],
        in_whole,
        rest[:3].reshape(3 * width),
        rest[3:12].reshape(3, 3 * width),
        rest[12:15].reshape(3 * width),
        shared_out[6],
        shared_out[7],
        shared_out[8],
        shared_out[9],
        rest[17:],
        rest[15],
        rest[16],
        out_whole,
        shared_out[2],
        shared_out[3],
        shared_out[4],
        up_whole,
        grad_b_up,
        down_whole,
        shared_out[5],
    )


def input_back_call(inputs, kept, arrived, gain, grad_resid):
    tokens, width = inputs.shape

    def body(in_ref, kept_ref, arrived_ref, gain_ref, resid_ref, out_ref):
        grad = kept_ref[...].astype(WIDE) + arrived_ref[...].astype(WIDE)
        normal, scale = norm_parts(in_ref[...].astype(WIDE))
        scaled = grad * gain_ref[...]
        back = scaled - jnp.mean(scaled, axis=-1, keepdims=True)
        back = back - normal * jnp.mean(scaled * normal, axis=-1, keepdims=True)
        out_ref[...] = resid_ref[...] + back * scale

    return pl.pallas_call(
        body,
        out_shape=jax.ShapeDtypeStruct((tokens, width), WIDE),
        in_specs=[VMEM_SPACE] * 5,
        out_specs=VMEM_SPACE,
        compiler_params=pltpu.CompilerParams(vmem_limit_bytes=LIMIT),
        cost_estimate=cost(4),
    )(inputs, kept, arrived, gain, grad_resid)


def mark_call(value):
    def body(in_ref, out_ref):
        out_ref[...] = in_ref[...]

    return pl.pallas_call(
        body,
        out_shape=jax.ShapeDtypeStruct(value.shape, value.dtype),
        in_specs=[VMEM_SPACE],
        out_specs=VMEM_SPACE,
        compiler_params=pltpu.CompilerParams(vmem_limit_bytes=LIMIT // 8),
        cost_estimate=cost(15),
    )(value)


def after(value, *others):
    return lax.optimization_barrier((value, *others))[0]


def together(values, *others):
    return lax.optimization_barrier((*values, *others))[: len(values)]


def local_kernels(
    block_in,
    doc_starts,
    norm1_gain,
    norm1_bias,
    w_in,
    b_in,
    short_taps,
    short_bias,
    filter_w1,
    filter_b1,
    filter_w2,
    filter_b2,
    filter_w3,
    filter_decay,
    conv_bias,
    w_out,
    b_out,
    norm2_gain,
    norm2_bias,
    w_up,
    b_up,
    w_down,
    b_down,
    cotangent,
):
    count_dp, blocks = lax.axis_size("dp"), lax.axis_size("block")
    grid = Grid(count_dp, blocks)
    row, place = grid.row, grid.place
    places = jnp.stack([row, place]).astype(jnp.int32)
    _, block_len, width = block_in.shape
    dp_steps = grid.dp_steps
    block_steps = grid.chip_steps + [grid.core_step]
    block_offsets = [b for _, b in offsets_of(block_steps)]
    shard_in = w_in.shape[1]
    share = math.gcd(width, shard_in) // blocks
    shard_up = w_up.shape[1]
    starts = doc_starts[0]
    inputs = block_in.reshape(block_len, width)
    cot = cotangent.reshape(block_len, width)
    forward_table, inverse_table, _, _ = transform_tables(block_len)
    forward_three, inverse_three = triple(forward_table), triple(inverse_table)
    forward_back, inverse_back = triple(forward_table.T), triple(inverse_table.T)
    table = turned_table(position_table(block_len * blocks, filter_w1.shape[0])[0])
    third_at = 17

    order_one = dp_steps[::-1]
    order_two = order_one[:-2] + order_one[:-3:-1]
    core_step = grid.core_step

    def dp_offsets(steps):
        return [a for a, _ in offsets_of(steps)]

    parts = 2
    in_orders = [order_one, order_two]
    in_offsets = [dp_offsets(order) for order in in_orders]
    up_order, down_order, out_order = order_one, order_two, order_one
    up_offsets, down_offsets, out_offsets = map(dp_offsets, (up_order, down_order, out_order))
    core, chip = core_step, block_steps[0]

    def joined(pieces):
        return jnp.concatenate(pieces, axis=0)

    def split(values, *counts):
        parts, at = [], 0
        for count in counts:
            parts.append(list(values[at : at + count]))
            at += count
        return parts

    *in_own, out_own, normed_own = first_call(
        places,
        blocks,
        share,
        w_in,
        w_out,
        inputs,
        (norm1_gain[None], norm1_bias[None]),
        parts,
    )
    in_got = [grid.swap(own, order[0]) for own, order in zip(in_own, in_orders)]
    normed_got = grid.swap(normed_own, chip)
    out_got = grid.swap(out_own, out_order[0])
    second = second_call(
        after(places, normed_own),
        blocks,
        share,
        w_up,
        w_down,
        b_up[None],
        [
            (b_in[None], 3),
            (short_taps, 9),
            (short_bias[None], 3),
            (filter_decay[None], 1),
            (conv_bias[None], 1),
        ],
        [(filter_w1, filter_b1[None]), (filter_w2, filter_b2[None])],
        filter_w3,
    )

    in_got, (out_got,), second = split(together((*in_got, out_got, *second)), parts, 1, 6)
    up_own, down_own, b_up_own, vectors, layer_one, layer_two = second
    in_held = [joined(pair) for pair in zip(in_own, in_got)]
    out_held = joined((out_own, out_got))
    in_got = [grid.swap(held, order[1]) for held, order in zip(in_held, in_orders)]
    out_got = grid.swap(out_held, out_order[1])
    up_got = grid.swap(up_own, up_order[0])
    spectra, layer_one = filter_call(
        block_len, blocks, table, forward_three, layer_one, layer_two, vectors, third_at
    )

    in_got, rest = split(
        together((*in_got, out_got, up_got, normed_got, layer_one, layer_two, down_own)), parts, 6
    )
    out_got, up_got, normed_got, layer_one, layer_two, down_own = rest
    in_last = [joined(pair) for pair in zip(in_held, in_got)]
    out_held = joined((out_held, out_got))
    up_held = joined((up_own, up_got))
    normed_held = joined((normed_own, normed_got))
    in_last_got = [grid.swap(held, order[2]) for held, order in zip(in_last, in_orders)]
    normed_last = grid.swap(normed_held, core)
    out_got = grid.swap(out_held, out_order[2])
    down_got = grid.swap(down_own, down_order[0])
    cot_own = after(cot, normed_got)[None]
    cot_got = grid.swap(cot_own, chip)
    layer_two = mark_call(layer_two)

    in_last_got, rest = split(
        together((*in_last_got, out_got, down_got, normed_last, cot_got, layer_two)), parts, 5
    )
    out_got, down_got, normed_last, cot_got, layer_two = rest
    down_held = joined((down_own, down_got))
    out_whole = joined((out_held, out_got))[None]
    cot_held = joined((cot_own, cot_got))
    up_two = grid.swap(up_held, up_order[1])
    down_two = grid.swap(down_held, down_order[1])
    out_got = grid.swap(out_whole, chip)
    cot_last = grid.swap(cot_held, core)
    made = conv_call(
        block_len,
        blocks,
        places,
        starts,
        [normed_held, normed_last],
        [list(pair) for pair in zip(in_last, in_last_got)],
        in_offsets,
        block_offsets,
        vectors,
        spectra,
        forward_three,
        inverse_three,
    )

    gated_own, (proj, entries, mixed, in_rows, normed) = made[:blocks], made[blocks:]
    gated_own, (up_two, down_two, out_got, cot_last, layer_two) = split(
        together((*gated_own, up_two, down_two, out_got, cot_last, layer_two)), blocks, 5
    )
    gated_got = [
        grid.swap(part, (0, offset)) for part, offset in zip(gated_own[1:], block_offsets[1:])
    ]
    out_held = joined((out_whole, out_got))
    out_last = grid.swap(out_held, core)
    up_three = grid.swap(up_held, up_order[2])
    down_three = grid.swap(down_held, down_order[2])
    layer_two = mark_call(layer_two)

    gated_got, (out_last, layer_two) = split(
        together((*gated_got, out_last, layer_two)), blocks - 1, 2
    )
    gated_parts = [gated_own[0], *gated_got]
    out_pieces = [out_held, out_last]
    resid, normed2 = branch_call(
        places,
        inputs,
        gated_parts,
        out_pieces,
        out_offsets,
        (b_out[None], norm2_gain[None], norm2_bias[None]),
    )
    normed2, up_three, down_three = together((normed2, up_three, down_three))
    normed2_got = grid.swap(normed2[None], chip)
    up_four = grid.swap(up_two, up_order[2])
    down_four = grid.swap(down_two, down_order[2])

    normed2_got, up_four, down_four = together((normed2_got, up_four, down_four))
    normed2_held = joined((normed2[None], normed2_got))
    normed2_last = grid.swap(normed2_held, core)
    made = forward_call(
        places,
        [normed2_held, normed2_last],
        [cot_held, cot_last],
        [up_held, up_two, up_three, up_four],
        [down_held, down_two, down_three, down_four],
        up_offsets,
        down_offsets,
        b_up_own,
    )
    block_kept, block_sent, grad_kept, grad_sent = made[:4]
    act, grad_hidden, b_up_sum = made[4:]

    grad_got = grid.swap(grad_sent, core)
    block_got = grid.swap(block_sent, core)

    grad_kept, grad_sent = halves(grad_kept, grad_got)
    grad_got = grid.swap(grad_sent, chip)
    dealt = weight_grad_call(
        after(places, grad_kept),
        [([grad_hidden], [normed2_held, normed2_last]), ([cot_held, cot_last], [act])],
        [up_offsets, down_offsets],
    )

    up_dealt, down_dealt = split(dealt, 4, 4)
    up_got = grid.swap(up_dealt[3], up_order[2])
    down_got = grid.swap(down_dealt[3], down_order[2])

    grad_got, block_got, *dealt = together(
        (grad_got, block_got, *up_dealt[:3], *down_dealt[:3])
    )
    up_dealt, down_dealt = split(dealt, 3, 3)
    made = branch_back_call(
        places, resid, grad_kept[0], grad_got[0], cot, out_pieces, out_offsets, norm2_gain[None]
    )
    grad_resid, grad_branch, norm2_sums = made[blocks:]
    made, (up_got, down_got, grad_branch) = split(
        together((*made[:blocks], up_got, down_got, grad_branch)), blocks, 3
    )
    grad_own = made[0]
    grad_got = [
        grid.swap(part, (0, offset)) for part, offset in zip(made[1:], block_offsets[1:])
    ]
    up_high = add_low(up_dealt[1], up_got)
    down_high = add_low(down_dealt[1], down_got)
    out_kept, out_sent = out_grad_call(places, grad_branch, gated_parts, out_offsets)

    grad_got, rest = split(
        together((*grad_got, out_kept, out_sent, block_kept, up_high, down_high)), blocks - 1, 5
    )
    out_kept, out_sent, block_kept, up_high, down_high = rest
    grad_parts = [grad_own, *grad_got]
    up_got = grid.swap(up_dealt[2], up_order[2])
    down_got = grid.swap(down_dealt[2], down_order[2])
    out_got = grid.swap(out_sent, core)
    block_kept, block_sent = halves(block_kept, block_got)
    block_got = grid.swap(block_sent, chip)
    grad_lags, direct_sum, grad_short = back_call(
        block_len,
        blocks,
        places,
        starts,
        grad_parts,
        block_offsets,
        vectors,
        spectra,
        proj,
        entries,
        mixed,
        inverse_back,
        forward_back,
    )

    up_got, down_got, out_got, block_got, direct_sum = together(
        (up_got, down_got, out_got, block_got, direct_sum)
    )
    up_low = add_low(up_dealt[0], up_got)
    down_low = add_low(down_dealt[0], down_got)
    out_kept, out_sent = halves(out_kept, out_got)
    up_got = grid.swap(up_high, up_order[1])
    down_got = grid.swap(down_high, down_order[1])
    out_got = grid.swap(out_sent, chip)
    made = project_back_call(
        block_len,
        blocks,
        places,
        starts,
        in_offsets,
        block_offsets,
        vectors,
        (norm1_gain[None], norm1_bias[None]),
        direct_sum,
        grad_short,
        proj,
        in_rows,
        normed,
    )

    made, (up_got, down_got, out_got, layer_one) = split(
        together((*made, up_got, down_got, out_got, layer_one)), len(made), 4
    )
    in_dealt = [(made[2 * i], made[2 * i + 1]) for i in range(parts)]
    normed_kept, normed_sent, sums, norm1_sums = made[2 * parts :]
    up_kept, up_sent = halves(up_low, up_got)
    down_kept, down_sent = halves(down_low, down_got)
    out_kept, out_sent = halves(out_kept, out_got)
    in_got = [grid.swap(pair[1], order[2]) for pair, order in zip(in_dealt, in_orders)]
    normed_got = grid.swap(normed_sent, core)
    up_got = grid.swap(up_sent, up_order[0])
    out_got = grid.swap(out_sent, out_order[2])
    layer_one_grad, layer_two_grad, third_grad, decay_grad = filter_back_call(
        block_len, blocks, table, forward_back, layer_one, layer_two, vectors, third_at, grad_lags
    )
    small = small_pack_call(
        [norm2_sums, norm1_sums],
        [layer_one_grad, layer_two_grad],
        b_up_sum,
        sums,
        third_grad,
        decay_grad,
    )

    in_got, (normed_got, up_got, out_got, small) = split(
        together((*in_got, normed_got, up_got, out_got, small)), parts, 4
    )
    in_half = [halves(pair[0], got) for pair, got in zip(in_dealt, in_got)]
    normed_kept, normed_sent = halves(normed_kept, normed_got)
    out_kept, out_sent = halves(out_kept, out_got)
    in_got = [grid.swap(pair[1], order[1]) for pair, order in zip(in_half, in_orders)]
    normed_got = grid.swap(normed_sent, chip)
    small_got = grid.swap(small, dp_steps[0])
    out_got = grid.swap(out_sent, out_order[1])
    down_got = grid.swap(down_sent, down_order[0])
    up_grad = add_low(up_kept, up_got)

    in_got, (normed_got, small_got, out_got, down_got) = split(
        together((*in_got, normed_got, small_got, out_got, down_got)), parts, 4
    )
    ff_own = jnp.concatenate([up_grad, add_low(down_kept, down_got)], axis=1)
    in_half = [halves(pair[0], got) for pair, got in zip(in_half, in_got)]
    out_kept, out_sent = halves(out_kept, out_got)
    small = small + small_got
    in_got = [grid.swap(pair[1], order[0]) for pair, order in zip(in_half, in_orders)]
    small_got = grid.swap(small, dp_steps[1])
    ff_got = grid.swap(ff_own, chip)
    out_got = grid.swap(out_sent, out_order[0])
    grad_input = input_back_call(
        inputs, normed_kept[0], normed_got[0], norm1_gain[None], grad_resid
    )[None]

    in_got, (small_got, ff_got, out_got, grad_input) = split(
        together((*in_got, small_got, ff_got, out_got, grad_input)), parts, 4
    )
    in_grad = jnp.concatenate(
        [add_low(pair[0], got) for pair, got in zip(in_half, in_got)], axis=1
    )
    out_grad = add_low(out_kept, out_got)
    small = small + small_got
    ff_held = joined((ff_own, ff_got))
    ff_last = grid.swap(ff_held, core)
    in_got = grid.swap(in_grad, chip)
    out_got = grid.swap(out_grad, chip)
    small = small.astype(LOW)
    small_got = grid.swap(small, dp_steps[2])
    output = resid + block_kept[0].astype(WIDE) + block_got[0].astype(WIDE) + b_down
    block_out = output.astype(LOW)[None]

    ff_last, in_got, out_got, small_got, block_out = together(
        (ff_last, in_got, out_got, small_got, block_out)
    )
    in_held, out_held = joined((in_grad, in_got)), joined((out_grad, out_got))
    small = add_low(small, small_got)[None]
    small_got = grid.swap(small, chip)
    in_last = grid.swap(in_held, core)
    out_last = grid.swap(out_held, core)
    up_whole, down_whole = wide_call(
        places, block_offsets, [ff_held, ff_last], up_own.shape[1], count_dp
    )

    small_got, in_last, out_last, up_whole = together((small_got, in_last, out_last, up_whole))
    small_held = joined((small, small_got))
    small_last = grid.swap(small_held, core)
    in_whole = in_wide_call(places, block_offsets, share, [in_held, in_last])
    out_whole = out_wide_call(places, block_offsets, share, [out_held, out_last])
    small_pieces = [small_held, small_last]
    (
        grad_b_out,
        grad_gain_two,
        grad_bias_two,
        grad_b_down,
        grad_gain_one,
        grad_bias_one,
        grad_w1,
        grad_b1,
        grad_w2,
        grad_b2,
        grad_b_up,
        grad_b_in,
        grad_taps,
        grad_short,
        grad_direct,
        grad_w3,
        grad_decay,
    ) = small_out_call(
        places,
        block_offsets,
        share,
        small_pieces,
        norm2_sums.shape[0] + norm1_sums.shape[0],
        [filter_w1.shape, filter_w2.shape],
        b_up_sum.shape[1],
        shard_up,
    )
    return (
        block_out,
        grad_input,
        grad_gain_one[0],
        grad_bias_one[0],
        in_whole,
        grad_b_in[0],
        grad_taps,
        grad_short[0],
        grad_w1,
        grad_b1[0],
        grad_w2,
        grad_b2[0],
        grad_w3,
        grad_decay[0],
        grad_direct[0],
        out_whole,
        grad_b_out[0],
        grad_gain_two[0],
        grad_bias_two[0],
        up_whole,
        grad_b_up[0],
        down_whole,
        grad_b_down[0],
    )


def local(*args):
    blocks, width, shard_in = lax.axis_size("block"), args[0].shape[2], args[4].shape[1]
    channels, group = width // blocks, math.gcd(width, shard_in)
    fits = (
        channels % 128 == 0
        and group // blocks % 32 == 0
        and shard_in // blocks % 32 == 0
        and args[19].shape[1] // blocks % 128 == 0
        and args[15].shape[1] % 128 == 0
        and args[10].shape[1] * blocks == channels
        and lax.axis_size("dp") > 1
    )
    return (local_kernels if fits else local_plain)(*args)


def solution(mesh):
    placed = (
        P("dp", "block", None),
        P("dp", None),
        P(),
        P(),
        P(None, "dp"),
        P(),
        P(),
        P(),
        P(),
        P(),
        P(),
        P(),
        P(),
        P(),
        P(),
        P(None, "dp"),
        P(),
        P(),
        P(),
        P(None, "dp"),
        P(),
        P(None, "dp"),
        P(),
        P("dp", "block", None),
    )
    return jax.shard_map(
        local,
        mesh=mesh,
        in_specs=placed,
        out_specs=(
            P("dp", "block", None),
            P("dp", "block", None),
            P(),
            P(),
            P(None, "dp"),
            P(),
            P(),
            P(),
            P(),
            P(),
            P(),
            P(),
            P(),
            P(),
            P(),
            P(None, "dp"),
            P(),
            P(),
            P(),
            P(None, "dp"),
            P(),
            P(None, "dp"),
            P(),
        ),
        check_vma=False,
    )
```
